32 devices in a mesh: section: 2 (over y), dp: 8 (over z, x), tensor: 2 (over core).
Axes of the slice: x: 2, y: 2, z: 4, core: 2. Of those that a mesh axis runs over, the one named last changes fastest.
Arguments:
- mel: bfloat16 [16, 3000, 80], P('dp'), may hold values from -6 to 6
- conv_first: bfloat16 [3, 80, 512], replicated, may hold values from -0.375 to 0.375
- conv_second: bfloat16 [3, 512, 512], replicated, may hold values from -0.15625 to 0.15625
- enc_gain: float32 [3, 512], replicated, may hold values from 0.5 to 1.5
- enc_shift: float32 [3, 512], replicated, may hold values from -3 to 3
- enc_qkv: bfloat16 [512, 1536], P(None, 'tensor'), may hold values from -0.25 to 0.25
- enc_proj: bfloat16 [512, 512], P('tensor'), may hold values from -6 to 6
- enc_up: bfloat16 [512, 2048], P(None, 'tensor'), may hold values from -0.25 to 0.25
- enc_down: bfloat16 [2048, 512], P('tensor'), may hold values from -0.125 to 0.125
- cross_kv: bfloat16 [512, 1024], P(None, 'tensor'), may hold values from -0.25 to 0.25
- text: bfloat16 [16, 448, 512], P('dp', 'tensor'), may hold values from -6 to 6
- lengths: int32 [16], P('dp'), may hold values from 5 to 448, as said below
- dec_gain: float32 [3, 512], replicated, may hold values from 0.5 to 1.5
- dec_shift: float32 [3, 512], replicated, may hold values from -3 to 3
- dec_qkv: bfloat16 [512, 1536], P(None, 'tensor'), may hold values from -0.25 to 0.25
- dec_proj: bfloat16 [512, 512], P('tensor'), may hold values from -1.5 to 1.5
- cross_query: bfloat16 [512, 512], P(None, 'tensor'), may hold values from -0.25 to 0.25
- cross_proj: bfloat16 [512, 512], P('tensor'), may hold values from -6 to 6
- dec_up: bfloat16 [512, 2048], P(None, 'tensor'), may hold values from -0.25 to 0.25
- dec_down: bfloat16 [2048, 512], P('tensor'), may hold values from -0.125 to 0.125
- cotangent: bfloat16 [16, 448, 512], P('dp', 'tensor'), may hold values from -6 to 6
Outputs:
- decoded: bfloat16 [16, 448, 512], P('dp', 'tensor', 'section')
- text_grad: float32 [16, 448, 512], P('dp', 'tensor', 'section')
- conv_first_grad: float32 [3, 80, 512], P(None, None, ('dp', 'tensor'))
- conv_second_grad: float32 [3, 512, 512], P(None, None, ('dp', 'tensor'))
- enc_gain_grad: float32 [3, 512], P(None, ('dp', 'tensor'))
- enc_shift_grad: float32 [3, 512], P(None, ('dp', 'tensor'))
- enc_qkv_grad: float32 [512, 1536], P(('section', 'dp'), 'tensor')
- enc_proj_grad: float32 [512, 512], P('tensor', ('section', 'dp'))
- enc_up_grad: float32 [512, 2048], P(('section', 'dp'), 'tensor')
- enc_down_grad: float32 [2048, 512], P('tensor', ('section', 'dp'))
- cross_kv_grad: float32 [512, 1024], P(('section', 'dp'), 'tensor')
- dec_gain_grad: float32 [3, 512], P(None, ('dp', 'tensor'))
- dec_shift_grad: float32 [3, 512], P(None, ('dp', 'tensor'))
- dec_qkv_grad: float32 [512, 1536], P(('section', 'dp'), 'tensor')
- dec_proj_grad: float32 [512, 512], P('tensor', ('section', 'dp'))
- cross_query_grad: float32 [512, 512], P(('section', 'dp'), 'tensor')
- cross_proj_grad: float32 [512, 512], P('tensor', ('section', 'dp'))
- dec_up_grad: float32 [512, 2048], P(('section', 'dp'), 'tensor')
- dec_down_grad: float32 [2048, 512], P('tensor', ('section', 'dp'))
The draws below stay inside these ranges and needn't reach their ends.
Inputs may be any that keep to these rules, and one draw needn't show every extreme that they name: `lengths`: in each aligned block of 2 clips (those of one index of dp), one text has all 448 tokens.
All inputs are finite; a program needn't handle non-finite values.
Results may differ from the reference program's by a relative error of at most 0.013.
Values may be sent and summed in bfloat16 or wider, within the bound.
No kernel may reach another device: no remote copies, remote signals or barrier semaphores. Data moves between devices by JAX's collectives and lax.ppermute only.
A program may use at most 256 MiB of HBM per device.

```python
import math
import jax
import jax.numpy as jnp
from jax import lax

D = 512
FF = 2048
MEL = 80
FRAMES = 1500
TEXT = 448
MICRO = 2
HEAD_DIM = 64
CLIPS = 16


def draw_lengths(key, part):
    key = jax.random.fold_in(key, 7)
    key_values, key_spots = jax.random.split(key)
    drawn = jax.random.randint(key_values, (CLIPS,), 5, TEXT + 1)
    spots = jax.random.randint(key_spots, (CLIPS // MICRO,), 0, MICRO)
    clip_index = jnp.arange(CLIPS)
    chosen = spots[clip_index // MICRO] == clip_index % MICRO
    return jnp.where(chosen, TEXT, drawn).astype(jnp.int32)


def steps_of(rng, dims, cuts, low, largest):
    loudness, own = 1.0, jax.random.fold_in(rng, 6)
    for dim, parts in cuts:
        steps = jnp.exp(jax.random.uniform(jax.random.fold_in(own, dim), (parts,), jnp.float32, low / len(cuts), largest / len(cuts)))
        loudness = loudness * jnp.repeat(steps, dims[dim] // parts).reshape([-1 if axis == dim else 1 for axis in range(len(dims))])
    return loudness


def gaussian(own_key, extent, deviation, most, shards=(), kind=jnp.bfloat16):
    values = jax.random.normal(own_key, extent, jnp.float32) * deviation
    if len(shards) > 0:
        values = steps_of(own_key, extent, shards, -0.22, 0.18) * values
    return jnp.clip(values, min=-most, max=most).astype(kind)


def setup_inputs(seed: int = 0) -> dict:
    seeds = jax.random.split(jax.random.key(seed), 22)
    mel = gaussian(seeds[0], (CLIPS, 2 * FRAMES, MEL), 1.0, 6.0, ((0, 8),))
    conv_first = gaussian(seeds[1], (3, MEL, D), (3 * MEL) ** -0.5, 0.375)
    conv_second = gaussian(seeds[2], (3, D, D), (3 * D) ** -0.5, 0.15625)
    enc_gain = jnp.clip(1.0 + 0.1 * jax.random.normal(seeds[3], (3, D), jnp.float32), 0.5, 1.5)
    enc_shift = gaussian(seeds[4], (3, D), 0.3, 3.0, (), jnp.float32)
    enc_qkv = gaussian(seeds[5], (D, 3 * D), D ** -0.5, 0.25, ((1, 2),))
    enc_proj = gaussian(seeds[6], (D, D), (max(1, 4 * D // FRAMES)) ** -0.5, 6.0, ((0, 2),))
    enc_up = gaussian(seeds[7], (D, FF), D ** -0.5, 0.25, ((1, 2),))
    enc_down = gaussian(seeds[8], (FF, D), FF ** -0.5, 0.125, ((0, 2),))
    cross_kv = gaussian(seeds[9], (D, 2 * D), D ** -0.5, 0.25, ((1, 2),))
    text = gaussian(seeds[10], (CLIPS, TEXT, D), 1.0, 6.0, ((0, 8), (1, 2)))
    lengths = draw_lengths(jax.random.fold_in(seeds[21], 71), 0)
    dec_gain = jnp.clip(1.0 + 0.1 * jax.random.normal(seeds[12], (3, D), jnp.float32), 0.5, 1.5)
    dec_shift = gaussian(seeds[13], (3, D), 0.3, 3.0, (), jnp.float32)
    dec_qkv = gaussian(seeds[14], (D, 3 * D), D ** -0.5, 0.25, ((1, 2),))
    dec_proj = gaussian(seeds[15], (D, D), (max(1, 16 * D // TEXT)) ** -0.5, 1.5, ((0, 2),))
    cross_query = gaussian(seeds[16], (D, D), D ** -0.5, 0.25, ((1, 2),))
    cross_proj = gaussian(seeds[17], (D, D), (max(1, 4 * D // FRAMES)) ** -0.5, 6.0, ((0, 2),))
    dec_up = gaussian(seeds[18], (D, FF), D ** -0.5, 0.25, ((1, 2),))
    dec_down = gaussian(seeds[19], (FF, D), FF ** -0.5, 0.125, ((0, 2),))
    cotangent = gaussian(seeds[20], (CLIPS, TEXT, D), 1.0, 6.0, ((0, 8), (1, 2)))
    return dict(mel=mel, conv_first=conv_first, conv_second=conv_second, enc_gain=enc_gain, enc_shift=enc_shift, enc_qkv=enc_qkv, enc_proj=enc_proj, enc_up=enc_up, enc_down=enc_down, cross_kv=cross_kv, text=text, lengths=lengths, dec_gain=dec_gain, dec_shift=dec_shift, dec_qkv=dec_qkv, dec_proj=dec_proj, cross_query=cross_query, cross_proj=cross_proj, dec_up=dec_up, dec_down=dec_down, cotangent=cotangent)


@jax.custom_vjp
def low(v):
    return lax.optimization_barrier(v.astype(jnp.bfloat16)).astype(jnp.float32)

@jax.custom_vjp
def low_back(v):
    return v

def low_keep(v):
    return (low(v), None)

def low_pass(kept, grad):
    return (grad,)

def back_keep(v):
    return (v, None)

def back_low(kept, grad):
    return (low(grad),)
low.defvjp(low_keep, low_pass)
low_back.defvjp(back_keep, back_low)
NEG = -1000000000.0
EPS = 1e-05
HIGH = lax.Precision.HIGHEST

def matmul_high(left, right):
    return jnp.dot(left, right, precision=HIGH)

def norm_rows(residual, gain_row, bias_row):
    centre = residual - lax.optimization_barrier(jnp.mean(residual, axis=-1, keepdims=True))
    spread = lax.optimization_barrier(jnp.mean(centre * centre, axis=-1, keepdims=True))
    return centre * lax.rsqrt(spread + EPS) * gain_row + bias_row

def gelu_exact(values_in):
    return jax.nn.gelu(values_in, approximate=False)

def sinusoid_table(count, width_all):
    step_size = math.log(10000.0) / (width_all // 2 - 1)
    rates = jnp.exp(-step_size * jnp.arange(width_all // 2, dtype=jnp.float32))
    angles = jnp.arange(count, dtype=jnp.float32)[:, None] * rates[None, :]
    return jnp.concatenate([jnp.sin(angles), jnp.cos(angles)], axis=1)

def heads_attend(queries, keys, values_in, key_mask):
    scaling = queries.shape[-1] ** (-0.5)

    def single_head(operands):
        query_head, key_head, value_head = operands
        scores = low_back(matmul_high(query_head, key_head.T) * scaling)
        if key_mask is not None:
            scores = jnp.where(key_mask, scores, NEG)
        probabilities = low(jax.nn.softmax(scores, axis=-1))
        return low_back(low(matmul_high(probabilities, value_head)))
    return lax.map(jax.checkpoint(single_head), (queries, keys, values_in))

def attention_branch(residual, gain_row, bias_row, w_qkv, w_proj, key_mask):
    row_count = residual.shape[0]
    head_count = w_qkv.shape[1] // (3 * HEAD_DIM)
    normed = low(norm_rows(residual, gain_row, bias_row))
    packed = low_back(low(matmul_high(normed, w_qkv)))
    packed = packed.reshape(row_count, head_count, 3, HEAD_DIM).transpose(2, 1, 0, 3)
    mixed = heads_attend(packed[0], packed[1], packed[2], key_mask)
    merged = mixed.transpose(1, 0, 2).reshape(row_count, head_count * HEAD_DIM)
    return low_back(matmul_high(merged, w_proj))

def mlp_branch(residual, gain_row, bias_row, w_up, w_down):
    normed = low(norm_rows(residual, gain_row, bias_row))
    hidden = low(gelu_exact(low_back(matmul_high(normed, w_up))))
    return low_back(matmul_high(hidden, w_down))

def clip_forward(weights, text_clip, mel_clip, length):
    conv_first, conv_second, enc_gain, enc_shift, enc_qkv, enc_proj, enc_up, enc_down, cross_kv, dec_gain, dec_shift, dec_qkv, dec_proj, cross_query, cross_proj, dec_up, dec_down = weights
    frame_count = mel_clip.shape[0] // 2
    padded = jnp.pad(mel_clip, ((1, 1), (0, 0)))
    mel_cat = jnp.concatenate([padded[tap:tap + 2 * frame_count] for tap in range(3)], axis=1)
    first_act = low(gelu_exact(low_back(matmul_high(mel_cat, conv_first.reshape(-1, D)))))
    padded = jnp.pad(first_act, ((1, 1), (0, 0)))
    second_cat = jnp.concatenate([padded[tap:tap + 2 * frame_count:2] for tap in range(3)], axis=1)
    second_pre = low_back(matmul_high(second_cat, conv_second.reshape(-1, D)))
    residual = gelu_exact(second_pre) + sinusoid_table(frame_count, D)
    residual = residual + attention_branch(residual, enc_gain[0], enc_shift[0], enc_qkv, enc_proj, None)
    residual = residual + mlp_branch(residual, enc_gain[1], enc_shift[1], enc_up, enc_down)
    memory = low(norm_rows(residual, enc_gain[2], enc_shift[2]))
    head_count = cross_kv.shape[1] // (2 * HEAD_DIM)
    key_values = low_back(low(matmul_high(memory, cross_kv)))
    key_values = key_values.reshape(frame_count, head_count, 2, HEAD_DIM).transpose(2, 1, 0, 3)
    slot_count = text_clip.shape[0]
    position = jnp.arange(slot_count)
    self_mask = (position[:, None] >= position[None, :]) & (position[None, :] < length)
    stream_dec = text_clip
    stream_dec = stream_dec + attention_branch(stream_dec, dec_gain[0], dec_shift[0], dec_qkv, dec_proj, self_mask)
    normed = low(norm_rows(stream_dec, dec_gain[1], dec_shift[1]))
    queries = low_back(low(matmul_high(normed, cross_query)))
    queries = queries.reshape(slot_count, head_count, HEAD_DIM).transpose(1, 0, 2)
    crossed = heads_attend(queries, key_values[0], key_values[1], None)
    crossed = crossed.transpose(1, 0, 2).reshape(slot_count, head_count * HEAD_DIM)
    stream_dec = stream_dec + low_back(matmul_high(crossed, cross_proj))
    stream_dec = stream_dec + mlp_branch(stream_dec, dec_gain[2], dec_shift[2], dec_up, dec_down)
    live_rows = (position < length).astype(stream_dec.dtype)[:, None]
    return stream_dec * live_rows

def reference(mel, conv_first, conv_second, enc_gain, enc_shift, enc_qkv, enc_proj, enc_up, enc_down, cross_kv, text, lengths, dec_gain, dec_shift, dec_qkv, dec_proj, cross_query, cross_proj, dec_up, dec_down, cotangent):
    weights = tuple((weight.astype(jnp.float32) for weight in (conv_first, conv_second, enc_gain, enc_shift, enc_qkv, enc_proj, enc_up, enc_down, cross_kv, dec_gain, dec_shift, dec_qkv, dec_proj, cross_query, cross_proj, dec_up, dec_down)))

    def one_clip(running, element):
        mel_clip, text_clip, length, cot_clip = element

        def forward(params, text_value):
            return clip_forward(params, text_value, mel_clip.astype(jnp.float32), length)
        output, pull_back = jax.vjp(forward, weights, text_clip.astype(jnp.float32))
        grads, grad_text = pull_back(cot_clip.astype(jnp.float32))
        running = jax.tree.map(lambda left, right: left + right, running, grads)
        return (running, (output.astype(jnp.bfloat16), grad_text))
    start = jax.tree.map(jnp.zeros_like, weights)
    running, (decoded, text_grad) = lax.scan(one_clip, start, (mel, text, lengths, cotangent))
    grad_c1, grad_c2, grad_eg, grad_es, grad_eq, grad_ep, grad_eu, grad_ed, grad_kv, grad_dg, grad_ds, grad_dq, grad_dp, grad_cq, grad_cp, grad_du, grad_dd = running
    return (decoded, text_grad, grad_c1, grad_c2, grad_eg, grad_es, grad_eq, grad_ep, grad_eu, grad_ed, grad_kv, grad_dg, grad_ds, grad_dq, grad_dp, grad_cq, grad_cp, grad_du, grad_dd)
```

```python
import functools
import math

import jax
import jax.numpy as jnp
import numpy as np
from jax import lax
from jax.experimental import pallas as pl
from jax.experimental.pallas import tpu as pltpu
from jax.sharding import PartitionSpec as P

HEAD_DIM = 64
NEG = -1000000000.0
EPS = 1e-05
CHUNK = 256
BF, F32 = jnp.bfloat16, jnp.float32
INV_SQRT2 = 0.7071067811865476
INV_SQRT2PI = 0.3989422804014327


def dot_nn(left, right):
    return lax.dot_general(left, right, (((1,), (0,)), ((), ())), preferred_element_type=F32)


def dot_nt(left, right):
    return lax.dot_general(left, right, (((1,), (1,)), ((), ())), preferred_element_type=F32)


def dot_tn(left, right):
    return lax.dot_general(left, right, (((0,), (0,)), ((), ())), preferred_element_type=F32)


def norm_stats(rows):
    centre = rows - jnp.mean(rows, axis=-1, keepdims=True)
    spread = jnp.mean(centre * centre, axis=-1, keepdims=True)
    inverse = lax.rsqrt(spread + EPS)
    return centre * inverse, inverse


def norm_back(unit, inverse, gain_row, upstream):
    scaled = upstream * gain_row
    first = jnp.mean(scaled, axis=-1, keepdims=True)
    second = jnp.mean(scaled * unit, axis=-1, keepdims=True)
    grad_rows = inverse * (scaled - first - unit * second)
    grad_gain = jnp.sum(upstream * unit, axis=0, keepdims=True)
    grad_bias = jnp.sum(upstream, axis=0, keepdims=True)
    return grad_rows, grad_gain, grad_bias


def gelu_pair(v):
    size = jnp.abs(v)
    part = 1.0 / (1.0 + (0.3275911 * INV_SQRT2) * size)
    bell = jnp.exp(-0.5 * (v * v))
    tail = part * (
        0.5 * 0.254829592
        + part
        * (
            0.5 * -0.284496736
            + part * (0.5 * 1.421413741 + part * (0.5 * -1.453152027 + part * (0.5 * 1.061405429)))
        )
    )
    tail = tail * bell
    phi = jnp.where(v >= 0.0, 1.0 - tail, tail)
    return v * phi, phi + (v * INV_SQRT2PI) * bell


def split3(value):
    first = value.astype(BF)
    rest = value - first.astype(F32)
    second = rest.astype(BF)
    third = (rest - second.astype(F32)).astype(BF)
    return first, second, third


def key_pads(rows, valid, ones):
    lane = lax.broadcasted_iota(jnp.int32, (rows, HEAD_DIM), 1)
    row = lax.broadcasted_iota(jnp.int32, (rows, HEAD_DIM), 0)
    base = jnp.where((lane >= 1) & (lane <= ones), 1.0, 0.0)
    key_pad = jnp.where((lane == 0) & (row >= valid), NEG, base).astype(BF)
    value_pad = jnp.where(lane <= 2, 1.0, 0.0).astype(BF)
    return key_pad, value_pad


def causal_bias(scal_ref, key_rows, query_rows, valid):
    place, length = scal_ref[0], scal_ref[1]
    key_id = lax.broadcasted_iota(jnp.int32, (2 * key_rows, query_rows), 0)
    query_id = lax.broadcasted_iota(jnp.int32, (2 * key_rows, query_rows), 1)
    query_pos = query_id + place * valid
    key_pos = jnp.where(
        key_id < key_rows, key_id + place * valid, key_id - key_rows + (1 - place) * valid
    )
    return jnp.where((key_pos <= query_pos) & (key_pos < length), 0.0, NEG)


def attention_fwd_kernel(*refs, valid, masked):
    if masked:
        scal_ref, q_ref, kl_ref, kr_ref, out_ref, rest_ref, stat_ref = refs
    else:
        q_ref, kl_ref, kr_ref, out_ref, rest_ref, stat_ref = refs
    rows, queries = kl_ref.shape[0], q_ref.shape[0]
    key_pad, value_pad = key_pads(rows, valid, 0)
    lane_q = lax.broadcasted_iota(jnp.int32, (queries, HEAD_DIM), 1)
    q_pad = jnp.where(lane_q == 0, 1.0, 0.0).astype(BF)
    if masked:
        bias = causal_bias(scal_ref, rows, queries, valid)
    for h in range(2):
        low, mid, high = h * 2 * HEAD_DIM, h * 2 * HEAD_DIM + HEAD_DIM, (h + 1) * 2 * HEAD_DIM
        keys = jnp.concatenate(
            [jnp.concatenate([ref[:, low:mid], key_pad], axis=1) for ref in (kl_ref, kr_ref)], axis=0
        )
        values = jnp.concatenate(
            [jnp.concatenate([ref[:, mid:high], value_pad], axis=1) for ref in (kl_ref, kr_ref)],
            axis=0,
        )
        span = slice(h * HEAD_DIM, (h + 1) * HEAD_DIM)
        q = (q_ref[:, span].astype(F32) * HEAD_DIM**-0.5).astype(BF)
        q = jnp.concatenate([q, q_pad], axis=1)
        scores = dot_nt(keys, q)
        if masked:
            scores = scores + bias
        top = jnp.max(scores, axis=0, keepdims=True)
        raised = jnp.exp(scores - top).astype(BF)
        mixed = dot_nn(values.T, raised)
        total = mixed[HEAD_DIM : HEAD_DIM + 1]
        both = jnp.concatenate(
            [
                mixed[:HEAD_DIM] / total,
                jnp.broadcast_to(top + jnp.log(total), (HEAD_DIM, queries)),
            ],
            axis=0,
        ).T
        mixed = both[:, :HEAD_DIM]
        rounded = mixed.astype(BF)
        out_ref[:, span] = rounded
        rest_ref[:, span] = (mixed - rounded.astype(F32)).astype(BF)
        stat_ref[:, span] = both[:, HEAD_DIM:]


def attention_bwd_kernel(*refs, valid, masked):
    if masked:
        (
            scal_ref, q_ref, kl_ref, kr_ref, out_ref, rest_ref, stat_ref, up_ref,
            dq_ref, dkl_ref, dkr_ref,
        ) = refs
    else:
        q_ref, kl_ref, kr_ref, out_ref, rest_ref, stat_ref, up_ref, dq_ref, dkl_ref, dkr_ref = refs
    rows, queries = kl_ref.shape[0], q_ref.shape[0]
    key_pad, value_pad = key_pads(rows, valid, 3)
    lane_q = lax.broadcasted_iota(jnp.int32, (queries, HEAD_DIM), 1)
    if masked:
        bias = causal_bias(scal_ref, rows, queries, valid)
    for h in range(2):
        low, mid, high = h * 2 * HEAD_DIM, h * 2 * HEAD_DIM + HEAD_DIM, (h + 1) * 2 * HEAD_DIM
        plain = [ref[:, low:mid] for ref in (kl_ref, kr_ref)]
        keys = jnp.concatenate(
            [jnp.concatenate([part, key_pad], axis=1) for part in plain], axis=0
        )
        values = jnp.concatenate(
            [jnp.concatenate([ref[:, mid:high], value_pad], axis=1) for ref in (kl_ref, kr_ref)],
            axis=0,
        )
        keys_t = keys.T[:HEAD_DIM]
        span = slice(h * HEAD_DIM, (h + 1) * HEAD_DIM)
        q = q_ref[:, span]
        up = up_ref[:, span]
        a0, a1, a2 = split3(-stat_ref[:, span])
        one, zero = jnp.ones_like(a0), jnp.zeros_like(a0)
        q_pad = jnp.where(
            lane_q == 0,
            one,
            jnp.where(lane_q == 1, a0, jnp.where(lane_q == 2, a1, jnp.where(lane_q == 3, a2, zero))),
        )
        q_aug = jnp.concatenate([(q.astype(F32) * HEAD_DIM**-0.5).astype(BF), q_pad], axis=1)
        mixed = out_ref[:, span].astype(F32) + rest_ref[:, span].astype(F32)
        centre = jnp.sum(up.astype(F32) * mixed, axis=1, keepdims=True)
        d0, d1, d2 = split3(-jnp.broadcast_to(centre, (queries, HEAD_DIM)))
        up_pad = jnp.where(
            lane_q == 0, d0, jnp.where(lane_q == 1, d1, jnp.where(lane_q == 2, d2, zero))
        )
        up_aug = jnp.concatenate([up, up_pad], axis=1)
        scores = dot_nt(keys, q_aug)
        if masked:
            scores = scores + bias
        probs = jnp.exp(scores)
        grad_scores = (probs * dot_nt(values, up_aug)).astype(BF)
        grad_value = dot_nn(probs.astype(BF), up)
        grad_key = dot_nn(grad_scores, q) * HEAD_DIM**-0.5
        grad_query = dot_nn(keys_t, grad_scores).T
        dq_ref[:, span] = (grad_query * HEAD_DIM**-0.5).astype(BF)
        pair = jnp.concatenate([grad_key, grad_value], axis=1).astype(BF)
        dkl_ref[:, low:high] = pair[:rows]
        dkr_ref[:, low:high] = pair[rows:]


def shape_of(rows, width, kind=BF):
    return jax.ShapeDtypeStruct((rows, width), kind)


def params(megabytes, *semantics):
    return pltpu.CompilerParams(vmem_limit_bytes=megabytes * 2**20)


def attention_cost(q, kl, products):
    flops = 2 * products * q.shape[0] * 2 * kl.shape[0] * q.shape[1] * 3
    return pl.CostEstimate(
        flops=flops, bytes_accessed=8 * q.size + 6 * kl.size, transcendentals=0
    )


def attention_specs(q, kl):
    pairs = q.shape[1] // (2 * HEAD_DIM)
    mine = pl.BlockSpec((q.shape[0], 2 * HEAD_DIM), lambda i: (0, i))
    near = pl.BlockSpec((kl.shape[0], 4 * HEAD_DIM), lambda i: (0, i))
    far = pl.BlockSpec((kl.shape[0], 4 * HEAD_DIM), lambda i: (0, lax.rem(i + pairs // 2, pairs)))
    return pairs, mine, near, far


def attention_fwd(q, kl, kr, valid, scal=None):
    pairs, mine, near, far = attention_specs(q, kl)
    masked = scal is not None
    extra = [pl.BlockSpec(memory_space=pltpu.SMEM)] if masked else []
    return pl.pallas_call(
        functools.partial(attention_fwd_kernel, valid=valid, masked=masked),
        grid=(pairs,),
        in_specs=extra + [mine, near, far],
        out_specs=[mine, mine, mine],
        out_shape=[shape_of(*q.shape), shape_of(*q.shape), shape_of(*q.shape, F32)],
        compiler_params=params(48),
        cost_estimate=attention_cost(q, kl, 2),
    )(*([scal] if masked else []), q, kl, kr)


def attention_bwd(q, kl, kr, out, rest, stat, up, valid, scal=None):
    pairs, mine, near, far = attention_specs(q, kl)
    masked = scal is not None
    extra = [pl.BlockSpec(memory_space=pltpu.SMEM)] if masked else []
    return pl.pallas_call(
        functools.partial(attention_bwd_kernel, valid=valid, masked=masked),
        grid=(pairs,),
        in_specs=extra + [mine, near, far, mine, mine, mine, mine],
        out_specs=[mine, near, far],
        out_shape=[shape_of(*q.shape), shape_of(*kl.shape), shape_of(*kl.shape)],
        compiler_params=params(48),
        cost_estimate=attention_cost(q, kl, 4),
    )(*([scal] if masked else []), q, kl, kr, out, rest, stat, up)


def rows_call(kernel, rows, blocked, whole, outs, sums=(), scratch=(), reverse=False, flops=0, megabytes=40):
    steps = rows // CHUNK

    def place(i):
        return (steps - 1 - i if reverse else i, 0)

    in_specs = [pl.BlockSpec((CHUNK, v.shape[1]), place) for v in blocked]
    in_specs += [pl.BlockSpec(v.shape, lambda i: (0, 0)) for v in whole]
    out_specs = [pl.BlockSpec((CHUNK, width), place) for width, _ in outs]
    out_specs += [pl.BlockSpec(shape, lambda i: (0, 0)) for shape, _ in sums]
    out_shape = [shape_of(rows, width, kind) for width, kind in outs]
    out_shape += [jax.ShapeDtypeStruct(shape, kind) for shape, kind in sums]
    touched = sum(v.size * v.dtype.itemsize for v in (*blocked, *whole))
    return pl.pallas_call(
        kernel,
        grid=(steps,),
        in_specs=in_specs,
        out_specs=out_specs,
        out_shape=out_shape,
        scratch_shapes=list(scratch),
        compiler_params=params(megabytes),
        cost_estimate=pl.CostEstimate(flops=flops, bytes_accessed=touched, transcendentals=0),
    )(*blocked, *whole)


def stem_fwd_kernel(
    me_ref, mo_ref, pos_ref, mh_ref, first_ref, second_ref,
    even_ref, odd_ref, before_ref, ge_ref, go_ref, gs_ref, x_ref, gh_ref, carry_ref,
):
    first = first_ref[...]

    @pl.when(pl.program_id(0) == 0)
    def _():
        act, slope = gelu_pair(dot_nn(mh_ref[...], first))
        carry_ref[...] = act[:8]
        gh_ref[...] = slope

    width = even_ref.shape[1]
    even, slope = gelu_pair(dot_nn(me_ref[...], first))
    even = even.astype(BF)
    even_ref[...] = even
    ge_ref[...] = slope.astype(BF)
    odd, slope = gelu_pair(dot_nn(mo_ref[...], first))
    go_ref[...] = slope.astype(BF)
    row = lax.broadcasted_iota(jnp.int32, odd.shape, 0)
    before = jnp.where(row == 0, carry_ref[0:1, :], pltpu.roll(odd, 1, 0)).astype(BF)
    carry_ref[0:1, :] = odd[CHUNK - 1 :]
    odd = odd.astype(BF)
    odd_ref[...] = odd
    before_ref[...] = before
    pre = dot_nn(before, second_ref[:width])
    pre += dot_nn(even, second_ref[width : 2 * width])
    pre += dot_nn(odd, second_ref[2 * width :])
    act, slope = gelu_pair(pre)
    gs_ref[...] = slope.astype(BF)
    x_ref[...] = act + pos_ref[...]


def qkv_kernel(x_ref, gain_ref, bias_ref, own_ref, oth_ref, normed_ref, q_ref, kv_ref):
    unit, _ = norm_stats(x_ref[...].astype(F32))
    normed = (unit * gain_ref[...] + bias_ref[...]).astype(BF)
    normed_ref[...] = normed
    heads = own_ref.shape[1] // (3 * HEAD_DIM)
    for part, w_ref in enumerate((own_ref, oth_ref)):
        packed = dot_nn(normed, w_ref[...]).astype(BF)
        for h in range(heads):
            at, to = h * 3 * HEAD_DIM, part * heads + h
            q_ref[:, to * HEAD_DIM : (to + 1) * HEAD_DIM] = packed[:, at : at + HEAD_DIM]
            kv_ref[:, to * 2 * HEAD_DIM : (to + 1) * 2 * HEAD_DIM] = packed[
                :, at + HEAD_DIM : at + 3 * HEAD_DIM
            ]


def two_parts(rows, own_ref, oth_ref):
    depth = own_ref.shape[0]
    return dot_nn(rows[:, :depth], own_ref[...]) + dot_nn(rows[:, depth:], oth_ref[...])


def two_parts_t(rows, own_ref, oth_ref):
    depth = own_ref.shape[1]
    return dot_nt(rows[:, :depth], own_ref[...]) + dot_nt(rows[:, depth:], oth_ref[...])


def enc_mid_kernel(
    x_ref, att_ref, gb_ref, bb_ref, gc_ref, bc_ref, po_ref, pt_ref, uo_ref, ut_ref, do_ref, dt_ref,
    ko_ref, kt_ref,
    x1_ref, x2_ref, normed_ref, hidden_ref, slope_ref, memory_ref, kv_ref,
):
    x1 = x_ref[...] + two_parts(att_ref[...], po_ref, pt_ref)
    x1_ref[...] = x1
    unit, _ = norm_stats(x1)
    normed = (unit * gb_ref[...] + bb_ref[...]).astype(BF)
    normed_ref[...] = normed
    half = uo_ref.shape[1]
    x2 = x1
    for part, (up_ref, down_ref) in enumerate(((uo_ref, do_ref), (ut_ref, dt_ref))):
        act, slope = gelu_pair(dot_nn(normed, up_ref[...]))
        act = act.astype(BF)
        hidden_ref[:, part * half : (part + 1) * half] = act
        slope_ref[:, part * half : (part + 1) * half] = slope.astype(BF)
        x2 = x2 + dot_nn(act, down_ref[...])
    x2_ref[...] = x2
    unit, _ = norm_stats(x2)
    memory = (unit * gc_ref[...] + bc_ref[...]).astype(BF)
    memory_ref[...] = memory
    half = ko_ref.shape[1]
    kv_ref[:, :half] = dot_nn(memory, ko_ref[...]).astype(BF)
    kv_ref[:, half:] = dot_nn(memory, kt_ref[...]).astype(BF)


def dec_mid_kernel(
    x_ref, att_ref, gain_ref, bias_ref, po_ref, pt_ref, qo_ref, qt_ref, y_ref, normed_ref, q_ref
):
    y = x_ref[...].astype(F32) + two_parts(att_ref[...], po_ref, pt_ref)
    y_ref[...] = y
    unit, _ = norm_stats(y)
    normed = (unit * gain_ref[...] + bias_ref[...]).astype(BF)
    normed_ref[...] = normed
    half = qo_ref.shape[1]
    q_ref[:, :half] = dot_nn(normed, qo_ref[...]).astype(BF)
    q_ref[:, half:] = dot_nn(normed, qt_ref[...]).astype(BF)


def mlp_back(gb, slope_ref, dpre_ref, uo_ref, ut_ref, do_ref, dt_ref):
    half = uo_ref.shape[1]
    total = 0.0
    for part, (up_ref, down_ref) in enumerate(((uo_ref, do_ref), (ut_ref, dt_ref))):
        span = slice(part * half, (part + 1) * half)
        dpre = (dot_nt(gb, down_ref[...]) * slope_ref[:, span].astype(F32)).astype(BF)
        dpre_ref[:, span] = dpre
        total = total + dot_nt(dpre, up_ref[...])
    return total


def dec_top_kernel(
    scal_ref, y1_ref, crossed_ref, cot_ref, gain_ref, bias_ref, po_ref, pt_ref, uo_ref, ut_ref,
    do_ref, dt_ref,
    decoded_ref, normed_ref, hidden_ref, dpre_ref, gb3_ref, gb2_ref, dcrossed_ref, u2_ref, sums_ref,
    slope_ref, *, valid,
):
    rows = y1_ref.shape[0]
    y2 = y1_ref[...] + two_parts(crossed_ref[...], po_ref, pt_ref)
    unit, inverse = norm_stats(y2)
    normed = (unit * gain_ref[...] + bias_ref[...]).astype(BF)
    normed_ref[...] = normed
    half = uo_ref.shape[1]
    y3 = y2
    for part, (up_ref, down_ref) in enumerate(((uo_ref, do_ref), (ut_ref, dt_ref))):
        act, slope = gelu_pair(dot_nn(normed, up_ref[...]))
        act = act.astype(BF)
        hidden_ref[:, part * half : (part + 1) * half] = act
        slope_ref[:, part * half : (part + 1) * half] = slope.astype(BF)
        y3 = y3 + dot_nn(act, down_ref[...])
    row = lax.broadcasted_iota(jnp.int32, y2.shape, 0)
    live = ((row < valid) & (row + scal_ref[0] * valid < scal_ref[1])).astype(F32)
    decoded_ref[...] = (y3 * live).astype(BF)
    u3 = cot_ref[...].astype(F32) * live
    gb3 = u3.astype(BF)
    gb3_ref[...] = gb3
    dnormed = mlp_back(gb3, slope_ref, dpre_ref, uo_ref, ut_ref, do_ref, dt_ref)
    dy, dgain, dbias = norm_back(unit, inverse, gain_ref[...], dnormed)
    u2 = u3 + dy
    u2_ref[...] = u2
    gb2 = u2.astype(BF)
    gb2_ref[...] = gb2
    half = po_ref.shape[0]
    dcrossed_ref[:, :half] = dot_nt(gb2, po_ref[...]).astype(BF)
    dcrossed_ref[:, half:] = dot_nt(gb2, pt_ref[...]).astype(BF)
    sums_ref[...] = jnp.zeros_like(sums_ref)
    sums_ref[0:1, :] = dgain
    sums_ref[1:2, :] = dbias


def dec_back_kernel(
    dq_ref, y1_ref, u2_ref, gain_ref, qo_ref, qt_ref, po_ref, pt_ref,
    u1_ref, gb1_ref, datt_ref, sums_ref,
):
    dnormed = two_parts_t(dq_ref[...], qo_ref, qt_ref)
    unit, inverse = norm_stats(y1_ref[...])
    dy, dgain, dbias = norm_back(unit, inverse, gain_ref[...], dnormed)
    u1 = u2_ref[...] + dy
    u1_ref[...] = u1
    gb1 = u1.astype(BF)
    gb1_ref[...] = gb1
    half = po_ref.shape[0]
    datt_ref[:, :half] = dot_nt(gb1, po_ref[...]).astype(BF)
    datt_ref[:, half:] = dot_nt(gb1, pt_ref[...]).astype(BF)
    sums_ref[...] = jnp.zeros_like(sums_ref)
    sums_ref[0:1, :] = dgain
    sums_ref[1:2, :] = dbias


def packed_back(dq_ref, dkl_ref, dkr_ref, own_ref, oth_ref, dpo_ref, dpt_ref):
    dkv = (dkl_ref[...].astype(F32) + dkr_ref[...].astype(F32)).astype(BF)
    dq = dq_ref[...]
    heads = own_ref.shape[1] // (3 * HEAD_DIM)
    total = 0.0
    for part, (w_ref, out_ref) in enumerate(((own_ref, dpo_ref), (oth_ref, dpt_ref))):
        pieces = []
        for h in range(part * heads, (part + 1) * heads):
            pieces.append(dq[:, h * HEAD_DIM : (h + 1) * HEAD_DIM])
            pieces.append(dkv[:, h * 2 * HEAD_DIM : (h + 1) * 2 * HEAD_DIM])
        packed = jnp.concatenate(pieces, axis=1)
        out_ref[...] = packed
        total = total + dot_nt(packed, w_ref[...])
    return total


def dec_last_kernel(
    dq_ref, dkl_ref, dkr_ref, x_ref, u1_ref, gain_ref, own_ref, oth_ref,
    dpo_ref, dpt_ref, grad_ref, sums_ref,
):
    dnormed = packed_back(dq_ref, dkl_ref, dkr_ref, own_ref, oth_ref, dpo_ref, dpt_ref)
    unit, inverse = norm_stats(x_ref[...].astype(F32))
    dx, dgain, dbias = norm_back(unit, inverse, gain_ref[...], dnormed)
    grad_ref[...] = u1_ref[...] + dx
    sums_ref[...] = jnp.zeros_like(sums_ref)
    sums_ref[0:1, :] = dgain
    sums_ref[1:2, :] = dbias


def enc_back_kernel(
    gl_ref, gr_ref, x2_ref, x1_ref, slope_ref, gc_ref, gb_ref, ko_ref, kt_ref, uo_ref, ut_ref,
    do_ref, dt_ref, po_ref, pt_ref,
    gkv_ref, gb2_ref, dpre_ref, gb1_ref, datt_ref, u1_ref, sums_ref,
):
    @pl.when(pl.program_id(0) == 0)
    def _():
        sums_ref[...] = jnp.zeros_like(sums_ref)

    gkv = (gl_ref[...].astype(F32) + gr_ref[...].astype(F32)).astype(BF)
    gkv_ref[...] = gkv
    dmemory = two_parts_t(gkv, ko_ref, kt_ref)
    unit, inverse = norm_stats(x2_ref[...])
    u2, dgain, dbias = norm_back(unit, inverse, gc_ref[...], dmemory)
    sums_ref[0:1, :] += dgain
    sums_ref[1:2, :] += dbias
    gb2 = u2.astype(BF)
    gb2_ref[...] = gb2
    dnormed = mlp_back(gb2, slope_ref, dpre_ref, uo_ref, ut_ref, do_ref, dt_ref)
    unit, inverse = norm_stats(x1_ref[...])
    dx, dgain, dbias = norm_back(unit, inverse, gb_ref[...], dnormed)
    sums_ref[2:3, :] += dgain
    sums_ref[3:4, :] += dbias
    u1 = u2 + dx
    u1_ref[...] = u1
    gb1 = u1.astype(BF)
    gb1_ref[...] = gb1
    half = po_ref.shape[0]
    datt_ref[:, :half] = dot_nt(gb1, po_ref[...]).astype(BF)
    datt_ref[:, half:] = dot_nt(gb1, pt_ref[...]).astype(BF)


def stem_back_kernel(
    dq_ref, dkl_ref, dkr_ref, x0_ref, u1_ref, ge_ref, go_ref, gs_ref, gain_ref, own_ref, oth_ref,
    second_ref, gh_ref,
    dpo_ref, dpt_ref, g2_ref, ede_ref, edo_ref, sums_ref, edh_ref, carry_ref,
):
    @pl.when(pl.program_id(0) == 0)
    def _():
        sums_ref[...] = jnp.zeros_like(sums_ref)
        carry_ref[...] = jnp.zeros_like(carry_ref)

    dnormed = packed_back(dq_ref, dkl_ref, dkr_ref, own_ref, oth_ref, dpo_ref, dpt_ref)
    unit, inverse = norm_stats(x0_ref[...])
    dx, dgain, dbias = norm_back(unit, inverse, gain_ref[...], dnormed)
    sums_ref[0:1, :] += dgain
    sums_ref[1:2, :] += dbias
    g2 = ((u1_ref[...] + dx) * gs_ref[...].astype(F32)).astype(BF)
    g2_ref[...] = g2
    width = g2.shape[1]
    before = dot_nt(g2, second_ref[:width])
    even = dot_nt(g2, second_ref[width : 2 * width])
    odd = dot_nt(g2, second_ref[2 * width :])
    ede_ref[...] = (even * ge_ref[...].astype(F32)).astype(BF)
    row = lax.broadcasted_iota(jnp.int32, before.shape, 0)
    later = jnp.where(
        row == CHUNK - 1, carry_ref[0:1, :], pltpu.roll(before, CHUNK - 1, 0)
    )
    carry_ref[0:1, :] = before[0:1]
    edo_ref[...] = ((odd + later) * go_ref[...].astype(F32)).astype(BF)
    front = lax.broadcasted_iota(jnp.int32, edh_ref.shape, 0)
    edh_ref[...] = jnp.where(front == 0, before[0:1] * gh_ref[...], 0.0).astype(BF)


def swap(value, axis):
    return lax.ppermute(value, axis, [(0, 1), (1, 0)])


def flip_bit(value, axis, bit):
    count = lax.axis_size(axis)
    return lax.ppermute(value, axis, [(i, i ^ bit) for i in range(count)])


def add_low(left, right):
    return (left.astype(F32) + right.astype(F32)).astype(BF)


def halve(value, dim, place, send):
    mine = lax.dynamic_index_in_dim(value, place, dim, keepdims=False)
    other = lax.dynamic_index_in_dim(value, 1 - place, dim, keepdims=False)
    return mine, send(other)


def reduce_blocks(value, names):
    section, clip_group = lax.axis_index("section"), lax.axis_index("dp")
    dims = list(names)
    order = [name for name, _ in sorted(names.items(), key=lambda item: item[1])]
    held = value
    for step, name in enumerate(order):
        dim = [n for n in dims if n in order[step:]].index(name)
        if name == "section":
            mine, got = halve(held, dim, section, functools.partial(swap, axis="section"))
        else:
            place = (clip_group // name) % 2
            mine, got = halve(held, dim, place, functools.partial(flip_bit, axis="dp", bit=name))
        held = mine.astype(F32) + got.astype(F32)
        if step < len(order) - 1:
            held = held.astype(BF)
    return held


def dp_bits():
    count, bits = lax.axis_size("dp"), []
    while count > 1:
        count //= 2
        bits.append(count)
    return bits


def sum_projections(value):
    rows, columns = value.shape
    bits = dp_bits()
    lead = (2,) * (1 + len(bits))
    half = columns // 256 * 128
    out = []
    for which, part in enumerate((value[:, :half], value[:, half:])):
        shaped = part.reshape(*lead, rows // 2 ** len(lead), part.shape[1])
        early = {"section": 1, bits[-1]: 0} if which == 0 else {"section": 0, bits[-1]: 1}
        names = {"section": early["section"]}
        for at, bit in enumerate(bits):
            names[bit] = early.get(bit, 2 + at)
        out.append(reduce_blocks(shaped, names))
    return jnp.concatenate(out, axis=1)


def sum_stem(value):
    rows, columns = value.shape
    bits = dp_bits()
    place = lax.axis_index("tensor")
    groups = 2 ** len(bits)
    block = rows // (groups * 2)
    shaped = value.reshape(groups, 2, block, columns)
    mine, got = halve(shaped, 1, place, functools.partial(swap, axis="tensor"))
    held = add_low(mine, got)
    half = columns // 256 * 128
    out = []
    for which, part in enumerate((held[:, :, :half], held[:, :, half:])):
        shaped = part.reshape(*((2,) * len(bits)), 2, block // 2, part.shape[2])
        names = {bit: 2 + at for at, bit in enumerate(bits)}
        names[bits[-1]] = which
        names["section"] = 1 - which
        out.append(reduce_blocks(shaped, names))
    mine = jnp.concatenate(out, axis=1)
    got = swap(mine, "section")
    first = lax.axis_index("section") == 0
    return jnp.concatenate(
        [jnp.where(first, mine, got), jnp.where(first, got, mine)], axis=0
    )


def core_sum(pairs):
    full = [dot_tn(left, right).astype(BF) for left, right in pairs]
    mine = jnp.concatenate([v[:, : v.shape[1] // 2] for v in full], axis=1)
    sent = jnp.concatenate([v[:, v.shape[1] // 2 :] for v in full], axis=1)
    return add_low(mine, swap(sent, "tensor"))


def sinusoid_table(count, width_all):
    step_size = math.log(10000.0) / (width_all // 2 - 1)
    rates = np.exp(-step_size * np.arange(width_all // 2))
    angles = np.arange(count)[:, None] * rates[None, :]
    return np.concatenate([np.sin(angles), np.cos(angles)], axis=1).astype(np.float32)


def pad_rows(value, rows):
    return jnp.pad(value, ((0, rows - value.shape[0]), (0, 0)))


def round_up(count):
    return -(-count // CHUNK) * CHUNK


def body(
    mel,
    conv_first,
    conv_second,
    enc_gain,
    enc_shift,
    enc_qkv,
    enc_proj,
    enc_up,
    enc_down,
    cross_kv,
    text,
    lengths,
    dec_gain,
    dec_shift,
    dec_qkv,
    dec_proj,
    cross_query,
    cross_proj,
    dec_up,
    dec_down,
    cotangent,
):
    section = lax.axis_index("section")
    place = lax.axis_index("tensor")
    cores = lax.axis_size("tensor")
    width = text.shape[2]
    frames = mel.shape[1] // 2
    valid = frames // cores
    rows = round_up(valid)
    slots = text.shape[1]
    text_rows = round_up(slots)
    channels = mel.shape[2]

    def pick(value):
        return lax.dynamic_index_in_dim(value, section, 0, keepdims=False)

    mel_clip, text_clip, cot_clip = pick(mel), pick(text), pick(cotangent)
    scal = jnp.stack([place.astype(jnp.int32), pick(lengths)])
    text_clip = pad_rows(text_clip, text_rows)
    cot_clip = pad_rows(cot_clip, text_rows)

    pair = lambda w: (w, swap(w, "tensor"))
    w_dqkv, w_eqkv = pair(dec_qkv), pair(enc_qkv)
    w_dproj, w_cq = pair(dec_proj), pair(cross_query)
    w_eproj, w_eup, w_edown, w_ckv = pair(enc_proj), pair(enc_up), pair(enc_down), pair(cross_kv)
    w_cproj, w_dup, w_ddown = pair(cross_proj), pair(dec_up), pair(dec_down)
    eg, es = [enc_gain[i : i + 1] for i in range(3)], [enc_shift[i : i + 1] for i in range(3)]
    dg, ds = [dec_gain[i : i + 1] for i in range(3)], [dec_shift[i : i + 1] for i in range(3)]

    taps = conv_first.shape[0] * channels
    depth = -(-taps // 256) * 256
    window = lax.dynamic_slice_in_dim(
        jnp.pad(mel_clip, ((2, 2 * (rows - valid) + 2), (0, 0))), 2 * valid * place, 2 * rows + 4, 0
    ).reshape(rows + 2, 2 * channels)
    tail = jnp.zeros((rows, depth - taps), BF)
    mel_even = jnp.concatenate([window[:rows, channels:], window[1 : rows + 1], tail], axis=1)
    mel_odd = jnp.concatenate([window[1 : rows + 1], window[2:, :channels], tail], axis=1)
    mel_halo = jnp.concatenate([window[0:1], window[1:2, :channels], tail[:1]], axis=1)
    mel_halo = pad_rows(jnp.where(place > 0, mel_halo, jnp.zeros_like(mel_halo)), 16)
    first = pad_rows(conv_first.reshape(taps, width), depth)
    second = conv_second.reshape(-1, width)
    table = jnp.asarray(np.pad(sinusoid_table(frames, width), ((0, rows - valid), (0, 0))))
    table = lax.dynamic_slice_in_dim(table, valid * place, rows, 0)

    dn_a, dq_self, dkv_self = rows_call(
        qkv_kernel, text_rows, [text_clip], [dg[0], ds[0], *w_dqkv],
        [(width, BF), (width, BF), (2 * width, BF)], flops=2 * text_rows * width * 3 * width,
    )
    dkv_self_r = swap(dkv_self, "tensor")

    even, odd, before, ge, go, gs, x0, gh = rows_call(
        stem_fwd_kernel, rows, [mel_even, mel_odd, table], [mel_halo, first, second],
        [(width, BF)] * 6 + [(width, F32)], sums=[((16, width), F32)],
        scratch=[pltpu.VMEM((8, width), F32)], flops=2 * rows * width * 2000,
    )
    en_a, eq, ekv = rows_call(
        qkv_kernel, rows, [x0], [eg[0], es[0], *w_eqkv],
        [(width, BF), (width, BF), (2 * width, BF)], flops=2 * rows * width * 3 * width,
    )
    ekv_r = swap(ekv, "tensor")

    datt, drest, dstat = attention_fwd(dq_self, dkv_self, dkv_self_r, slots, scal)
    y1, dn_b, cq = rows_call(
        dec_mid_kernel, text_rows, [text_clip, datt], [dg[1], ds[1], *w_dproj, *w_cq],
        [(width, F32), (width, BF), (width, BF)], flops=2 * text_rows * width * 2 * width,
    )

    eatt, erest, estat = attention_fwd(eq, ekv, ekv_r, valid)
    units = 2 * enc_up.shape[1]
    x1, x2, en_b, ehid, eslope, memory, ckv = rows_call(
        enc_mid_kernel, rows, [x0, eatt],
        [eg[1], es[1], eg[2], es[2], *w_eproj, *w_eup, *w_edown, *w_ckv],
        [(width, F32), (width, F32), (width, BF), (units, BF), (units, BF), (width, BF), (2 * width, BF)],
        flops=2 * rows * width * (3 * width + 2 * units), megabytes=48,
    )
    ckv_r = swap(ckv, "tensor")

    crossed, crest, cstat = attention_fwd(cq, ckv, ckv_r, valid)
    dec_units = 2 * dec_up.shape[1]
    top_outs = [
        (width, BF), (width, BF), (dec_units, BF), (dec_units, BF), (width, BF), (width, BF),
        (width, BF), (width, F32),
    ]
    whole = [scal, y1, crossed, cot_clip, dg[2], ds[2], *w_cproj, *w_dup, *w_ddown]
    decoded, dn_c, dhid, dpre, dgb3, dgb2, dcrossed, u2, sums_c = pl.pallas_call(
        functools.partial(dec_top_kernel, valid=slots),
        in_specs=[pl.BlockSpec(memory_space=pltpu.SMEM)]
        + [pl.BlockSpec(memory_space=pltpu.VMEM)] * (len(whole) - 1),
        out_shape=[shape_of(text_rows, w, k) for w, k in top_outs] + [shape_of(8, width, F32)],
        scratch_shapes=[pltpu.VMEM((text_rows, dec_units), BF)],
        compiler_params=params(40),
        cost_estimate=pl.CostEstimate(
            flops=2 * text_rows * width * (2 * width + 4 * dec_units),
            bytes_accessed=10 * 2**20,
            transcendentals=0,
        ),
    )(*whole)
    dcq, dckv, dckv_r = attention_bwd(cq, ckv, ckv_r, crossed, crest, cstat, dcrossed, valid)
    dckv_got = swap(dckv_r, "tensor")
    u1, dgb1, ddatt, sums_b = rows_call(
        dec_back_kernel, text_rows, [dcq, y1, u2], [dg[1], *w_cq, *w_dproj],
        [(width, F32), (width, BF), (width, BF)], sums=[((8, width), F32)],
        flops=2 * text_rows * width * 2 * width,
    )
    dqs, dkvs, dkvs_r = attention_bwd(
        dq_self, dkv_self, dkv_self_r, datt, drest, dstat, ddatt, slots, scal
    )
    dkvs_got = swap(dkvs_r, "tensor")

    gkv, egb2, edpre, egb1, deatt, eu1, sums_e = rows_call(
        enc_back_kernel, rows, [dckv, dckv_got, x2, x1, eslope],
        [eg[2], eg[1], *w_ckv, *w_eup, *w_edown, *w_eproj],
        [(2 * width, BF), (width, BF), (units, BF), (width, BF), (width, BF), (width, F32)],
        sums=[((8, width), F32)], flops=2 * rows * width * (3 * width + 2 * units), megabytes=48,
    )
    dqkv_o, dqkv_t, text_rows_grad, sums_a = rows_call(
        dec_last_kernel, text_rows, [dqs, dkvs, dkvs_got, text_clip, u1], [dg[0], *w_dqkv],
        [(dec_qkv.shape[1], BF), (dec_qkv.shape[1], BF), (width, F32)], sums=[((8, width), F32)],
        flops=2 * text_rows * width * 3 * width,
    )

    dec_sum = sum_projections(
        core_sum(
            [
                (dn_c, dpre),
                (dgb3, dhid),
                (dgb2, crossed),
                (dn_b, dcq),
                (dgb1, datt),
                (dn_a, jnp.concatenate([dqkv_o, dqkv_t], axis=1)),
            ]
        )
    )
    mid_sum = sum_projections(
        core_sum([(en_b, edpre), (egb2, ehid), (memory, gkv), (egb1, eatt)])
    )

    deq, dekv, dekv_r = attention_bwd(eq, ekv, ekv_r, eatt, erest, estat, deatt, valid)
    dekv_got = swap(dekv_r, "tensor")
    eqkv_o, eqkv_t, g2, ede, edo, sums_f, edh = rows_call(
        stem_back_kernel, rows, [deq, dekv, dekv_got, x0, eu1, ge, go, gs],
        [eg[0], *w_eqkv, second, gh],
        [(enc_qkv.shape[1], BF), (enc_qkv.shape[1], BF), (width, BF), (width, BF), (width, BF)],
        sums=[((8, width), F32), ((16, width), BF)], scratch=[pltpu.VMEM((8, width), F32)],
        reverse=True, flops=2 * rows * width * 6 * width,
    )
    late_sum = sum_projections(core_sum([(en_a, jnp.concatenate([eqkv_o, eqkv_t], axis=1))]))
    conv_first_t = dot_tn(ede, mel_even) + dot_tn(edo, mel_odd) + dot_tn(edh, mel_halo)
    vectors = jnp.concatenate(
        [
            sums_f[0:1], sums_e[2:3], sums_e[0:1], sums_f[1:2], sums_e[3:4], sums_e[1:2],
            sums_a[0:1], sums_b[0:1], sums_c[0:1], sums_a[1:2], sums_b[1:2], sums_c[1:2],
        ],
        axis=0,
    )
    stem = jnp.concatenate(
        [
            *(dot_tn(g2, act).astype(BF) for act in (before, even, odd)),
            conv_first_t[:, :taps].astype(BF),
            vectors.T.astype(BF),
            jnp.zeros((width, depth - taps - vectors.shape[0]), BF),
        ],
        axis=1,
    )
    stem = sum_stem(stem)

    half = width // 2
    decoded, text_rows_grad = decoded[:slots], text_rows_grad[:slots]

    def to_owners(value):
        mine = lax.dynamic_slice_in_dim(value, section * half, half, 1)
        got = swap(lax.dynamic_slice_in_dim(value, (1 - section) * half, half, 1).astype(BF), "section")
        got = got.astype(value.dtype)
        first_clip = section == 0
        return jnp.stack([jnp.where(first_clip, mine, got), jnp.where(first_clip, got, mine)])

    def cuts(value, widths):
        ends = np.cumsum([0, *widths])
        return [value[:, a:b] for a, b in zip(ends[:-1], ends[1:])]

    shard = dec_up.shape[1]
    d_up, d_down, d_cproj, d_cq, d_proj, d_qkv = cuts(
        dec_sum, [shard, shard, cross_proj.shape[0], cross_query.shape[1], dec_proj.shape[0], dec_qkv.shape[1]]
    )
    e_up, e_down, e_kv, e_proj = cuts(
        mid_sum, [enc_up.shape[1], enc_down.shape[0], cross_kv.shape[1], enc_proj.shape[0]]
    )
    stem_t = stem.T
    conv_second_grad = stem_t[: 3 * width].reshape(3, width, -1)
    conv_first_grad = stem_t[3 * width : 3 * width + taps].reshape(3, channels, -1)
    vec = stem_t[3 * width + taps : 3 * width + taps + 12]
    return (
        to_owners(decoded),
        to_owners(text_rows_grad),
        conv_first_grad,
        conv_second_grad,
        vec[0:3],
        vec[3:6],
        late_sum,
        e_proj.T,
        e_up,
        e_down.T,
        e_kv,
        vec[6:9],
        vec[9:12],
        d_qkv,
        d_proj.T,
        d_cq,
        d_cproj.T,
        d_up,
        d_down.T,
    )


def solution(mesh):
    in_specs = (
        P("dp", None, None),
        P(),
        P(),
        P(),
        P(),
        P(None, "tensor"),
        P("tensor", None),
        P(None, "tensor"),
        P("tensor", None),
        P(None, "tensor"),
        P("dp", "tensor", None),
        P("dp"),
        P(),
        P(),
        P(None, "tensor"),
        P("tensor", None),
        P(None, "tensor"),
        P("tensor", None),
        P(None, "tensor"),
        P("tensor", None),
        P("dp", "tensor", None),
    )
    out_specs = (
        P("dp", "tensor", "section"),
        P("dp", "tensor", "section"),
        P(None, None, ("dp", "tensor")),
        P(None, None, ("dp", "tensor")),
        P(None, ("dp", "tensor")),
        P(None, ("dp", "tensor")),
        P(("section", "dp"), "tensor"),
        P("tensor", ("section", "dp")),
        P(("section", "dp"), "tensor"),
        P("tensor", ("section", "dp")),
        P(("section", "dp"), "tensor"),
        P(None, ("dp", "tensor")),
        P(None, ("dp", "tensor")),
        P(("section", "dp"), "tensor"),
        P("tensor", ("section", "dp")),
        P(("section", "dp"), "tensor"),
        P("tensor", ("section", "dp")),
        P(("section", "dp"), "tensor"),
        P("tensor", ("section", "dp")),
    )
    return jax.shard_map(body, mesh=mesh, in_specs=in_specs, out_specs=out_specs, check_vma=False)
```

```python
import functools
import math

import jax
import jax.numpy as jnp
import numpy as np
from jax import lax
from jax.experimental import pallas as pl
from jax.experimental.pallas import tpu as pltpu
from jax.sharding import PartitionSpec as P

HEAD_DIM = 64
NEG = -1000000000.0
EPS = 1e-05
TINY = 1e-28
CHUNK = 256
LANES = 128
BF, F32 = jnp.bfloat16, jnp.float32
INV_SQRT2 = 0.7071067811865476
INV_SQRT2PI = 0.3989422804014327


def dot_nn(left, right):
    return lax.dot_general(left, right, (((1,), (0,)), ((), ())), preferred_element_type=F32)


def dot_nt(left, right):
    return lax.dot_general(left, right, (((1,), (1,)), ((), ())), preferred_element_type=F32)


def dot_tn(left, right):
    return lax.dot_general(left, right, (((0,), (0,)), ((), ())), preferred_element_type=F32)


def norm_stats(rows):
    centre = rows - jnp.mean(rows, axis=-1, keepdims=True)
    spread = jnp.mean(centre * centre, axis=-1, keepdims=True)
    inverse = lax.rsqrt(spread + EPS)
    return centre * inverse, inverse


def norm_back(unit, inverse, gain_row, upstream):
    scaled = upstream * gain_row
    first = jnp.mean(scaled, axis=-1, keepdims=True)
    second = jnp.mean(scaled * unit, axis=-1, keepdims=True)
    grad_rows = inverse * (scaled - first - unit * second)
    grad_gain = jnp.sum(upstream * unit, axis=0, keepdims=True)
    grad_bias = jnp.sum(upstream, axis=0, keepdims=True)
    return grad_rows, grad_gain, grad_bias


def gelu_pair(v):
    phi = 0.5 * (1.0 + lax.erf(v * INV_SQRT2))
    return v * phi, phi + (v * INV_SQRT2PI) * jnp.exp(-0.5 * (v * v))


def lanes(rows):
    return lax.broadcasted_iota(jnp.int32, (rows, 2 * HEAD_DIM), 1)

def key_aug(kv, valid, ones):
    lane = lanes(kv.shape[0])
    row = lax.broadcasted_iota(jnp.int32, kv.shape, 0)
    pad = jnp.where((lane > HEAD_DIM) & (lane <= HEAD_DIM + ones), 1.0, 0.0)
    pad = jnp.where((lane == HEAD_DIM) & (row >= valid), NEG, pad).astype(BF)
    return jnp.where(lane < HEAD_DIM, kv, pad)

def causal_bias(scal_ref, key_rows, query_rows, valid):
    place, length = scal_ref[SCAL_CORE], scal_ref[SCAL_LENGTHS + scal_ref[SCAL_SECTION]]
    key_id = lax.broadcasted_iota(jnp.int32, (2 * key_rows, query_rows), 0)
    query_id = lax.broadcasted_iota(jnp.int32, (2 * key_rows, query_rows), 1)
    query_pos = query_id + place * valid
    key_pos = jnp.where(key_id < key_rows, key_id + place * valid, key_id - key_rows + (1 - place) * valid)
    return jnp.where((key_pos <= query_pos) & (key_pos < length), 0.0, NEG)

def fwd_setup(q_ref, kl_ref, kr_ref, valid):
    lane_q = lanes(q_ref.shape[0])
    q_all = q_ref[...].astype(F32) * HEAD_DIM**-0.5
    wide = 2 * HEAD_DIM

    def operands(h):
        q = jnp.where(lane_q < HEAD_DIM, q_all if h == 0 else pltpu.roll(q_all, HEAD_DIM, 1), 0.0)
        kv = [ref[:, h * wide : (h + 1) * wide] for ref in (kl_ref, kr_ref)]
        turned = [v.T for v in kv]
        sub = lax.broadcasted_iota(jnp.int32, turned[0].shape, 0)
        ones = [jnp.where(sub == 0, jnp.ones_like(v), v) for v in turned]
        return q, [key_aug(v, valid, 1) for v in kv], turned, ones

    return lane_q, operands


def fwd_finish(parts, logs, shift, out_ref, rest_ref, stat_ref):
    queries = out_ref.shape[0]
    mixed = jnp.concatenate([v[HEAD_DIM:] / v[0:1] for v in parts], axis=0).T
    logs = [jnp.broadcast_to(v, (HEAD_DIM, queries)) for v in logs]
    stat = jnp.concatenate(logs[::-1], axis=0).T
    if shift is not None:
        stat = stat + shift
    rounded = mixed.astype(BF)
    out_ref[...] = rounded
    rest_ref[...] = (mixed - rounded.astype(F32)).astype(BF)
    stat_ref[...] = stat


def fwd_fast(q_ref, kl_ref, kr_ref, out_ref, rest_ref, stat_ref, bias, valid, kc, depth):
    rows, queries = kl_ref.shape[0], q_ref.shape[0]
    lane_q, operands = fwd_setup(q_ref, kl_ref, kr_ref, valid)
    tops, heads = [], []
    for h in range(2):
        q, keys, turned, ones = operands(h)
        size = 0.0
        for v in turned:
            k = v[:HEAD_DIM].astype(F32)
            size = jnp.maximum(size, jnp.max(jnp.sum(k * k, axis=0, keepdims=True), axis=1, keepdims=True))
        bound = jnp.sqrt(jnp.sum(q * q, axis=1, keepdims=True) * size)
        bound = bound.astype(BF).astype(F32)
        q = jnp.where(lane_q == HEAD_DIM, 1.0, jnp.where(lane_q == HEAD_DIM + 1, -bound, q)).astype(BF)
        heads.append((q, keys, ones)); tops.append(bound)
    def score(item):
        h, side, at = item
        s = dot_nt(heads[h][1][side][at : at + kc], heads[h][0])
        if bias is not None:
            s = s + bias[side * rows + at : side * rows + at + kc]
        return s
    items = [(h, side, at) for h in range(2) for side in range(2) for at in range(0, rows, kc)]
    parts = [0.0, 0.0]
    ahead = [score(i) for i in items[:depth]]
    for n, (h, side, at) in enumerate(items):
        if n + depth < len(items):
            ahead.append(score(items[n + depth]))
        p = jnp.exp(ahead.pop(0)).astype(BF)
        parts[h] = parts[h] + dot_nn(heads[h][2][side][:, at : at + kc], p)
    fwd_finish(parts, [jnp.log(v[0:1]) for v in parts], jnp.where(lane_q < HEAD_DIM, tops[1], tops[0]), out_ref, rest_ref, stat_ref)
    return jnp.minimum(parts[0][0:1], parts[1][0:1])


def fwd_safe(q_ref, kl_ref, kr_ref, out_ref, rest_ref, stat_ref, bias, valid):
    rows = kl_ref.shape[0]
    lane_q, operands = fwd_setup(q_ref, kl_ref, kr_ref, valid)
    parts, logs = [], []
    for h in range(2):
        q, keys, _, ones = operands(h)
        q = jnp.where(lane_q == HEAD_DIM, 1.0, q).astype(BF)
        scores = []
        for side in range(2):
            s = dot_nt(keys[side], q)
            if bias is not None:
                s = s + bias[side * rows : (side + 1) * rows]
            scores.append(s)
        top = jnp.maximum(jnp.max(scores[0], axis=0, keepdims=True), jnp.max(scores[1], axis=0, keepdims=True))
        parts.append(sum(dot_nn(ones[i], jnp.exp(scores[i] - top).astype(BF)) for i in range(2)))
        logs.append(top + jnp.log(parts[h][0:1]))
    fwd_finish(parts, logs, None, out_ref, rest_ref, stat_ref)


def views(refs, i, pairs):
    narrow, near, far = refs
    wide = 2 * HEAD_DIM
    j = (i + pairs // 2) % pairs if isinstance(i, int) else lax.rem(i + pairs // 2, pairs)
    at = (lambda n, w: pl.ds(n * w, w)) if isinstance(i, int) else (lambda n, w: pl.ds(pl.multiple_of(n * w, w), w))
    return [r.at[:, at(i, wide)] for r in narrow], [r.at[:, at(i, 2 * wide)] for r in near], [r.at[:, at(j, 2 * wide)] for r in far]


def fwd_kernel(*refs, valid, masked, kc, depth):
    scal_ref = refs[0] if masked else None
    q_ref, kl_ref, kr_ref, out_ref, rest_ref, stat_ref = refs[1:] if masked else refs
    pairs = q_ref.shape[1] // (2 * HEAD_DIM)
    bias = causal_bias(scal_ref, kl_ref.shape[0], q_ref.shape[0], valid) if masked else None
    least = None
    for i in range(pairs):
        (q, out, rest, stat), (kl,), (kr,) = views(((q_ref, out_ref, rest_ref, stat_ref), (kl_ref,), (kr_ref,)), i, pairs)
        low = fwd_fast(q, kl, kr, out, rest, stat, bias, valid, kc, depth)
        least = low if least is None else jnp.minimum(least, low)
        for ref in (rest_ref, stat_ref):
            push(ref, (slice(None), pl.ds(i * 2 * HEAD_DIM, 2 * HEAD_DIM)))
    for ref in (rest_ref, stat_ref):
        if isinstance(ref, Outgoing):
            ref.finish()

    @pl.when(jnp.min(least) < TINY)
    def _():
        @pl.loop(0, pairs)
        def _(i):
            (q, out, rest, stat), (kl,), (kr,) = views(((q_ref, out_ref, rest_ref, stat_ref), (kl_ref,), (kr_ref,)), i, pairs)
            again = causal_bias(scal_ref, kl_ref.shape[0], q_ref.shape[0], valid) if masked else None
            fwd_safe(q, kl, kr, out, rest, stat, again, valid)

        for ref in (rest_ref, stat_ref):
            if isinstance(ref, Outgoing):
                ref.again()


def split3(value):
    first = value.astype(BF); rest = value - first.astype(F32)
    second = rest.astype(BF); third = (rest - second.astype(F32)).astype(BF)
    return first.astype(F32), second.astype(F32), third.astype(F32)


def bwd_views(refs, i, pairs):
    q_ref, kl_ref, kr_ref, out_ref, rest_ref, stat_ref, up_ref, dq_ref, dkl_ref, dkr_ref = refs
    narrow = (q_ref, out_ref, rest_ref, stat_ref, up_ref, dq_ref)
    (q, out, rest, stat, up, dq), (kl, dkl), (kr, dkr) = views(
        (narrow, (kl_ref, dkl_ref), (kr_ref, dkr_ref)), i, pairs
    )
    return q, kl, kr, out, rest, stat, up, dq, dkl, dkr


def bwd_kernel(*refs, valid, masked):
    scal_ref = refs[0] if masked else None
    refs = refs[1:] if masked else refs
    q_ref, kl_ref = refs[:2]
    pairs = q_ref.shape[1] // (2 * HEAD_DIM)
    bias = causal_bias(scal_ref, kl_ref.shape[0], q_ref.shape[0], valid) if masked else None
    for i in range(pairs):
        q, kl, kr, out, rest, stat, up, dq, dkl, dkr = bwd_views(refs, i, pairs)
        fn = bwd_pair if masked else bwd_pair_s
        fn(q, out, rest, stat, up, dq, [(kl, dkl), (kr, dkr)], bias, valid)


def bwd_side_kernel(*refs, valid, far, first, count, joined):
    q_ref, kv_ref, out_ref, rest_ref, stat_ref, up_ref, *more, dq_ref, dkv_ref = refs
    pairs = q_ref.shape[1] // (2 * HEAD_DIM)
    wide = 2 * HEAD_DIM
    base_refs = () if far else more
    if joined:
        earlier, at = more[0], dkv_ref.shape[1] - more[0].shape[1]
        dkv_ref[:, at:] = earlier[...]

    def one(i):
        (q, out, rest, stat, up), near, other = views(
            ((q_ref, out_ref, rest_ref, stat_ref, up_ref), () if far else (kv_ref,), (kv_ref,) if far else ()),
            first + i, pairs,
        )
        dq = dq_ref.at[:, i * wide : (i + 1) * wide]
        dkv = dkv_ref.at[:, i * 2 * wide : (i + 1) * 2 * wide]
        base = None
        if base_refs:
            each = base_refs[0].shape[1] // wide
            base = base_refs[i // each].at[:, i % each * wide : (i % each + 1) * wide]
        bwd_pair(q, out, rest, stat, up, dq, [(*near, *other, dkv)], None, valid, base)

    for i in range(count):
        one(i)


def bwd_pair_s(q_ref, out_ref, rest_ref, stat_ref, up_ref, dq_ref, key_sides, bias, valid, base_ref=None):
    rows, queries, depth = key_sides[0][0].shape[0], q_ref.shape[0], 1
    kc = rows
    wide = 2 * HEAD_DIM
    lane_q, lane_k = lanes(queries), lanes(rows)
    low_q = lane_q < HEAD_DIM
    q_all = q_ref[...].astype(F32) * HEAD_DIM**-0.5
    up_all = up_ref[...].astype(F32)
    stat = stat_ref[...]
    prods = up_all * (out_ref[...].astype(F32) + rest_ref[...].astype(F32))
    q_turned = (q_all.astype(BF)).T
    up_turned = up_ref[...].T
    heads, both = [], []
    for h in range(2):
        q = q_all if h == 0 else pltpu.roll(q_all, HEAD_DIM, 1)
        lse = stat if h == 0 else pltpu.roll(stat, HEAD_DIM, 1)
        up = up_all if h == 1 else pltpu.roll(up_all, HEAD_DIM, 1)
        a0, a1, a2 = split3(-lse)
        pad = jnp.where(lane_q == HEAD_DIM, 1.0, jnp.where(lane_q == HEAD_DIM + 1, a0, jnp.where(lane_q == HEAD_DIM + 2, a1, jnp.where(lane_q == HEAD_DIM + 3, a2, 0.0))))
        q_aug = jnp.where(low_q, q, pad).astype(BF)
        centre = jnp.sum(jnp.where(low_q if h == 0 else ~low_q, prods, 0.0), axis=1, keepdims=True)
        d0, d1, d2 = split3(-centre)
        pad = jnp.where(lane_q == 0, d0, jnp.where(lane_q == 1, d1, jnp.where(lane_q == 2, d2, 0.0)))
        up_aug = jnp.where(low_q, pad, up).astype(BF)
        heads.append((q_aug, up_aug, q_turned[h * HEAD_DIM : (h + 1) * HEAD_DIM], up_turned[h * HEAD_DIM : (h + 1) * HEAD_DIM]))
        sides = []
        for ref, out in key_sides:
            kv = ref[:, h * wide : (h + 1) * wide]
            keys = key_aug(kv, valid, 3)
            values = jnp.where(lane_k < HEAD_DIM, jnp.where(lane_k < 3, 1.0, 0.0).astype(BF), kv)
            sides.append((keys, values, kv, out))
        both.append(sides)
    items = [(h, side, at) for h in range(2) for side in range(len(key_sides)) for at in range(0, rows, kc)]
    def score(item):
        h, side, at = item
        keys, values, _, _ = both[h][side]
        return dot_nt(heads[h][0], keys[at : at + kc]), dot_nt(heads[h][1], values[at : at + kc])
    ahead = [score(i) for i in items[:depth]]
    totals = [0.0, 0.0]
    for n, (h, side, at) in enumerate(items):
        if n + depth < len(items):
            ahead.append(score(items[n + depth]))
        s, dp = ahead.pop(0)
        p = jnp.exp(s)
        ds = (p * dp).astype(BF)
        p = p.astype(BF)
        _, _, kv, out = both[h][side]
        pair = jnp.concatenate([dot_nn(heads[h][2], ds), dot_nn(heads[h][3], p)], axis=0)
        out[at : at + kc, h * wide : (h + 1) * wide] = pair.T.astype(BF)
        totals[h] = totals[h] + dot_nn(ds, kv[at : at + kc])
    dq = jnp.where(low_q, totals[0], pltpu.roll(totals[1], HEAD_DIM, 1)) * HEAD_DIM**-0.5
    dq_ref[...] = dq.astype(BF)


def bwd_pair(q_ref, out_ref, rest_ref, stat_ref, up_ref, dq_ref, key_sides, bias, valid, base_ref=None):
    masked, depth = bias is not None, 1
    rows, queries = key_sides[0][0].shape[0], q_ref.shape[0]
    kc = rows
    wide = 2 * HEAD_DIM
    lane_q, lane_k = lanes(queries), lanes(rows)
    low_q = lane_q < HEAD_DIM
    q_all = q_ref[...].astype(F32) * HEAD_DIM**-0.5
    up_all = up_ref[...].astype(F32)
    stat = stat_ref[...]
    prods = up_all * (out_ref[...].astype(F32) + rest_ref[...].astype(F32))
    heads, both = [], []
    for h in range(2):
        q = q_all if h == 0 else pltpu.roll(q_all, HEAD_DIM, 1)
        lse = stat if h == 0 else pltpu.roll(stat, HEAD_DIM, 1)
        up = up_all if h == 1 else pltpu.roll(up_all, HEAD_DIM, 1)
        a0, a1, a2 = split3(-lse)
        pad = jnp.where(lane_q == HEAD_DIM, 1.0, jnp.where(lane_q == HEAD_DIM + 1, a0, jnp.where(lane_q == HEAD_DIM + 2, a1, jnp.where(lane_q == HEAD_DIM + 3, a2, 0.0))))
        q_aug = jnp.where(low_q, q, pad).astype(BF)
        q_rhs = jnp.where(low_q, q, 0.0).astype(BF)
        centre = jnp.sum(jnp.where(low_q if h == 0 else ~low_q, prods, 0.0), axis=1, keepdims=True)
        d0, d1, d2 = split3(-centre)
        pad = jnp.where(lane_q == 0, d0, jnp.where(lane_q == 1, d1, jnp.where(lane_q == 2, d2, 0.0)))
        up_aug = jnp.where(low_q, pad, up).astype(BF)
        up_rhs = jnp.where(low_q, 0.0, up).astype(BF)
        heads.append((q_aug, q_rhs, up_aug, up_rhs))
        sides = []
        for ref, out in key_sides:
            kv = ref[:, h * wide : (h + 1) * wide]
            keys = key_aug(kv, valid, 3)
            values = jnp.where(lane_k < HEAD_DIM, jnp.where(lane_k < 3, 1.0, 0.0).astype(BF), kv)
            sides.append((keys, values, kv.T, out))
        both.append(sides)
    items = [(h, side, at) for h in range(2) for side in range(len(key_sides)) for at in range(0, rows, kc)]
    def score(item):
        h, side, at = item
        keys, values, _, _ = both[h][side]
        s = dot_nt(keys[at : at + kc], heads[h][0])
        if masked:
            first = at + side * rows
            s = s + bias[first : first + kc]
        return s, dot_nt(values[at : at + kc], heads[h][2])
    ahead = [score(i) for i in items[:depth]]
    totals = [0.0, 0.0]
    for n, (h, side, at) in enumerate(items):
        if n + depth < len(items):
            ahead.append(score(items[n + depth]))
        s, dp = ahead.pop(0)
        p = jnp.exp(s)
        ds = (p * dp).astype(BF)
        p = p.astype(BF)
        _, _, turned, out = both[h][side]
        out[at : at + kc, h * wide : (h + 1) * wide] = (dot_nn(ds, heads[h][1]) + dot_nn(p, heads[h][3])).astype(BF)
        totals[h] = totals[h] + dot_nn(turned[:, at : at + kc], ds)
    turned_dq = [v[:HEAD_DIM] for v in totals]
    dq = jnp.concatenate(turned_dq, axis=0).T * HEAD_DIM**-0.5
    if base_ref is not None:
        dq = dq + base_ref[...]
    dq_ref[...] = dq.astype(dq_ref.dtype)


def shape_of(rows, width, kind=BF):
    return jax.ShapeDtypeStruct((rows, width), kind)


def params(megabytes, *semantics):
    return pltpu.CompilerParams(vmem_limit_bytes=megabytes * 2**20)


def attention_cost(q, kl, products):
    flops = 2 * products * q.shape[0] * 2 * kl.shape[0] * q.shape[1] * 3
    return pl.CostEstimate(
        flops=flops, bytes_accessed=8 * q.size + 6 * kl.size, transcendentals=0
    )


class Far:
    def __init__(self, value, pieces=1, by_core=False):
        self.value, self.pieces, self.by_core = value, pieces, by_core
        self.shape, self.dtype = value.shape[1:] if by_core else value.shape, value.dtype
        self.size = math.prod(self.shape)


class Clip:
    def __init__(self, value):
        self.value, self.shape, self.dtype, self.size = value, value.shape, value.dtype, value.size


class Incoming:
    def __init__(self, source, held, arrived, pieces):
        self.held, self.shape, self.dtype = held, held.shape, held.dtype
        rows = held.shape[0] // pieces
        self.spans = [pl.ds(n * rows, rows) for n in range(pieces)]
        self.copies = [
            pltpu.make_async_copy(source.at[span], held.at[span], arrived.at[n])
            for n, span in enumerate(self.spans)
        ]

    def start(self, n):
        if n < len(self.copies):
            self.copies[n].start()

    def wait(self, n):
        if self.copies[n] is not None:
            self.copies[n].wait()
            self.copies[n] = None

    def piece(self, n):
        return Piece(self, n)

    def settle(self):
        for n in range(len(self.copies)):
            self.wait(n)
        return self.held

    @property
    def at(self):
        return self.settle().at

    def __getitem__(self, index):
        return self.settle()[index]


class Piece:
    def __init__(self, whole, n):
        self.whole, self.n = whole, n
        rows = whole.held.shape[0] // len(whole.spans)
        self.shape, self.dtype = (rows, *whole.held.shape[1:]), whole.held.dtype

    def __getitem__(self, index):
        self.whole.wait(self.n)
        return self.whole.held.at[self.whole.spans[self.n]][index]


class Padded:
    def __init__(self, ref, section, rows):
        self.ref, self.section, self.rows = ref, section, rows
        self.shape, self.dtype = (rows, ref.shape[2]), ref.dtype

    def __getitem__(self, index):
        value = self.ref[self.section]
        behind = jnp.zeros((self.rows - value.shape[0], value.shape[1]), value.dtype)
        return jnp.concatenate([value, behind], axis=0)[index]


class Outgoing:
    def __init__(self, target, held, left):
        self.target, self.held, self.left, self.copies = target, held, left, []
        self.at, self.shape, self.dtype = held.at, held.shape, held.dtype

    def __setitem__(self, index, value):
        self.held[index] = value

    def push(self, index=(slice(None), slice(None))):
        copy = pltpu.make_async_copy(
            self.held.at[index], self.target.at[index], self.left.at[len(self.copies)]
        )
        copy.start()
        self.copies.append(copy)

    def finish(self):
        for copy in self.copies or ():
            copy.wait()
        self.copies = None

    def again(self):
        copy = pltpu.make_async_copy(self.held, self.target, self.left.at[0])
        copy.start()
        copy.wait()


def push(ref, *index):
    if isinstance(ref, Outgoing):
        ref.push(*index)


def in_vmem():
    return pl.BlockSpec(memory_space=pltpu.VMEM)


def in_hbm():
    return pl.BlockSpec(memory_space=pltpu.HBM)


def flat_call(kernel, operands, out_shape, scal=None, scratch=(), flops=0, megabytes=40):
    touched = sum(v.size * v.dtype.itemsize for v in operands)
    touched += sum(math.prod(v.shape) * v.dtype.itemsize for v in out_shape)
    far_in = [v for v in operands if isinstance(v, Far)]
    far_out = [v for v in out_shape if isinstance(v, Far)]
    extra = []
    for v in (*far_in, *far_out):
        extra += [pltpu.VMEM(v.shape, v.dtype), pltpu.SemaphoreType.DMA((v.pieces,))]
        megabytes += -(-v.size * v.dtype.itemsize // 2**20)

    def run(*refs):
        refs = list(refs)
        take = lambda count: [refs.pop(0) for _ in range(count)]
        head = take(0 if scal is None else 1)
        ins, outs, own = take(len(operands)), take(len(out_shape)), take(len(scratch))
        moving = []
        for n, v in enumerate(operands):
            if isinstance(v, Far):
                source = ins[n].at[head[0][SCAL_CORE]] if v.by_core else ins[n]
                ins[n] = Incoming(source, *take(2), v.pieces)
                moving.append(ins[n])
            elif isinstance(v, Clip):
                ins[n] = Padded(ins[n], head[0][SCAL_SECTION], round_up(v.shape[1]))
        for n, v in enumerate(out_shape):
            if isinstance(v, Far):
                outs[n] = Outgoing(outs[n], *take(2))
        for n in range(max((len(v.copies) for v in moving), default=0)):
            for v in moving:
                v.start(n)
        kernel(*head, *ins, *outs, *own)
        for v in moving:
            v.settle()
        for v in outs:
            if isinstance(v, Outgoing):
                if v.copies == []:
                    v.push()
                v.finish()

    bare = lambda v: v.value if isinstance(v, (Far, Clip)) else v
    pin = lambda v: pltpu.with_memory_space_constraint(v.value, pltpu.HBM) if isinstance(v, Far) else bare(v)
    pin_shape = lambda v: pltpu.HBM(v.shape, v.dtype) if isinstance(v, Far) else v
    place = lambda v: in_hbm() if isinstance(v, Far) else in_vmem()
    return pl.pallas_call(
        run,
        in_specs=([] if scal is None else [pl.BlockSpec(memory_space=pltpu.SMEM)])
        + [place(v) for v in operands],
        out_specs=[place(v) for v in out_shape],
        out_shape=[pin_shape(v) for v in out_shape],
        scratch_shapes=list(scratch) + extra,
        compiler_params=params(megabytes),
        cost_estimate=pl.CostEstimate(flops=flops, bytes_accessed=touched, transcendentals=0),
    )(*([] if scal is None else [scal]), *[pin(v) for v in operands])


def attention_flops(q, kl, products, share=1):
    return 2 * products * q.shape[0] * 2 * kl.shape[0] * q.shape[1] * 4 // share


def attention_fwd(q, kl, kr, valid, scal=None):
    return flat_call(
        functools.partial(fwd_kernel, valid=valid, masked=scal is not None, kc=kl.shape[0], depth=1),
        [q, kl, kr],
        [shape_of(*q.shape), Far(shape_of(*q.shape), 8), Far(shape_of(*q.shape, F32), 8)],
        scal=scal, flops=attention_flops(q, kl, 2), megabytes=24 if q.shape[0] > CHUNK else 12,
    )


def attention_bwd(q, kl, kr, out, rest, stat, up, valid, scal=None):
    return flat_call(
        functools.partial(bwd_kernel, valid=valid, masked=scal is not None),
        [q, kl, kr, out, rest, stat, up],
        [shape_of(*q.shape), shape_of(*kl.shape), shape_of(*kl.shape)],
        scal=scal, flops=attention_flops(q, kl, 5), megabytes=12,
    )


def attention_bwd_side(q, kv, out, rest, stat, up, valid, base=(), pairs=None, earlier=()):
    far = not base
    total = q.shape[1] // (2 * HEAD_DIM)
    first, count = pairs or (0, total)
    width = kv.shape[1] // total * count + sum(v.shape[1] for v in earlier)
    return flat_call(
        functools.partial(
            bwd_side_kernel, valid=valid, far=far, first=first, count=count, joined=bool(earlier)
        ),
        [q, kv, out, rest, stat, up, *base, *earlier],
        [shape_of(q.shape[0], q.shape[1] // total * count, F32 if far else BF), shape_of(kv.shape[0], width)],
        flops=attention_flops(q, kv, 5, 2), megabytes=18,
    )


def rows_call(
    kernel, rows, blocked, whole, outs, sums=(), scratch=(), reverse=False, flops=0, megabytes=10, scal=None,
    told=False,
):
    steps = rows // CHUNK
    order = list(range(steps))
    if reverse:
        order = order[::-1]

    def chunk_of(ref, chunk):
        if isinstance(ref, Incoming):
            return ref.piece(chunk)
        return ref if isinstance(ref, Padded) else ref.at[pl.ds(chunk * CHUNK, CHUNK)]

    def run(*refs):
        refs = list(refs)
        take = lambda count: [refs.pop(0) for _ in range(count)]
        head = take(0 if scal is None else 1)
        kept, by_chunk = take(len(whole)), take(len(blocked))
        out, total = take(len(outs)), take(len(sums))
        for n, chunk in enumerate(order):
            kernel(
                n, *(head if told else ()), *[chunk_of(r, chunk) for r in by_chunk], *kept,
                *[chunk_of(r, chunk) for r in out], *total, *refs,
            )
            for r in out:
                push(r, (pl.ds(chunk * CHUNK, CHUNK), slice(None)))

    out_shape = []
    for width, kind, *far in outs:
        shape = shape_of(rows, width, kind)
        out_shape.append(Far(shape, steps) if far else shape)
    for shape, kind, *far in sums:
        shape = jax.ShapeDtypeStruct(shape, kind)
        out_shape.append(Far(shape) if far else shape)
    blocked = [Far(v.value, steps, v.by_core) if isinstance(v, Far) else v for v in blocked]
    return flat_call(run, [*whole, *blocked], out_shape, scal, scratch, flops, megabytes)


def tap_weights(first_ref):
    pieces = []
    for tap in range(first_ref.shape[0]):
        rows = first_ref[tap]
        pieces += [rows, jnp.zeros((LANES - rows.shape[0], rows.shape[1]), rows.dtype)]
    return jnp.concatenate(pieces, axis=0)


def mel_windows(scal_ref, mel_ref, mel_rows_ref, windows_ref, halo_ref, valid):
    rows = windows_ref.shape[0]
    channels, frames = mel_ref.shape[1:]
    front = 8
    mel_rows_ref[...] = jnp.zeros_like(mel_rows_ref)
    mel_rows_ref[front : front + frames, :channels] = mel_ref[scal_ref[SCAL_SECTION]].astype(F32).T
    lanes_all = slice(None)
    for core in range(frames // (2 * valid)):

        @pl.when(scal_ref[SCAL_CORE] == core)
        def _():
            base = front + 2 * valid * core
            for n in range(4):
                taken = mel_rows_ref[pl.ds(base + n - 1, rows, stride=2), lanes_all]
                windows_ref[:, n * LANES : (n + 1) * LANES] = taken.astype(BF)
            halo_ref[...] = jnp.zeros_like(halo_ref)
            if core > 0:
                for n in range(3):
                    part = mel_rows_ref[pl.ds(base - 2 + n, 16), lanes_all]
                    first = lax.broadcasted_iota(jnp.int32, part.shape, 0) == 0
                    halo_ref[:, n * LANES : (n + 1) * LANES] = jnp.where(first, part, 0.0).astype(BF)


def stem_fwd_kernel(
    chunk, scal_ref, pos_ref, mel_ref, first_ref, second_ref,
    even_ref, odd_ref, before_ref, ge_ref, go_ref, gs_ref, x_ref, gh_ref, windows_ref, halo_ref,
    carry_ref, mel_rows_ref, *, valid,
):
    first = tap_weights(first_ref)
    if chunk == 0:
        mel_windows(scal_ref, mel_ref, mel_rows_ref, windows_ref, halo_ref, valid)
        push(windows_ref)
        act, slope = gelu_pair(dot_nn(halo_ref[...], first))
        carry_ref[...] = act[:8]
        gh_ref[...] = slope
    span = pl.ds(chunk * CHUNK, CHUNK)
    me_ref = windows_ref.at[span, : 3 * LANES]
    mo_ref = windows_ref.at[span, LANES:]

    width = even_ref.shape[1]
    even, slope = gelu_pair(dot_nn(me_ref[...], first))
    even = even.astype(BF)
    even_ref[...] = even
    ge_ref[...] = slope.astype(BF)
    odd, slope = gelu_pair(dot_nn(mo_ref[...], first))
    go_ref[...] = slope.astype(BF)
    row = lax.broadcasted_iota(jnp.int32, odd.shape, 0)
    before = jnp.where(row == 0, carry_ref[0:1, :], pltpu.roll(odd, 1, 0)).astype(BF)
    carry_ref[0:1, :] = odd[CHUNK - 1 :]
    odd = odd.astype(BF)
    odd_ref[...] = odd
    before_ref[...] = before
    pre = dot_nn(before, second_ref[:width])
    pre += dot_nn(even, second_ref[width : 2 * width])
    pre += dot_nn(odd, second_ref[2 * width :])
    act, slope = gelu_pair(pre)
    gs_ref[...] = slope.astype(BF)
    x_ref[...] = act + pos_ref[...]


def qkv_kernel(step, x_ref, gain_ref, bias_ref, own_ref, oth_ref, normed_ref, q_ref, kv_ref):
    unit, _ = norm_stats(x_ref[...].astype(F32))
    normed = (unit * gain_ref[...] + bias_ref[...]).astype(BF)
    normed_ref[...] = normed
    heads = own_ref.shape[1] // (3 * HEAD_DIM)
    for part, w_ref in enumerate((own_ref, oth_ref)):
        packed = dot_nn(normed, w_ref[...]).astype(BF)
        for h in range(heads):
            at, to = h * 3 * HEAD_DIM, part * heads + h
            q_ref[:, to * HEAD_DIM : (to + 1) * HEAD_DIM] = packed[:, at : at + HEAD_DIM]
            kv_ref[:, to * 2 * HEAD_DIM : (to + 1) * 2 * HEAD_DIM] = packed[
                :, at + HEAD_DIM : at + 3 * HEAD_DIM
            ]


def two_parts(rows, own_ref, oth_ref):
    depth = own_ref.shape[0]
    return dot_nn(rows[:, :depth], own_ref[...]) + dot_nn(rows[:, depth:], oth_ref[...])


def two_parts_t(rows, own_ref, oth_ref):
    depth = own_ref.shape[1]
    return dot_nt(rows[:, :depth], own_ref[...]) + dot_nt(rows[:, depth:], oth_ref[...])


def enc_mid_kernel(
    step, x_ref, att_ref, gb_ref, bb_ref, gc_ref, bc_ref, po_ref, pt_ref, uo_ref, ut_ref, do_ref, dt_ref,
    ko_ref, kt_ref,
    x1_ref, x2_ref, normed_ref, hidden_ref, slope_ref, memory_ref, kv_ref,
):
    x1 = x_ref[...] + two_parts(att_ref[...], po_ref, pt_ref)
    x1_ref[...] = x1
    unit, _ = norm_stats(x1)
    normed = (unit * gb_ref[...] + bb_ref[...]).astype(BF)
    normed_ref[...] = normed
    half = uo_ref.shape[1]
    x2 = x1
    for part, (up_ref, down_ref) in enumerate(((uo_ref, do_ref), (ut_ref, dt_ref))):
        act, slope = gelu_pair(dot_nn(normed, up_ref[...]))
        act = act.astype(BF)
        hidden_ref[:, part * half : (part + 1) * half] = act
        slope_ref[:, part * half : (part + 1) * half] = slope.astype(BF)
        x2 = x2 + dot_nn(act, down_ref[...])
    x2_ref[...] = x2
    unit, _ = norm_stats(x2)
    memory = (unit * gc_ref[...] + bc_ref[...]).astype(BF)
    memory_ref[...] = memory
    half = ko_ref.shape[1]
    kv_ref[:, :half] = dot_nn(memory, ko_ref[...]).astype(BF)
    kv_ref[:, half:] = dot_nn(memory, kt_ref[...]).astype(BF)


def dec_mid_kernel(
    step, x_ref, att_ref, gain_ref, bias_ref, po_ref, pt_ref, qo_ref, qt_ref, y_ref, normed_ref, q_ref
):
    y = x_ref[...].astype(F32) + two_parts(att_ref[...], po_ref, pt_ref)
    y_ref[...] = y
    unit, _ = norm_stats(y)
    normed = (unit * gain_ref[...] + bias_ref[...]).astype(BF)
    normed_ref[...] = normed
    half = qo_ref.shape[1]
    q_ref[:, :half] = dot_nn(normed, qo_ref[...]).astype(BF)
    q_ref[:, half:] = dot_nn(normed, qt_ref[...]).astype(BF)


def mlp_back(gb, slope_ref, dpre_ref, uo_ref, ut_ref, do_ref, dt_ref):
    half = uo_ref.shape[1]
    total = 0.0
    for part, (up_ref, down_ref) in enumerate(((uo_ref, do_ref), (ut_ref, dt_ref))):
        span = slice(part * half, (part + 1) * half)
        dpre = (dot_nt(gb, down_ref[...]) * slope_ref[:, span].astype(F32)).astype(BF)
        dpre_ref[:, span] = dpre
        total = total + dot_nt(dpre, up_ref[...])
    return total


def section_halves(scal_ref, value, mine_ref, sent_ref):
    rows, half = mine_ref.shape
    left, right = value[:rows, :half], value[:rows, half:]
    lower = scal_ref[SCAL_SECTION] == 0
    mine_ref[...] = jnp.where(lower, left, right).astype(mine_ref.dtype)
    sent_ref[...] = jnp.where(lower, right, left).astype(sent_ref.dtype)


def owners_kernel(scal_ref, *refs):
    count = len(refs) // 3
    section = scal_ref[SCAL_SECTION]
    for mine_ref, got_ref, out_ref in zip(refs[:count], refs[count : 2 * count], refs[2 * count :]):
        out_ref[section] = mine_ref[...]
        out_ref[1 - section] = got_ref[...].astype(out_ref.dtype)


def dec_top_kernel(
    scal_ref, y1_ref, crossed_ref, cot_ref, gain_ref, bias_ref, po_ref, pt_ref, uo_ref, ut_ref,
    do_ref, dt_ref,
    decoded_ref, sent_ref, normed_ref, hidden_ref, dpre_ref, gb3_ref, gb2_ref, dcrossed_ref, u2_ref,
    sums_ref, slope_ref, *, valid,
):
    rows = y1_ref.shape[0]
    y2 = y1_ref[...] + two_parts(crossed_ref[...], po_ref, pt_ref)
    unit, inverse = norm_stats(y2)
    normed = (unit * gain_ref[...] + bias_ref[...]).astype(BF)
    normed_ref[...] = normed
    push(normed_ref)
    half = uo_ref.shape[1]
    y3 = y2
    for part, (up_ref, down_ref) in enumerate(((uo_ref, do_ref), (ut_ref, dt_ref))):
        act, slope = gelu_pair(dot_nn(normed, up_ref[...]))
        act = act.astype(BF)
        hidden_ref[:, part * half : (part + 1) * half] = act
        slope_ref[:, part * half : (part + 1) * half] = slope.astype(BF)
        y3 = y3 + dot_nn(act, down_ref[...])
    push(hidden_ref)
    row = lax.broadcasted_iota(jnp.int32, y2.shape, 0)
    length = scal_ref[SCAL_LENGTHS + scal_ref[SCAL_SECTION]]
    live = ((row < valid) & (row + scal_ref[SCAL_CORE] * valid < length)).astype(F32)
    section_halves(scal_ref, y3 * live, decoded_ref, sent_ref)
    u3 = cot_ref[...].astype(F32) * live
    gb3 = u3.astype(BF)
    gb3_ref[...] = gb3
    push(gb3_ref)
    dnormed = mlp_back(gb3, slope_ref, dpre_ref, uo_ref, ut_ref, do_ref, dt_ref)
    push(dpre_ref)
    dy, dgain, dbias = norm_back(unit, inverse, gain_ref[...], dnormed)
    u2 = u3 + dy
    u2_ref[...] = u2
    gb2 = u2.astype(BF)
    gb2_ref[...] = gb2
    push(gb2_ref)
    half = po_ref.shape[0]
    dcrossed_ref[:, :half] = dot_nt(gb2, po_ref[...]).astype(BF)
    dcrossed_ref[:, half:] = dot_nt(gb2, pt_ref[...]).astype(BF)
    sums_ref[...] = jnp.zeros_like(sums_ref)
    sums_ref[0:1, :] = dgain
    sums_ref[1:2, :] = dbias


def dec_back_kernel(
    step, dq_ref, y1_ref, u2_ref, gain_ref, qo_ref, qt_ref, po_ref, pt_ref,
    u1_ref, gb1_ref, datt_ref, sums_ref,
):
    dnormed = two_parts_t(dq_ref[...], qo_ref, qt_ref)
    unit, inverse = norm_stats(y1_ref[...])
    dy, dgain, dbias = norm_back(unit, inverse, gain_ref[...], dnormed)
    u1 = u2_ref[...] + dy
    u1_ref[...] = u1
    gb1 = u1.astype(BF)
    gb1_ref[...] = gb1
    half = po_ref.shape[0]
    datt_ref[:, :half] = dot_nt(gb1, po_ref[...]).astype(BF)
    datt_ref[:, half:] = dot_nt(gb1, pt_ref[...]).astype(BF)
    sums_ref[...] = jnp.zeros_like(sums_ref)
    sums_ref[0:1, :] = dgain
    sums_ref[1:2, :] = dbias


def packed_back(dq_ref, dkl_ref, dkr_ref, own_ref, oth_ref, out_ref):
    dkv = (dkl_ref[...].astype(F32) + dkr_ref[...].astype(F32)).astype(BF)
    dq = dq_ref[...]
    heads = own_ref.shape[1] // (3 * HEAD_DIM)
    total = 0.0
    for part, w_ref in enumerate((own_ref, oth_ref)):
        pieces = []
        for h in range(part * heads, (part + 1) * heads):
            pieces.append(dq[:, h * HEAD_DIM : (h + 1) * HEAD_DIM])
            pieces.append(dkv[:, h * 2 * HEAD_DIM : (h + 1) * 2 * HEAD_DIM])
        packed = jnp.concatenate(pieces, axis=1)
        out_ref[:, part * w_ref.shape[1] : (part + 1) * w_ref.shape[1]] = packed
        total = total + dot_nt(packed, w_ref[...])
    return total


def dec_last_kernel(
    step, scal_ref, dq_ref, dkl_ref, dkr_ref, x_ref, u1_ref, gain_ref, own_ref, oth_ref,
    packed_ref, sums_ref, mine_ref, sent_ref,
):
    dnormed = packed_back(dq_ref, dkl_ref, dkr_ref, own_ref, oth_ref, packed_ref)
    unit, inverse = norm_stats(x_ref[...].astype(F32))
    dx, dgain, dbias = norm_back(unit, inverse, gain_ref[...], dnormed)
    section_halves(scal_ref, u1_ref[...] + dx, mine_ref, sent_ref)
    sums_ref[...] = jnp.zeros_like(sums_ref)
    sums_ref[0:1, :] = dgain
    sums_ref[1:2, :] = dbias


def enc_back_kernel(
    step, gl_ref, gr_ref, x2_ref, x1_ref, slope_ref, gc_ref, gb_ref, ko_ref, kt_ref, uo_ref, ut_ref,
    do_ref, dt_ref, po_ref, pt_ref,
    gkv_ref, gb2_ref, dpre_ref, gb1_ref, datt_ref, u1_ref, sums_ref,
):
    if step == 0:
        sums_ref[...] = jnp.zeros_like(sums_ref)

    gkv = (gl_ref[...].astype(F32) + gr_ref[...].astype(F32)).astype(BF)
    gkv_ref[...] = gkv
    dmemory = two_parts_t(gkv, ko_ref, kt_ref)
    unit, inverse = norm_stats(x2_ref[...])
    u2, dgain, dbias = norm_back(unit, inverse, gc_ref[...], dmemory)
    sums_ref[0:1, :] += dgain
    sums_ref[1:2, :] += dbias
    gb2 = u2.astype(BF)
    gb2_ref[...] = gb2
    dnormed = mlp_back(gb2, slope_ref, dpre_ref, uo_ref, ut_ref, do_ref, dt_ref)
    unit, inverse = norm_stats(x1_ref[...])
    dx, dgain, dbias = norm_back(unit, inverse, gb_ref[...], dnormed)
    sums_ref[2:3, :] += dgain
    sums_ref[3:4, :] += dbias
    u1 = u2 + dx
    u1_ref[...] = u1
    gb1 = u1.astype(BF)
    gb1_ref[...] = gb1
    half = po_ref.shape[0]
    datt_ref[:, :half] = dot_nt(gb1, po_ref[...]).astype(BF)
    datt_ref[:, half:] = dot_nt(gb1, pt_ref[...]).astype(BF)


def stem_back_kernel(
    step, dq_ref, dkl_ref, dkr_ref, x0_ref, u1_ref, ge_ref, go_ref, gs_ref, gain_ref, own_ref, oth_ref,
    second_ref, gh_ref,
    packed_ref, g2_ref, ede_ref, edo_ref, sums_ref, edh_ref, carry_ref,
):
    if step == 0:
        sums_ref[...] = jnp.zeros_like(sums_ref)
        carry_ref[...] = jnp.zeros_like(carry_ref)

    dnormed = packed_back(dq_ref, dkl_ref, dkr_ref, own_ref, oth_ref, packed_ref)
    unit, inverse = norm_stats(x0_ref[...])
    dx, dgain, dbias = norm_back(unit, inverse, gain_ref[...], dnormed)
    sums_ref[0:1, :] += dgain
    sums_ref[1:2, :] += dbias
    g2 = ((u1_ref[...] + dx) * gs_ref[...].astype(F32)).astype(BF)
    g2_ref[...] = g2
    width = g2.shape[1]
    before = dot_nt(g2, second_ref[:width])
    even = dot_nt(g2, second_ref[width : 2 * width])
    odd = dot_nt(g2, second_ref[2 * width :])
    ede_ref[...] = (even * ge_ref[...].astype(F32)).astype(BF)
    row = lax.broadcasted_iota(jnp.int32, before.shape, 0)
    later = jnp.where(
        row == CHUNK - 1, carry_ref[0:1, :], pltpu.roll(before, CHUNK - 1, 0)
    )
    carry_ref[0:1, :] = before[0:1]
    edo_ref[...] = ((odd + later) * go_ref[...].astype(F32)).astype(BF)
    front = lax.broadcasted_iota(jnp.int32, edh_ref.shape, 0)
    edh_ref[...] = jnp.where(front == 0, before[0:1] * gh_ref[...], 0.0).astype(BF)


SCAL_CORE, SCAL_SECTION, SCAL_X, SCAL_Z, SCAL_Z_LOW, SCAL_Z_HIGH, SCAL_LENGTHS = range(7)
TILE = 512


def gradient_tiles(left, right_ref, own_ref, oth_ref, at):
    turned, half = left.T, right_ref.shape[1] // 2
    for part, out_ref in enumerate((own_ref, oth_ref)):
        for first in range(0, half, TILE):
            width = min(TILE, half - first)
            piece = dot_nn(turned, right_ref[:, part * half + first : part * half + first + width])
            out_ref[:, at + first : at + first + width] = piece.astype(BF)
    return at + half


def gradients_kernel(*refs):
    *pairs, own_ref, oth_ref = refs
    at = 0
    for left_ref, right_ref in zip(pairs[::2], pairs[1::2]):
        at = gradient_tiles(left_ref[...], right_ref, own_ref, oth_ref, at)


def gradients(pairs):
    columns = sum(right.shape[1] // 2 for _, right in pairs)
    width = pairs[0][0].shape[1]
    return flat_call(
        gradients_kernel,
        [v for pair in pairs for v in pair],
        [shape_of(width, columns)] * 2,
        flops=sum(2 * left.size * right.shape[1] for left, right in pairs), megabytes=12,
    )


def late_kernel(
    scal_ref, normed_ref, packed_ref, g2_ref, before_ref, even_ref, odd_ref, ede_ref, edo_ref, edh_ref,
    windows_ref, mh_ref, va_ref, vb_ref, vc_ref, ve_ref, vf_ref, own_ref, oth_ref, stem_ref, *, channels,
):
    at = gradient_tiles(normed_ref[...], packed_ref, own_ref, oth_ref, 0)
    turned, width = g2_ref[...].T, g2_ref.shape[1]
    for n, ref in enumerate((before_ref, even_ref, odd_ref)):
        stem_ref[:, n * width : (n + 1) * width] = dot_nn(turned, ref[...]).astype(BF)
    windows = windows_ref[...].T
    first = dot_nn(windows[: 3 * LANES], ede_ref[...]) + dot_nn(windows[LANES:], edo_ref[...])
    first = first + dot_nn(mh_ref[...].T, edh_ref[...])
    vectors = [
        vf_ref[0:1], ve_ref[2:3], ve_ref[0:1], vf_ref[1:2], ve_ref[3:4], ve_ref[1:2],
        va_ref[0:1], vb_ref[0:1], vc_ref[0:1], va_ref[1:2], vb_ref[1:2], vc_ref[1:2],
        jnp.zeros((4, width), F32),
    ]
    taps = [first[n * LANES : n * LANES + channels] for n in range(first.shape[0] // LANES)]
    first = jnp.concatenate([*taps, jnp.concatenate(vectors, axis=0)], axis=0)
    stem_ref[:, 3 * width :] = first.T.astype(BF)
    core, half = scal_ref[SCAL_CORE], stem_ref.shape[1] // 2
    block = 16
    groups = width // (4 * block)
    for part, out_ref in enumerate((own_ref, oth_ref)):
        bit = core if part == 0 else 1 - core
        for group in range(groups):
            for section in range(2):
                source = pl.multiple_of(group * 4 * block + bit * 2 * block + section * block, block)
                rows = stem_ref[pl.ds(source, block), :]
                to = (section * groups + group) * 2 * block
                out_ref[to : to + block, at:] = rows[:, :half]
                out_ref[to + block : to + 2 * block, at:] = rows[:, half:]


def halves(scal_ref, bit, groups, size, total, keep_ref, send_ref, columns=slice(None)):
    for group in range(groups):
        for place, out_ref in ((scal_ref[bit], keep_ref), (1 - scal_ref[bit], send_ref)):
            source = pl.ds(pl.multiple_of((group * 2 + place) * size, size), size)
            out_ref[group * size : (group + 1) * size, columns] = total(source)


def first_kernel(scal_ref, own_ref, got_ref, am_ref, as_ref, bm_ref, bs_ref, *, cut, block):
    low = lambda rows: own_ref[rows, :cut] + got_ref[rows, :cut]
    high = lambda rows: own_ref[rows, cut:] + got_ref[rows, cut:]
    rows = own_ref.shape[0]
    halves(scal_ref, SCAL_X, rows // (2 * block), block, low, am_ref, as_ref)
    halves(scal_ref, SCAL_SECTION, 1, rows // 2, high, bm_ref, bs_ref)


def second_kernel(
    scal_ref, am_ref, ag_ref, bm_ref, bg_ref, akeep_ref, asend_ref, bkeep_ref, bsend_ref, *, block
):
    low = lambda rows: am_ref[rows, :] + ag_ref[rows, :]
    high = lambda rows: bm_ref[rows, :] + bg_ref[rows, :]
    rows = am_ref.shape[0]
    halves(scal_ref, SCAL_SECTION, 1, rows // 2, low, akeep_ref, asend_ref)
    halves(scal_ref, SCAL_X, rows // (2 * block), block, high, bkeep_ref, bsend_ref)


def third_kernel(scal_ref, am_ref, ag_ref, bm_ref, bg_ref, *out_refs, cut, block):
    for flip, out_ref in enumerate(out_refs):
        rows = pl.ds(pl.multiple_of((scal_ref[SCAL_Z] ^ flip) * block, block), block)
        out_ref[:, :cut] = am_ref[rows, :] + ag_ref[rows, :]
        out_ref[:, cut:] = bm_ref[rows, :] + bg_ref[rows, :]


def third_half_kernel(scal_ref, am_ref, ag_ref, bm_ref, bg_ref, keep_ref, send_ref, *, cut, block):
    low = lambda rows: am_ref[rows, :] + ag_ref[rows, :]
    high = lambda rows: bm_ref[rows, :] + bg_ref[rows, :]
    groups = am_ref.shape[0] // (2 * block)
    halves(scal_ref, SCAL_Z_LOW, groups, block, low, keep_ref, send_ref, slice(0, cut))
    halves(scal_ref, SCAL_Z_LOW, groups, block, high, keep_ref, send_ref, slice(cut, None))


def fourth_half_kernel(scal_ref, mine_ref, got_ref, keep_ref, send_ref, *, block):
    both = lambda rows: mine_ref[rows, :] + got_ref[rows, :]
    halves(scal_ref, SCAL_Z_HIGH, 1, block, both, keep_ref, send_ref)


def last_kernel(*refs, widths):
    count = len(refs) - len(widths)
    at = 0
    for out_ref, width in zip(refs[count:], widths):
        total = sum(ref[:, at : at + width].astype(F32) for ref in refs[:count])
        out_ref[...] = total
        at += width


def stem_last_kernel(scal_ref, mine_ref, got_ref, second_ref, first_ref, *vec_refs):
    mine, got = mine_ref[...], got_ref[...]
    lower = scal_ref[SCAL_SECTION] == 0
    block = mine.shape[0] // 2
    parts = []
    for half in (jnp.where(lower, mine, got), jnp.where(lower, got, mine)):
        parts.append(jnp.concatenate([half[:block], half[block:]], axis=1))
    full = jnp.concatenate(parts, axis=0)
    count, _, width = second_ref.shape
    channels = first_ref.shape[2]
    for n in range(count):
        second_ref[n] = full[:, n * width : (n + 1) * width]
        first_ref[n] = full[:, count * width + n * channels : count * width + (n + 1) * channels]
    turned = full[:, full.shape[1] - 2 * HEAD_DIM :].T
    at = turned.shape[0] - 16
    for n, ref in enumerate(vec_refs):
        ref[...] = turned[at + 3 * n : at + 3 * n + 3]


def sum_over_chips(own, oth, scal, cut, widths, direct=False):
    after = lambda value, other: value if other is None else tie(value, other)
    got = swap(oth, "tensor")
    rows, columns = own.shape
    block = rows // (2 * lax.axis_size("dp"))
    some = lambda n, w: shape_of(n, w)
    left, right = cut, columns - cut
    am, asend, bm, bsend = flat_call(
        functools.partial(first_kernel, cut=cut, block=block), [own, got],
        [some(rows // 2, left)] * 2 + [some(rows // 2, right)] * 2, scal, megabytes=6,
    )
    am = after(am, (yield am))
    ag, bg = flip_bit(asend, "dp", 1), swap(bsend, "section")
    am, asend, bm, bsend = flat_call(
        functools.partial(second_kernel, block=block), [am, ag, bm, bg],
        [some(rows // 4, left)] * 2 + [some(rows // 4, right)] * 2, scal, megabytes=6,
    )
    am = after(am, (yield am))
    ag, bg = swap(asend, "section"), flip_bit(bsend, "dp", 1)
    if direct:
        mine, *send = flat_call(
            functools.partial(third_kernel, cut=cut, block=block), [am, ag, bm, bg],
            [some(block, columns)] * (rows // (4 * block)), scal, megabytes=6,
        )
        mine = after(mine, (yield mine))
        got = [flip_bit(v, "dp", 2 * (n + 1)) for n, v in enumerate(send)]
    else:
        mine, send = flat_call(
            functools.partial(third_half_kernel, cut=cut, block=block), [am, ag, bm, bg],
            [some(2 * block, columns)] * 2, scal, megabytes=6,
        )
        mine = after(mine, (yield mine))
        mine, send = flat_call(
            functools.partial(fourth_half_kernel, block=block), [mine, flip_bit(send, "dp", 2)],
            [some(block, columns)] * 2, scal, megabytes=6,
        )
        mine = after(mine, (yield mine))
        got = [flip_bit(send, "dp", 4)]
    yield flat_call(
        functools.partial(last_kernel, widths=widths), [mine, *got],
        [shape_of(block, width, F32) for width in widths], megabytes=6,
    )


def tie(value, *others):
    return lax.optimization_barrier((value, *others))[0]


def swap(value, axis):
    return lax.ppermute(value, axis, [(0, 1), (1, 0)])


def flip_bit(value, axis, bit):
    count = lax.axis_size(axis)
    return lax.ppermute(value, axis, [(i, i ^ bit) for i in range(count)])


def add_low(left, right):
    return (left.astype(F32) + right.astype(F32)).astype(BF)


def halve(value, dim, place, send):
    mine = lax.dynamic_index_in_dim(value, place, dim, keepdims=False)
    other = lax.dynamic_index_in_dim(value, 1 - place, dim, keepdims=False)
    return mine, send(other)


def reduce_blocks(value, names):
    section, clip_group = lax.axis_index("section"), lax.axis_index("dp")
    dims = list(names)
    order = [name for name, _ in sorted(names.items(), key=lambda item: item[1])]
    held = value
    for step, name in enumerate(order):
        dim = [n for n in dims if n in order[step:]].index(name)
        if name == "section":
            mine, got = halve(held, dim, section, functools.partial(swap, axis="section"))
        else:
            place = (clip_group // name) % 2
            mine, got = halve(held, dim, place, functools.partial(flip_bit, axis="dp", bit=name))
        held = mine.astype(F32) + got.astype(F32)
        if step < len(order) - 1:
            held = held.astype(BF)
    return held


def dp_bits():
    count, bits = lax.axis_size("dp"), []
    while count > 1:
        count //= 2
        bits.append(count)
    return bits


def sum_projections(value):
    rows, columns = value.shape
    bits = dp_bits()
    lead = (2,) * (1 + len(bits))
    half = columns // 256 * 128
    out = []
    for which, part in enumerate((value[:, :half], value[:, half:])):
        shaped = part.reshape(*lead, rows // 2 ** len(lead), part.shape[1])
        early = {"section": 1, bits[-1]: 0} if which == 0 else {"section": 0, bits[-1]: 1}
        names = {"section": early["section"]}
        for at, bit in enumerate(bits):
            names[bit] = early.get(bit, 2 + at)
        out.append(reduce_blocks(shaped, names))
    return jnp.concatenate(out, axis=1)


def sum_stem(value):
    rows, columns = value.shape
    bits = dp_bits()
    place = lax.axis_index("tensor")
    groups = 2 ** len(bits)
    block = rows // (groups * 2)
    shaped = value.reshape(groups, 2, block, columns)
    mine, got = halve(shaped, 1, place, functools.partial(swap, axis="tensor"))
    held = add_low(mine, got)
    half = columns // 256 * 128
    out = []
    for which, part in enumerate((held[:, :, :half], held[:, :, half:])):
        shaped = part.reshape(*((2,) * len(bits)), 2, block // 2, part.shape[2])
        names = {bit: 2 + at for at, bit in enumerate(bits)}
        names[bits[-1]] = which
        names["section"] = 1 - which
        out.append(reduce_blocks(shaped, names))
    mine = jnp.concatenate(out, axis=1)
    got = swap(mine, "section")
    first = lax.axis_index("section") == 0
    return jnp.concatenate(
        [jnp.where(first, mine, got), jnp.where(first, got, mine)], axis=0
    )


def core_sum(pairs):
    full = [dot_tn(left, right).astype(BF) for left, right in pairs]
    mine = jnp.concatenate([v[:, : v.shape[1] // 2] for v in full], axis=1)
    sent = jnp.concatenate([v[:, v.shape[1] // 2 :] for v in full], axis=1)
    return add_low(mine, swap(sent, "tensor"))


def sinusoid_table(count, width_all):
    step_size = math.log(10000.0) / (width_all // 2 - 1)
    rates = np.exp(-step_size * np.arange(width_all // 2))
    angles = np.arange(count)[:, None] * rates[None, :]
    return np.concatenate([np.sin(angles), np.cos(angles)], axis=1).astype(np.float32)


def pad_rows(value, rows):
    return jnp.pad(value, ((0, rows - value.shape[0]), (0, 0)))


def round_up(count):
    return -(-count // CHUNK) * CHUNK


def body(
    mel,
    conv_first,
    conv_second,
    enc_gain,
    enc_shift,
    enc_qkv,
    enc_proj,
    enc_up,
    enc_down,
    cross_kv,
    text,
    lengths,
    dec_gain,
    dec_shift,
    dec_qkv,
    dec_proj,
    cross_query,
    cross_proj,
    dec_up,
    dec_down,
    cotangent,
):
    section = lax.axis_index("section")
    place = lax.axis_index("tensor")
    cores = lax.axis_size("tensor")
    width = text.shape[2]
    frames = mel.shape[1] // 2
    valid = frames // cores
    rows = round_up(valid)
    slots = text.shape[1]
    text_rows = round_up(slots)
    channels = mel.shape[2]

    group = lax.axis_index("dp")
    bits = [place, section, group % 2, group // 2, group // 2 % 2, group // 4 % 2]
    scal = jnp.concatenate([jnp.stack([bit.astype(jnp.int32) for bit in bits]), lengths])
    pair = lambda w: (w, swap(w, "tensor"))
    w_dqkv, w_eqkv, w_eproj, w_dproj, w_cq = map(pair, (dec_qkv, enc_qkv, enc_proj, dec_proj, cross_query))
    w_eup, w_edown, w_ckv = map(pair, (enc_up, enc_down, cross_kv))
    w_cproj, w_dup, w_ddown = map(pair, (cross_proj, dec_up, dec_down))
    early = [w[1] for w in (w_eproj, w_dproj, w_cq, w_cproj)]
    late = [w[1] for w in (w_eup, w_edown, w_ckv, w_dup, w_ddown)]
    eg, es = [enc_gain[i : i + 1] for i in range(3)], [enc_shift[i : i + 1] for i in range(3)]
    dg, ds = [dec_gain[i : i + 1] for i in range(3)], [dec_shift[i : i + 1] for i in range(3)]

    taps = conv_first.shape[0] * channels
    depth = -(-(taps + 12) // LANES) * LANES
    second = conv_second.reshape(-1, width)
    table = np.pad(sinusoid_table(frames, width), ((0, rows - valid), (0, 0)))
    table = jnp.asarray(np.stack([table[valid * core : valid * core + rows] for core in range(cores)]))

    dn_a, dq_self, dkv_self = rows_call(
        qkv_kernel, text_rows, [Clip(text)], [dg[0], ds[0], *w_dqkv],
        [(width, BF, Far), (width, BF), (2 * width, BF)], flops=2 * text_rows * width * 3 * width, scal=scal,
    )
    dkv_self_r = swap(dkv_self, "tensor")

    mel_rows = 2 * frames + 8 + 2 * (rows - valid) + 16
    even, odd, before, ge, go, gs, x0, gh, windows, halo = rows_call(
        functools.partial(stem_fwd_kernel, valid=valid), rows, [Far(table, 1, True)],
        [Far(jnp.swapaxes(mel, 1, 2)), Far(conv_first), Far(second)],
        [(width, BF, Far)] * 6 + [(width, F32)],
        sums=[((16, width), F32), ((rows, 4 * LANES), BF, Far), ((16, 3 * LANES), BF)],
        scratch=[pltpu.VMEM((8, width), F32), pltpu.VMEM((mel_rows, LANES), F32)],
        flops=2 * rows * width * 2000, scal=scal, told=True, megabytes=14,
    )
    en_a, eq, ekv = rows_call(
        qkv_kernel, rows, [tie(x0, dq_self, *early)], [eg[0], es[0], *w_eqkv],
        [(width, BF, Far), (width, BF), (2 * width, BF)], flops=2 * rows * width * 3 * width,
    )
    ekv_r = swap(ekv, "tensor")

    datt, drest, dstat = attention_fwd(dq_self, dkv_self, dkv_self_r, slots, scal)
    eq = tie(eq, datt)
    eatt, erest, estat = attention_fwd(eq, ekv, ekv_r, valid)
    units = 2 * enc_up.shape[1]
    x1, x2, en_b, ehid, eslope, memory, ckv = rows_call(
        enc_mid_kernel, rows, [x0, tie(eatt, *late)],
        [eg[1], es[1], eg[2], es[2], *w_eproj, *w_eup, *w_edown, *w_ckv],
        [
            (width, F32, Far), (width, F32, Far), (width, BF, Far), (units, BF, Far), (units, BF, Far),
            (width, BF, Far), (2 * width, BF),
        ],
        flops=2 * rows * width * (3 * width + 2 * units), megabytes=20,
    )
    ckv_r = swap(ckv, "tensor")
    y1, dn_b, cq = rows_call(
        dec_mid_kernel, text_rows, [Clip(text), tie(datt, ckv)], [dg[1], ds[1], *w_dproj, *w_cq],
        [(width, F32), (width, BF, Far), (width, BF)], flops=2 * text_rows * width * 2 * width, scal=scal,
    )

    crossed, crest, cstat = attention_fwd(cq, ckv, ckv_r, valid)
    dec_units = 2 * dec_up.shape[1]
    top_outs = [
        (width, BF), (dec_units, BF), (dec_units, BF), (width, BF), (width, BF), (width, BF), (width, F32),
    ]
    owned = lambda kind: shape_of(slots, width // 2, kind)
    decoded, decoded_sent, dn_c, dhid, dpre, dgb3, dgb2, dcrossed, u2, sums_c = flat_call(
        functools.partial(dec_top_kernel, valid=slots),
        [y1, crossed, Clip(cotangent), dg[2], ds[2], *w_cproj, *w_dup, *w_ddown],
        [owned(BF), owned(BF)] + [shape_of(text_rows, w, k) for w, k in top_outs] + [shape_of(8, width, F32)],
        scal=scal, scratch=[pltpu.VMEM((text_rows, dec_units), BF)],
        flops=2 * text_rows * width * (2 * width + 4 * dec_units), megabytes=12,
    )
    decoded_got = swap(decoded_sent, "section")
    fast = lax.axis_size("dp") == 8 and width % (4 * 8 * 16) == 0
    top_pairs = [(dn_c, dpre), (dgb3, dhid), (dgb2, crossed)]
    top_widths = [dec_up.shape[1], dec_down.shape[0], cross_proj.shape[0]]
    if fast:
        own, oth = gradients(top_pairs)
        top_steps = sum_over_chips(own, oth, scal, sum(top_widths) // 2, top_widths)
        dcrossed = tie(dcrossed, own)
    dcq, dckv, dckv_r = attention_bwd(cq, ckv, ckv_r, crossed, crest, cstat, dcrossed, valid)
    if fast:
        dcq = tie(dcq, next(top_steps))
    dckv_got = swap(dckv_r, "tensor")
    u1, dgb1, ddatt, sums_b = rows_call(
        dec_back_kernel, text_rows, [dcq, y1, u2], [dg[1], *w_cq, *w_dproj],
        [(width, F32), (width, BF, Far), (width, BF)], sums=[((8, width), F32)],
        flops=2 * text_rows * width * 2 * width,
    )
    dqs, dkvs, dkvs_r = attention_bwd(
        dq_self, dkv_self, dkv_self_r, datt, drest, dstat, ddatt, slots, scal
    )
    dkvs_got = swap(dkvs_r, "tensor")

    gkv, egb2, edpre, egb1, deatt, eu1, sums_e = rows_call(
        enc_back_kernel, rows, [tie(dckv, dqs), dckv_got, x2, x1, eslope],
        [eg[2], eg[1], *w_ckv, *w_eup, *w_edown, *w_eproj],
        [(2 * width, BF), (width, BF), (units, BF), (width, BF), (width, BF), (width, F32, Far)],
        sums=[((8, width), F32)], flops=2 * rows * width * (3 * width + 2 * units), megabytes=13,
    )
    d_packed, sums_a, text_mine, text_sent = rows_call(
        dec_last_kernel, text_rows, [dqs, dkvs, dkvs_got, Clip(text), tie(u1, deatt)], [dg[0], *w_dqkv],
        [(2 * dec_qkv.shape[1], BF)],
        sums=[((8, width), F32), ((slots, width // 2), F32), ((slots, width // 2), BF)],
        flops=2 * text_rows * width * 3 * width, scal=scal, told=True,
    )
    text_got = swap(text_sent, "section")
    owned = [jax.ShapeDtypeStruct((2, *text_mine.shape), kind) for kind in (BF, F32)]
    decoded, text_grad = flat_call(
        owners_kernel, [decoded, text_mine, decoded_got, text_got], owned, scal=scal, megabytes=4
    )
    mid_pairs = [
        (en_b, edpre), (egb2, ehid), (memory, gkv), (egb1, eatt), (dn_b, dcq), (dgb1, datt), (dn_a, d_packed),
    ]
    mid_widths = [enc_up.shape[1], enc_down.shape[0], cross_kv.shape[1], enc_proj.shape[0]]
    mid_widths += [cross_query.shape[1], dec_proj.shape[0], dec_qkv.shape[1]]
    if fast:
        egb2 = tie(egb2, top_steps.send(d_packed))
        mid_pairs[1] = (egb2, ehid)
        own, oth = gradients(mid_pairs)
        mid_steps = sum_over_chips(own, oth, scal, sum(mid_widths) // 2, mid_widths)
        waits = [
            lambda: (own,), lambda: (top_steps.send(base_a),), lambda: (next(mid_steps), text_grad)
        ]
    else:
        waits = [lambda: ()] * 3

    half = width // (4 * HEAD_DIM)
    deatt = tie(deatt, *waits[0]())
    side = (eatt, erest, estat)
    base_a, dekv_a = attention_bwd_side(eq, ekv_r, *side, deatt, valid, pairs=(0, half))
    deatt = tie(deatt, base_a, *waits[1]())
    base_b, dekv_r = attention_bwd_side(
        eq, ekv_r, *side, deatt, valid, pairs=(half, half), earlier=(dekv_a,)
    )
    dekv_got = swap(dekv_r, "tensor")
    deatt = tie(deatt, base_b, *waits[2]())
    deq, dekv = attention_bwd_side(eq, ekv, *side, deatt, valid, (base_a, base_b))
    e_packed, g2, ede, edo, sums_f, edh = rows_call(
        stem_back_kernel, rows, [deq, dekv, dekv_got, x0, eu1, ge, go, gs],
        [eg[0], *w_eqkv, second, gh],
        [(2 * enc_qkv.shape[1], BF), (width, BF), (width, BF), (width, BF)],
        sums=[((8, width), F32), ((16, width), BF)], scratch=[pltpu.VMEM((8, width), F32)],
        reverse=True, flops=2 * rows * width * 6 * width,
    )
    sums = [sums_a, sums_b, sums_c, sums_e, sums_f]
    if fast:
        late_waits = (top_steps.send(e_packed), mid_steps.send(e_packed))
        stem_width = 3 * width + depth
        late_columns = enc_qkv.shape[1] + stem_width // 2
        own, oth = flat_call(
            functools.partial(late_kernel, channels=channels),
            [
                en_a, tie(e_packed, *late_waits), g2, before, even, odd, ede, edo, edh, windows, halo,
                *sums,
            ],
            [shape_of(width, late_columns)] * 2, scal=scal, scratch=[pltpu.VMEM((width, stem_width), BF)],
            flops=2 * rows * width * (3 * width + 3 * width + 2 * depth), megabytes=10,
        )
        late_steps = sum_over_chips(
            own, oth, scal, enc_qkv.shape[1], [enc_qkv.shape[1], stem_width // 2], True
        )
        later = mid_steps.send(next(late_steps))
        top_sums = top_steps.send(later)
        later = mid_steps.send(late_steps.send(top_sums[0]))
        mid_sums = mid_steps.send(late_steps.send(later))
        late_qkv, stem = late_steps.send(mid_sums[0])
        block = 2 * width // (2 * lax.axis_size("dp") * cores)
        conv_second_grad, conv_first_grad, *vec = flat_call(
            stem_last_kernel, [stem, swap(stem, "section")],
            [
                jax.ShapeDtypeStruct((conv_second.shape[0], block, width), F32),
                jax.ShapeDtypeStruct((conv_first.shape[0], block, channels), F32),
            ] + [shape_of(3, block, F32)] * 4,
            scal=scal, megabytes=6,
        )
        conv_second_grad = conv_second_grad.transpose(0, 2, 1)
        conv_first_grad = conv_first_grad.transpose(0, 2, 1)
    else:
        cuts = lambda value, widths: jnp.split(value, list(np.cumsum(widths)[:-1]), axis=1)
        top_sums = cuts(sum_projections(core_sum(top_pairs)), top_widths)
        mid_sums = cuts(sum_projections(core_sum(mid_pairs)), mid_widths)
        late_qkv = sum_projections(core_sum([(en_a, e_packed)]))
        first_t = dot_tn(ede, windows[:, : 3 * LANES]) + dot_tn(edo, windows[:, LANES:]) + dot_tn(edh, halo)
        first_t = first_t.reshape(width, -1, LANES)[:, :, :channels].reshape(width, taps)
        vectors = jnp.concatenate(
            [
                sums_f[0:1], sums_e[2:3], sums_e[0:1], sums_f[1:2], sums_e[3:4], sums_e[1:2],
                sums_a[0:1], sums_b[0:1], sums_c[0:1], sums_a[1:2], sums_b[1:2], sums_c[1:2],
            ],
            axis=0,
        )
        stem = [dot_tn(g2, act) for act in (before, even, odd)] + [first_t, vectors.T]
        stem.append(jnp.zeros((width, depth - taps - vectors.shape[0]), F32))
        stem = sum_stem(jnp.concatenate([v.astype(BF) for v in stem], axis=1)).T
        conv_second_grad, conv_first_grad = stem[: 3 * width], stem[3 * width : 3 * width + taps]
        vec = [stem[3 * width + taps + 3 * n : 3 * width + taps + 3 * n + 3] for n in range(4)]

    d_up, d_down_t, d_cproj_t = top_sums
    e_up, e_down_t, e_kv, e_proj_t, d_cq, d_proj_t, d_qkv = mid_sums
    return (
        decoded,
        text_grad,
        conv_first_grad.reshape(*conv_first.shape[:2], -1),
        conv_second_grad.reshape(*conv_second.shape[:2], -1),
        vec[0],
        vec[1],
        late_qkv,
        e_proj_t.T,
        e_up,
        e_down_t.T,
        e_kv,
        vec[2],
        vec[3],
        d_qkv,
        d_proj_t.T,
        d_cq,
        d_cproj_t.T,
        d_up,
        d_down_t.T,
    )


def solution(mesh):
    in_specs = (
        P("dp", None, None),
        P(),
        P(),
        P(),
        P(),
        P(None, "tensor"),
        P("tensor", None),
        P(None, "tensor"),
        P("tensor", None),
        P(None, "tensor"),
        P("dp", "tensor", None),
        P("dp"),
        P(),
        P(),
        P(None, "tensor"),
        P("tensor", None),
        P(None, "tensor"),
        P("tensor", None),
        P(None, "tensor"),
        P("tensor", None),
        P("dp", "tensor", None),
    )
    out_specs = (
        P("dp", "tensor", "section"),
        P("dp", "tensor", "section"),
        P(None, None, ("dp", "tensor")),
        P(None, None, ("dp", "tensor")),
        P(None, ("dp", "tensor")),
        P(None, ("dp", "tensor")),
        P(("section", "dp"), "tensor"),
        P("tensor", ("section", "dp")),
        P(("section", "dp"), "tensor"),
        P("tensor", ("section", "dp")),
        P(("section", "dp"), "tensor"),
        P(None, ("dp", "tensor")),
        P(None, ("dp", "tensor")),
        P(("section", "dp"), "tensor"),
        P("tensor", ("section", "dp")),
        P(("section", "dp"), "tensor"),
        P("tensor", ("section", "dp")),
        P(("section", "dp"), "tensor"),
        P("tensor", ("section", "dp")),
    )
    return jax.shard_map(body, mesh=mesh, in_specs=in_specs, out_specs=out_specs, check_vma=False)
```

```python
import functools
import math

import jax
import jax.numpy as jnp
import numpy as np
from jax import lax
from jax.experimental import pallas as pl
from jax.experimental.pallas import tpu as pltpu
from jax.sharding import PartitionSpec as P

HEAD_DIM = 64
NEG = -1000000000.0
EPS = 1e-05
TINY = 1e-28
CHUNK = 256
LANES = 128
BF, F32 = jnp.bfloat16, jnp.float32
INV_SQRT2 = 0.7071067811865476
INV_SQRT2PI = 0.3989422804014327


def dot_nn(left, right):
    return lax.dot_general(left, right, (((1,), (0,)), ((), ())), preferred_element_type=F32)


def dot_nt(left, right):
    return lax.dot_general(left, right, (((1,), (1,)), ((), ())), preferred_element_type=F32)


def dot_tn(left, right):
    return lax.dot_general(left, right, (((0,), (0,)), ((), ())), preferred_element_type=F32)


def norm_stats(rows):
    centre = rows - jnp.mean(rows, axis=-1, keepdims=True)
    spread = jnp.mean(centre * centre, axis=-1, keepdims=True)
    inverse = lax.rsqrt(spread + EPS)
    return centre * inverse, inverse


def norm_back(unit, inverse, gain_row, upstream):
    scaled = upstream * gain_row
    first = jnp.mean(scaled, axis=-1, keepdims=True)
    second = jnp.mean(scaled * unit, axis=-1, keepdims=True)
    grad_rows = inverse * (scaled - first - unit * second)
    grad_gain = jnp.sum(upstream * unit, axis=0, keepdims=True)
    grad_bias = jnp.sum(upstream, axis=0, keepdims=True)
    return grad_rows, grad_gain, grad_bias


def gelu_pair(v):
    phi = 0.5 * (1.0 + lax.erf(v * INV_SQRT2))
    return v * phi, phi + (v * INV_SQRT2PI) * jnp.exp(-0.5 * (v * v))


def lanes(rows):
    return lax.broadcasted_iota(jnp.int32, (rows, 2 * HEAD_DIM), 1)

def key_aug(kv, valid, ones):
    lane = lanes(kv.shape[0])
    row = lax.broadcasted_iota(jnp.int32, kv.shape, 0)
    pad = jnp.where((lane > HEAD_DIM) & (lane <= HEAD_DIM + ones), 1.0, 0.0)
    pad = jnp.where((lane == HEAD_DIM) & (row >= valid), NEG, pad).astype(BF)
    return jnp.where(lane < HEAD_DIM, kv, pad)

def causal_bias(scal_ref, key_rows, query_rows, valid):
    place, length = scal_ref[SCAL_CORE], scal_ref[SCAL_LENGTHS + scal_ref[SCAL_SECTION]]
    key_id = lax.broadcasted_iota(jnp.int32, (2 * key_rows, query_rows), 0)
    query_id = lax.broadcasted_iota(jnp.int32, (2 * key_rows, query_rows), 1)
    query_pos = query_id + place * valid
    key_pos = jnp.where(key_id < key_rows, key_id + place * valid, key_id - key_rows + (1 - place) * valid)
    return jnp.where((key_pos <= query_pos) & (key_pos < length), 0.0, NEG)

def fwd_setup(q_ref, kl_ref, kr_ref, valid):
    lane_q = lanes(q_ref.shape[0])
    q_all = q_ref[...].astype(F32) * HEAD_DIM**-0.5
    wide = 2 * HEAD_DIM

    def operands(h):
        q = jnp.where(lane_q < HEAD_DIM, q_all if h == 0 else pltpu.roll(q_all, HEAD_DIM, 1), 0.0)
        kv = [ref[:, h * wide : (h + 1) * wide] for ref in (kl_ref, kr_ref)]
        turned = [v.T for v in kv]
        sub = lax.broadcasted_iota(jnp.int32, turned[0].shape, 0)
        ones = [jnp.where(sub == 0, jnp.ones_like(v), v) for v in turned]
        return q, [key_aug(v, valid, 1) for v in kv], turned, ones

    return lane_q, operands


def fwd_finish(parts, logs, shift, out_ref, rest_ref, stat_ref):
    queries = out_ref.shape[0]
    mixed = jnp.concatenate([v[HEAD_DIM:] / v[0:1] for v in parts], axis=0).T
    logs = [jnp.broadcast_to(v, (HEAD_DIM, queries)) for v in logs]
    stat = jnp.concatenate(logs[::-1], axis=0).T
    if shift is not None:
        stat = stat + shift
    rounded = mixed.astype(BF)
    out_ref[...] = rounded
    rest_ref[...] = (mixed - rounded.astype(F32)).astype(BF)
    stat_ref[...] = stat


def fwd_fast(q_ref, kl_ref, kr_ref, out_ref, rest_ref, stat_ref, bias, valid, kc, depth):
    rows, queries = kl_ref.shape[0], q_ref.shape[0]
    lane_q, operands = fwd_setup(q_ref, kl_ref, kr_ref, valid)
    tops, heads = [], []
    for h in range(2):
        q, keys, turned, ones = operands(h)
        size = 0.0
        for v in turned:
            k = v[:HEAD_DIM].astype(F32)
            size = jnp.maximum(size, jnp.max(jnp.sum(k * k, axis=0, keepdims=True), axis=1, keepdims=True))
        bound = jnp.sqrt(jnp.sum(q * q, axis=1, keepdims=True) * size)
        bound = bound.astype(BF).astype(F32)
        q = jnp.where(lane_q == HEAD_DIM, 1.0, jnp.where(lane_q == HEAD_DIM + 1, -bound, q)).astype(BF)
        heads.append((q, keys, ones)); tops.append(bound)
    def score(item):
        h, side, at = item
        s = dot_nt(heads[h][1][side][at : at + kc], heads[h][0])
        if bias is not None:
            s = s + bias[side * rows + at : side * rows + at + kc]
        return s
    items = [(h, side, at) for h in range(2) for side in range(2) for at in range(0, rows, kc)]
    parts = [0.0, 0.0]
    ahead = [score(i) for i in items[:depth]]
    for n, (h, side, at) in enumerate(items):
        if n + depth < len(items):
            ahead.append(score(items[n + depth]))
        p = jnp.exp(ahead.pop(0)).astype(BF)
        parts[h] = parts[h] + dot_nn(heads[h][2][side][:, at : at + kc], p)
    fwd_finish(parts, [jnp.log(v[0:1]) for v in parts], jnp.where(lane_q < HEAD_DIM, tops[1], tops[0]), out_ref, rest_ref, stat_ref)
    return jnp.minimum(parts[0][0:1], parts[1][0:1])


def fwd_safe(q_ref, kl_ref, kr_ref, out_ref, rest_ref, stat_ref, bias, valid):
    rows = kl_ref.shape[0]
    lane_q, operands = fwd_setup(q_ref, kl_ref, kr_ref, valid)
    parts, logs = [], []
    for h in range(2):
        q, keys, _, ones = operands(h)
        q = jnp.where(lane_q == HEAD_DIM, 1.0, q).astype(BF)
        scores = []
        for side in range(2):
            s = dot_nt(keys[side], q)
            if bias is not None:
                s = s + bias[side * rows : (side + 1) * rows]
            scores.append(s)
        top = jnp.maximum(jnp.max(scores[0], axis=0, keepdims=True), jnp.max(scores[1], axis=0, keepdims=True))
        parts.append(sum(dot_nn(ones[i], jnp.exp(scores[i] - top).astype(BF)) for i in range(2)))
        logs.append(top + jnp.log(parts[h][0:1]))
    fwd_finish(parts, logs, None, out_ref, rest_ref, stat_ref)


def views(refs, i, pairs):
    narrow, near, far = refs
    wide = 2 * HEAD_DIM
    j = (i + pairs // 2) % pairs if isinstance(i, int) else lax.rem(i + pairs // 2, pairs)
    at = (lambda n, w: pl.ds(n * w, w)) if isinstance(i, int) else (lambda n, w: pl.ds(pl.multiple_of(n * w, w), w))
    return [r.at[:, at(i, wide)] for r in narrow], [r.at[:, at(i, 2 * wide)] for r in near], [r.at[:, at(j, 2 * wide)] for r in far]


def fwd_kernel(*refs, valid, masked, kc, depth):
    scal_ref = refs[0] if masked else None
    q_ref, kl_ref, kr_ref, out_ref, rest_ref, stat_ref = refs[1:] if masked else refs
    pairs = q_ref.shape[1] // (2 * HEAD_DIM)
    bias = causal_bias(scal_ref, kl_ref.shape[0], q_ref.shape[0], valid) if masked else None
    least = None
    for i in range(pairs):
        (q, out, rest, stat), (kl,), (kr,) = views(((q_ref, out_ref, rest_ref, stat_ref), (kl_ref,), (kr_ref,)), i, pairs)
        low = fwd_fast(q, kl, kr, out, rest, stat, bias, valid, kc, depth)
        least = low if least is None else jnp.minimum(least, low)
        for ref in (rest_ref, stat_ref):
            push(ref, (slice(None), pl.ds(i * 2 * HEAD_DIM, 2 * HEAD_DIM)))
    for ref in (rest_ref, stat_ref):
        if isinstance(ref, Outgoing):
            ref.finish()

    @pl.when(jnp.min(least) < TINY)
    def _():
        @pl.loop(0, pairs)
        def _(i):
            (q, out, rest, stat), (kl,), (kr,) = views(((q_ref, out_ref, rest_ref, stat_ref), (kl_ref,), (kr_ref,)), i, pairs)
            again = causal_bias(scal_ref, kl_ref.shape[0], q_ref.shape[0], valid) if masked else None
            fwd_safe(q, kl, kr, out, rest, stat, again, valid)

        for ref in (rest_ref, stat_ref):
            if isinstance(ref, Outgoing):
                ref.again()


def split3(value):
    first = value.astype(BF); rest = value - first.astype(F32)
    second = rest.astype(BF); third = (rest - second.astype(F32)).astype(BF)
    return first.astype(F32), second.astype(F32), third.astype(F32)


def bwd_views(refs, i, pairs):
    q_ref, kl_ref, kr_ref, out_ref, rest_ref, stat_ref, up_ref, dq_ref, dkl_ref, dkr_ref = refs
    narrow = (q_ref, out_ref, rest_ref, stat_ref, up_ref, dq_ref)
    (q, out, rest, stat, up, dq), (kl, dkl), (kr, dkr) = views(
        (narrow, (kl_ref, dkl_ref), (kr_ref, dkr_ref)), i, pairs
    )
    return q, kl, kr, out, rest, stat, up, dq, dkl, dkr


def bwd_kernel(*refs, valid, masked):
    scal_ref = refs[0] if masked else None
    refs = refs[1:] if masked else refs
    q_ref, kl_ref = refs[:2]
    pairs = q_ref.shape[1] // (2 * HEAD_DIM)
    bias = causal_bias(scal_ref, kl_ref.shape[0], q_ref.shape[0], valid) if masked else None
    for i in range(pairs):
        q, kl, kr, out, rest, stat, up, dq, dkl, dkr = bwd_views(refs, i, pairs)
        fn = bwd_pair if masked else bwd_pair_s
        fn(q, out, rest, stat, up, dq, [(kl, dkl), (kr, dkr)], bias, valid)


def bwd_side_kernel(*refs, valid, far, first, count, joined):
    q_ref, kv_ref, out_ref, rest_ref, stat_ref, up_ref, *more, dq_ref, dkv_ref = refs
    pairs = q_ref.shape[1] // (2 * HEAD_DIM)
    wide = 2 * HEAD_DIM
    base_refs = () if far else more
    if joined:
        earlier, at = more[0], dkv_ref.shape[1] - more[0].shape[1]
        dkv_ref[:, at:] = earlier[...]

    def one(i):
        (q, out, rest, stat, up), near, other = views(
            ((q_ref, out_ref, rest_ref, stat_ref, up_ref), () if far else (kv_ref,), (kv_ref,) if far else ()),
            first + i, pairs,
        )
        dq = dq_ref.at[:, i * wide : (i + 1) * wide]
        dkv = dkv_ref.at[:, i * 2 * wide : (i + 1) * 2 * wide]
        base = None
        if base_refs:
            each = base_refs[0].shape[1] // wide
            base = base_refs[i // each].at[:, i % each * wide : (i % each + 1) * wide]
        bwd_pair(q, out, rest, stat, up, dq, [(*near, *other, dkv)], None, valid, base)

    for i in range(count):
        one(i)


def bwd_pair_s(q_ref, out_ref, rest_ref, stat_ref, up_ref, dq_ref, key_sides, bias, valid, base_ref=None):
    rows, queries, depth = key_sides[0][0].shape[0], q_ref.shape[0], 1
    kc = rows
    wide = 2 * HEAD_DIM
    lane_q, lane_k = lanes(queries), lanes(rows)
    low_q = lane_q < HEAD_DIM
    q_all = q_ref[...].astype(F32) * HEAD_DIM**-0.5
    up_all = up_ref[...].astype(F32)
    stat = stat_ref[...]
    prods = up_all * (out_ref[...].astype(F32) + rest_ref[...].astype(F32))
    q_turned = (q_all.astype(BF)).T
    up_turned = up_ref[...].T
    heads, both = [], []
    for h in range(2):
        q = q_all if h == 0 else pltpu.roll(q_all, HEAD_DIM, 1)
        lse = stat if h == 0 else pltpu.roll(stat, HEAD_DIM, 1)
        up = up_all if h == 1 else pltpu.roll(up_all, HEAD_DIM, 1)
        a0, a1, a2 = split3(-lse)
        pad = jnp.where(lane_q == HEAD_DIM, 1.0, jnp.where(lane_q == HEAD_DIM + 1, a0, jnp.where(lane_q == HEAD_DIM + 2, a1, jnp.where(lane_q == HEAD_DIM + 3, a2, 0.0))))
        q_aug = jnp.where(low_q, q, pad).astype(BF)
        centre = jnp.sum(jnp.where(low_q if h == 0 else ~low_q, prods, 0.0), axis=1, keepdims=True)
        d0, d1, d2 = split3(-centre)
        pad = jnp.where(lane_q == 0, d0, jnp.where(lane_q == 1, d1, jnp.where(lane_q == 2, d2, 0.0)))
        up_aug = jnp.where(low_q, pad, up).astype(BF)
        heads.append((q_aug, up_aug, q_turned[h * HEAD_DIM : (h + 1) * HEAD_DIM], up_turned[h * HEAD_DIM : (h + 1) * HEAD_DIM]))
        sides = []
        for ref, out in key_sides:
            kv = ref[:, h * wide : (h + 1) * wide]
            keys = key_aug(kv, valid, 3)
            values = jnp.where(lane_k < HEAD_DIM, jnp.where(lane_k < 3, 1.0, 0.0).astype(BF), kv)
            sides.append((keys, values, kv, out))
        both.append(sides)
    items = [(h, side, at) for h in range(2) for side in range(len(key_sides)) for at in range(0, rows, kc)]
    def score(item):
        h, side, at = item
        keys, values, _, _ = both[h][side]
        return dot_nt(heads[h][0], keys[at : at + kc]), dot_nt(heads[h][1], values[at : at + kc])
    ahead = [score(i) for i in items[:depth]]
    totals = [0.0, 0.0]
    for n, (h, side, at) in enumerate(items):
        if n + depth < len(items):
            ahead.append(score(items[n + depth]))
        s, dp = ahead.pop(0)
        p = jnp.exp(s)
        ds = (p * dp).astype(BF)
        p = p.astype(BF)
        _, _, kv, out = both[h][side]
        pair = jnp.concatenate([dot_nn(heads[h][2], ds), dot_nn(heads[h][3], p)], axis=0)
        out[at : at + kc, h * wide : (h + 1) * wide] = pair.T.astype(BF)
        totals[h] = totals[h] + dot_nn(ds, kv[at : at + kc])
    dq = jnp.where(low_q, totals[0], pltpu.roll(totals[1], HEAD_DIM, 1)) * HEAD_DIM**-0.5
    dq_ref[...] = dq.astype(BF)


def bwd_pair(q_ref, out_ref, rest_ref, stat_ref, up_ref, dq_ref, key_sides, bias, valid, base_ref=None):
    masked, depth = bias is not None, 1
    rows, queries = key_sides[0][0].shape[0], q_ref.shape[0]
    kc = rows
    wide = 2 * HEAD_DIM
    lane_q, lane_k = lanes(queries), lanes(rows)
    low_q = lane_q < HEAD_DIM
    q_all = q_ref[...].astype(F32) * HEAD_DIM**-0.5
    up_all = up_ref[...].astype(F32)
    stat = stat_ref[...]
    prods = up_all * (out_ref[...].astype(F32) + rest_ref[...].astype(F32))
    heads, both = [], []
    for h in range(2):
        q = q_all if h == 0 else pltpu.roll(q_all, HEAD_DIM, 1)
        lse = stat if h == 0 else pltpu.roll(stat, HEAD_DIM, 1)
        up = up_all if h == 1 else pltpu.roll(up_all, HEAD_DIM, 1)
        a0, a1, a2 = split3(-lse)
        pad = jnp.where(lane_q == HEAD_DIM, 1.0, jnp.where(lane_q == HEAD_DIM + 1, a0, jnp.where(lane_q == HEAD_DIM + 2, a1, jnp.where(lane_q == HEAD_DIM + 3, a2, 0.0))))
        q_aug = jnp.where(low_q, q, pad).astype(BF)
        q_rhs = jnp.where(low_q, q, 0.0).astype(BF)
        centre = jnp.sum(jnp.where(low_q if h == 0 else ~low_q, prods, 0.0), axis=1, keepdims=True)
        d0, d1, d2 = split3(-centre)
        pad = jnp.where(lane_q == 0, d0, jnp.where(lane_q == 1, d1, jnp.where(lane_q == 2, d2, 0.0)))
        up_aug = jnp.where(low_q, pad, up).astype(BF)
        up_rhs = jnp.where(low_q, 0.0, up).astype(BF)
        heads.append((q_aug, q_rhs, up_aug, up_rhs))
        sides = []
        for ref, out in key_sides:
            kv = ref[:, h * wide : (h + 1) * wide]
            keys = key_aug(kv, valid, 3)
            values = jnp.where(lane_k < HEAD_DIM, jnp.where(lane_k < 3, 1.0, 0.0).astype(BF), kv)
            sides.append((keys, values, kv.T, out))
        both.append(sides)
    items = [(h, side, at) for h in range(2) for side in range(len(key_sides)) for at in range(0, rows, kc)]
    def score(item):
        h, side, at = item
        keys, values, _, _ = both[h][side]
        s = dot_nt(keys[at : at + kc], heads[h][0])
        if masked:
            first = at + side * rows
            s = s + bias[first : first + kc]
        return s, dot_nt(values[at : at + kc], heads[h][2])
    ahead = [score(i) for i in items[:depth]]
    totals = [0.0, 0.0]
    for n, (h, side, at) in enumerate(items):
        if n + depth < len(items):
            ahead.append(score(items[n + depth]))
        s, dp = ahead.pop(0)
        p = jnp.exp(s)
        ds = (p * dp).astype(BF)
        p = p.astype(BF)
        _, _, turned, out = both[h][side]
        out[at : at + kc, h * wide : (h + 1) * wide] = (dot_nn(ds, heads[h][1]) + dot_nn(p, heads[h][3])).astype(BF)
        totals[h] = totals[h] + dot_nn(turned[:, at : at + kc], ds)
    turned_dq = [v[:HEAD_DIM] for v in totals]
    dq = jnp.concatenate(turned_dq, axis=0).T * HEAD_DIM**-0.5
    if base_ref is not None:
        dq = dq + base_ref[...]
    dq_ref[...] = dq.astype(dq_ref.dtype)


def shape_of(rows, width, kind=BF):
    return jax.ShapeDtypeStruct((rows, width), kind)


def params(megabytes, *semantics):
    return pltpu.CompilerParams(vmem_limit_bytes=megabytes * 2**20)


def attention_cost(q, kl, products):
    flops = 2 * products * q.shape[0] * 2 * kl.shape[0] * q.shape[1] * 3
    return pl.CostEstimate(
        flops=flops, bytes_accessed=8 * q.size + 6 * kl.size, transcendentals=0
    )


class Far:
    def __init__(self, value, pieces=1, by_core=False):
        self.value, self.pieces, self.by_core = value, pieces, by_core
        self.shape, self.dtype = value.shape[1:] if by_core else value.shape, value.dtype
        self.size = math.prod(self.shape)


class Clip:
    def __init__(self, value):
        self.value, self.shape, self.dtype, self.size = value, value.shape, value.dtype, value.size


class Incoming:
    def __init__(self, source, held, arrived, pieces):
        self.held, self.shape, self.dtype = held, held.shape, held.dtype
        rows = held.shape[0] // pieces
        self.spans = [pl.ds(n * rows, rows) for n in range(pieces)]
        self.copies = [
            pltpu.make_async_copy(source.at[span], held.at[span], arrived.at[n])
            for n, span in enumerate(self.spans)
        ]

    def start(self, n):
        if n < len(self.copies):
            self.copies[n].start()

    def wait(self, n):
        if self.copies[n] is not None:
            self.copies[n].wait()
            self.copies[n] = None

    def piece(self, n):
        return Piece(self, n)

    def settle(self):
        for n in range(len(self.copies)):
            self.wait(n)
        return self.held

    @property
    def at(self):
        return self.settle().at

    def __getitem__(self, index):
        return self.settle()[index]


class Piece:
    def __init__(self, whole, n):
        self.whole, self.n = whole, n
        rows = whole.held.shape[0] // len(whole.spans)
        self.shape, self.dtype = (rows, *whole.held.shape[1:]), whole.held.dtype

    def __getitem__(self, index):
        self.whole.wait(self.n)
        return self.whole.held.at[self.whole.spans[self.n]][index]


class Padded:
    def __init__(self, ref, section, rows):
        self.ref, self.section, self.rows = ref, section, rows
        self.shape, self.dtype = (rows, ref.shape[2]), ref.dtype

    def __getitem__(self, index):
        value = self.ref[self.section]
        behind = jnp.zeros((self.rows - value.shape[0], value.shape[1]), value.dtype)
        return jnp.concatenate([value, behind], axis=0)[index]


class Outgoing:
    def __init__(self, target, held, left):
        self.target, self.held, self.left, self.copies = target, held, left, []
        self.at, self.shape, self.dtype = held.at, held.shape, held.dtype

    def __setitem__(self, index, value):
        self.held[index] = value

    def push(self, index=(slice(None), slice(None))):
        copy = pltpu.make_async_copy(
            self.held.at[index], self.target.at[index], self.left.at[len(self.copies)]
        )
        copy.start()
        self.copies.append(copy)

    def finish(self):
        for copy in self.copies or ():
            copy.wait()
        self.copies = None

    def again(self):
        copy = pltpu.make_async_copy(self.held, self.target, self.left.at[0])
        copy.start()
        copy.wait()


def push(ref, *index):
    if isinstance(ref, Outgoing):
        ref.push(*index)


def in_vmem():
    return pl.BlockSpec(memory_space=pltpu.VMEM)


def in_hbm():
    return pl.BlockSpec(memory_space=pltpu.HBM)


def flat_call(kernel, operands, out_shape, scal=None, scratch=(), flops=0, megabytes=40):
    touched = sum(v.size * v.dtype.itemsize for v in operands)
    touched += sum(math.prod(v.shape) * v.dtype.itemsize for v in out_shape)
    far_in = [v for v in operands if isinstance(v, Far)]
    far_out = [v for v in out_shape if isinstance(v, Far)]
    extra = []
    for v in (*far_in, *far_out):
        extra += [pltpu.VMEM(v.shape, v.dtype), pltpu.SemaphoreType.DMA((v.pieces,))]
        megabytes += -(-v.size * v.dtype.itemsize // 2**20)

    def run(*refs):
        refs = list(refs)
        take = lambda count: [refs.pop(0) for _ in range(count)]
        head = take(0 if scal is None else 1)
        ins, outs, own = take(len(operands)), take(len(out_shape)), take(len(scratch))
        moving = []
        for n, v in enumerate(operands):
            if isinstance(v, Far):
                source = ins[n].at[head[0][SCAL_CORE]] if v.by_core else ins[n]
                ins[n] = Incoming(source, *take(2), v.pieces)
                moving.append(ins[n])
            elif isinstance(v, Clip):
                ins[n] = Padded(ins[n], head[0][SCAL_SECTION], round_up(v.shape[1]))
        for n, v in enumerate(out_shape):
            if isinstance(v, Far):
                outs[n] = Outgoing(outs[n], *take(2))
        for n in range(max((len(v.copies) for v in moving), default=0)):
            for v in moving:
                v.start(n)
        kernel(*head, *ins, *outs, *own)
        for v in moving:
            v.settle()
        for v in outs:
            if isinstance(v, Outgoing):
                if v.copies == []:
                    v.push()
                v.finish()

    bare = lambda v: v.value if isinstance(v, (Far, Clip)) else v
    pin = lambda v: pltpu.with_memory_space_constraint(v.value, pltpu.HBM) if isinstance(v, Far) else bare(v)
    pin_shape = lambda v: pltpu.HBM(v.shape, v.dtype) if isinstance(v, Far) else v
    place = lambda v: in_hbm() if isinstance(v, Far) else in_vmem()
    return pl.pallas_call(
        run,
        in_specs=([] if scal is None else [pl.BlockSpec(memory_space=pltpu.SMEM)])
        + [place(v) for v in operands],
        out_specs=[place(v) for v in out_shape],
        out_shape=[pin_shape(v) for v in out_shape],
        scratch_shapes=list(scratch) + extra,
        compiler_params=params(megabytes),
        cost_estimate=pl.CostEstimate(flops=flops, bytes_accessed=touched, transcendentals=0),
    )(*([] if scal is None else [scal]), *[pin(v) for v in operands])


def attention_flops(q, kl, products, share=1):
    return 2 * products * q.shape[0] * 2 * kl.shape[0] * q.shape[1] * 4 // share


def attention_fwd(q, kl, kr, valid, scal=None):
    return flat_call(
        functools.partial(fwd_kernel, valid=valid, masked=scal is not None, kc=kl.shape[0], depth=1),
        [q, kl, kr],
        [shape_of(*q.shape), Far(shape_of(*q.shape), 8), Far(shape_of(*q.shape, F32), 8)],
        scal=scal, flops=attention_flops(q, kl, 2), megabytes=24 if q.shape[0] > CHUNK else 12,
    )


def attention_bwd(q, kl, kr, out, rest, stat, up, valid, scal=None):
    return flat_call(
        functools.partial(bwd_kernel, valid=valid, masked=scal is not None),
        [q, kl, kr, out, rest, stat, up],
        [shape_of(*q.shape), shape_of(*kl.shape), shape_of(*kl.shape)],
        scal=scal, flops=attention_flops(q, kl, 5), megabytes=12,
    )


def attention_bwd_side(q, kv, out, rest, stat, up, valid, base=(), pairs=None, earlier=()):
    far = not base
    total = q.shape[1] // (2 * HEAD_DIM)
    first, count = pairs or (0, total)
    width = kv.shape[1] // total * count + sum(v.shape[1] for v in earlier)
    return flat_call(
        functools.partial(
            bwd_side_kernel, valid=valid, far=far, first=first, count=count, joined=bool(earlier)
        ),
        [q, kv, out, rest, stat, up, *base, *earlier],
        [shape_of(q.shape[0], q.shape[1] // total * count, F32 if far else BF), shape_of(kv.shape[0], width)],
        flops=attention_flops(q, kv, 5, 2), megabytes=18,
    )


def rows_call(
    kernel, rows, blocked, whole, outs, sums=(), scratch=(), reverse=False, flops=0, megabytes=10, scal=None,
    told=False,
):
    chunk_rows = next(n for n in (384, CHUNK) if rows % n == 0)
    steps = rows // chunk_rows
    order = list(range(steps))
    if reverse:
        order = order[::-1]

    def chunk_of(ref, chunk):
        if isinstance(ref, Incoming):
            return ref.piece(chunk)
        return ref if isinstance(ref, Padded) else ref.at[pl.ds(chunk * chunk_rows, chunk_rows)]

    def run(*refs):
        refs = list(refs)
        take = lambda count: [refs.pop(0) for _ in range(count)]
        head = take(0 if scal is None else 1)
        kept, by_chunk = take(len(whole)), take(len(blocked))
        out, total = take(len(outs)), take(len(sums))
        for n, chunk in enumerate(order):
            kernel(
                n, *(head if told else ()), *[chunk_of(r, chunk) for r in by_chunk], *kept,
                *[chunk_of(r, chunk) for r in out], *total, *refs,
            )
            for r in out:
                push(r, (pl.ds(chunk * chunk_rows, chunk_rows), slice(None)))

    out_shape = []
    for width, kind, *far in outs:
        shape = shape_of(rows, width, kind)
        out_shape.append(Far(shape, steps) if far else shape)
    for shape, kind, *far in sums:
        shape = jax.ShapeDtypeStruct(shape, kind)
        out_shape.append(Far(shape) if far else shape)
    blocked = [Far(v.value, steps, v.by_core) if isinstance(v, Far) else v for v in blocked]
    return flat_call(run, [*whole, *blocked], out_shape, scal, scratch, flops, megabytes)


def tap_weights(first_ref):
    pieces = []
    for tap in range(first_ref.shape[0]):
        rows = first_ref[tap]
        pieces += [rows, jnp.zeros((LANES - rows.shape[0], rows.shape[1]), rows.dtype)]
    return jnp.concatenate(pieces, axis=0)


def mel_windows(scal_ref, mel_ref, mel_rows_ref, windows_ref, halo_ref, valid):
    rows = windows_ref.shape[0]
    channels, frames = mel_ref.shape[1:]
    front = 8
    mel_rows_ref[...] = jnp.zeros_like(mel_rows_ref)
    mel_rows_ref[front : front + frames, :channels] = mel_ref[scal_ref[SCAL_SECTION]].astype(F32).T
    lanes_all = slice(None)
    for core in range(frames // (2 * valid)):

        @pl.when(scal_ref[SCAL_CORE] == core)
        def _():
            base = front + 2 * valid * core
            for n in range(4):
                taken = mel_rows_ref[pl.ds(base + n - 1, rows, stride=2), lanes_all]
                windows_ref[:, n * LANES : (n + 1) * LANES] = taken.astype(BF)
            halo_ref[...] = jnp.zeros_like(halo_ref)
            if core > 0:
                for n in range(3):
                    part = mel_rows_ref[pl.ds(base - 2 + n, 16), lanes_all]
                    first = lax.broadcasted_iota(jnp.int32, part.shape, 0) == 0
                    halo_ref[:, n * LANES : (n + 1) * LANES] = jnp.where(first, part, 0.0).astype(BF)


def stem_fwd_kernel(
    chunk, scal_ref, pos_ref, mel_ref, first_ref, second_ref,
    even_ref, odd_ref, before_ref, ge_ref, go_ref, gs_ref, x_ref, gh_ref, windows_ref, halo_ref,
    carry_ref, mel_rows_ref, *, valid,
):
    first = tap_weights(first_ref)
    if chunk == 0:
        mel_windows(scal_ref, mel_ref, mel_rows_ref, windows_ref, halo_ref, valid)
        push(windows_ref)
        act, slope = gelu_pair(dot_nn(halo_ref[...], first))
        carry_ref[...] = act[:8]
        gh_ref[...] = slope
    span = pl.ds(chunk * even_ref.shape[0], even_ref.shape[0])
    me_ref = windows_ref.at[span, : 3 * LANES]
    mo_ref = windows_ref.at[span, LANES:]

    width = even_ref.shape[1]
    even, slope = gelu_pair(dot_nn(me_ref[...], first))
    even = even.astype(BF)
    even_ref[...] = even
    ge_ref[...] = slope.astype(BF)
    odd, slope = gelu_pair(dot_nn(mo_ref[...], first))
    go_ref[...] = slope.astype(BF)
    row = lax.broadcasted_iota(jnp.int32, odd.shape, 0)
    before = jnp.where(row == 0, carry_ref[0:1, :], pltpu.roll(odd, 1, 0)).astype(BF)
    carry_ref[0:1, :] = odd[odd.shape[0] - 1 :]
    odd = odd.astype(BF)
    odd_ref[...] = odd
    before_ref[...] = before
    pre = dot_nn(before, second_ref[:width])
    pre += dot_nn(even, second_ref[width : 2 * width])
    pre += dot_nn(odd, second_ref[2 * width :])
    act, slope = gelu_pair(pre)
    gs_ref[...] = slope.astype(BF)
    x_ref[...] = act + pos_ref[...]


def qkv_kernel(step, x_ref, gain_ref, bias_ref, own_ref, oth_ref, normed_ref, q_ref, kv_ref):
    unit, _ = norm_stats(x_ref[...].astype(F32))
    normed = (unit * gain_ref[...] + bias_ref[...]).astype(BF)
    normed_ref[...] = normed
    heads = own_ref.shape[1] // (3 * HEAD_DIM)
    for part, w_ref in enumerate((own_ref, oth_ref)):
        packed = dot_nn(normed, w_ref[...]).astype(BF)
        for h in range(heads):
            at, to = h * 3 * HEAD_DIM, part * heads + h
            q_ref[:, to * HEAD_DIM : (to + 1) * HEAD_DIM] = packed[:, at : at + HEAD_DIM]
            kv_ref[:, to * 2 * HEAD_DIM : (to + 1) * 2 * HEAD_DIM] = packed[
                :, at + HEAD_DIM : at + 3 * HEAD_DIM
            ]


def two_parts(rows, own_ref, oth_ref):
    depth = own_ref.shape[0]
    return dot_nn(rows[:, :depth], own_ref[...]) + dot_nn(rows[:, depth:], oth_ref[...])


def two_parts_t(rows, own_ref, oth_ref):
    depth = own_ref.shape[1]
    return dot_nt(rows[:, :depth], own_ref[...]) + dot_nt(rows[:, depth:], oth_ref[...])


def enc_mid_kernel(
    step, x_ref, att_ref, gb_ref, bb_ref, gc_ref, bc_ref, po_ref, pt_ref, uo_ref, ut_ref, do_ref, dt_ref,
    ko_ref, kt_ref,
    x1_ref, x2_ref, normed_ref, hidden_ref, slope_ref, memory_ref, kv_ref,
):
    x1 = x_ref[...] + two_parts(att_ref[...], po_ref, pt_ref)
    x1_ref[...] = x1
    unit, _ = norm_stats(x1)
    normed = (unit * gb_ref[...] + bb_ref[...]).astype(BF)
    normed_ref[...] = normed
    half = uo_ref.shape[1]
    x2 = x1
    for part, (up_ref, down_ref) in enumerate(((uo_ref, do_ref), (ut_ref, dt_ref))):
        act, slope = gelu_pair(dot_nn(normed, up_ref[...]))
        act = act.astype(BF)
        hidden_ref[:, part * half : (part + 1) * half] = act
        slope_ref[:, part * half : (part + 1) * half] = slope.astype(BF)
        x2 = x2 + dot_nn(act, down_ref[...])
    x2_ref[...] = x2
    unit, _ = norm_stats(x2)
    memory = (unit * gc_ref[...] + bc_ref[...]).astype(BF)
    memory_ref[...] = memory
    half = ko_ref.shape[1]
    kv_ref[:, :half] = dot_nn(memory, ko_ref[...]).astype(BF)
    kv_ref[:, half:] = dot_nn(memory, kt_ref[...]).astype(BF)


def dec_mid_kernel(
    step, x_ref, att_ref, gain_ref, bias_ref, po_ref, pt_ref, qo_ref, qt_ref, y_ref, normed_ref, q_ref
):
    y = x_ref[...].astype(F32) + two_parts(att_ref[...], po_ref, pt_ref)
    y_ref[...] = y
    unit, _ = norm_stats(y)
    normed = (unit * gain_ref[...] + bias_ref[...]).astype(BF)
    normed_ref[...] = normed
    half = qo_ref.shape[1]
    q_ref[:, :half] = dot_nn(normed, qo_ref[...]).astype(BF)
    q_ref[:, half:] = dot_nn(normed, qt_ref[...]).astype(BF)


def mlp_back(gb, slope_ref, dpre_ref, uo_ref, ut_ref, do_ref, dt_ref):
    half = uo_ref.shape[1]
    total = 0.0
    for part, (up_ref, down_ref) in enumerate(((uo_ref, do_ref), (ut_ref, dt_ref))):
        span = slice(part * half, (part + 1) * half)
        dpre = (dot_nt(gb, down_ref[...]) * slope_ref[:, span].astype(F32)).astype(BF)
        dpre_ref[:, span] = dpre
        total = total + dot_nt(dpre, up_ref[...])
    return total


def section_halves(scal_ref, value, mine_ref, sent_ref):
    rows, half = mine_ref.shape
    left, right = value[:rows, :half], value[:rows, half:]
    lower = scal_ref[SCAL_SECTION] == 0
    mine_ref[...] = jnp.where(lower, left, right).astype(mine_ref.dtype)
    sent_ref[...] = jnp.where(lower, right, left).astype(sent_ref.dtype)


def owners_kernel(scal_ref, *refs):
    count = len(refs) // 3
    section = scal_ref[SCAL_SECTION]
    for mine_ref, got_ref, out_ref in zip(refs[:count], refs[count : 2 * count], refs[2 * count :]):
        out_ref[section] = mine_ref[...]
        out_ref[1 - section] = got_ref[...].astype(out_ref.dtype)


def dec_top_kernel(
    scal_ref, y1_ref, crossed_ref, cot_ref, gain_ref, bias_ref, po_ref, pt_ref, uo_ref, ut_ref,
    do_ref, dt_ref,
    decoded_ref, sent_ref, normed_ref, hidden_ref, dpre_ref, gb3_ref, gb2_ref, dcrossed_ref, u2_ref,
    sums_ref, slope_ref, *, valid,
):
    rows = y1_ref.shape[0]
    y2 = y1_ref[...] + two_parts(crossed_ref[...], po_ref, pt_ref)
    unit, inverse = norm_stats(y2)
    normed = (unit * gain_ref[...] + bias_ref[...]).astype(BF)
    normed_ref[...] = normed
    push(normed_ref)
    half = uo_ref.shape[1]
    y3 = y2
    for part, (up_ref, down_ref) in enumerate(((uo_ref, do_ref), (ut_ref, dt_ref))):
        act, slope = gelu_pair(dot_nn(normed, up_ref[...]))
        act = act.astype(BF)
        hidden_ref[:, part * half : (part + 1) * half] = act
        slope_ref[:, part * half : (part + 1) * half] = slope.astype(BF)
        y3 = y3 + dot_nn(act, down_ref[...])
    push(hidden_ref)
    row = lax.broadcasted_iota(jnp.int32, y2.shape, 0)
    length = scal_ref[SCAL_LENGTHS + scal_ref[SCAL_SECTION]]
    live = ((row < valid) & (row + scal_ref[SCAL_CORE] * valid < length)).astype(F32)
    section_halves(scal_ref, y3 * live, decoded_ref, sent_ref)
    u3 = cot_ref[...].astype(F32) * live
    gb3 = u3.astype(BF)
    gb3_ref[...] = gb3
    push(gb3_ref)
    dnormed = mlp_back(gb3, slope_ref, dpre_ref, uo_ref, ut_ref, do_ref, dt_ref)
    push(dpre_ref)
    dy, dgain, dbias = norm_back(unit, inverse, gain_ref[...], dnormed)
    u2 = u3 + dy
    u2_ref[...] = u2
    gb2 = u2.astype(BF)
    gb2_ref[...] = gb2
    push(gb2_ref)
    half = po_ref.shape[0]
    dcrossed_ref[:, :half] = dot_nt(gb2, po_ref[...]).astype(BF)
    dcrossed_ref[:, half:] = dot_nt(gb2, pt_ref[...]).astype(BF)
    sums_ref[...] = jnp.zeros_like(sums_ref)
    sums_ref[0:1, :] = dgain
    sums_ref[1:2, :] = dbias


def dec_back_kernel(
    step, dq_ref, y1_ref, u2_ref, gain_ref, qo_ref, qt_ref, po_ref, pt_ref,
    u1_ref, gb1_ref, datt_ref, sums_ref,
):
    dnormed = two_parts_t(dq_ref[...], qo_ref, qt_ref)
    unit, inverse = norm_stats(y1_ref[...])
    dy, dgain, dbias = norm_back(unit, inverse, gain_ref[...], dnormed)
    u1 = u2_ref[...] + dy
    u1_ref[...] = u1
    gb1 = u1.astype(BF)
    gb1_ref[...] = gb1
    half = po_ref.shape[0]
    datt_ref[:, :half] = dot_nt(gb1, po_ref[...]).astype(BF)
    datt_ref[:, half:] = dot_nt(gb1, pt_ref[...]).astype(BF)
    sums_ref[...] = jnp.zeros_like(sums_ref)
    sums_ref[0:1, :] = dgain
    sums_ref[1:2, :] = dbias


def packed_back(dq_ref, dkl_ref, dkr_ref, own_ref, oth_ref, out_ref):
    dkv = (dkl_ref[...].astype(F32) + dkr_ref[...].astype(F32)).astype(BF)
    dq = dq_ref[...]
    heads = own_ref.shape[1] // (3 * HEAD_DIM)
    total = 0.0
    for part, w_ref in enumerate((own_ref, oth_ref)):
        pieces = []
        for h in range(part * heads, (part + 1) * heads):
            pieces.append(dq[:, h * HEAD_DIM : (h + 1) * HEAD_DIM])
            pieces.append(dkv[:, h * 2 * HEAD_DIM : (h + 1) * 2 * HEAD_DIM])
        packed = jnp.concatenate(pieces, axis=1)
        out_ref[:, part * w_ref.shape[1] : (part + 1) * w_ref.shape[1]] = packed
        total = total + dot_nt(packed, w_ref[...])
    return total


def dec_last_kernel(
    step, scal_ref, dq_ref, dkl_ref, dkr_ref, x_ref, u1_ref, gain_ref, own_ref, oth_ref,
    packed_ref, sums_ref, mine_ref, sent_ref,
):
    dnormed = packed_back(dq_ref, dkl_ref, dkr_ref, own_ref, oth_ref, packed_ref)
    unit, inverse = norm_stats(x_ref[...].astype(F32))
    dx, dgain, dbias = norm_back(unit, inverse, gain_ref[...], dnormed)
    section_halves(scal_ref, u1_ref[...] + dx, mine_ref, sent_ref)
    sums_ref[...] = jnp.zeros_like(sums_ref)
    sums_ref[0:1, :] = dgain
    sums_ref[1:2, :] = dbias


def enc_back_kernel(
    step, gl_ref, gr_ref, x2_ref, x1_ref, slope_ref, gc_ref, gb_ref, ko_ref, kt_ref, uo_ref, ut_ref,
    do_ref, dt_ref, po_ref, pt_ref,
    gkv_ref, gb2_ref, dpre_ref, gb1_ref, datt_ref, u1_ref, sums_ref,
):
    if step == 0:
        sums_ref[...] = jnp.zeros_like(sums_ref)

    gkv = (gl_ref[...].astype(F32) + gr_ref[...].astype(F32)).astype(BF)
    gkv_ref[...] = gkv
    dmemory = two_parts_t(gkv, ko_ref, kt_ref)
    unit, inverse = norm_stats(x2_ref[...])
    u2, dgain, dbias = norm_back(unit, inverse, gc_ref[...], dmemory)
    sums_ref[0:1, :] += dgain
    sums_ref[1:2, :] += dbias
    gb2 = u2.astype(BF)
    gb2_ref[...] = gb2
    dnormed = mlp_back(gb2, slope_ref, dpre_ref, uo_ref, ut_ref, do_ref, dt_ref)
    unit, inverse = norm_stats(x1_ref[...])
    dx, dgain, dbias = norm_back(unit, inverse, gb_ref[...], dnormed)
    sums_ref[2:3, :] += dgain
    sums_ref[3:4, :] += dbias
    u1 = u2 + dx
    u1_ref[...] = u1
    gb1 = u1.astype(BF)
    gb1_ref[...] = gb1
    half = po_ref.shape[0]
    datt_ref[:, :half] = dot_nt(gb1, po_ref[...]).astype(BF)
    datt_ref[:, half:] = dot_nt(gb1, pt_ref[...]).astype(BF)


def stem_back_kernel(
    step, dq_ref, dkl_ref, dkr_ref, x0_ref, u1_ref, ge_ref, go_ref, gs_ref, gain_ref, own_ref, oth_ref,
    second_ref, gh_ref,
    packed_ref, g2_ref, ede_ref, edo_ref, sums_ref, edh_ref, carry_ref,
):
    if step == 0:
        sums_ref[...] = jnp.zeros_like(sums_ref)
        carry_ref[...] = jnp.zeros_like(carry_ref)

    dnormed = packed_back(dq_ref, dkl_ref, dkr_ref, own_ref, oth_ref, packed_ref)
    unit, inverse = norm_stats(x0_ref[...])
    dx, dgain, dbias = norm_back(unit, inverse, gain_ref[...], dnormed)
    sums_ref[0:1, :] += dgain
    sums_ref[1:2, :] += dbias
    g2 = ((u1_ref[...] + dx) * gs_ref[...].astype(F32)).astype(BF)
    g2_ref[...] = g2
    width = g2.shape[1]
    before = dot_nt(g2, second_ref[:width])
    even = dot_nt(g2, second_ref[width : 2 * width])
    odd = dot_nt(g2, second_ref[2 * width :])
    ede_ref[...] = (even * ge_ref[...].astype(F32)).astype(BF)
    row = lax.broadcasted_iota(jnp.int32, before.shape, 0)
    later = jnp.where(
        row == before.shape[0] - 1, carry_ref[0:1, :], pltpu.roll(before, before.shape[0] - 1, 0)
    )
    carry_ref[0:1, :] = before[0:1]
    edo_ref[...] = ((odd + later) * go_ref[...].astype(F32)).astype(BF)
    front = lax.broadcasted_iota(jnp.int32, edh_ref.shape, 0)
    edh_ref[...] = jnp.where(front == 0, before[0:1] * gh_ref[...], 0.0).astype(BF)


SCAL_CORE, SCAL_SECTION, SCAL_X, SCAL_Z, SCAL_Z_LOW, SCAL_Z_HIGH, SCAL_LENGTHS = range(7)
TILE = 512


def gradient_tiles(left, right_ref, own_ref, oth_ref, at):
    turned, half = left.T, right_ref.shape[1] // 2
    for part, out_ref in enumerate((own_ref, oth_ref)):
        for first in range(0, half, TILE):
            width = min(TILE, half - first)
            piece = dot_nn(turned, right_ref[:, part * half + first : part * half + first + width])
            out_ref[:, at + first : at + first + width] = piece.astype(BF)
    return at + half


def gradients_kernel(*refs):
    *pairs, own_ref, oth_ref = refs
    at = 0
    for left_ref, right_ref in zip(pairs[::2], pairs[1::2]):
        at = gradient_tiles(left_ref[...], right_ref, own_ref, oth_ref, at)


def gradients(pairs, held=()):
    columns = sum(right.shape[1] // 2 for _, right in pairs)
    width = pairs[0][0].shape[1]
    return flat_call(
        gradients_kernel,
        [Far(v) if any(v is h for h in held) else v for pair in pairs for v in pair],
        [shape_of(width, columns)] * 2,
        flops=sum(2 * left.size * right.shape[1] for left, right in pairs), megabytes=9,
    )


def late_kernel(
    scal_ref, normed_ref, packed_ref, g2_ref, before_ref, even_ref, odd_ref, ede_ref, edo_ref, edh_ref,
    windows_ref, mh_ref, va_ref, vb_ref, vc_ref, ve_ref, vf_ref, own_ref, oth_ref, own_stem_ref, oth_stem_ref, stem_ref, *,
    channels,
):
    gradient_tiles(normed_ref[...], packed_ref, own_ref, oth_ref, 0)
    turned, width = g2_ref[...].T, g2_ref.shape[1]
    for n, ref in enumerate((before_ref, even_ref, odd_ref)):
        stem_ref[:, n * width : (n + 1) * width] = dot_nn(turned, ref[...]).astype(BF)
    windows = windows_ref[...].T
    first = dot_nn(windows[: 3 * LANES], ede_ref[...]) + dot_nn(windows[LANES:], edo_ref[...])
    first = first + dot_nn(mh_ref[...].T, edh_ref[...])
    vectors = [
        vf_ref[0:1], ve_ref[2:3], ve_ref[0:1], vf_ref[1:2], ve_ref[3:4], ve_ref[1:2],
        va_ref[0:1], vb_ref[0:1], vc_ref[0:1], va_ref[1:2], vb_ref[1:2], vc_ref[1:2],
        jnp.zeros((4, width), F32),
    ]
    taps = [first[n * LANES : n * LANES + channels] for n in range(first.shape[0] // LANES)]
    first = jnp.concatenate([*taps, jnp.concatenate(vectors, axis=0)], axis=0)
    stem_ref[:, 3 * width :] = first.T.astype(BF)
    core, half = scal_ref[SCAL_CORE], stem_ref.shape[1] // 2
    block = 16
    groups = width // (4 * block)
    for part, out_ref in enumerate((own_stem_ref, oth_stem_ref)):
        bit = core if part == 0 else 1 - core
        for group in range(groups):
            for section in range(2):
                source = pl.multiple_of(group * 4 * block + bit * 2 * block + section * block, block)
                rows = stem_ref[pl.ds(source, block), :]
                to = (section * groups + group) * 2 * block
                out_ref[to : to + block, :] = rows[:, :half]
                out_ref[to + block : to + 2 * block, :] = rows[:, half:]


def halves(scal_ref, bit, groups, size, total, keep_ref, send_ref, columns=slice(None)):
    for group in range(groups):
        for place, out_ref in ((scal_ref[bit], keep_ref), (1 - scal_ref[bit], send_ref)):
            source = pl.ds(pl.multiple_of((group * 2 + place) * size, size), size)
            out_ref[group * size : (group + 1) * size, columns] = total(source)


def first_kernel(scal_ref, *refs, cut, block):
    *parts, am_ref, as_ref, bm_ref, bg_ref = refs
    if len(parts) == 2:
        parts = [ref.at[:, span] for ref in parts for span in (slice(0, cut), slice(cut, None))]
        parts = [parts[0], parts[2], parts[1], parts[3]]
    low_own, low_got, high_own, high_got = parts
    low = lambda rows: low_own[rows, :] + low_got[rows, :]
    high = lambda rows: high_own[rows, :] + high_got[rows, :]
    rows = low_own.shape[0]
    halves(scal_ref, SCAL_X, rows // (2 * block), block, low, am_ref, as_ref)
    halves(scal_ref, SCAL_SECTION, 1, rows // 2, high, bm_ref, bg_ref)


def second_kernel(
    scal_ref, am_ref, ag_ref, bm_ref, bg_ref, akeep_ref, asend_ref, bkeep_ref, bsend_ref, *, block
):
    low = lambda rows: am_ref[rows, :] + ag_ref[rows, :]
    high = lambda rows: bm_ref[rows, :] + bg_ref[rows, :]
    rows = am_ref.shape[0]
    halves(scal_ref, SCAL_SECTION, 1, rows // 2, low, akeep_ref, asend_ref)
    halves(scal_ref, SCAL_X, rows // (2 * block), block, high, bkeep_ref, bsend_ref)


def third_kernel(scal_ref, am_ref, ag_ref, bm_ref, bg_ref, *out_refs, cut, block):
    for flip, out_ref in enumerate(out_refs):
        rows = pl.ds(pl.multiple_of((scal_ref[SCAL_Z] ^ flip) * block, block), block)
        out_ref[:, :cut] = am_ref[rows, :] + ag_ref[rows, :]
        out_ref[:, cut:] = bm_ref[rows, :] + bg_ref[rows, :]


def third_half_kernel(scal_ref, am_ref, ag_ref, bm_ref, bg_ref, keep_ref, send_ref, *, cut, block):
    low = lambda rows: am_ref[rows, :] + ag_ref[rows, :]
    high = lambda rows: bm_ref[rows, :] + bg_ref[rows, :]
    groups = am_ref.shape[0] // (2 * block)
    halves(scal_ref, SCAL_Z_LOW, groups, block, low, keep_ref, send_ref, slice(0, cut))
    halves(scal_ref, SCAL_Z_LOW, groups, block, high, keep_ref, send_ref, slice(cut, None))


def fourth_half_kernel(scal_ref, mine_ref, got_ref, keep_ref, send_ref, *, block):
    both = lambda rows: mine_ref[rows, :] + got_ref[rows, :]
    halves(scal_ref, SCAL_Z_HIGH, 1, block, both, keep_ref, send_ref)


def last_kernel(*refs, widths):
    count = len(refs) - len(widths)
    at = 0
    for out_ref, width in zip(refs[count:], widths):
        total = sum(ref[:, at : at + width].astype(F32) for ref in refs[:count])
        out_ref[...] = total
        at += width


def stem_last_kernel(scal_ref, mine_ref, got_ref, second_ref, first_ref, *vec_refs):
    mine, got = mine_ref[...], got_ref[...]
    lower = scal_ref[SCAL_SECTION] == 0
    block = mine.shape[0] // 2
    parts = []
    for half in (jnp.where(lower, mine, got), jnp.where(lower, got, mine)):
        parts.append(jnp.concatenate([half[:block], half[block:]], axis=1))
    full = jnp.concatenate(parts, axis=0)
    count, _, width = second_ref.shape
    channels = first_ref.shape[2]
    for n in range(count):
        second_ref[n] = full[:, n * width : (n + 1) * width]
        first_ref[n] = full[:, count * width + n * channels : count * width + (n + 1) * channels]
    turned = full[:, full.shape[1] - 2 * HEAD_DIM :].T
    at = turned.shape[0] - 16
    for n, ref in enumerate(vec_refs):
        ref[...] = turned[at + 3 * n : at + 3 * n + 3]


def sum_over_chips(own, oth, scal, cut, widths, direct=False):
    after = lambda value, other: value if other is None else tie(value, other)
    if not isinstance(own, tuple):
        own, oth = (own,), (oth,)
    parts = [v for mine, other in zip(own, oth) for v in (mine, swap(other, "tensor"))]
    rows, columns = own[0].shape[0], sum(v.shape[1] for v in own)
    block = rows // (2 * lax.axis_size("dp"))
    some = lambda n, w: shape_of(n, w)
    left, right = cut, columns - cut
    am, asend, bm, bsend = flat_call(
        functools.partial(first_kernel, cut=cut, block=block), parts,
        [some(rows // 2, left)] * 2 + [some(rows // 2, right)] * 2, scal, megabytes=6,
    )
    am = after(am, (yield am))
    ag, bg = flip_bit(asend, "dp", 1), swap(bsend, "section")
    am, asend, bm, bsend = flat_call(
        functools.partial(second_kernel, block=block), [am, ag, bm, bg],
        [some(rows // 4, left)] * 2 + [some(rows // 4, right)] * 2, scal, megabytes=6,
    )
    am = after(am, (yield am))
    ag, bg = swap(asend, "section"), flip_bit(bsend, "dp", 1)
    if direct:
        mine, *send = flat_call(
            functools.partial(third_kernel, cut=cut, block=block), [am, ag, bm, bg],
            [some(block, columns)] * (rows // (4 * block)), scal, megabytes=6,
        )
        mine = after(mine, (yield mine))
        got = [flip_bit(v, "dp", 2 * (n + 1)) for n, v in enumerate(send)]
    else:
        mine, send = flat_call(
            functools.partial(third_half_kernel, cut=cut, block=block), [am, ag, bm, bg],
            [some(2 * block, columns)] * 2, scal, megabytes=6,
        )
        mine = after(mine, (yield mine))
        mine, send = flat_call(
            functools.partial(fourth_half_kernel, block=block), [mine, flip_bit(send, "dp", 2)],
            [some(block, columns)] * 2, scal, megabytes=6,
        )
        mine = after(mine, (yield mine))
        got = [flip_bit(send, "dp", 4)]
    yield flat_call(
        functools.partial(last_kernel, widths=widths), [mine, *got],
        [shape_of(block, width, F32) for width in widths], megabytes=6,
    )


def tie(value, *others):
    return lax.optimization_barrier((value, *others))[0]


def swap(value, axis):
    return lax.ppermute(value, axis, [(0, 1), (1, 0)])


def flip_bit(value, axis, bit):
    count = lax.axis_size(axis)
    return lax.ppermute(value, axis, [(i, i ^ bit) for i in range(count)])


def add_low(left, right):
    return (left.astype(F32) + right.astype(F32)).astype(BF)


def halve(value, dim, place, send):
    mine = lax.dynamic_index_in_dim(value, place, dim, keepdims=False)
    other = lax.dynamic_index_in_dim(value, 1 - place, dim, keepdims=False)
    return mine, send(other)


def reduce_blocks(value, names):
    section, clip_group = lax.axis_index("section"), lax.axis_index("dp")
    dims = list(names)
    order = [name for name, _ in sorted(names.items(), key=lambda item: item[1])]
    held = value
    for step, name in enumerate(order):
        dim = [n for n in dims if n in order[step:]].index(name)
        if name == "section":
            mine, got = halve(held, dim, section, functools.partial(swap, axis="section"))
        else:
            place = (clip_group // name) % 2
            mine, got = halve(held, dim, place, functools.partial(flip_bit, axis="dp", bit=name))
        held = mine.astype(F32) + got.astype(F32)
        if step < len(order) - 1:
            held = held.astype(BF)
    return held


def dp_bits():
    count, bits = lax.axis_size("dp"), []
    while count > 1:
        count //= 2
        bits.append(count)
    return bits


def sum_projections(value):
    rows, columns = value.shape
    bits = dp_bits()
    lead = (2,) * (1 + len(bits))
    half = columns // 256 * 128
    out = []
    for which, part in enumerate((value[:, :half], value[:, half:])):
        shaped = part.reshape(*lead, rows // 2 ** len(lead), part.shape[1])
        early = {"section": 1, bits[-1]: 0} if which == 0 else {"section": 0, bits[-1]: 1}
        names = {"section": early["section"]}
        for at, bit in enumerate(bits):
            names[bit] = early.get(bit, 2 + at)
        out.append(reduce_blocks(shaped, names))
    return jnp.concatenate(out, axis=1)


def sum_stem(value):
    rows, columns = value.shape
    bits = dp_bits()
    place = lax.axis_index("tensor")
    groups = 2 ** len(bits)
    block = rows // (groups * 2)
    shaped = value.reshape(groups, 2, block, columns)
    mine, got = halve(shaped, 1, place, functools.partial(swap, axis="tensor"))
    held = add_low(mine, got)
    half = columns // 256 * 128
    out = []
    for which, part in enumerate((held[:, :, :half], held[:, :, half:])):
        shaped = part.reshape(*((2,) * len(bits)), 2, block // 2, part.shape[2])
        names = {bit: 2 + at for at, bit in enumerate(bits)}
        names[bits[-1]] = which
        names["section"] = 1 - which
        out.append(reduce_blocks(shaped, names))
    mine = jnp.concatenate(out, axis=1)
    got = swap(mine, "section")
    first = lax.axis_index("section") == 0
    return jnp.concatenate(
        [jnp.where(first, mine, got), jnp.where(first, got, mine)], axis=0
    )


def core_sum(pairs):
    full = [dot_tn(left, right).astype(BF) for left, right in pairs]
    mine = jnp.concatenate([v[:, : v.shape[1] // 2] for v in full], axis=1)
    sent = jnp.concatenate([v[:, v.shape[1] // 2 :] for v in full], axis=1)
    return add_low(mine, swap(sent, "tensor"))


def sinusoid_table(count, width_all):
    step_size = math.log(10000.0) / (width_all // 2 - 1)
    rates = np.exp(-step_size * np.arange(width_all // 2))
    angles = np.arange(count)[:, None] * rates[None, :]
    return np.concatenate([np.sin(angles), np.cos(angles)], axis=1).astype(np.float32)


def pad_rows(value, rows):
    return jnp.pad(value, ((0, rows - value.shape[0]), (0, 0)))


def round_up(count):
    return -(-count // CHUNK) * CHUNK


def body(
    mel,
    conv_first,
    conv_second,
    enc_gain,
    enc_shift,
    enc_qkv,
    enc_proj,
    enc_up,
    enc_down,
    cross_kv,
    text,
    lengths,
    dec_gain,
    dec_shift,
    dec_qkv,
    dec_proj,
    cross_query,
    cross_proj,
    dec_up,
    dec_down,
    cotangent,
):
    section = lax.axis_index("section")
    place = lax.axis_index("tensor")
    cores = lax.axis_size("tensor")
    width = text.shape[2]
    frames = mel.shape[1] // 2
    valid = frames // cores
    rows = round_up(valid)
    slots = text.shape[1]
    text_rows = round_up(slots)
    channels = mel.shape[2]

    group = lax.axis_index("dp")
    bits = [place, section, group % 2, group // 2, group // 2 % 2, group // 4 % 2]
    scal = jnp.concatenate([jnp.stack([bit.astype(jnp.int32) for bit in bits]), lengths])
    pair = lambda w: (w, swap(w, "tensor"))
    w_dqkv, w_eqkv, w_eproj, w_dproj, w_cq = map(pair, (dec_qkv, enc_qkv, enc_proj, dec_proj, cross_query))
    w_eup, w_edown, w_ckv = map(pair, (enc_up, enc_down, cross_kv))
    w_cproj, w_dup, w_ddown = map(pair, (cross_proj, dec_up, dec_down))
    early = [w[1] for w in (w_eproj, w_dproj, w_cq, w_cproj)]
    late = [w[1] for w in (w_eup, w_edown, w_ckv, w_dup, w_ddown)]
    eg, es = [enc_gain[i : i + 1] for i in range(3)], [enc_shift[i : i + 1] for i in range(3)]
    dg, ds = [dec_gain[i : i + 1] for i in range(3)], [dec_shift[i : i + 1] for i in range(3)]

    taps = conv_first.shape[0] * channels
    depth = -(-(taps + 12) // LANES) * LANES
    second = conv_second.reshape(-1, width)
    table = np.pad(sinusoid_table(frames, width), ((0, rows - valid), (0, 0)))
    table = jnp.asarray(np.stack([table[valid * core : valid * core + rows] for core in range(cores)]))

    dn_a, dq_self, dkv_self = rows_call(
        qkv_kernel, text_rows, [Clip(text)], [dg[0], ds[0], *w_dqkv],
        [(width, BF, Far), (width, BF), (2 * width, BF)], flops=2 * text_rows * width * 3 * width, scal=scal,
    )
    dkv_self_r = swap(dkv_self, "tensor")

    mel_rows = 2 * frames + 8 + 2 * (rows - valid) + 16
    even, odd, before, ge, go, gs, x0, gh, windows, halo = rows_call(
        functools.partial(stem_fwd_kernel, valid=valid), rows, [Far(table, 1, True)],
        [Far(jnp.swapaxes(mel, 1, 2)), Far(conv_first), Far(second)],
        [(width, BF, Far)] * 6 + [(width, F32)],
        sums=[((16, width), F32), ((rows, 4 * LANES), BF, Far), ((16, 3 * LANES), BF)],
        scratch=[pltpu.VMEM((8, width), F32), pltpu.VMEM((mel_rows, LANES), F32)],
        flops=2 * rows * width * 2000, scal=scal, told=True, megabytes=14,
    )
    en_a, eq, ekv = rows_call(
        qkv_kernel, rows, [tie(x0, dq_self, *early)], [eg[0], es[0], *w_eqkv],
        [(width, BF, Far), (width, BF), (2 * width, BF)], flops=2 * rows * width * 3 * width,
    )
    ekv_r = swap(ekv, "tensor")

    datt, drest, dstat = attention_fwd(dq_self, dkv_self, dkv_self_r, slots, scal)
    eq = tie(eq, datt)
    eatt, erest, estat = attention_fwd(eq, ekv, ekv_r, valid)
    units = 2 * enc_up.shape[1]
    x1, x2, en_b, ehid, eslope, memory, ckv = rows_call(
        enc_mid_kernel, rows, [x0, tie(eatt, *late)],
        [eg[1], es[1], eg[2], es[2], *w_eproj, *w_eup, *w_edown, *w_ckv],
        [
            (width, F32, Far), (width, F32, Far), (width, BF, Far), (units, BF, Far), (units, BF, Far),
            (width, BF, Far), (2 * width, BF),
        ],
        flops=2 * rows * width * (3 * width + 2 * units), megabytes=20,
    )
    ckv_r = swap(ckv, "tensor")
    y1, dn_b, cq = rows_call(
        dec_mid_kernel, text_rows, [Clip(text), tie(datt, ckv)], [dg[1], ds[1], *w_dproj, *w_cq],
        [(width, F32), (width, BF, Far), (width, BF)], flops=2 * text_rows * width * 2 * width, scal=scal,
    )

    crossed, crest, cstat = attention_fwd(cq, ckv, ckv_r, valid)
    dec_units = 2 * dec_up.shape[1]
    top_outs = [
        (width, BF), (dec_units, BF), (dec_units, BF), (width, BF), (width, BF), (width, BF), (width, F32),
    ]
    owned = lambda kind: shape_of(slots, width // 2, kind)
    decoded, decoded_sent, dn_c, dhid, dpre, dgb3, dgb2, dcrossed, u2, sums_c = flat_call(
        functools.partial(dec_top_kernel, valid=slots),
        [y1, crossed, Clip(cotangent), dg[2], ds[2], *w_cproj, *w_dup, *w_ddown],
        [owned(BF), owned(BF)] + [shape_of(text_rows, w, k) for w, k in top_outs] + [shape_of(8, width, F32)],
        scal=scal, scratch=[pltpu.VMEM((text_rows, dec_units), BF)],
        flops=2 * text_rows * width * (2 * width + 4 * dec_units), megabytes=12,
    )
    decoded_got = swap(decoded_sent, "section")
    fast = lax.axis_size("dp") == 8 and width % (4 * 8 * 16) == 0
    top_pairs = [(dn_c, dpre), (dgb3, dhid), (dgb2, crossed)]
    top_widths = [dec_up.shape[1], dec_down.shape[0], cross_proj.shape[0]]
    if fast:
        own, oth = gradients(top_pairs)
        top_steps = sum_over_chips(own, oth, scal, sum(top_widths) // 2, top_widths)
        dcrossed = tie(dcrossed, own)
    dcq, dckv, dckv_r = attention_bwd(cq, ckv, ckv_r, crossed, crest, cstat, dcrossed, valid)
    if fast:
        dcq = tie(dcq, next(top_steps))
    dckv_got = swap(dckv_r, "tensor")
    u1, dgb1, ddatt, sums_b = rows_call(
        dec_back_kernel, text_rows, [dcq, y1, u2], [dg[1], *w_cq, *w_dproj],
        [(width, F32), (width, BF, Far), (width, BF)], sums=[((8, width), F32)],
        flops=2 * text_rows * width * 2 * width,
    )
    dqs, dkvs, dkvs_r = attention_bwd(
        dq_self, dkv_self, dkv_self_r, datt, drest, dstat, ddatt, slots, scal
    )
    dkvs_got = swap(dkvs_r, "tensor")

    gkv, egb2, edpre, egb1, deatt, eu1, sums_e = rows_call(
        enc_back_kernel, rows, [tie(dckv, dqs), dckv_got, x2, x1, eslope],
        [eg[2], eg[1], *w_ckv, *w_eup, *w_edown, *w_eproj],
        [(2 * width, BF), (width, BF), (units, BF, Far), (width, BF), (width, BF), (width, F32, Far)],
        sums=[((8, width), F32)], flops=2 * rows * width * (3 * width + 2 * units), megabytes=13,
    )
    d_packed, sums_a, text_mine, text_sent = rows_call(
        dec_last_kernel, text_rows, [dqs, dkvs, dkvs_got, Clip(text), tie(u1, deatt)], [dg[0], *w_dqkv],
        [(2 * dec_qkv.shape[1], BF)],
        sums=[((8, width), F32), ((slots, width // 2), F32), ((slots, width // 2), BF)],
        flops=2 * text_rows * width * 3 * width, scal=scal, told=True,
    )
    text_got = swap(text_sent, "section")
    owned = [jax.ShapeDtypeStruct((2, *text_mine.shape), kind) for kind in (BF, F32)]
    decoded, text_grad = flat_call(
        owners_kernel, [decoded, text_mine, decoded_got, text_got], owned, scal=scal, megabytes=4
    )
    mid_pairs = [
        (dn_a, d_packed), (dn_b, dcq), (dgb1, datt), (egb1, eatt), (memory, gkv), (en_b, edpre), (egb2, ehid),
    ]
    mid_widths = [dec_qkv.shape[1], cross_query.shape[1], dec_proj.shape[0], enc_proj.shape[0]]
    mid_widths += [cross_kv.shape[1], enc_up.shape[1], enc_down.shape[0]]
    if fast:
        mid_pairs[0] = (dn_a, tie(d_packed, top_steps.send(d_packed)))
        own, oth = gradients(mid_pairs, [memory, en_b, edpre, ehid])
        mid_steps = sum_over_chips(own, oth, scal, sum(mid_widths) // 2, mid_widths)
        waits = [
            lambda: (own,), lambda: (top_steps.send(base_a), text_grad), lambda: (next(mid_steps),)
        ]
    else:
        waits = [lambda: ()] * 3

    half = width // (4 * HEAD_DIM)
    deatt = tie(deatt, *waits[0]())
    side = (eatt, erest, estat)
    base_a, dekv_a = attention_bwd_side(eq, ekv_r, *side, deatt, valid, pairs=(0, half))
    deatt = tie(deatt, base_a, *waits[1]())
    base_b, dekv_r = attention_bwd_side(
        eq, ekv_r, *side, deatt, valid, pairs=(half, half), earlier=(dekv_a,)
    )
    dekv_got = swap(dekv_r, "tensor")
    deatt = tie(deatt, base_b, *waits[2]())
    deq, dekv = attention_bwd_side(eq, ekv, *side, deatt, valid, (base_a, base_b))
    e_packed, g2, ede, edo, sums_f, edh = rows_call(
        stem_back_kernel, rows, [deq, dekv, dekv_got, x0, eu1, ge, go, gs],
        [eg[0], *w_eqkv, second, gh],
        [(2 * enc_qkv.shape[1], BF), (width, BF), (width, BF), (width, BF)],
        sums=[((8, width), F32), ((16, width), BF)], scratch=[pltpu.VMEM((8, width), F32)],
        reverse=True, flops=2 * rows * width * 6 * width,
    )
    sums = [sums_a, sums_b, sums_c, sums_e, sums_f]
    if fast:
        late_waits = (top_steps.send(e_packed),)
        stem_width = 3 * width + depth
        late_columns = (enc_qkv.shape[1], enc_qkv.shape[1], stem_width // 2, stem_width // 2)
        own, oth, own_stem, oth_stem = flat_call(
            functools.partial(late_kernel, channels=channels),
            [
                en_a, tie(e_packed, *late_waits), g2, before, even, odd, ede, edo, edh, windows, halo,
                *sums,
            ],
            [shape_of(width, columns) for columns in late_columns], scal=scal, scratch=[pltpu.VMEM((width, stem_width), BF)],
            flops=2 * rows * width * (3 * width + 3 * width + 2 * depth), megabytes=10,
        )
        own = tie(own, mid_steps.send(own))
        late_steps = sum_over_chips(
            (own, own_stem), (oth, oth_stem), scal, enc_qkv.shape[1], [enc_qkv.shape[1], stem_width // 2], True
        )
        top_sums = top_steps.send(next(late_steps))
        later = mid_steps.send(top_sums[0])
        later = mid_steps.send(late_steps.send(later))
        mid_sums = mid_steps.send(late_steps.send(later))
        late_qkv, stem = late_steps.send(mid_sums[0])
        block = 2 * width // (2 * lax.axis_size("dp") * cores)
        conv_second_grad, conv_first_grad, *vec = flat_call(
            stem_last_kernel, [stem, swap(stem, "section")],
            [
                jax.ShapeDtypeStruct((conv_second.shape[0], block, width), F32),
                jax.ShapeDtypeStruct((conv_first.shape[0], block, channels), F32),
            ] + [shape_of(3, block, F32)] * 4,
            scal=scal, megabytes=6,
        )
        conv_second_grad = conv_second_grad.transpose(0, 2, 1)
        conv_first_grad = conv_first_grad.transpose(0, 2, 1)
    else:
        cuts = lambda value, widths: jnp.split(value, list(np.cumsum(widths)[:-1]), axis=1)
        top_sums = cuts(sum_projections(core_sum(top_pairs)), top_widths)
        mid_sums = cuts(sum_projections(core_sum(mid_pairs)), mid_widths)
        late_qkv = sum_projections(core_sum([(en_a, e_packed)]))
        first_t = dot_tn(ede, windows[:, : 3 * LANES]) + dot_tn(edo, windows[:, LANES:]) + dot_tn(edh, halo)
        first_t = first_t.reshape(width, -1, LANES)[:, :, :channels].reshape(width, taps)
        vectors = jnp.concatenate(
            [
                sums_f[0:1], sums_e[2:3], sums_e[0:1], sums_f[1:2], sums_e[3:4], sums_e[1:2],
                sums_a[0:1], sums_b[0:1], sums_c[0:1], sums_a[1:2], sums_b[1:2], sums_c[1:2],
            ],
            axis=0,
        )
        stem = [dot_tn(g2, act) for act in (before, even, odd)] + [first_t, vectors.T]
        stem.append(jnp.zeros((width, depth - taps - vectors.shape[0]), F32))
        stem = sum_stem(jnp.concatenate([v.astype(BF) for v in stem], axis=1)).T
        conv_second_grad, conv_first_grad = stem[: 3 * width], stem[3 * width : 3 * width + taps]
        vec = [stem[3 * width + taps + 3 * n : 3 * width + taps + 3 * n + 3] for n in range(4)]

    d_up, d_down_t, d_cproj_t = top_sums
    d_qkv, d_cq, d_proj_t, e_proj_t, e_kv, e_up, e_down_t = mid_sums
    return (
        decoded,
        text_grad,
        conv_first_grad.reshape(*conv_first.shape[:2], -1),
        conv_second_grad.reshape(*conv_second.shape[:2], -1),
        vec[0],
        vec[1],
        late_qkv,
        e_proj_t.T,
        e_up,
        e_down_t.T,
        e_kv,
        vec[2],
        vec[3],
        d_qkv,
        d_proj_t.T,
        d_cq,
        d_cproj_t.T,
        d_up,
        d_down_t.T,
    )


def solution(mesh):
    in_specs = (
        P("dp", None, None),
        P(),
        P(),
        P(),
        P(),
        P(None, "tensor"),
        P("tensor", None),
        P(None, "tensor"),
        P("tensor", None),
        P(None, "tensor"),
        P("dp", "tensor", None),
        P("dp"),
        P(),
        P(),
        P(None, "tensor"),
        P("tensor", None),
        P(None, "tensor"),
        P("tensor", None),
        P(None, "tensor"),
        P("tensor", None),
        P("dp", "tensor", None),
    )
    out_specs = (
        P("dp", "tensor", "section"),
        P("dp", "tensor", "section"),
        P(None, None, ("dp", "tensor")),
        P(None, None, ("dp", "tensor")),
        P(None, ("dp", "tensor")),
        P(None, ("dp", "tensor")),
        P(("section", "dp"), "tensor"),
        P("tensor", ("section", "dp")),
        P(("section", "dp"), "tensor"),
        P("tensor", ("section", "dp")),
        P(("section", "dp"), "tensor"),
        P(None, ("dp", "tensor")),
        P(None, ("dp", "tensor")),
        P(("section", "dp"), "tensor"),
        P("tensor", ("section", "dp")),
        P(("section", "dp"), "tensor"),
        P("tensor", ("section", "dp")),
        P(("section", "dp"), "tensor"),
        P("tensor", ("section", "dp")),
    )
    return jax.shard_map(body, mesh=mesh, in_specs=in_specs, out_specs=out_specs, check_vma=False)
```

```python
import functools
import math

import jax
import jax.numpy as jnp
import numpy as np
from jax import lax
from jax.experimental import pallas as pl
from jax.experimental.pallas import tpu as pltpu
from jax.sharding import PartitionSpec as P

HEAD_DIM = 64
NEG = -1000000000.0
EPS = 1e-05
TINY = 1e-28
CHUNK = 256
LANES = 128
BF, F32 = jnp.bfloat16, jnp.float32
INV_SQRT2 = 0.7071067811865476
INV_SQRT2PI = 0.3989422804014327


def dot_nn(left, right):
    return lax.dot_general(left, right, (((1,), (0,)), ((), ())), preferred_element_type=F32)


def dot_nt(left, right):
    return lax.dot_general(left, right, (((1,), (1,)), ((), ())), preferred_element_type=F32)


def dot_tn(left, right):
    return lax.dot_general(left, right, (((0,), (0,)), ((), ())), preferred_element_type=F32)


def norm_stats(rows):
    centre = rows - jnp.mean(rows, axis=-1, keepdims=True)
    spread = jnp.mean(centre * centre, axis=-1, keepdims=True)
    inverse = lax.rsqrt(spread + EPS)
    return centre * inverse, inverse


def norm_back(unit, inverse, gain_row, upstream):
    scaled = upstream * gain_row
    first = jnp.mean(scaled, axis=-1, keepdims=True)
    second = jnp.mean(scaled * unit, axis=-1, keepdims=True)
    grad_rows = inverse * (scaled - first - unit * second)
    grad_gain = jnp.sum(upstream * unit, axis=0, keepdims=True)
    grad_bias = jnp.sum(upstream, axis=0, keepdims=True)
    return grad_rows, grad_gain, grad_bias


def gelu_pair(v):
    phi = 0.5 * (1.0 + lax.erf(v * INV_SQRT2))
    return v * phi, phi + (v * INV_SQRT2PI) * jnp.exp(-0.5 * (v * v))


def lanes(rows):
    return lax.broadcasted_iota(jnp.int32, (rows, 2 * HEAD_DIM), 1)

def key_aug(kv, valid, ones):
    lane = lanes(kv.shape[0])
    row = lax.broadcasted_iota(jnp.int32, kv.shape, 0)
    pad = jnp.where((lane > HEAD_DIM) & (lane <= HEAD_DIM + ones), 1.0, 0.0)
    pad = jnp.where((lane == HEAD_DIM) & (row >= valid), NEG, pad).astype(BF)
    return jnp.where(lane < HEAD_DIM, kv, pad)

def causal_bias(scal_ref, key_rows, query_rows, valid):
    place, length = scal_ref[SCAL_CORE], scal_ref[SCAL_LENGTHS + scal_ref[SCAL_SECTION]]
    key_id = lax.broadcasted_iota(jnp.int32, (2 * key_rows, query_rows), 0)
    query_id = lax.broadcasted_iota(jnp.int32, (2 * key_rows, query_rows), 1)
    query_pos = query_id + place * valid
    key_pos = jnp.where(key_id < key_rows, key_id + place * valid, key_id - key_rows + (1 - place) * valid)
    return jnp.where((key_pos <= query_pos) & (key_pos < length), 0.0, NEG)

def fwd_setup(q_ref, kl_ref, kr_ref, valid):
    lane_q = lanes(q_ref.shape[0])
    q_all = q_ref[...].astype(F32) * HEAD_DIM**-0.5
    wide = 2 * HEAD_DIM

    def operands(h):
        q = jnp.where(lane_q < HEAD_DIM, q_all if h == 0 else pltpu.roll(q_all, HEAD_DIM, 1), 0.0)
        kv = [ref[:, h * wide : (h + 1) * wide] for ref in (kl_ref, kr_ref)]
        turned = [v.T for v in kv]
        sub = lax.broadcasted_iota(jnp.int32, turned[0].shape, 0)
        ones = [jnp.where(sub == 0, jnp.ones_like(v), v) for v in turned]
        return q, [key_aug(v, valid, 1) for v in kv], turned, ones

    return lane_q, operands


def fwd_finish(parts, logs, shift, out_ref, rest_ref, stat_ref):
    queries = out_ref.shape[0]
    mixed = jnp.concatenate([v[HEAD_DIM:] / v[0:1] for v in parts], axis=0).T
    logs = [jnp.broadcast_to(v, (HEAD_DIM, queries)) for v in logs]
    stat = jnp.concatenate(logs[::-1], axis=0).T
    if shift is not None:
        stat = stat + shift
    rounded = mixed.astype(BF)
    out_ref[...] = rounded
    rest_ref[...] = (mixed - rounded.astype(F32)).astype(BF)
    stat_ref[...] = stat


def fwd_fast(q_ref, kl_ref, kr_ref, out_ref, rest_ref, stat_ref, bias, valid, kc, depth):
    rows, queries = kl_ref.shape[0], q_ref.shape[0]
    lane_q, operands = fwd_setup(q_ref, kl_ref, kr_ref, valid)
    tops, heads = [], []
    for h in range(2):
        q, keys, turned, ones = operands(h)
        size = 0.0
        for v in turned:
            k = v[:HEAD_DIM].astype(F32)
            size = jnp.maximum(size, jnp.max(jnp.sum(k * k, axis=0, keepdims=True), axis=1, keepdims=True))
        bound = jnp.sqrt(jnp.sum(q * q, axis=1, keepdims=True) * size)
        bound = bound.astype(BF).astype(F32)
        q = jnp.where(lane_q == HEAD_DIM, 1.0, jnp.where(lane_q == HEAD_DIM + 1, -bound, q)).astype(BF)
        heads.append((q, keys, ones)); tops.append(bound)
    def score(item):
        h, side, at = item
        s = dot_nt(heads[h][1][side][at : at + kc], heads[h][0])
        if bias is not None:
            s = s + bias[side * rows + at : side * rows + at + kc]
        return s
    items = [(h, side, at) for h in range(2) for side in range(2) for at in range(0, rows, kc)]
    parts = [0.0, 0.0]
    ahead = [score(i) for i in items[:depth]]
    for n, (h, side, at) in enumerate(items):
        if n + depth < len(items):
            ahead.append(score(items[n + depth]))
        p = jnp.exp(ahead.pop(0)).astype(BF)
        parts[h] = parts[h] + dot_nn(heads[h][2][side][:, at : at + kc], p)
    fwd_finish(parts, [jnp.log(v[0:1]) for v in parts], jnp.where(lane_q < HEAD_DIM, tops[1], tops[0]), out_ref, rest_ref, stat_ref)
    return jnp.minimum(parts[0][0:1], parts[1][0:1])


def fwd_safe(q_ref, kl_ref, kr_ref, out_ref, rest_ref, stat_ref, bias, valid):
    rows = kl_ref.shape[0]
    lane_q, operands = fwd_setup(q_ref, kl_ref, kr_ref, valid)
    parts, logs = [], []
    for h in range(2):
        q, keys, _, ones = operands(h)
        q = jnp.where(lane_q == HEAD_DIM, 1.0, q).astype(BF)
        scores = []
        for side in range(2):
            s = dot_nt(keys[side], q)
            if bias is not None:
                s = s + bias[side * rows : (side + 1) * rows]
            scores.append(s)
        top = jnp.maximum(jnp.max(scores[0], axis=0, keepdims=True), jnp.max(scores[1], axis=0, keepdims=True))
        parts.append(sum(dot_nn(ones[i], jnp.exp(scores[i] - top).astype(BF)) for i in range(2)))
        logs.append(top + jnp.log(parts[h][0:1]))
    fwd_finish(parts, logs, None, out_ref, rest_ref, stat_ref)


def views(refs, i, pairs):
    narrow, near, far = refs
    wide = 2 * HEAD_DIM
    j = (i + pairs // 2) % pairs if isinstance(i, int) else lax.rem(i + pairs // 2, pairs)
    at = (lambda n, w: pl.ds(n * w, w)) if isinstance(i, int) else (lambda n, w: pl.ds(pl.multiple_of(n * w, w), w))
    return [r.at[:, at(i, wide)] for r in narrow], [r.at[:, at(i, 2 * wide)] for r in near], [r.at[:, at(j, 2 * wide)] for r in far]


def fwd_kernel(*refs, valid, masked, kc, depth):
    scal_ref = refs[0] if masked else None
    q_ref, kl_ref, kr_ref, out_ref, rest_ref, stat_ref = refs[1:] if masked else refs
    pairs = q_ref.shape[1] // (2 * HEAD_DIM)
    bias = causal_bias(scal_ref, kl_ref.shape[0], q_ref.shape[0], valid) if masked else None
    least = None
    for i in range(pairs):
        (q, out, rest, stat), (kl,), (kr,) = views(((q_ref, out_ref, rest_ref, stat_ref), (kl_ref,), (kr_ref,)), i, pairs)
        low = fwd_fast(q, kl, kr, out, rest, stat, bias, valid, kc, depth)
        least = low if least is None else jnp.minimum(least, low)
        for ref in (rest_ref, stat_ref):
            push(ref, (slice(None), pl.ds(i * 2 * HEAD_DIM, 2 * HEAD_DIM)))
    for ref in (rest_ref, stat_ref):
        if isinstance(ref, Outgoing):
            ref.finish()

    @pl.when(jnp.min(least) < TINY)
    def _():
        @pl.loop(0, pairs)
        def _(i):
            (q, out, rest, stat), (kl,), (kr,) = views(((q_ref, out_ref, rest_ref, stat_ref), (kl_ref,), (kr_ref,)), i, pairs)
            again = causal_bias(scal_ref, kl_ref.shape[0], q_ref.shape[0], valid) if masked else None
            fwd_safe(q, kl, kr, out, rest, stat, again, valid)

        for ref in (rest_ref, stat_ref):
            if isinstance(ref, Outgoing):
                ref.again()


def split3(value):
    first = value.astype(BF); rest = value - first.astype(F32)
    second = rest.astype(BF); third = (rest - second.astype(F32)).astype(BF)
    return first.astype(F32), second.astype(F32), third.astype(F32)


def bwd_views(refs, i, pairs):
    q_ref, kl_ref, kr_ref, out_ref, rest_ref, stat_ref, up_ref, dq_ref, dkl_ref, dkr_ref = refs
    narrow = (q_ref, out_ref, rest_ref, stat_ref, up_ref, dq_ref)
    (q, out, rest, stat, up, dq), (kl, dkl), (kr, dkr) = views(
        (narrow, (kl_ref, dkl_ref), (kr_ref, dkr_ref)), i, pairs
    )
    return q, kl, kr, out, rest, stat, up, dq, dkl, dkr


def bwd_kernel(*refs, valid, masked):
    scal_ref = refs[0] if masked else None
    refs = refs[1:] if masked else refs
    q_ref, kl_ref = refs[:2]
    pairs = q_ref.shape[1] // (2 * HEAD_DIM)
    bias = causal_bias(scal_ref, kl_ref.shape[0], q_ref.shape[0], valid) if masked else None
    for i in range(pairs):
        q, kl, kr, out, rest, stat, up, dq, dkl, dkr = bwd_views(refs, i, pairs)
        fn = bwd_pair if masked else bwd_pair_s
        fn(q, out, rest, stat, up, dq, [(kl, dkl), (kr, dkr)], bias, valid)


def bwd_side_kernel(*refs, valid, far, first, count, joined):
    q_ref, kv_ref, out_ref, rest_ref, stat_ref, up_ref, *more, dq_ref, dkv_ref = refs
    pairs = q_ref.shape[1] // (2 * HEAD_DIM)
    wide = 2 * HEAD_DIM
    base_refs = () if far else more
    if joined:
        earlier, at = more[0], dkv_ref.shape[1] - more[0].shape[1]
        dkv_ref[:, at:] = earlier[...]

    def one(i):
        (q, out, rest, stat, up), near, other = views(
            ((q_ref, out_ref, rest_ref, stat_ref, up_ref), () if far else (kv_ref,), (kv_ref,) if far else ()),
            first + i, pairs,
        )
        dq = dq_ref.at[:, i * wide : (i + 1) * wide]
        dkv = dkv_ref.at[:, i * 2 * wide : (i + 1) * 2 * wide]
        base = None
        if base_refs:
            each = base_refs[0].shape[1] // wide
            base = base_refs[i // each].at[:, i % each * wide : (i % each + 1) * wide]
        bwd_pair(q, out, rest, stat, up, dq, [(*near, *other, dkv)], None, valid, base)

    for i in range(count):
        one(i)


def bwd_pair_s(q_ref, out_ref, rest_ref, stat_ref, up_ref, dq_ref, key_sides, bias, valid, base_ref=None):
    rows, queries, depth = key_sides[0][0].shape[0], q_ref.shape[0], 1
    kc = rows
    wide = 2 * HEAD_DIM
    lane_q, lane_k = lanes(queries), lanes(rows)
    low_q = lane_q < HEAD_DIM
    q_all = q_ref[...].astype(F32) * HEAD_DIM**-0.5
    up_all = up_ref[...].astype(F32)
    stat = stat_ref[...]
    prods = up_all * (out_ref[...].astype(F32) + rest_ref[...].astype(F32))
    q_turned = (q_all.astype(BF)).T
    up_turned = up_ref[...].T
    heads, both = [], []
    for h in range(2):
        q = q_all if h == 0 else pltpu.roll(q_all, HEAD_DIM, 1)
        lse = stat if h == 0 else pltpu.roll(stat, HEAD_DIM, 1)
        up = up_all if h == 1 else pltpu.roll(up_all, HEAD_DIM, 1)
        a0, a1, a2 = split3(-lse)
        pad = jnp.where(lane_q == HEAD_DIM, 1.0, jnp.where(lane_q == HEAD_DIM + 1, a0, jnp.where(lane_q == HEAD_DIM + 2, a1, jnp.where(lane_q == HEAD_DIM + 3, a2, 0.0))))
        q_aug = jnp.where(low_q, q, pad).astype(BF)
        centre = jnp.sum(jnp.where(low_q if h == 0 else ~low_q, prods, 0.0), axis=1, keepdims=True)
        d0, d1, d2 = split3(-centre)
        pad = jnp.where(lane_q == 0, d0, jnp.where(lane_q == 1, d1, jnp.where(lane_q == 2, d2, 0.0)))
        up_aug = jnp.where(low_q, pad, up).astype(BF)
        heads.append((q_aug, up_aug, q_turned[h * HEAD_DIM : (h + 1) * HEAD_DIM], up_turned[h * HEAD_DIM : (h + 1) * HEAD_DIM]))
        sides = []
        for ref, out in key_sides:
            kv = ref[:, h * wide : (h + 1) * wide]
            keys = key_aug(kv, valid, 3)
            values = jnp.where(lane_k < HEAD_DIM, jnp.where(lane_k < 3, 1.0, 0.0).astype(BF), kv)
            sides.append((keys, values, kv, out))
        both.append(sides)
    items = [(h, side, at) for h in range(2) for side in range(len(key_sides)) for at in range(0, rows, kc)]
    def score(item):
        h, side, at = item
        keys, values, _, _ = both[h][side]
        return dot_nt(heads[h][0], keys[at : at + kc]), dot_nt(heads[h][1], values[at : at + kc])
    ahead = [score(i) for i in items[:depth]]
    totals = [0.0, 0.0]
    for n, (h, side, at) in enumerate(items):
        if n + depth < len(items):
            ahead.append(score(items[n + depth]))
        s, dp = ahead.pop(0)
        p = jnp.exp(s)
        ds = (p * dp).astype(BF)
        p = p.astype(BF)
        _, _, kv, out = both[h][side]
        pair = jnp.concatenate([dot_nn(heads[h][2], ds), dot_nn(heads[h][3], p)], axis=0)
        out[at : at + kc, h * wide : (h + 1) * wide] = pair.T.astype(BF)
        totals[h] = totals[h] + dot_nn(ds, kv[at : at + kc])
    dq = jnp.where(low_q, totals[0], pltpu.roll(totals[1], HEAD_DIM, 1)) * HEAD_DIM**-0.5
    dq_ref[...] = dq.astype(BF)


def bwd_pair(q_ref, out_ref, rest_ref, stat_ref, up_ref, dq_ref, key_sides, bias, valid, base_ref=None):
    masked, depth = bias is not None, 1
    rows, queries = key_sides[0][0].shape[0], q_ref.shape[0]
    kc = rows
    wide = 2 * HEAD_DIM
    lane_q, lane_k = lanes(queries), lanes(rows)
    low_q = lane_q < HEAD_DIM
    q_all = q_ref[...].astype(F32) * HEAD_DIM**-0.5
    up_all = up_ref[...].astype(F32)
    stat = stat_ref[...]
    prods = up_all * (out_ref[...].astype(F32) + rest_ref[...].astype(F32))
    heads, both = [], []
    for h in range(2):
        q = q_all if h == 0 else pltpu.roll(q_all, HEAD_DIM, 1)
        lse = stat if h == 0 else pltpu.roll(stat, HEAD_DIM, 1)
        up = up_all if h == 1 else pltpu.roll(up_all, HEAD_DIM, 1)
        a0, a1, a2 = split3(-lse)
        pad = jnp.where(lane_q == HEAD_DIM, 1.0, jnp.where(lane_q == HEAD_DIM + 1, a0, jnp.where(lane_q == HEAD_DIM + 2, a1, jnp.where(lane_q == HEAD_DIM + 3, a2, 0.0))))
        q_aug = jnp.where(low_q, q, pad).astype(BF)
        q_rhs = jnp.where(low_q, q, 0.0).astype(BF)
        centre = jnp.sum(jnp.where(low_q if h == 0 else ~low_q, prods, 0.0), axis=1, keepdims=True)
        d0, d1, d2 = split3(-centre)
        pad = jnp.where(lane_q == 0, d0, jnp.where(lane_q == 1, d1, jnp.where(lane_q == 2, d2, 0.0)))
        up_aug = jnp.where(low_q, pad, up).astype(BF)
        up_rhs = jnp.where(low_q, 0.0, up).astype(BF)
        heads.append((q_aug, q_rhs, up_aug, up_rhs))
        sides = []
        for ref, out in key_sides:
            kv = ref[:, h * wide : (h + 1) * wide]
            keys = key_aug(kv, valid, 3)
            values = jnp.where(lane_k < HEAD_DIM, jnp.where(lane_k < 3, 1.0, 0.0).astype(BF), kv)
            sides.append((keys, values, kv.T, out))
        both.append(sides)
    items = [(h, side, at) for h in range(2) for side in range(len(key_sides)) for at in range(0, rows, kc)]
    def score(item):
        h, side, at = item
        keys, values, _, _ = both[h][side]
        s = dot_nt(keys[at : at + kc], heads[h][0])
        if masked:
            first = at + side * rows
            s = s + bias[first : first + kc]
        return s, dot_nt(values[at : at + kc], heads[h][2])
    ahead = [score(i) for i in items[:depth]]
    totals = [0.0, 0.0]
    for n, (h, side, at) in enumerate(items):
        if n + depth < len(items):
            ahead.append(score(items[n + depth]))
        s, dp = ahead.pop(0)
        p = jnp.exp(s)
        ds = (p * dp).astype(BF)
        p = p.astype(BF)
        _, _, turned, out = both[h][side]
        out[at : at + kc, h * wide : (h + 1) * wide] = (dot_nn(ds, heads[h][1]) + dot_nn(p, heads[h][3])).astype(BF)
        totals[h] = totals[h] + dot_nn(turned[:, at : at + kc], ds)
    turned_dq = [v[:HEAD_DIM] for v in totals]
    dq = jnp.concatenate(turned_dq, axis=0).T * HEAD_DIM**-0.5
    if base_ref is not None:
        dq = dq + base_ref[...]
    dq_ref[...] = dq.astype(dq_ref.dtype)


def shape_of(rows, width, kind=BF):
    return jax.ShapeDtypeStruct((rows, width), kind)


def params(megabytes, *semantics):
    return pltpu.CompilerParams(vmem_limit_bytes=megabytes * 2**20)


def attention_cost(q, kl, products):
    flops = 2 * products * q.shape[0] * 2 * kl.shape[0] * q.shape[1] * 3
    return pl.CostEstimate(
        flops=flops, bytes_accessed=8 * q.size + 6 * kl.size, transcendentals=0
    )


class Far:
    def __init__(self, value, pieces=1, by_core=False):
        self.value, self.pieces, self.by_core = value, pieces, by_core
        self.shape, self.dtype = value.shape[1:] if by_core else value.shape, value.dtype
        self.size = math.prod(self.shape)


class Clip:
    def __init__(self, value):
        self.value, self.shape, self.dtype, self.size = value, value.shape, value.dtype, value.size


class Incoming:
    def __init__(self, source, held, arrived, pieces):
        self.held, self.shape, self.dtype = held, held.shape, held.dtype
        rows = held.shape[0] // pieces
        self.spans = [pl.ds(n * rows, rows) for n in range(pieces)]
        self.copies = [
            pltpu.make_async_copy(source.at[span], held.at[span], arrived.at[n])
            for n, span in enumerate(self.spans)
        ]

    def start(self, n):
        if n < len(self.copies):
            self.copies[n].start()

    def wait(self, n):
        if self.copies[n] is not None:
            self.copies[n].wait()
            self.copies[n] = None

    def piece(self, n):
        return Piece(self, n)

    def settle(self):
        for n in range(len(self.copies)):
            self.wait(n)
        return self.held

    @property
    def at(self):
        return self.settle().at

    def __getitem__(self, index):
        return self.settle()[index]


class Piece:
    def __init__(self, whole, n):
        self.whole, self.n = whole, n
        rows = whole.held.shape[0] // len(whole.spans)
        self.shape, self.dtype = (rows, *whole.held.shape[1:]), whole.held.dtype

    def __getitem__(self, index):
        self.whole.wait(self.n)
        return self.whole.held.at[self.whole.spans[self.n]][index]


class Padded:
    def __init__(self, ref, section, rows):
        self.ref, self.section, self.rows = ref, section, rows
        self.shape, self.dtype = (rows, ref.shape[2]), ref.dtype

    def __getitem__(self, index):
        value = self.ref[self.section]
        behind = jnp.zeros((self.rows - value.shape[0], value.shape[1]), value.dtype)
        return jnp.concatenate([value, behind], axis=0)[index]


class Outgoing:
    def __init__(self, target, held, left):
        self.target, self.held, self.left, self.copies = target, held, left, []
        self.at, self.shape, self.dtype = held.at, held.shape, held.dtype

    def __setitem__(self, index, value):
        self.held[index] = value

    def push(self, index=(slice(None), slice(None))):
        copy = pltpu.make_async_copy(
            self.held.at[index], self.target.at[index], self.left.at[len(self.copies)]
        )
        copy.start()
        self.copies.append(copy)

    def finish(self):
        for copy in self.copies or ():
            copy.wait()
        self.copies = None

    def again(self):
        copy = pltpu.make_async_copy(self.held, self.target, self.left.at[0])
        copy.start()
        copy.wait()


def push(ref, *index):
    if isinstance(ref, Outgoing):
        ref.push(*index)


def in_vmem():
    return pl.BlockSpec(memory_space=pltpu.VMEM)


def in_hbm():
    return pl.BlockSpec(memory_space=pltpu.HBM)


def flat_call(kernel, operands, out_shape, scal=None, scratch=(), flops=0, megabytes=40):
    touched = sum(v.size * v.dtype.itemsize for v in operands)
    touched += sum(math.prod(v.shape) * v.dtype.itemsize for v in out_shape)
    far_in = [v for v in operands if isinstance(v, Far)]
    far_out = [v for v in out_shape if isinstance(v, Far)]
    extra = []
    for v in (*far_in, *far_out):
        extra += [pltpu.VMEM(v.shape, v.dtype), pltpu.SemaphoreType.DMA((v.pieces,))]
        megabytes += -(-v.size * v.dtype.itemsize // 2**20)

    def run(*refs):
        refs = list(refs)
        take = lambda count: [refs.pop(0) for _ in range(count)]
        head = take(0 if scal is None else 1)
        ins, outs, own = take(len(operands)), take(len(out_shape)), take(len(scratch))
        moving = []
        for n, v in enumerate(operands):
            if isinstance(v, Far):
                source = ins[n].at[head[0][SCAL_CORE]] if v.by_core else ins[n]
                ins[n] = Incoming(source, *take(2), v.pieces)
                moving.append(ins[n])
            elif isinstance(v, Clip):
                ins[n] = Padded(ins[n], head[0][SCAL_SECTION], round_up(v.shape[1]))
        for n, v in enumerate(out_shape):
            if isinstance(v, Far):
                outs[n] = Outgoing(outs[n], *take(2))
        for n in range(max((len(v.copies) for v in moving), default=0)):
            for v in moving:
                v.start(n)
        kernel(*head, *ins, *outs, *own)
        for v in moving:
            v.settle()
        for v in outs:
            if isinstance(v, Outgoing):
                if v.copies == []:
                    v.push()
                v.finish()

    bare = lambda v: v.value if isinstance(v, (Far, Clip)) else v
    pin = lambda v: pltpu.with_memory_space_constraint(v.value, pltpu.HBM) if isinstance(v, Far) else bare(v)
    pin_shape = lambda v: pltpu.HBM(v.shape, v.dtype) if isinstance(v, Far) else v
    place = lambda v: in_hbm() if isinstance(v, Far) else in_vmem()
    return pl.pallas_call(
        run,
        in_specs=([] if scal is None else [pl.BlockSpec(memory_space=pltpu.SMEM)])
        + [place(v) for v in operands],
        out_specs=[place(v) for v in out_shape],
        out_shape=[pin_shape(v) for v in out_shape],
        scratch_shapes=list(scratch) + extra,
        compiler_params=params(megabytes),
        cost_estimate=pl.CostEstimate(flops=flops, bytes_accessed=touched, transcendentals=0),
    )(*([] if scal is None else [scal]), *[pin(v) for v in operands])


def attention_flops(q, kl, products, share=1):
    return 2 * products * q.shape[0] * 2 * kl.shape[0] * q.shape[1] * 4 // share


def attention_fwd(q, kl, kr, valid, scal=None):
    return flat_call(
        functools.partial(fwd_kernel, valid=valid, masked=scal is not None, kc=kl.shape[0], depth=1),
        [q, kl, kr],
        [shape_of(*q.shape), Far(shape_of(*q.shape), 8), Far(shape_of(*q.shape, F32), 8)],
        scal=scal, flops=attention_flops(q, kl, 2), megabytes=24 if q.shape[0] > CHUNK else 12,
    )


def attention_bwd(q, kl, kr, out, rest, stat, up, valid, scal=None):
    return flat_call(
        functools.partial(bwd_kernel, valid=valid, masked=scal is not None),
        [q, kl, kr, out, rest, stat, up],
        [shape_of(*q.shape), shape_of(*kl.shape), shape_of(*kl.shape)],
        scal=scal, flops=attention_flops(q, kl, 5), megabytes=12,
    )


def attention_bwd_side(q, kv, out, rest, stat, up, valid, base=(), pairs=None, earlier=()):
    far = not base
    total = q.shape[1] // (2 * HEAD_DIM)
    first, count = pairs or (0, total)
    width = kv.shape[1] // total * count + sum(v.shape[1] for v in earlier)
    return flat_call(
        functools.partial(
            bwd_side_kernel, valid=valid, far=far, first=first, count=count, joined=bool(earlier)
        ),
        [q, kv, out, rest, stat, up, *base, *earlier],
        [shape_of(q.shape[0], q.shape[1] // total * count, F32 if far else BF), shape_of(kv.shape[0], width)],
        flops=attention_flops(q, kv, 5, 2), megabytes=21 if count > 2 else 14,
    )


def rows_call(
    kernel, rows, blocked, whole, outs, sums=(), scratch=(), reverse=False, flops=0, megabytes=10, scal=None,
    told=False,
):
    chunk_rows = next(n for n in (384, CHUNK) if rows % n == 0)
    steps = rows // chunk_rows
    order = list(range(steps))
    if reverse:
        order = order[::-1]

    def chunk_of(ref, chunk):
        if isinstance(ref, Incoming):
            return ref.piece(chunk)
        return ref if isinstance(ref, Padded) else ref.at[pl.ds(chunk * chunk_rows, chunk_rows)]

    def run(*refs):
        refs = list(refs)
        take = lambda count: [refs.pop(0) for _ in range(count)]
        head = take(0 if scal is None else 1)
        kept, by_chunk = take(len(whole)), take(len(blocked))
        out, total = take(len(outs)), take(len(sums))
        for n, chunk in enumerate(order):
            kernel(
                n, *(head if told else ()), *[chunk_of(r, chunk) for r in by_chunk], *kept,
                *[chunk_of(r, chunk) for r in out], *total, *refs,
            )
            for r in out:
                push(r, (pl.ds(chunk * chunk_rows, chunk_rows), slice(None)))

    out_shape = []
    for width, kind, *far in outs:
        shape = shape_of(rows, width, kind)
        out_shape.append(Far(shape, steps) if far else shape)
    for shape, kind, *far in sums:
        shape = jax.ShapeDtypeStruct(shape, kind)
        out_shape.append(Far(shape) if far else shape)
    blocked = [Far(v.value, steps, v.by_core) if isinstance(v, Far) else v for v in blocked]
    return flat_call(run, [*whole, *blocked], out_shape, scal, scratch, flops, megabytes)


def tap_weights(first_ref):
    pieces = []
    for tap in range(first_ref.shape[0]):
        rows = first_ref[tap]
        pieces += [rows, jnp.zeros((LANES - rows.shape[0], rows.shape[1]), rows.dtype)]
    return jnp.concatenate(pieces, axis=0)


def mel_windows(scal_ref, mel_ref, mel_rows_ref, windows_ref, halo_ref, valid):
    rows = windows_ref.shape[0]
    channels, frames = mel_ref.shape[1:]
    front = 8
    mel_rows_ref[...] = jnp.zeros_like(mel_rows_ref)
    mel_rows_ref[front : front + frames, :channels] = mel_ref[scal_ref[SCAL_SECTION]].astype(F32).T
    lanes_all = slice(None)
    for core in range(frames // (2 * valid)):

        @pl.when(scal_ref[SCAL_CORE] == core)
        def _():
            base = front + 2 * valid * core
            for n in range(4):
                taken = mel_rows_ref[pl.ds(base + n - 1, rows, stride=2), lanes_all]
                windows_ref[:, n * LANES : (n + 1) * LANES] = taken.astype(BF)
            halo_ref[...] = jnp.zeros_like(halo_ref)
            if core > 0:
                for n in range(3):
                    part = mel_rows_ref[pl.ds(base - 2 + n, 16), lanes_all]
                    first = lax.broadcasted_iota(jnp.int32, part.shape, 0) == 0
                    halo_ref[:, n * LANES : (n + 1) * LANES] = jnp.where(first, part, 0.0).astype(BF)


def stem_fwd_kernel(
    chunk, scal_ref, pos_ref, mel_ref, first_ref, second_ref,
    even_ref, odd_ref, before_ref, ge_ref, go_ref, gs_ref, x_ref, gh_ref, windows_ref, halo_ref,
    carry_ref, mel_rows_ref, *, valid,
):
    first = tap_weights(first_ref)
    if chunk == 0:
        mel_windows(scal_ref, mel_ref, mel_rows_ref, windows_ref, halo_ref, valid)
        push(windows_ref)
        act, slope = gelu_pair(dot_nn(halo_ref[...], first))
        carry_ref[...] = act[:8]
        gh_ref[...] = slope
    span = pl.ds(chunk * even_ref.shape[0], even_ref.shape[0])
    me_ref = windows_ref.at[span, : 3 * LANES]
    mo_ref = windows_ref.at[span, LANES:]

    width = even_ref.shape[1]
    even, slope = gelu_pair(dot_nn(me_ref[...], first))
    even = even.astype(BF)
    even_ref[...] = even
    ge_ref[...] = slope.astype(BF)
    odd, slope = gelu_pair(dot_nn(mo_ref[...], first))
    go_ref[...] = slope.astype(BF)
    row = lax.broadcasted_iota(jnp.int32, odd.shape, 0)
    before = jnp.where(row == 0, carry_ref[0:1, :], pltpu.roll(odd, 1, 0)).astype(BF)
    carry_ref[0:1, :] = odd[odd.shape[0] - 1 :]
    odd = odd.astype(BF)
    odd_ref[...] = odd
    before_ref[...] = before
    pre = dot_nn(before, second_ref[:width])
    pre += dot_nn(even, second_ref[width : 2 * width])
    pre += dot_nn(odd, second_ref[2 * width :])
    act, slope = gelu_pair(pre)
    gs_ref[...] = slope.astype(BF)
    x_ref[...] = act + pos_ref[...]


def qkv_kernel(step, x_ref, gain_ref, bias_ref, own_ref, oth_ref, normed_ref, q_ref, kv_ref):
    unit, _ = norm_stats(x_ref[...].astype(F32))
    normed = (unit * gain_ref[...] + bias_ref[...]).astype(BF)
    normed_ref[...] = normed
    heads = own_ref.shape[1] // (3 * HEAD_DIM)
    for part, w_ref in enumerate((own_ref, oth_ref)):
        packed = dot_nn(normed, w_ref[...]).astype(BF)
        for h in range(heads):
            at, to = h * 3 * HEAD_DIM, part * heads + h
            q_ref[:, to * HEAD_DIM : (to + 1) * HEAD_DIM] = packed[:, at : at + HEAD_DIM]
            kv_ref[:, to * 2 * HEAD_DIM : (to + 1) * 2 * HEAD_DIM] = packed[
                :, at + HEAD_DIM : at + 3 * HEAD_DIM
            ]


def two_parts(rows, own_ref, oth_ref):
    depth = own_ref.shape[0]
    return dot_nn(rows[:, :depth], own_ref[...]) + dot_nn(rows[:, depth:], oth_ref[...])


def two_parts_t(rows, own_ref, oth_ref):
    depth = own_ref.shape[1]
    return dot_nt(rows[:, :depth], own_ref[...]) + dot_nt(rows[:, depth:], oth_ref[...])


def enc_mid_kernel(
    step, x_ref, att_ref, gb_ref, bb_ref, gc_ref, bc_ref, po_ref, pt_ref, uo_ref, ut_ref, do_ref, dt_ref,
    ko_ref, kt_ref,
    x1_ref, x2_ref, normed_ref, hidden_ref, slope_ref, memory_ref, kv_ref,
):
    x1 = x_ref[...] + two_parts(att_ref[...], po_ref, pt_ref)
    x1_ref[...] = x1
    unit, _ = norm_stats(x1)
    normed = (unit * gb_ref[...] + bb_ref[...]).astype(BF)
    normed_ref[...] = normed
    half = uo_ref.shape[1]
    x2 = x1
    for part, (up_ref, down_ref) in enumerate(((uo_ref, do_ref), (ut_ref, dt_ref))):
        act, slope = gelu_pair(dot_nn(normed, up_ref[...]))
        act = act.astype(BF)
        hidden_ref[:, part * half : (part + 1) * half] = act
        slope_ref[:, part * half : (part + 1) * half] = slope.astype(BF)
        x2 = x2 + dot_nn(act, down_ref[...])
    x2_ref[...] = x2
    unit, _ = norm_stats(x2)
    memory = (unit * gc_ref[...] + bc_ref[...]).astype(BF)
    memory_ref[...] = memory
    half = ko_ref.shape[1]
    kv_ref[:, :half] = dot_nn(memory, ko_ref[...]).astype(BF)
    kv_ref[:, half:] = dot_nn(memory, kt_ref[...]).astype(BF)


def dec_mid_kernel(
    step, x_ref, att_ref, gain_ref, bias_ref, po_ref, pt_ref, qo_ref, qt_ref, y_ref, normed_ref, q_ref
):
    y = x_ref[...].astype(F32) + two_parts(att_ref[...], po_ref, pt_ref)
    y_ref[...] = y
    unit, _ = norm_stats(y)
    normed = (unit * gain_ref[...] + bias_ref[...]).astype(BF)
    normed_ref[...] = normed
    half = qo_ref.shape[1]
    q_ref[:, :half] = dot_nn(normed, qo_ref[...]).astype(BF)
    q_ref[:, half:] = dot_nn(normed, qt_ref[...]).astype(BF)


def mlp_back(gb, slope_ref, dpre_ref, uo_ref, ut_ref, do_ref, dt_ref):
    half = uo_ref.shape[1]
    total = 0.0
    for part, (up_ref, down_ref) in enumerate(((uo_ref, do_ref), (ut_ref, dt_ref))):
        span = slice(part * half, (part + 1) * half)
        dpre = (dot_nt(gb, down_ref[...]) * slope_ref[:, span].astype(F32)).astype(BF)
        dpre_ref[:, span] = dpre
        total = total + dot_nt(dpre, up_ref[...])
    return total


def section_halves(scal_ref, value, mine_ref, sent_ref):
    rows, half = mine_ref.shape
    left, right = value[:rows, :half], value[:rows, half:]
    lower = scal_ref[SCAL_SECTION] == 0
    mine_ref[...] = jnp.where(lower, left, right).astype(mine_ref.dtype)
    sent_ref[...] = jnp.where(lower, right, left).astype(sent_ref.dtype)


def owners_kernel(scal_ref, *refs):
    count = len(refs) // 3
    section = scal_ref[SCAL_SECTION]
    for mine_ref, got_ref, out_ref in zip(refs[:count], refs[count : 2 * count], refs[2 * count :]):
        out_ref[section] = mine_ref[...]
        out_ref[1 - section] = got_ref[...].astype(out_ref.dtype)


def dec_top_kernel(
    scal_ref, y1_ref, crossed_ref, cot_ref, gain_ref, bias_ref, po_ref, pt_ref, uo_ref, ut_ref,
    do_ref, dt_ref,
    decoded_ref, sent_ref, normed_ref, hidden_ref, dpre_ref, gb3_ref, gb2_ref, dcrossed_ref, u2_ref,
    sums_ref, slope_ref, *, valid,
):
    rows = y1_ref.shape[0]
    y2 = y1_ref[...] + two_parts(crossed_ref[...], po_ref, pt_ref)
    unit, inverse = norm_stats(y2)
    normed = (unit * gain_ref[...] + bias_ref[...]).astype(BF)
    normed_ref[...] = normed
    push(normed_ref)
    half = uo_ref.shape[1]
    y3 = y2
    for part, (up_ref, down_ref) in enumerate(((uo_ref, do_ref), (ut_ref, dt_ref))):
        act, slope = gelu_pair(dot_nn(normed, up_ref[...]))
        act = act.astype(BF)
        hidden_ref[:, part * half : (part + 1) * half] = act
        slope_ref[:, part * half : (part + 1) * half] = slope.astype(BF)
        y3 = y3 + dot_nn(act, down_ref[...])
    push(hidden_ref)
    row = lax.broadcasted_iota(jnp.int32, y2.shape, 0)
    length = scal_ref[SCAL_LENGTHS + scal_ref[SCAL_SECTION]]
    live = ((row < valid) & (row + scal_ref[SCAL_CORE] * valid < length)).astype(F32)
    section_halves(scal_ref, y3 * live, decoded_ref, sent_ref)
    u3 = cot_ref[...].astype(F32) * live
    gb3 = u3.astype(BF)
    gb3_ref[...] = gb3
    push(gb3_ref)
    dnormed = mlp_back(gb3, slope_ref, dpre_ref, uo_ref, ut_ref, do_ref, dt_ref)
    push(dpre_ref)
    dy, dgain, dbias = norm_back(unit, inverse, gain_ref[...], dnormed)
    u2 = u3 + dy
    u2_ref[...] = u2
    gb2 = u2.astype(BF)
    gb2_ref[...] = gb2
    push(gb2_ref)
    half = po_ref.shape[0]
    dcrossed_ref[:, :half] = dot_nt(gb2, po_ref[...]).astype(BF)
    dcrossed_ref[:, half:] = dot_nt(gb2, pt_ref[...]).astype(BF)
    sums_ref[...] = jnp.zeros_like(sums_ref)
    sums_ref[0:1, :] = dgain
    sums_ref[1:2, :] = dbias


def dec_back_kernel(
    step, dq_ref, y1_ref, u2_ref, gain_ref, qo_ref, qt_ref, po_ref, pt_ref,
    u1_ref, gb1_ref, datt_ref, sums_ref,
):
    dnormed = two_parts_t(dq_ref[...], qo_ref, qt_ref)
    unit, inverse = norm_stats(y1_ref[...])
    dy, dgain, dbias = norm_back(unit, inverse, gain_ref[...], dnormed)
    u1 = u2_ref[...] + dy
    u1_ref[...] = u1
    gb1 = u1.astype(BF)
    gb1_ref[...] = gb1
    half = po_ref.shape[0]
    datt_ref[:, :half] = dot_nt(gb1, po_ref[...]).astype(BF)
    datt_ref[:, half:] = dot_nt(gb1, pt_ref[...]).astype(BF)
    sums_ref[...] = jnp.zeros_like(sums_ref)
    sums_ref[0:1, :] = dgain
    sums_ref[1:2, :] = dbias


def packed_back(dq_ref, dkl_ref, dkr_ref, own_ref, oth_ref, out_ref):
    dkv = (dkl_ref[...].astype(F32) + dkr_ref[...].astype(F32)).astype(BF)
    dq = dq_ref[...]
    heads = own_ref.shape[1] // (3 * HEAD_DIM)
    total = 0.0
    for part, w_ref in enumerate((own_ref, oth_ref)):
        pieces = []
        for h in range(part * heads, (part + 1) * heads):
            pieces.append(dq[:, h * HEAD_DIM : (h + 1) * HEAD_DIM])
            pieces.append(dkv[:, h * 2 * HEAD_DIM : (h + 1) * 2 * HEAD_DIM])
        packed = jnp.concatenate(pieces, axis=1)
        out_ref[:, part * w_ref.shape[1] : (part + 1) * w_ref.shape[1]] = packed
        total = total + dot_nt(packed, w_ref[...])
    return total


def dec_last_kernel(
    step, scal_ref, dq_ref, dkl_ref, dkr_ref, x_ref, u1_ref, gain_ref, own_ref, oth_ref,
    packed_ref, sums_ref, mine_ref, sent_ref,
):
    dnormed = packed_back(dq_ref, dkl_ref, dkr_ref, own_ref, oth_ref, packed_ref)
    unit, inverse = norm_stats(x_ref[...].astype(F32))
    dx, dgain, dbias = norm_back(unit, inverse, gain_ref[...], dnormed)
    section_halves(scal_ref, u1_ref[...] + dx, mine_ref, sent_ref)
    sums_ref[...] = jnp.zeros_like(sums_ref)
    sums_ref[0:1, :] = dgain
    sums_ref[1:2, :] = dbias


def enc_back_kernel(
    step, gl_ref, gr_ref, x2_ref, x1_ref, slope_ref, gc_ref, gb_ref, ko_ref, kt_ref, uo_ref, ut_ref,
    do_ref, dt_ref, po_ref, pt_ref,
    gkv_ref, gb2_ref, dpre_ref, gb1_ref, datt_ref, u1_ref, sums_ref,
):
    if step == 0:
        sums_ref[...] = jnp.zeros_like(sums_ref)

    gkv = (gl_ref[...].astype(F32) + gr_ref[...].astype(F32)).astype(BF)
    gkv_ref[...] = gkv
    dmemory = two_parts_t(gkv, ko_ref, kt_ref)
    unit, inverse = norm_stats(x2_ref[...])
    u2, dgain, dbias = norm_back(unit, inverse, gc_ref[...], dmemory)
    sums_ref[0:1, :] += dgain
    sums_ref[1:2, :] += dbias
    gb2 = u2.astype(BF)
    gb2_ref[...] = gb2
    dnormed = mlp_back(gb2, slope_ref, dpre_ref, uo_ref, ut_ref, do_ref, dt_ref)
    unit, inverse = norm_stats(x1_ref[...])
    dx, dgain, dbias = norm_back(unit, inverse, gb_ref[...], dnormed)
    sums_ref[2:3, :] += dgain
    sums_ref[3:4, :] += dbias
    u1 = u2 + dx
    u1_ref[...] = u1
    gb1 = u1.astype(BF)
    gb1_ref[...] = gb1
    half = po_ref.shape[0]
    datt_ref[:, :half] = dot_nt(gb1, po_ref[...]).astype(BF)
    datt_ref[:, half:] = dot_nt(gb1, pt_ref[...]).astype(BF)


def stem_back_kernel(
    step, dq_ref, dkl_ref, dkr_ref, x0_ref, u1_ref, ge_ref, go_ref, gs_ref, gain_ref, own_ref, oth_ref,
    second_ref, gh_ref,
    packed_ref, g2_ref, ede_ref, edo_ref, sums_ref, edh_ref, carry_ref,
):
    if step == 0:
        sums_ref[...] = jnp.zeros_like(sums_ref)
        carry_ref[...] = jnp.zeros_like(carry_ref)

    dnormed = packed_back(dq_ref, dkl_ref, dkr_ref, own_ref, oth_ref, packed_ref)
    unit, inverse = norm_stats(x0_ref[...])
    dx, dgain, dbias = norm_back(unit, inverse, gain_ref[...], dnormed)
    sums_ref[0:1, :] += dgain
    sums_ref[1:2, :] += dbias
    g2 = ((u1_ref[...] + dx) * gs_ref[...].astype(F32)).astype(BF)
    g2_ref[...] = g2
    width = g2.shape[1]
    before = dot_nt(g2, second_ref[:width])
    even = dot_nt(g2, second_ref[width : 2 * width])
    odd = dot_nt(g2, second_ref[2 * width :])
    ede_ref[...] = (even * ge_ref[...].astype(F32)).astype(BF)
    row = lax.broadcasted_iota(jnp.int32, before.shape, 0)
    later = jnp.where(
        row == before.shape[0] - 1, carry_ref[0:1, :], pltpu.roll(before, before.shape[0] - 1, 0)
    )
    carry_ref[0:1, :] = before[0:1]
    edo_ref[...] = ((odd + later) * go_ref[...].astype(F32)).astype(BF)
    front = lax.broadcasted_iota(jnp.int32, edh_ref.shape, 0)
    edh_ref[...] = jnp.where(front == 0, before[0:1] * gh_ref[...], 0.0).astype(BF)


SCAL_CORE, SCAL_SECTION, SCAL_X, SCAL_Z, SCAL_Z_LOW, SCAL_Z_HIGH, SCAL_LENGTHS = range(7)
TILE = 512


def gradient_tiles(left, right_ref, own_ref, oth_ref, at):
    turned, half = left.T, right_ref.shape[1] // 2
    for part, out_ref in enumerate((own_ref, oth_ref)):
        for first in range(0, half, TILE):
            width = min(TILE, half - first)
            piece = dot_nn(turned, right_ref[:, part * half + first : part * half + first + width])
            out_ref[:, at + first : at + first + width] = piece.astype(BF)
    return at + half


def gradients_kernel(*refs):
    *pairs, own_ref, oth_ref = refs
    at = 0
    for left_ref, right_ref in zip(pairs[::2], pairs[1::2]):
        at = gradient_tiles(left_ref[...], right_ref, own_ref, oth_ref, at)


def gradients(pairs, held=()):
    columns = sum(right.shape[1] // 2 for _, right in pairs)
    width = pairs[0][0].shape[1]
    return flat_call(
        gradients_kernel,
        [Far(v) if any(v is h for h in held) else v for pair in pairs for v in pair],
        [shape_of(width, columns)] * 2,
        flops=sum(2 * left.size * right.shape[1] for left, right in pairs), megabytes=9,
    )


def late_kernel(
    scal_ref, normed_ref, packed_ref, g2_ref, before_ref, even_ref, odd_ref, ede_ref, edo_ref, edh_ref,
    windows_ref, mh_ref, va_ref, vb_ref, vc_ref, ve_ref, vf_ref, own_ref, oth_ref, own_stem_ref, oth_stem_ref, stem_ref, *,
    channels,
):
    gradient_tiles(normed_ref[...], packed_ref, own_ref, oth_ref, 0)
    turned, width = g2_ref[...].T, g2_ref.shape[1]
    for n, ref in enumerate((before_ref, even_ref, odd_ref)):
        stem_ref[:, n * width : (n + 1) * width] = dot_nn(turned, ref[...]).astype(BF)
    windows = windows_ref[...].T
    first = dot_nn(windows[: 3 * LANES], ede_ref[...]) + dot_nn(windows[LANES:], edo_ref[...])
    first = first + dot_nn(mh_ref[...].T, edh_ref[...])
    vectors = [
        vf_ref[0:1], ve_ref[2:3], ve_ref[0:1], vf_ref[1:2], ve_ref[3:4], ve_ref[1:2],
        va_ref[0:1], vb_ref[0:1], vc_ref[0:1], va_ref[1:2], vb_ref[1:2], vc_ref[1:2],
        jnp.zeros((4, width), F32),
    ]
    taps = [first[n * LANES : n * LANES + channels] for n in range(first.shape[0] // LANES)]
    first = jnp.concatenate([*taps, jnp.concatenate(vectors, axis=0)], axis=0)
    stem_ref[:, 3 * width :] = first.T.astype(BF)
    core, half = scal_ref[SCAL_CORE], stem_ref.shape[1] // 2
    block = 16
    groups = width // (4 * block)
    for part, out_ref in enumerate((own_stem_ref, oth_stem_ref)):
        bit = core if part == 0 else 1 - core
        for group in range(groups):
            for section in range(2):
                source = pl.multiple_of(group * 4 * block + bit * 2 * block + section * block, block)
                rows = stem_ref[pl.ds(source, block), :]
                to = (section * groups + group) * 2 * block
                out_ref[to : to + block, :] = rows[:, :half]
                out_ref[to + block : to + 2 * block, :] = rows[:, half:]


def halves(scal_ref, bit, groups, size, total, keep_ref, send_ref, columns=slice(None)):
    for group in range(groups):
        for place, out_ref in ((scal_ref[bit], keep_ref), (1 - scal_ref[bit], send_ref)):
            source = pl.ds(pl.multiple_of((group * 2 + place) * size, size), size)
            out_ref[group * size : (group + 1) * size, columns] = total(source)


def first_kernel(scal_ref, *refs, cut, block):
    *parts, am_ref, as_ref, bm_ref, bg_ref = refs
    if len(parts) == 2:
        parts = [ref.at[:, span] for ref in parts for span in (slice(0, cut), slice(cut, None))]
        parts = [parts[0], parts[2], parts[1], parts[3]]
    low_own, low_got, high_own, high_got = parts
    low = lambda rows: low_own[rows, :] + low_got[rows, :]
    high = lambda rows: high_own[rows, :] + high_got[rows, :]
    rows = low_own.shape[0]
    halves(scal_ref, SCAL_X, rows // (2 * block), block, low, am_ref, as_ref)
    halves(scal_ref, SCAL_SECTION, 1, rows // 2, high, bm_ref, bg_ref)


def second_kernel(
    scal_ref, am_ref, ag_ref, bm_ref, bg_ref, akeep_ref, asend_ref, bkeep_ref, bsend_ref, *, block
):
    low = lambda rows: am_ref[rows, :] + ag_ref[rows, :]
    high = lambda rows: bm_ref[rows, :] + bg_ref[rows, :]
    rows = am_ref.shape[0]
    halves(scal_ref, SCAL_SECTION, 1, rows // 2, low, akeep_ref, asend_ref)
    halves(scal_ref, SCAL_X, rows // (2 * block), block, high, bkeep_ref, bsend_ref)


def third_kernel(scal_ref, am_ref, ag_ref, bm_ref, bg_ref, *out_refs, cut, block):
    for flip, out_ref in enumerate(out_refs):
        rows = pl.ds(pl.multiple_of((scal_ref[SCAL_Z] ^ flip) * block, block), block)
        out_ref[:, :cut] = am_ref[rows, :] + ag_ref[rows, :]
        out_ref[:, cut:] = bm_ref[rows, :] + bg_ref[rows, :]


def third_half_kernel(scal_ref, am_ref, ag_ref, bm_ref, bg_ref, keep_ref, send_ref, *, cut, block):
    low = lambda rows: am_ref[rows, :] + ag_ref[rows, :]
    high = lambda rows: bm_ref[rows, :] + bg_ref[rows, :]
    groups = am_ref.shape[0] // (2 * block)
    halves(scal_ref, SCAL_Z_LOW, groups, block, low, keep_ref, send_ref, slice(0, cut))
    halves(scal_ref, SCAL_Z_LOW, groups, block, high, keep_ref, send_ref, slice(cut, None))


def fourth_half_kernel(scal_ref, mine_ref, got_ref, keep_ref, send_ref, *, block):
    both = lambda rows: mine_ref[rows, :] + got_ref[rows, :]
    halves(scal_ref, SCAL_Z_HIGH, 1, block, both, keep_ref, send_ref)


def last_kernel(*refs, widths):
    count = len(refs) - len(widths)
    at = 0
    for out_ref, width in zip(refs[count:], widths):
        total = sum(ref[:, at : at + width].astype(F32) for ref in refs[:count])
        out_ref[...] = total
        at += width


def stem_last_kernel(scal_ref, mine_ref, got_ref, second_ref, first_ref, *vec_refs):
    mine, got = mine_ref[...], got_ref[...]
    lower = scal_ref[SCAL_SECTION] == 0
    block = mine.shape[0] // 2
    parts = []
    for half in (jnp.where(lower, mine, got), jnp.where(lower, got, mine)):
        parts.append(jnp.concatenate([half[:block], half[block:]], axis=1))
    full = jnp.concatenate(parts, axis=0)
    count, _, width = second_ref.shape
    channels = first_ref.shape[2]
    for n in range(count):
        second_ref[n] = full[:, n * width : (n + 1) * width]
        first_ref[n] = full[:, count * width + n * channels : count * width + (n + 1) * channels]
    turned = full[:, full.shape[1] - 2 * HEAD_DIM :].T
    at = turned.shape[0] - 16
    for n, ref in enumerate(vec_refs):
        ref[...] = turned[at + 3 * n : at + 3 * n + 3]


def sum_over_chips(own, oth, scal, cut, widths, direct=False):
    after = lambda value, other: value if other is None else tie(value, other)
    if not isinstance(own, tuple):
        own, oth = (own,), (oth,)
    parts = [v for mine, other in zip(own, oth) for v in (mine, swap(other, "tensor"))]
    rows, columns = own[0].shape[0], sum(v.shape[1] for v in own)
    block = rows // (2 * lax.axis_size("dp"))
    some = lambda n, w: shape_of(n, w)
    left, right = cut, columns - cut
    am, asend, bm, bsend = flat_call(
        functools.partial(first_kernel, cut=cut, block=block), parts,
        [some(rows // 2, left)] * 2 + [some(rows // 2, right)] * 2, scal, megabytes=6,
    )
    am = after(am, (yield am))
    ag, bg = flip_bit(asend, "dp", 1), swap(bsend, "section")
    am, asend, bm, bsend = flat_call(
        functools.partial(second_kernel, block=block), [am, ag, bm, bg],
        [some(rows // 4, left)] * 2 + [some(rows // 4, right)] * 2, scal, megabytes=6,
    )
    am = after(am, (yield am))
    ag, bg = swap(asend, "section"), flip_bit(bsend, "dp", 1)
    if direct:
        mine, *send = flat_call(
            functools.partial(third_kernel, cut=cut, block=block), [am, ag, bm, bg],
            [some(block, columns)] * (rows // (4 * block)), scal, megabytes=6,
        )
        mine = after(mine, (yield mine))
        got = [flip_bit(v, "dp", 2 * (n + 1)) for n, v in enumerate(send)]
    else:
        mine, send = flat_call(
            functools.partial(third_half_kernel, cut=cut, block=block), [am, ag, bm, bg],
            [some(2 * block, columns)] * 2, scal, megabytes=6,
        )
        mine = after(mine, (yield mine))
        mine, send = flat_call(
            functools.partial(fourth_half_kernel, block=block), [mine, flip_bit(send, "dp", 2)],
            [some(block, columns)] * 2, scal, megabytes=6,
        )
        mine = after(mine, (yield mine))
        got = [flip_bit(send, "dp", 4)]
    yield flat_call(
        functools.partial(last_kernel, widths=widths), [mine, *got],
        [shape_of(block, width, F32) for width in widths], megabytes=6,
    )


def tie(value, *others):
    return lax.optimization_barrier((value, *others))[0]


def swap(value, axis):
    return lax.ppermute(value, axis, [(0, 1), (1, 0)])


def flip_bit(value, axis, bit):
    count = lax.axis_size(axis)
    return lax.ppermute(value, axis, [(i, i ^ bit) for i in range(count)])


def add_low(left, right):
    return (left.astype(F32) + right.astype(F32)).astype(BF)


def halve(value, dim, place, send):
    mine = lax.dynamic_index_in_dim(value, place, dim, keepdims=False)
    other = lax.dynamic_index_in_dim(value, 1 - place, dim, keepdims=False)
    return mine, send(other)


def reduce_blocks(value, names):
    section, clip_group = lax.axis_index("section"), lax.axis_index("dp")
    dims = list(names)
    order = [name for name, _ in sorted(names.items(), key=lambda item: item[1])]
    held = value
    for step, name in enumerate(order):
        dim = [n for n in dims if n in order[step:]].index(name)
        if name == "section":
            mine, got = halve(held, dim, section, functools.partial(swap, axis="section"))
        else:
            place = (clip_group // name) % 2
            mine, got = halve(held, dim, place, functools.partial(flip_bit, axis="dp", bit=name))
        held = mine.astype(F32) + got.astype(F32)
        if step < len(order) - 1:
            held = held.astype(BF)
    return held


def dp_bits():
    count, bits = lax.axis_size("dp"), []
    while count > 1:
        count //= 2
        bits.append(count)
    return bits


def sum_projections(value):
    rows, columns = value.shape
    bits = dp_bits()
    lead = (2,) * (1 + len(bits))
    half = columns // 256 * 128
    out = []
    for which, part in enumerate((value[:, :half], value[:, half:])):
        shaped = part.reshape(*lead, rows // 2 ** len(lead), part.shape[1])
        early = {"section": 1, bits[-1]: 0} if which == 0 else {"section": 0, bits[-1]: 1}
        names = {"section": early["section"]}
        for at, bit in enumerate(bits):
            names[bit] = early.get(bit, 2 + at)
        out.append(reduce_blocks(shaped, names))
    return jnp.concatenate(out, axis=1)


def sum_stem(value):
    rows, columns = value.shape
    bits = dp_bits()
    place = lax.axis_index("tensor")
    groups = 2 ** len(bits)
    block = rows // (groups * 2)
    shaped = value.reshape(groups, 2, block, columns)
    mine, got = halve(shaped, 1, place, functools.partial(swap, axis="tensor"))
    held = add_low(mine, got)
    half = columns // 256 * 128
    out = []
    for which, part in enumerate((held[:, :, :half], held[:, :, half:])):
        shaped = part.reshape(*((2,) * len(bits)), 2, block // 2, part.shape[2])
        names = {bit: 2 + at for at, bit in enumerate(bits)}
        names[bits[-1]] = which
        names["section"] = 1 - which
        out.append(reduce_blocks(shaped, names))
    mine = jnp.concatenate(out, axis=1)
    got = swap(mine, "section")
    first = lax.axis_index("section") == 0
    return jnp.concatenate(
        [jnp.where(first, mine, got), jnp.where(first, got, mine)], axis=0
    )


def core_sum(pairs):
    full = [dot_tn(left, right).astype(BF) for left, right in pairs]
    mine = jnp.concatenate([v[:, : v.shape[1] // 2] for v in full], axis=1)
    sent = jnp.concatenate([v[:, v.shape[1] // 2 :] for v in full], axis=1)
    return add_low(mine, swap(sent, "tensor"))


def sinusoid_table(count, width_all):
    step_size = math.log(10000.0) / (width_all // 2 - 1)
    rates = np.exp(-step_size * np.arange(width_all // 2))
    angles = np.arange(count)[:, None] * rates[None, :]
    return np.concatenate([np.sin(angles), np.cos(angles)], axis=1).astype(np.float32)


def pad_rows(value, rows):
    return jnp.pad(value, ((0, rows - value.shape[0]), (0, 0)))


def round_up(count):
    return -(-count // CHUNK) * CHUNK


def body(
    mel,
    conv_first,
    conv_second,
    enc_gain,
    enc_shift,
    enc_qkv,
    enc_proj,
    enc_up,
    enc_down,
    cross_kv,
    text,
    lengths,
    dec_gain,
    dec_shift,
    dec_qkv,
    dec_proj,
    cross_query,
    cross_proj,
    dec_up,
    dec_down,
    cotangent,
):
    section = lax.axis_index("section")
    place = lax.axis_index("tensor")
    cores = lax.axis_size("tensor")
    width = text.shape[2]
    frames = mel.shape[1] // 2
    valid = frames // cores
    rows = round_up(valid)
    slots = text.shape[1]
    text_rows = round_up(slots)
    channels = mel.shape[2]

    group = lax.axis_index("dp")
    bits = [place, section, group % 2, group // 2, group // 2 % 2, group // 4 % 2]
    scal = jnp.concatenate([jnp.stack([bit.astype(jnp.int32) for bit in bits]), lengths])
    pair = lambda w: (w, swap(w, "tensor"))
    w_dqkv, w_eqkv, w_eproj, w_dproj, w_cq = map(pair, (dec_qkv, enc_qkv, enc_proj, dec_proj, cross_query))
    w_eup, w_edown, w_ckv = map(pair, (enc_up, enc_down, cross_kv))
    w_cproj, w_dup, w_ddown = map(pair, (cross_proj, dec_up, dec_down))
    early = [w[1] for w in (w_eproj, w_dproj, w_cq, w_cproj)]
    late = [w[1] for w in (w_eup, w_edown, w_ckv, w_dup, w_ddown)]
    eg, es = [enc_gain[i : i + 1] for i in range(3)], [enc_shift[i : i + 1] for i in range(3)]
    dg, ds = [dec_gain[i : i + 1] for i in range(3)], [dec_shift[i : i + 1] for i in range(3)]

    taps = conv_first.shape[0] * channels
    depth = -(-(taps + 12) // LANES) * LANES
    second = conv_second.reshape(-1, width)
    table = np.pad(sinusoid_table(frames, width), ((0, rows - valid), (0, 0)))
    table = jnp.asarray(np.stack([table[valid * core : valid * core + rows] for core in range(cores)]))

    dn_a, dq_self, dkv_self = rows_call(
        qkv_kernel, text_rows, [Clip(text)], [dg[0], ds[0], *w_dqkv],
        [(width, BF, Far), (width, BF), (2 * width, BF)], flops=2 * text_rows * width * 3 * width, scal=scal,
    )
    dkv_self_r = swap(dkv_self, "tensor")

    mel_rows = 2 * frames + 8 + 2 * (rows - valid) + 16
    even, odd, before, ge, go, gs, x0, gh, windows, halo = rows_call(
        functools.partial(stem_fwd_kernel, valid=valid), rows, [Far(table, 1, True)],
        [Far(jnp.swapaxes(mel, 1, 2)), Far(conv_first), Far(second)],
        [(width, BF, Far)] * 6 + [(width, F32)],
        sums=[((16, width), F32), ((rows, 4 * LANES), BF, Far), ((16, 3 * LANES), BF)],
        scratch=[pltpu.VMEM((8, width), F32), pltpu.VMEM((mel_rows, LANES), F32)],
        flops=2 * rows * width * 2000, scal=scal, told=True, megabytes=14,
    )
    en_a, eq, ekv = rows_call(
        qkv_kernel, rows, [tie(x0, dq_self, *early)], [eg[0], es[0], *w_eqkv],
        [(width, BF, Far), (width, BF), (2 * width, BF)], flops=2 * rows * width * 3 * width,
    )
    ekv_r = swap(ekv, "tensor")

    datt, drest, dstat = attention_fwd(dq_self, dkv_self, dkv_self_r, slots, scal)
    eq = tie(eq, datt)
    eatt, erest, estat = attention_fwd(eq, ekv, ekv_r, valid)
    units = 2 * enc_up.shape[1]
    x1, x2, en_b, ehid, eslope, memory, ckv = rows_call(
        enc_mid_kernel, rows, [x0, tie(eatt, *late)],
        [eg[1], es[1], eg[2], es[2], *w_eproj, *w_eup, *w_edown, *w_ckv],
        [
            (width, F32, Far), (width, F32, Far), (width, BF, Far), (units, BF, Far), (units, BF, Far),
            (width, BF, Far), (2 * width, BF),
        ],
        flops=2 * rows * width * (3 * width + 2 * units), megabytes=20,
    )
    ckv_r = swap(ckv, "tensor")
    y1, dn_b, cq = rows_call(
        dec_mid_kernel, text_rows, [Clip(text), tie(datt, ckv)], [dg[1], ds[1], *w_dproj, *w_cq],
        [(width, F32), (width, BF, Far), (width, BF)], flops=2 * text_rows * width * 2 * width, scal=scal,
    )

    crossed, crest, cstat = attention_fwd(cq, ckv, ckv_r, valid)
    dec_units = 2 * dec_up.shape[1]
    top_outs = [
        (width, BF), (dec_units, BF), (dec_units, BF), (width, BF), (width, BF), (width, BF), (width, F32),
    ]
    owned = lambda kind: shape_of(slots, width // 2, kind)
    decoded, decoded_sent, dn_c, dhid, dpre, dgb3, dgb2, dcrossed, u2, sums_c = flat_call(
        functools.partial(dec_top_kernel, valid=slots),
        [y1, crossed, Clip(cotangent), dg[2], ds[2], *w_cproj, *w_dup, *w_ddown],
        [owned(BF), owned(BF)] + [shape_of(text_rows, w, k) for w, k in top_outs] + [shape_of(8, width, F32)],
        scal=scal, scratch=[pltpu.VMEM((text_rows, dec_units), BF)],
        flops=2 * text_rows * width * (2 * width + 4 * dec_units), megabytes=12,
    )
    decoded_got = swap(decoded_sent, "section")
    fast = lax.axis_size("dp") == 8 and width % (4 * 8 * 16) == 0
    top_pairs = [(dn_c, dpre), (dgb3, dhid), (dgb2, crossed)]
    top_widths = [dec_up.shape[1], dec_down.shape[0], cross_proj.shape[0]]
    if fast:
        own, oth = gradients(top_pairs)
        top_steps = sum_over_chips(own, oth, scal, sum(top_widths) // 2, top_widths)
        dcrossed = tie(dcrossed, own)
    dcq, dckv, dckv_r = attention_bwd(cq, ckv, ckv_r, crossed, crest, cstat, dcrossed, valid)
    if fast:
        dcq = tie(dcq, next(top_steps))
    dckv_got = swap(dckv_r, "tensor")
    u1, dgb1, ddatt, sums_b = rows_call(
        dec_back_kernel, text_rows, [dcq, y1, u2], [dg[1], *w_cq, *w_dproj],
        [(width, F32), (width, BF, Far), (width, BF)], sums=[((8, width), F32)],
        flops=2 * text_rows * width * 2 * width,
    )
    dqs, dkvs, dkvs_r = attention_bwd(
        dq_self, dkv_self, dkv_self_r, datt, drest, dstat, ddatt, slots, scal
    )
    dkvs_got = swap(dkvs_r, "tensor")

    gkv, egb2, edpre, egb1, deatt, eu1, sums_e = rows_call(
        enc_back_kernel, rows, [tie(dckv, dqs), dckv_got, x2, x1, eslope],
        [eg[2], eg[1], *w_ckv, *w_eup, *w_edown, *w_eproj],
        [(2 * width, BF), (width, BF), (units, BF, Far), (width, BF), (width, BF), (width, F32, Far)],
        sums=[((8, width), F32)], flops=2 * rows * width * (3 * width + 2 * units), megabytes=13,
    )
    d_packed, sums_a, text_mine, text_sent = rows_call(
        dec_last_kernel, text_rows, [dqs, dkvs, dkvs_got, Clip(text), tie(u1, deatt)], [dg[0], *w_dqkv],
        [(2 * dec_qkv.shape[1], BF)],
        sums=[((8, width), F32), ((slots, width // 2), F32), ((slots, width // 2), BF)],
        flops=2 * text_rows * width * 3 * width, scal=scal, told=True,
    )
    text_got = swap(text_sent, "section")
    mid_pairs = [
        (dn_a, d_packed), (dn_b, dcq), (dgb1, datt), (egb1, eatt), (memory, gkv), (en_b, edpre), (egb2, ehid),
    ]
    mid_widths = [dec_qkv.shape[1], cross_query.shape[1], dec_proj.shape[0], enc_proj.shape[0]]
    mid_widths += [cross_kv.shape[1], enc_up.shape[1], enc_down.shape[0]]
    if fast:
        mid_pairs[0] = (dn_a, tie(d_packed, top_steps.send(d_packed)))
        own, oth = gradients(mid_pairs, [memory, en_b, edpre, ehid])
        mid_steps = sum_over_chips(own, oth, scal, sum(mid_widths) // 2, mid_widths)
        waits = [
            lambda: (own,), lambda: (top_steps.send(base_a),), lambda: (next(mid_steps),)
        ]
    else:
        waits = [lambda: ()] * 3

    half = width // (4 * HEAD_DIM)
    deatt = tie(deatt, *waits[0]())
    side = (eatt, erest, estat)
    base_a, dekv_a = attention_bwd_side(eq, ekv_r, *side, deatt, valid, pairs=(0, half))
    deatt = tie(deatt, base_a, *waits[1]())
    base_b, dekv_r = attention_bwd_side(
        eq, ekv_r, *side, deatt, valid, pairs=(half, half), earlier=(dekv_a,)
    )
    dekv_got = swap(dekv_r, "tensor")
    deatt = tie(deatt, base_b, *waits[2]())
    deq, dekv = attention_bwd_side(eq, ekv, *side, deatt, valid, (base_a, base_b))
    e_packed, g2, ede, edo, sums_f, edh = rows_call(
        stem_back_kernel, rows, [deq, dekv, dekv_got, x0, eu1, ge, go, gs],
        [eg[0], *w_eqkv, second, gh],
        [(2 * enc_qkv.shape[1], BF), (width, BF), (width, BF), (width, BF)],
        sums=[((8, width), F32), ((16, width), BF)], scratch=[pltpu.VMEM((8, width), F32)],
        reverse=True, flops=2 * rows * width * 6 * width,
    )
    sums, end = [sums_a, sums_b, sums_c, sums_e, sums_f], ()
    if fast:
        stem_width = 3 * width + depth
        late_columns = (enc_qkv.shape[1], enc_qkv.shape[1], stem_width // 2, stem_width // 2)
        own, oth, own_stem, oth_stem = flat_call(
            functools.partial(late_kernel, channels=channels),
            [
                en_a, tie(e_packed, top_steps.send(e_packed)), g2, before, even, odd, ede, edo, edh, windows, halo,
                *sums,
            ],
            [shape_of(width, columns) for columns in late_columns], scal=scal, scratch=[pltpu.VMEM((width, stem_width), BF)],
            flops=2 * rows * width * (3 * width + 3 * width + 2 * depth), megabytes=10,
        )
        own = tie(own, mid_steps.send(own))
        late_steps = sum_over_chips(
            (own, own_stem), (oth, oth_stem), scal, enc_qkv.shape[1], [enc_qkv.shape[1], stem_width // 2], True
        )
        top_sums = top_steps.send(next(late_steps))
        later = mid_steps.send(top_sums[0])
        later = mid_steps.send(late_steps.send(later))
        later = late_steps.send(later)
        end = (later,)
        mid_sums = mid_steps.send(later)
        late_qkv, stem = late_steps.send(mid_sums[0])
        block = 2 * width // (2 * lax.axis_size("dp") * cores)
        conv_second_grad, conv_first_grad, *vec = flat_call(
            stem_last_kernel, [stem, swap(stem, "section")],
            [
                jax.ShapeDtypeStruct((conv_second.shape[0], block, width), F32),
                jax.ShapeDtypeStruct((conv_first.shape[0], block, channels), F32),
            ] + [shape_of(3, block, F32)] * 4,
            scal=scal, megabytes=6,
        )
        conv_second_grad = conv_second_grad.transpose(0, 2, 1)
        conv_first_grad = conv_first_grad.transpose(0, 2, 1)
    else:
        cuts = lambda value, widths: jnp.split(value, list(np.cumsum(widths)[:-1]), axis=1)
        top_sums = cuts(sum_projections(core_sum(top_pairs)), top_widths)
        mid_sums = cuts(sum_projections(core_sum(mid_pairs)), mid_widths)
        late_qkv = sum_projections(core_sum([(en_a, e_packed)]))
        first_t = dot_tn(ede, windows[:, : 3 * LANES]) + dot_tn(edo, windows[:, LANES:]) + dot_tn(edh, halo)
        first_t = first_t.reshape(width, -1, LANES)[:, :, :channels].reshape(width, taps)
        vectors = jnp.concatenate(
            [
                sums_f[0:1], sums_e[2:3], sums_e[0:1], sums_f[1:2], sums_e[3:4], sums_e[1:2],
                sums_a[0:1], sums_b[0:1], sums_c[0:1], sums_a[1:2], sums_b[1:2], sums_c[1:2],
            ],
            axis=0,
        )
        stem = [dot_tn(g2, act) for act in (before, even, odd)] + [first_t, vectors.T]
        stem.append(jnp.zeros((width, depth - taps - vectors.shape[0]), F32))
        stem = sum_stem(jnp.concatenate([v.astype(BF) for v in stem], axis=1)).T
        conv_second_grad, conv_first_grad = stem[: 3 * width], stem[3 * width : 3 * width + taps]
        vec = [stem[3 * width + taps + 3 * n : 3 * width + taps + 3 * n + 3] for n in range(4)]

    owned = [jax.ShapeDtypeStruct((2, *text_mine.shape), kind) for kind in (BF, F32)]
    decoded, text_grad = flat_call(
        owners_kernel, [decoded, tie(text_mine, *end), decoded_got, text_got], owned, scal=scal, megabytes=4
    )

    d_up, d_down_t, d_cproj_t = top_sums
    d_qkv, d_cq, d_proj_t, e_proj_t, e_kv, e_up, e_down_t = mid_sums
    return (
        decoded,
        text_grad,
        conv_first_grad.reshape(*conv_first.shape[:2], -1),
        conv_second_grad.reshape(*conv_second.shape[:2], -1),
        vec[0],
        vec[1],
        late_qkv,
        e_proj_t.T,
        e_up,
        e_down_t.T,
        e_kv,
        vec[2],
        vec[3],
        d_qkv,
        d_proj_t.T,
        d_cq,
        d_cproj_t.T,
        d_up,
        d_down_t.T,
    )


def solution(mesh):
    in_specs = (
        P("dp", None, None),
        P(),
        P(),
        P(),
        P(),
        P(None, "tensor"),
        P("tensor", None),
        P(None, "tensor"),
        P("tensor", None),
        P(None, "tensor"),
        P("dp", "tensor", None),
        P("dp"),
        P(),
        P(),
        P(None, "tensor"),
        P("tensor", None),
        P(None, "tensor"),
        P("tensor", None),
        P(None, "tensor"),
        P("tensor", None),
        P("dp", "tensor", None),
    )
    out_specs = (
        P("dp", "tensor", "section"),
        P("dp", "tensor", "section"),
        P(None, None, ("dp", "tensor")),
        P(None, None, ("dp", "tensor")),
        P(None, ("dp", "tensor")),
        P(None, ("dp", "tensor")),
        P(("section", "dp"), "tensor"),
        P("tensor", ("section", "dp")),
        P(("section", "dp"), "tensor"),
        P("tensor", ("section", "dp")),
        P(("section", "dp"), "tensor"),
        P(None, ("dp", "tensor")),
        P(None, ("dp", "tensor")),
        P(("section", "dp"), "tensor"),
        P("tensor", ("section", "dp")),
        P(("section", "dp"), "tensor"),
        P("tensor", ("section", "dp")),
        P(("section", "dp"), "tensor"),
        P("tensor", ("section", "dp")),
    )
    return jax.shard_map(body, mesh=mesh, in_specs=in_specs, out_specs=out_specs, check_vma=False)
```

```python
import functools
import math

import jax
import jax.numpy as jnp
import numpy as np
from jax import lax
from jax.experimental import pallas as pl
from jax.experimental.pallas import tpu as pltpu
from jax.sharding import PartitionSpec as P

HEAD_DIM = 64
NEG = -1000000000.0
EPS = 1e-05
TINY = 1e-28
CHUNK = 256
LANES = 128
BF, F32 = jnp.bfloat16, jnp.float32
INV_SQRT2 = 0.7071067811865476
INV_SQRT2PI = 0.3989422804014327


def dot_nn(left, right):
    return lax.dot_general(left, right, (((1,), (0,)), ((), ())), preferred_element_type=F32)


def dot_nt(left, right):
    return lax.dot_general(left, right, (((1,), (1,)), ((), ())), preferred_element_type=F32)


def dot_tn(left, right):
    return lax.dot_general(left, right, (((0,), (0,)), ((), ())), preferred_element_type=F32)


def norm_stats(rows):
    centre = rows - jnp.mean(rows, axis=-1, keepdims=True)
    spread = jnp.mean(centre * centre, axis=-1, keepdims=True)
    inverse = lax.rsqrt(spread + EPS)
    return centre * inverse, inverse


def norm_back(unit, inverse, gain_row, upstream):
    scaled = upstream * gain_row
    first = jnp.mean(scaled, axis=-1, keepdims=True)
    second = jnp.mean(scaled * unit, axis=-1, keepdims=True)
    grad_rows = inverse * (scaled - first - unit * second)
    grad_gain = jnp.sum(upstream * unit, axis=0, keepdims=True)
    grad_bias = jnp.sum(upstream, axis=0, keepdims=True)
    return grad_rows, grad_gain, grad_bias


def gelu_pair(v):
    phi = 0.5 * (1.0 + lax.erf(v * INV_SQRT2))
    return v * phi, phi + (v * INV_SQRT2PI) * jnp.exp(-0.5 * (v * v))


def lanes(rows):
    return lax.broadcasted_iota(jnp.int32, (rows, 2 * HEAD_DIM), 1)

def key_aug(kv, valid, ones):
    lane = lanes(kv.shape[0])
    row = lax.broadcasted_iota(jnp.int32, kv.shape, 0)
    pad = jnp.where((lane > HEAD_DIM) & (lane <= HEAD_DIM + ones), 1.0, 0.0)
    pad = jnp.where((lane == HEAD_DIM) & (row >= valid), NEG, pad).astype(BF)
    return jnp.where(lane < HEAD_DIM, kv, pad)

def causal_bias(scal_ref, key_rows, query_rows, valid):
    place, length = scal_ref[SCAL_CORE], scal_ref[SCAL_LENGTHS + scal_ref[SCAL_SECTION]]
    key_id = lax.broadcasted_iota(jnp.int32, (2 * key_rows, query_rows), 0)
    query_id = lax.broadcasted_iota(jnp.int32, (2 * key_rows, query_rows), 1)
    query_pos = query_id + place * valid
    key_pos = jnp.where(key_id < key_rows, key_id + place * valid, key_id - key_rows + (1 - place) * valid)
    return jnp.where((key_pos <= query_pos) & (key_pos < length), 0.0, NEG)

def fwd_setup(q_ref, kl_ref, kr_ref, valid):
    lane_q = lanes(q_ref.shape[0])
    q_all = q_ref[...].astype(F32) * HEAD_DIM**-0.5
    wide = 2 * HEAD_DIM

    def operands(h):
        q = jnp.where(lane_q < HEAD_DIM, q_all if h == 0 else pltpu.roll(q_all, HEAD_DIM, 1), 0.0)
        kv = [ref[:, h * wide : (h + 1) * wide] for ref in (kl_ref, kr_ref)]
        turned = [v.T for v in kv]
        sub = lax.broadcasted_iota(jnp.int32, turned[0].shape, 0)
        ones = [jnp.where(sub == 0, jnp.ones_like(v), v) for v in turned]
        return q, [key_aug(v, valid, 1) for v in kv], turned, ones

    return lane_q, operands


def fwd_finish(parts, logs, shift, out_ref, rest_ref, stat_ref):
    queries = out_ref.shape[0]
    mixed = jnp.concatenate([v[HEAD_DIM:] / v[0:1] for v in parts], axis=0).T
    logs = [jnp.broadcast_to(v, (HEAD_DIM, queries)) for v in logs]
    stat = jnp.concatenate(logs[::-1], axis=0).T
    if shift is not None:
        stat = stat + shift
    rounded = mixed.astype(BF)
    out_ref[...] = rounded
    rest_ref[...] = (mixed - rounded.astype(F32)).astype(BF)
    stat_ref[...] = stat


def fwd_fast(q_ref, kl_ref, kr_ref, out_ref, rest_ref, stat_ref, bias, valid, kc, depth):
    rows, queries = kl_ref.shape[0], q_ref.shape[0]
    lane_q, operands = fwd_setup(q_ref, kl_ref, kr_ref, valid)
    tops, heads = [], []
    for h in range(2):
        q, keys, turned, ones = operands(h)
        size = 0.0
        for v in turned:
            k = v[:HEAD_DIM].astype(F32)
            size = jnp.maximum(size, jnp.max(jnp.sum(k * k, axis=0, keepdims=True), axis=1, keepdims=True))
        bound = jnp.sqrt(jnp.sum(q * q, axis=1, keepdims=True) * size)
        bound = bound.astype(BF).astype(F32)
        q = jnp.where(lane_q == HEAD_DIM, 1.0, jnp.where(lane_q == HEAD_DIM + 1, -bound, q)).astype(BF)
        heads.append((q, keys, ones)); tops.append(bound)
    def score(item):
        h, side, at = item
        s = dot_nt(heads[h][1][side][at : at + kc], heads[h][0])
        if bias is not None:
            s = s + bias[side * rows + at : side * rows + at + kc]
        return s
    items = [(h, side, at) for h in range(2) for side in range(2) for at in range(0, rows, kc)]
    parts = [0.0, 0.0]
    ahead = [score(i) for i in items[:depth]]
    for n, (h, side, at) in enumerate(items):
        if n + depth < len(items):
            ahead.append(score(items[n + depth]))
        p = jnp.exp(ahead.pop(0)).astype(BF)
        parts[h] = parts[h] + dot_nn(heads[h][2][side][:, at : at + kc], p)
    fwd_finish(parts, [jnp.log(v[0:1]) for v in parts], jnp.where(lane_q < HEAD_DIM, tops[1], tops[0]), out_ref, rest_ref, stat_ref)
    return jnp.minimum(parts[0][0:1], parts[1][0:1])


def fwd_safe(q_ref, kl_ref, kr_ref, out_ref, rest_ref, stat_ref, bias, valid):
    rows = kl_ref.shape[0]
    lane_q, operands = fwd_setup(q_ref, kl_ref, kr_ref, valid)
    parts, logs = [], []
    for h in range(2):
        q, keys, _, ones = operands(h)
        q = jnp.where(lane_q == HEAD_DIM, 1.0, q).astype(BF)
        scores = []
        for side in range(2):
            s = dot_nt(keys[side], q)
            if bias is not None:
                s = s + bias[side * rows : (side + 1) * rows]
            scores.append(s)
        top = jnp.maximum(jnp.max(scores[0], axis=0, keepdims=True), jnp.max(scores[1], axis=0, keepdims=True))
        parts.append(sum(dot_nn(ones[i], jnp.exp(scores[i] - top).astype(BF)) for i in range(2)))
        logs.append(top + jnp.log(parts[h][0:1]))
    fwd_finish(parts, logs, None, out_ref, rest_ref, stat_ref)


def views(refs, i, pairs):
    narrow, near, far = refs
    wide = 2 * HEAD_DIM
    j = (i + pairs // 2) % pairs if isinstance(i, int) else lax.rem(i + pairs // 2, pairs)
    at = (lambda n, w: pl.ds(n * w, w)) if isinstance(i, int) else (lambda n, w: pl.ds(pl.multiple_of(n * w, w), w))
    return [r.at[:, at(i, wide)] for r in narrow], [r.at[:, at(i, 2 * wide)] for r in near], [r.at[:, at(j, 2 * wide)] for r in far]


def fwd_kernel(*refs, valid, masked, kc, depth):
    scal_ref = refs[0] if masked else None
    q_ref, kl_ref, kr_ref, out_ref, rest_ref, stat_ref = refs[1:] if masked else refs
    pairs = q_ref.shape[1] // (2 * HEAD_DIM)
    bias = causal_bias(scal_ref, kl_ref.shape[0], q_ref.shape[0], valid) if masked else None
    least = None
    for i in range(pairs):
        (q, out, rest, stat), (kl,), (kr,) = views(((q_ref, out_ref, rest_ref, stat_ref), (kl_ref,), (kr_ref,)), i, pairs)
        low = fwd_fast(q, kl, kr, out, rest, stat, bias, valid, kc, depth)
        least = low if least is None else jnp.minimum(least, low)
        for ref in (rest_ref, stat_ref):
            push(ref, (slice(None), pl.ds(i * 2 * HEAD_DIM, 2 * HEAD_DIM)))
    for ref in (rest_ref, stat_ref):
        if isinstance(ref, Outgoing):
            ref.finish()

    @pl.when(jnp.min(least) < TINY)
    def _():
        @pl.loop(0, pairs)
        def _(i):
            (q, out, rest, stat), (kl,), (kr,) = views(((q_ref, out_ref, rest_ref, stat_ref), (kl_ref,), (kr_ref,)), i, pairs)
            again = causal_bias(scal_ref, kl_ref.shape[0], q_ref.shape[0], valid) if masked else None
            fwd_safe(q, kl, kr, out, rest, stat, again, valid)

        for ref in (rest_ref, stat_ref):
            if isinstance(ref, Outgoing):
                ref.again()


def split3(value):
    first = value.astype(BF); rest = value - first.astype(F32)
    second = rest.astype(BF); third = (rest - second.astype(F32)).astype(BF)
    return first.astype(F32), second.astype(F32), third.astype(F32)


def bwd_views(refs, i, pairs):
    q_ref, kl_ref, kr_ref, out_ref, rest_ref, stat_ref, up_ref, dq_ref, dkl_ref, dkr_ref = refs
    narrow = (q_ref, out_ref, rest_ref, stat_ref, up_ref, dq_ref)
    (q, out, rest, stat, up, dq), (kl, dkl), (kr, dkr) = views(
        (narrow, (kl_ref, dkl_ref), (kr_ref, dkr_ref)), i, pairs
    )
    return q, kl, kr, out, rest, stat, up, dq, dkl, dkr


def bwd_kernel(*refs, valid, masked):
    scal_ref = refs[0] if masked else None
    refs = refs[1:] if masked else refs
    q_ref, kl_ref = refs[:2]
    pairs = q_ref.shape[1] // (2 * HEAD_DIM)
    bias = causal_bias(scal_ref, kl_ref.shape[0], q_ref.shape[0], valid) if masked else None
    for i in range(pairs):
        q, kl, kr, out, rest, stat, up, dq, dkl, dkr = bwd_views(refs, i, pairs)
        fn = bwd_pair if masked else bwd_pair_s
        fn(q, out, rest, stat, up, dq, [(kl, dkl), (kr, dkr)], bias, valid)


def bwd_side_kernel(*refs, valid, far, first, count, joined, turn):
    q_ref, kv_ref, out_ref, rest_ref, stat_ref, up_ref, *more, dq_ref, dkv_ref = refs
    pairs = q_ref.shape[1] // (2 * HEAD_DIM)
    wide = 2 * HEAD_DIM
    base_refs = () if far else more
    if joined:
        earlier, at = more[0], dkv_ref.shape[1] - more[0].shape[1]
        dkv_ref[:, at:] = earlier[...]

    def one(i):
        (q, out, rest, stat, up), near, other = views(
            ((q_ref, out_ref, rest_ref, stat_ref, up_ref), () if far else (kv_ref,), (kv_ref,) if far else ()),
            (first + i) % pairs, pairs,
        )
        dq = dq_ref.at[:, i * wide : (i + 1) * wide]
        dkv = dkv_ref.at[:, i * 2 * wide : (i + 1) * 2 * wide]
        base = None
        if base_refs:
            each, at = base_refs[0].shape[1] // wide, (first + i - turn) % pairs
            base = base_refs[at // each].at[:, at % each * wide : (at % each + 1) * wide]
        bwd_pair(q, out, rest, stat, up, dq, [(*near, *other, dkv)], None, valid, base)

    for i in range(count):
        one(i)


def bwd_pair_s(q_ref, out_ref, rest_ref, stat_ref, up_ref, dq_ref, key_sides, bias, valid, base_ref=None):
    rows, queries, depth = key_sides[0][0].shape[0], q_ref.shape[0], 1
    kc = rows
    wide = 2 * HEAD_DIM
    lane_q, lane_k = lanes(queries), lanes(rows)
    low_q = lane_q < HEAD_DIM
    q_all = q_ref[...].astype(F32) * HEAD_DIM**-0.5
    up_all = up_ref[...].astype(F32)
    stat = stat_ref[...]
    prods = up_all * (out_ref[...].astype(F32) + rest_ref[...].astype(F32))
    q_turned = (q_all.astype(BF)).T
    up_turned = up_ref[...].T
    heads, both = [], []
    for h in range(2):
        q = q_all if h == 0 else pltpu.roll(q_all, HEAD_DIM, 1)
        lse = stat if h == 0 else pltpu.roll(stat, HEAD_DIM, 1)
        up = up_all if h == 1 else pltpu.roll(up_all, HEAD_DIM, 1)
        a0, a1, a2 = split3(-lse)
        pad = jnp.where(lane_q == HEAD_DIM, 1.0, jnp.where(lane_q == HEAD_DIM + 1, a0, jnp.where(lane_q == HEAD_DIM + 2, a1, jnp.where(lane_q == HEAD_DIM + 3, a2, 0.0))))
        q_aug = jnp.where(low_q, q, pad).astype(BF)
        centre = jnp.sum(jnp.where(low_q if h == 0 else ~low_q, prods, 0.0), axis=1, keepdims=True)
        d0, d1, d2 = split3(-centre)
        pad = jnp.where(lane_q == 0, d0, jnp.where(lane_q == 1, d1, jnp.where(lane_q == 2, d2, 0.0)))
        up_aug = jnp.where(low_q, pad, up).astype(BF)
        heads.append((q_aug, up_aug, q_turned[h * HEAD_DIM : (h + 1) * HEAD_DIM], up_turned[h * HEAD_DIM : (h + 1) * HEAD_DIM]))
        sides = []
        for ref, out in key_sides:
            kv = ref[:, h * wide : (h + 1) * wide]
            keys = key_aug(kv, valid, 3)
            values = jnp.where(lane_k < HEAD_DIM, jnp.where(lane_k < 3, 1.0, 0.0).astype(BF), kv)
            sides.append((keys, values, kv, out))
        both.append(sides)
    items = [(h, side, at) for h in range(2) for side in range(len(key_sides)) for at in range(0, rows, kc)]
    def score(item):
        h, side, at = item
        keys, values, _, _ = both[h][side]
        return dot_nt(heads[h][0], keys[at : at + kc]), dot_nt(heads[h][1], values[at : at + kc])
    ahead = [score(i) for i in items[:depth]]
    totals = [0.0, 0.0]
    for n, (h, side, at) in enumerate(items):
        if n + depth < len(items):
            ahead.append(score(items[n + depth]))
        s, dp = ahead.pop(0)
        p = jnp.exp(s)
        ds = (p * dp).astype(BF)
        p = p.astype(BF)
        _, _, kv, out = both[h][side]
        pair = jnp.concatenate([dot_nn(heads[h][2], ds), dot_nn(heads[h][3], p)], axis=0)
        out[at : at + kc, h * wide : (h + 1) * wide] = pair.T.astype(BF)
        totals[h] = totals[h] + dot_nn(ds, kv[at : at + kc])
    dq = jnp.where(low_q, totals[0], pltpu.roll(totals[1], HEAD_DIM, 1)) * HEAD_DIM**-0.5
    dq_ref[...] = dq.astype(BF)


def bwd_pair(q_ref, out_ref, rest_ref, stat_ref, up_ref, dq_ref, key_sides, bias, valid, base_ref=None):
    masked, depth = bias is not None, 1
    rows, queries = key_sides[0][0].shape[0], q_ref.shape[0]
    kc = rows
    wide = 2 * HEAD_DIM
    lane_q, lane_k = lanes(queries), lanes(rows)
    low_q = lane_q < HEAD_DIM
    q_all = q_ref[...].astype(F32) * HEAD_DIM**-0.5
    up_all = up_ref[...].astype(F32)
    stat = stat_ref[...]
    prods = up_all * (out_ref[...].astype(F32) + rest_ref[...].astype(F32))
    heads, both = [], []
    for h in range(2):
        q = q_all if h == 0 else pltpu.roll(q_all, HEAD_DIM, 1)
        lse = stat if h == 0 else pltpu.roll(stat, HEAD_DIM, 1)
        up = up_all if h == 1 else pltpu.roll(up_all, HEAD_DIM, 1)
        a0, a1, a2 = split3(-lse)
        pad = jnp.where(lane_q == HEAD_DIM, 1.0, jnp.where(lane_q == HEAD_DIM + 1, a0, jnp.where(lane_q == HEAD_DIM + 2, a1, jnp.where(lane_q == HEAD_DIM + 3, a2, 0.0))))
        q_aug = jnp.where(low_q, q, pad).astype(BF)
        q_rhs = jnp.where(low_q, q, 0.0).astype(BF)
        centre = jnp.sum(jnp.where(low_q if h == 0 else ~low_q, prods, 0.0), axis=1, keepdims=True)
        d0, d1, d2 = split3(-centre)
        pad = jnp.where(lane_q == 0, d0, jnp.where(lane_q == 1, d1, jnp.where(lane_q == 2, d2, 0.0)))
        up_aug = jnp.where(low_q, pad, up).astype(BF)
        up_rhs = jnp.where(low_q, 0.0, up).astype(BF)
        heads.append((q_aug, q_rhs, up_aug, up_rhs))
        sides = []
        for ref, out in key_sides:
            kv = ref[:, h * wide : (h + 1) * wide]
            keys = key_aug(kv, valid, 3)
            values = jnp.where(lane_k < HEAD_DIM, jnp.where(lane_k < 3, 1.0, 0.0).astype(BF), kv)
            sides.append((keys, values, kv.T, out))
        both.append(sides)
    items = [(h, side, at) for h in range(2) for side in range(len(key_sides)) for at in range(0, rows, kc)]
    def score(item):
        h, side, at = item
        keys, values, _, _ = both[h][side]
        s = dot_nt(keys[at : at + kc], heads[h][0])
        if masked:
            first = at + side * rows
            s = s + bias[first : first + kc]
        return s, dot_nt(values[at : at + kc], heads[h][2])
    ahead = [score(i) for i in items[:depth]]
    totals = [0.0, 0.0]
    for n, (h, side, at) in enumerate(items):
        if n + depth < len(items):
            ahead.append(score(items[n + depth]))
        s, dp = ahead.pop(0)
        p = jnp.exp(s)
        ds = (p * dp).astype(BF)
        p = p.astype(BF)
        _, _, turned, out = both[h][side]
        out[at : at + kc, h * wide : (h + 1) * wide] = (dot_nn(ds, heads[h][1]) + dot_nn(p, heads[h][3])).astype(BF)
        totals[h] = totals[h] + dot_nn(turned[:, at : at + kc], ds)
    turned_dq = [v[:HEAD_DIM] for v in totals]
    dq = jnp.concatenate(turned_dq, axis=0).T * HEAD_DIM**-0.5
    if base_ref is not None:
        dq = dq + base_ref[...]
    dq_ref[...] = dq.astype(dq_ref.dtype)


def shape_of(rows, width, kind=BF):
    return jax.ShapeDtypeStruct((rows, width), kind)


def params(megabytes, *semantics):
    return pltpu.CompilerParams(vmem_limit_bytes=megabytes * 2**20)


def attention_cost(q, kl, products):
    flops = 2 * products * q.shape[0] * 2 * kl.shape[0] * q.shape[1] * 3
    return pl.CostEstimate(
        flops=flops, bytes_accessed=8 * q.size + 6 * kl.size, transcendentals=0
    )


class Far:
    def __init__(self, value, pieces=1, by_core=False):
        self.value, self.pieces, self.by_core = value, pieces, by_core
        self.shape, self.dtype = value.shape[1:] if by_core else value.shape, value.dtype
        self.size = math.prod(self.shape)


class Clip:
    def __init__(self, value):
        self.value, self.shape, self.dtype, self.size = value, value.shape, value.dtype, value.size


class Incoming:
    def __init__(self, source, held, arrived, pieces):
        self.held, self.shape, self.dtype = held, held.shape, held.dtype
        rows = held.shape[0] // pieces
        self.spans = [pl.ds(n * rows, rows) for n in range(pieces)]
        self.copies = [
            pltpu.make_async_copy(source.at[span], held.at[span], arrived.at[n])
            for n, span in enumerate(self.spans)
        ]

    def start(self, n):
        if n < len(self.copies):
            self.copies[n].start()

    def wait(self, n):
        if self.copies[n] is not None:
            self.copies[n].wait()
            self.copies[n] = None

    def piece(self, n):
        return Piece(self, n)

    def settle(self):
        for n in range(len(self.copies)):
            self.wait(n)
        return self.held

    @property
    def at(self):
        return self.settle().at

    def __getitem__(self, index):
        return self.settle()[index]


class Piece:
    def __init__(self, whole, n):
        self.whole, self.n = whole, n
        rows = whole.held.shape[0] // len(whole.spans)
        self.shape, self.dtype = (rows, *whole.held.shape[1:]), whole.held.dtype

    def __getitem__(self, index):
        self.whole.wait(self.n)
        return self.whole.held.at[self.whole.spans[self.n]][index]


class Padded:
    def __init__(self, ref, section, rows):
        self.ref, self.section, self.rows = ref, section, rows
        self.shape, self.dtype = (rows, ref.shape[2]), ref.dtype

    def __getitem__(self, index):
        value = self.ref[self.section]
        behind = jnp.zeros((self.rows - value.shape[0], value.shape[1]), value.dtype)
        return jnp.concatenate([value, behind], axis=0)[index]


class Outgoing:
    def __init__(self, target, held, left):
        self.target, self.held, self.left, self.copies = target, held, left, []
        self.at, self.shape, self.dtype = held.at, held.shape, held.dtype

    def __setitem__(self, index, value):
        self.held[index] = value

    def push(self, index=(slice(None), slice(None))):
        copy = pltpu.make_async_copy(
            self.held.at[index], self.target.at[index], self.left.at[len(self.copies)]
        )
        copy.start()
        self.copies.append(copy)

    def finish(self):
        for copy in self.copies or ():
            copy.wait()
        self.copies = None

    def again(self):
        copy = pltpu.make_async_copy(self.held, self.target, self.left.at[0])
        copy.start()
        copy.wait()


def push(ref, *index):
    if isinstance(ref, Outgoing):
        ref.push(*index)


def in_vmem():
    return pl.BlockSpec(memory_space=pltpu.VMEM)


def in_hbm():
    return pl.BlockSpec(memory_space=pltpu.HBM)


def flat_call(kernel, operands, out_shape, scal=None, scratch=(), flops=0, megabytes=40):
    touched = sum(v.size * v.dtype.itemsize for v in operands)
    touched += sum(math.prod(v.shape) * v.dtype.itemsize for v in out_shape)
    far_in = [v for v in operands if isinstance(v, Far)]
    far_out = [v for v in out_shape if isinstance(v, Far)]
    extra = []
    for v in (*far_in, *far_out):
        extra += [pltpu.VMEM(v.shape, v.dtype), pltpu.SemaphoreType.DMA((v.pieces,))]
        megabytes += -(-v.size * v.dtype.itemsize // 2**20)

    def run(*refs):
        refs = list(refs)
        take = lambda count: [refs.pop(0) for _ in range(count)]
        head = take(0 if scal is None else 1)
        ins, outs, own = take(len(operands)), take(len(out_shape)), take(len(scratch))
        moving = []
        for n, v in enumerate(operands):
            if isinstance(v, Far):
                source = ins[n].at[head[0][SCAL_CORE]] if v.by_core else ins[n]
                ins[n] = Incoming(source, *take(2), v.pieces)
                moving.append(ins[n])
            elif isinstance(v, Clip):
                ins[n] = Padded(ins[n], head[0][SCAL_SECTION], round_up(v.shape[1]))
        for n, v in enumerate(out_shape):
            if isinstance(v, Far):
                outs[n] = Outgoing(outs[n], *take(2))
        for n in range(max((len(v.copies) for v in moving), default=0)):
            for v in moving:
                v.start(n)
        kernel(*head, *ins, *outs, *own)
        for v in moving:
            v.settle()
        for v in outs:
            if isinstance(v, Outgoing):
                if v.copies == []:
                    v.push()
                v.finish()

    bare = lambda v: v.value if isinstance(v, (Far, Clip)) else v
    pin = lambda v: pltpu.with_memory_space_constraint(v.value, pltpu.HBM) if isinstance(v, Far) else bare(v)
    pin_shape = lambda v: pltpu.HBM(v.shape, v.dtype) if isinstance(v, Far) else v
    place = lambda v: in_hbm() if isinstance(v, Far) else in_vmem()
    return pl.pallas_call(
        run,
        in_specs=([] if scal is None else [pl.BlockSpec(memory_space=pltpu.SMEM)])
        + [place(v) for v in operands],
        out_specs=[place(v) for v in out_shape],
        out_shape=[pin_shape(v) for v in out_shape],
        scratch_shapes=list(scratch) + extra,
        compiler_params=params(megabytes),
        cost_estimate=pl.CostEstimate(flops=flops, bytes_accessed=touched, transcendentals=0),
    )(*([] if scal is None else [scal]), *[pin(v) for v in operands])


def attention_flops(q, kl, products, share=1):
    return 2 * products * q.shape[0] * 2 * kl.shape[0] * q.shape[1] * 4 // share


def attention_fwd(q, kl, kr, valid, scal=None):
    return flat_call(
        functools.partial(fwd_kernel, valid=valid, masked=scal is not None, kc=kl.shape[0], depth=1),
        [q, kl, kr],
        [shape_of(*q.shape), Far(shape_of(*q.shape), 8), Far(shape_of(*q.shape, F32), 8)],
        scal=scal, flops=attention_flops(q, kl, 2), megabytes=24 if q.shape[0] > CHUNK else 12,
    )


def attention_bwd(q, kl, kr, out, rest, stat, up, valid, scal=None):
    return flat_call(
        functools.partial(bwd_kernel, valid=valid, masked=scal is not None),
        [q, kl, kr, out, rest, stat, up],
        [shape_of(*q.shape), shape_of(*kl.shape), shape_of(*kl.shape)],
        scal=scal, flops=attention_flops(q, kl, 5), megabytes=12,
    )


def attention_bwd_side(q, kv, out, rest, stat, up, valid, base=(), pairs=None, earlier=(), turn=0):
    far = not base
    total = q.shape[1] // (2 * HEAD_DIM)
    first, count = pairs or (0, total)
    width = kv.shape[1] // total * count + sum(v.shape[1] for v in earlier)
    return flat_call(
        functools.partial(
            bwd_side_kernel, valid=valid, far=far, first=first, count=count, joined=bool(earlier), turn=turn
        ),
        [q, kv, out, rest, stat, up, *base, *earlier],
        [shape_of(q.shape[0], q.shape[1] // total * count, F32 if far else BF), shape_of(kv.shape[0], width)],
        flops=attention_flops(q, kv, 5, 2), megabytes=21 if count > 2 else 14,
    )


def rows_call(
    kernel, rows, blocked, whole, outs, sums=(), scratch=(), reverse=False, flops=0, megabytes=10, scal=None,
    told=False,
):
    chunk_rows = next(n for n in (384, CHUNK) if rows % n == 0)
    steps = rows // chunk_rows
    order = list(range(steps))
    if reverse:
        order = order[::-1]

    def chunk_of(ref, chunk):
        if isinstance(ref, Incoming):
            return ref.piece(chunk)
        return ref if isinstance(ref, Padded) else ref.at[pl.ds(chunk * chunk_rows, chunk_rows)]

    def run(*refs):
        refs = list(refs)
        take = lambda count: [refs.pop(0) for _ in range(count)]
        head = take(0 if scal is None else 1)
        kept, by_chunk = take(len(whole)), take(len(blocked))
        out, total = take(len(outs)), take(len(sums))
        for n, chunk in enumerate(order):
            kernel(
                n, *(head if told else ()), *[chunk_of(r, chunk) for r in by_chunk], *kept,
                *[chunk_of(r, chunk) for r in out], *total, *refs,
            )
            for r in out:
                push(r, (pl.ds(chunk * chunk_rows, chunk_rows), slice(None)))

    out_shape = []
    for width, kind, *far in outs:
        shape = shape_of(rows, width, kind)
        out_shape.append(Far(shape, steps) if far else shape)
    for shape, kind, *far in sums:
        shape = jax.ShapeDtypeStruct(shape, kind)
        out_shape.append(Far(shape) if far else shape)
    blocked = [Far(v.value, steps, v.by_core) if isinstance(v, Far) else v for v in blocked]
    return flat_call(run, [*whole, *blocked], out_shape, scal, scratch, flops, megabytes)


def tap_weights(first_ref):
    pieces = []
    for tap in range(first_ref.shape[0]):
        rows = first_ref[tap]
        pieces += [rows, jnp.zeros((LANES - rows.shape[0], rows.shape[1]), rows.dtype)]
    return jnp.concatenate(pieces, axis=0)


def mel_windows(scal_ref, mel_ref, mel_rows_ref, windows_ref, halo_ref, valid):
    rows = windows_ref.shape[0]
    channels, frames = mel_ref.shape[1:]
    front = 8
    mel_rows_ref[...] = jnp.zeros_like(mel_rows_ref)
    mel_rows_ref[front : front + frames, :channels] = mel_ref[scal_ref[SCAL_SECTION]].astype(F32).T
    lanes_all = slice(None)
    for core in range(frames // (2 * valid)):

        @pl.when(scal_ref[SCAL_CORE] == core)
        def _():
            base = front + 2 * valid * core
            for n in range(4):
                taken = mel_rows_ref[pl.ds(base + n - 1, rows, stride=2), lanes_all]
                windows_ref[:, n * LANES : (n + 1) * LANES] = taken.astype(BF)
            halo_ref[...] = jnp.zeros_like(halo_ref)
            if core > 0:
                for n in range(3):
                    part = mel_rows_ref[pl.ds(base - 2 + n, 16), lanes_all]
                    first = lax.broadcasted_iota(jnp.int32, part.shape, 0) == 0
                    halo_ref[:, n * LANES : (n + 1) * LANES] = jnp.where(first, part, 0.0).astype(BF)


def stem_fwd_kernel(
    chunk, scal_ref, pos_ref, mel_ref, first_ref, second_ref,
    even_ref, odd_ref, before_ref, ge_ref, go_ref, gs_ref, x_ref, gh_ref, windows_ref, halo_ref,
    carry_ref, mel_rows_ref, *, valid,
):
    first = tap_weights(first_ref)
    if chunk == 0:
        mel_windows(scal_ref, mel_ref, mel_rows_ref, windows_ref, halo_ref, valid)
        push(windows_ref)
        act, slope = gelu_pair(dot_nn(halo_ref[...], first))
        carry_ref[...] = act[:8]
        gh_ref[...] = slope
    span = pl.ds(chunk * even_ref.shape[0], even_ref.shape[0])
    me_ref = windows_ref.at[span, : 3 * LANES]
    mo_ref = windows_ref.at[span, LANES:]

    width = even_ref.shape[1]
    even, slope = gelu_pair(dot_nn(me_ref[...], first))
    even = even.astype(BF)
    even_ref[...] = even
    ge_ref[...] = slope.astype(BF)
    odd, slope = gelu_pair(dot_nn(mo_ref[...], first))
    go_ref[...] = slope.astype(BF)
    row = lax.broadcasted_iota(jnp.int32, odd.shape, 0)
    before = jnp.where(row == 0, carry_ref[0:1, :], pltpu.roll(odd, 1, 0)).astype(BF)
    carry_ref[0:1, :] = odd[odd.shape[0] - 1 :]
    odd = odd.astype(BF)
    odd_ref[...] = odd
    before_ref[...] = before
    pre = dot_nn(before, second_ref[:width])
    pre += dot_nn(even, second_ref[width : 2 * width])
    pre += dot_nn(odd, second_ref[2 * width :])
    act, slope = gelu_pair(pre)
    gs_ref[...] = slope.astype(BF)
    x_ref[...] = act + pos_ref[...]


def qkv_kernel(step, x_ref, gain_ref, bias_ref, own_ref, oth_ref, normed_ref, q_ref, kv_ref):
    unit, _ = norm_stats(x_ref[...].astype(F32))
    normed = (unit * gain_ref[...] + bias_ref[...]).astype(BF)
    normed_ref[...] = normed
    heads = own_ref.shape[1] // (3 * HEAD_DIM)
    for part, w_ref in enumerate((own_ref, oth_ref)):
        packed = dot_nn(normed, w_ref[...]).astype(BF)
        for h in range(heads):
            at, to = h * 3 * HEAD_DIM, part * heads + h
            q_ref[:, to * HEAD_DIM : (to + 1) * HEAD_DIM] = packed[:, at : at + HEAD_DIM]
            kv_ref[:, to * 2 * HEAD_DIM : (to + 1) * 2 * HEAD_DIM] = packed[
                :, at + HEAD_DIM : at + 3 * HEAD_DIM
            ]


def two_parts(rows, own_ref, oth_ref):
    depth = own_ref.shape[0]
    return dot_nn(rows[:, :depth], own_ref[...]) + dot_nn(rows[:, depth:], oth_ref[...])


def two_parts_t(rows, own_ref, oth_ref):
    depth = own_ref.shape[1]
    return dot_nt(rows[:, :depth], own_ref[...]) + dot_nt(rows[:, depth:], oth_ref[...])


def enc_mid_kernel(
    step, x_ref, att_ref, gb_ref, bb_ref, gc_ref, bc_ref, po_ref, pt_ref, uo_ref, ut_ref, do_ref, dt_ref,
    ko_ref, kt_ref,
    x1_ref, x2_ref, normed_ref, hidden_ref, slope_ref, memory_ref, kv_ref,
):
    x1 = x_ref[...] + two_parts(att_ref[...], po_ref, pt_ref)
    x1_ref[...] = x1
    unit, _ = norm_stats(x1)
    normed = (unit * gb_ref[...] + bb_ref[...]).astype(BF)
    normed_ref[...] = normed
    half = uo_ref.shape[1]
    x2 = x1
    for part, (up_ref, down_ref) in enumerate(((uo_ref, do_ref), (ut_ref, dt_ref))):
        act, slope = gelu_pair(dot_nn(normed, up_ref[...]))
        act = act.astype(BF)
        hidden_ref[:, part * half : (part + 1) * half] = act
        slope_ref[:, part * half : (part + 1) * half] = slope.astype(BF)
        x2 = x2 + dot_nn(act, down_ref[...])
    x2_ref[...] = x2
    unit, _ = norm_stats(x2)
    memory = (unit * gc_ref[...] + bc_ref[...]).astype(BF)
    memory_ref[...] = memory
    half = ko_ref.shape[1]
    kv_ref[:, :half] = dot_nn(memory, ko_ref[...]).astype(BF)
    kv_ref[:, half:] = dot_nn(memory, kt_ref[...]).astype(BF)


def dec_mid_kernel(
    step, x_ref, att_ref, gain_ref, bias_ref, po_ref, pt_ref, qo_ref, qt_ref, y_ref, normed_ref, q_ref
):
    y = x_ref[...].astype(F32) + two_parts(att_ref[...], po_ref, pt_ref)
    y_ref[...] = y
    unit, _ = norm_stats(y)
    normed = (unit * gain_ref[...] + bias_ref[...]).astype(BF)
    normed_ref[...] = normed
    half = qo_ref.shape[1]
    q_ref[:, :half] = dot_nn(normed, qo_ref[...]).astype(BF)
    q_ref[:, half:] = dot_nn(normed, qt_ref[...]).astype(BF)


def mlp_back(gb, slope_ref, dpre_ref, uo_ref, ut_ref, do_ref, dt_ref):
    half = uo_ref.shape[1]
    total = 0.0
    for part, (up_ref, down_ref) in enumerate(((uo_ref, do_ref), (ut_ref, dt_ref))):
        span = slice(part * half, (part + 1) * half)
        dpre = (dot_nt(gb, down_ref[...]) * slope_ref[:, span].astype(F32)).astype(BF)
        dpre_ref[:, span] = dpre
        total = total + dot_nt(dpre, up_ref[...])
    return total


def section_halves(scal_ref, value, mine_ref, sent_ref):
    rows, half = mine_ref.shape
    left, right = value[:rows, :half], value[:rows, half:]
    lower = scal_ref[SCAL_SECTION] == 0
    mine_ref[...] = jnp.where(lower, left, right).astype(mine_ref.dtype)
    sent_ref[...] = jnp.where(lower, right, left).astype(sent_ref.dtype)


def owners_kernel(scal_ref, *refs):
    count = len(refs) // 3
    section = scal_ref[SCAL_SECTION]
    for mine_ref, got_ref, out_ref in zip(refs[:count], refs[count : 2 * count], refs[2 * count :]):
        out_ref[section] = mine_ref[...]
        out_ref[1 - section] = got_ref[...].astype(out_ref.dtype)


def dec_top_kernel(
    scal_ref, y1_ref, crossed_ref, cot_ref, gain_ref, bias_ref, po_ref, pt_ref, uo_ref, ut_ref,
    do_ref, dt_ref,
    decoded_ref, sent_ref, normed_ref, hidden_ref, dpre_ref, gb3_ref, gb2_ref, dcrossed_ref, u2_ref,
    sums_ref, slope_ref, *, valid,
):
    rows = y1_ref.shape[0]
    y2 = y1_ref[...] + two_parts(crossed_ref[...], po_ref, pt_ref)
    unit, inverse = norm_stats(y2)
    normed = (unit * gain_ref[...] + bias_ref[...]).astype(BF)
    normed_ref[...] = normed
    push(normed_ref)
    half = uo_ref.shape[1]
    y3 = y2
    for part, (up_ref, down_ref) in enumerate(((uo_ref, do_ref), (ut_ref, dt_ref))):
        act, slope = gelu_pair(dot_nn(normed, up_ref[...]))
        act = act.astype(BF)
        hidden_ref[:, part * half : (part + 1) * half] = act
        slope_ref[:, part * half : (part + 1) * half] = slope.astype(BF)
        y3 = y3 + dot_nn(act, down_ref[...])
    push(hidden_ref)
    row = lax.broadcasted_iota(jnp.int32, y2.shape, 0)
    length = scal_ref[SCAL_LENGTHS + scal_ref[SCAL_SECTION]]
    live = ((row < valid) & (row + scal_ref[SCAL_CORE] * valid < length)).astype(F32)
    section_halves(scal_ref, y3 * live, decoded_ref, sent_ref)
    u3 = cot_ref[...].astype(F32) * live
    gb3 = u3.astype(BF)
    gb3_ref[...] = gb3
    push(gb3_ref)
    dnormed = mlp_back(gb3, slope_ref, dpre_ref, uo_ref, ut_ref, do_ref, dt_ref)
    push(dpre_ref)
    dy, dgain, dbias = norm_back(unit, inverse, gain_ref[...], dnormed)
    u2 = u3 + dy
    u2_ref[...] = u2
    gb2 = u2.astype(BF)
    gb2_ref[...] = gb2
    push(gb2_ref)
    half = po_ref.shape[0]
    dcrossed_ref[:, :half] = dot_nt(gb2, po_ref[...]).astype(BF)
    dcrossed_ref[:, half:] = dot_nt(gb2, pt_ref[...]).astype(BF)
    sums_ref[...] = jnp.zeros_like(sums_ref)
    sums_ref[0:1, :] = dgain
    sums_ref[1:2, :] = dbias


def dec_back_kernel(
    step, dq_ref, y1_ref, u2_ref, gain_ref, qo_ref, qt_ref, po_ref, pt_ref,
    u1_ref, gb1_ref, datt_ref, sums_ref,
):
    dnormed = two_parts_t(dq_ref[...], qo_ref, qt_ref)
    unit, inverse = norm_stats(y1_ref[...])
    dy, dgain, dbias = norm_back(unit, inverse, gain_ref[...], dnormed)
    u1 = u2_ref[...] + dy
    u1_ref[...] = u1
    gb1 = u1.astype(BF)
    gb1_ref[...] = gb1
    half = po_ref.shape[0]
    datt_ref[:, :half] = dot_nt(gb1, po_ref[...]).astype(BF)
    datt_ref[:, half:] = dot_nt(gb1, pt_ref[...]).astype(BF)
    sums_ref[...] = jnp.zeros_like(sums_ref)
    sums_ref[0:1, :] = dgain
    sums_ref[1:2, :] = dbias


def packed_back(dq_ref, dkl_ref, dkr_ref, own_ref, oth_ref, out_ref):
    dkv = (dkl_ref[...].astype(F32) + dkr_ref[...].astype(F32)).astype(BF)
    dq = dq_ref[...]
    heads = own_ref.shape[1] // (3 * HEAD_DIM)
    total = 0.0
    for part, w_ref in enumerate((own_ref, oth_ref)):
        pieces = []
        for h in range(part * heads, (part + 1) * heads):
            pieces.append(dq[:, h * HEAD_DIM : (h + 1) * HEAD_DIM])
            pieces.append(dkv[:, h * 2 * HEAD_DIM : (h + 1) * 2 * HEAD_DIM])
        packed = jnp.concatenate(pieces, axis=1)
        out_ref[:, part * w_ref.shape[1] : (part + 1) * w_ref.shape[1]] = packed
        total = total + dot_nt(packed, w_ref[...])
    return total


def dec_last_kernel(
    step, scal_ref, dq_ref, dkl_ref, dkr_ref, x_ref, u1_ref, gain_ref, own_ref, oth_ref,
    packed_ref, sums_ref, mine_ref, sent_ref,
):
    dnormed = packed_back(dq_ref, dkl_ref, dkr_ref, own_ref, oth_ref, packed_ref)
    unit, inverse = norm_stats(x_ref[...].astype(F32))
    dx, dgain, dbias = norm_back(unit, inverse, gain_ref[...], dnormed)
    section_halves(scal_ref, u1_ref[...] + dx, mine_ref, sent_ref)
    sums_ref[...] = jnp.zeros_like(sums_ref)
    sums_ref[0:1, :] = dgain
    sums_ref[1:2, :] = dbias


def enc_back_kernel(
    step, gl_ref, gr_ref, x2_ref, x1_ref, slope_ref, gc_ref, gb_ref, ko_ref, kt_ref, uo_ref, ut_ref,
    do_ref, dt_ref, po_ref, pt_ref,
    gkv_ref, gb2_ref, dpre_ref, gb1_ref, datt_ref, u1_ref, sums_ref,
):
    if step == 0:
        sums_ref[...] = jnp.zeros_like(sums_ref)

    gkv = (gl_ref[...].astype(F32) + gr_ref[...].astype(F32)).astype(BF)
    gkv_ref[...] = gkv
    dmemory = two_parts_t(gkv, ko_ref, kt_ref)
    unit, inverse = norm_stats(x2_ref[...])
    u2, dgain, dbias = norm_back(unit, inverse, gc_ref[...], dmemory)
    sums_ref[0:1, :] += dgain
    sums_ref[1:2, :] += dbias
    gb2 = u2.astype(BF)
    gb2_ref[...] = gb2
    dnormed = mlp_back(gb2, slope_ref, dpre_ref, uo_ref, ut_ref, do_ref, dt_ref)
    unit, inverse = norm_stats(x1_ref[...])
    dx, dgain, dbias = norm_back(unit, inverse, gb_ref[...], dnormed)
    sums_ref[2:3, :] += dgain
    sums_ref[3:4, :] += dbias
    u1 = u2 + dx
    u1_ref[...] = u1
    gb1 = u1.astype(BF)
    gb1_ref[...] = gb1
    half = po_ref.shape[0]
    datt_ref[:, :half] = dot_nt(gb1, po_ref[...]).astype(BF)
    datt_ref[:, half:] = dot_nt(gb1, pt_ref[...]).astype(BF)


def stem_back_kernel(
    step, dq_ref, dkl_ref, dkr_ref, x0_ref, u1_ref, ge_ref, go_ref, gs_ref, gain_ref, own_ref, oth_ref,
    second_ref, gh_ref,
    packed_ref, g2_ref, ede_ref, edo_ref, sums_ref, edh_ref, carry_ref,
):
    if step == 0:
        sums_ref[...] = jnp.zeros_like(sums_ref)
        carry_ref[...] = jnp.zeros_like(carry_ref)

    dnormed = packed_back(dq_ref, dkl_ref, dkr_ref, own_ref, oth_ref, packed_ref)
    unit, inverse = norm_stats(x0_ref[...])
    dx, dgain, dbias = norm_back(unit, inverse, gain_ref[...], dnormed)
    sums_ref[0:1, :] += dgain
    sums_ref[1:2, :] += dbias
    g2 = ((u1_ref[...] + dx) * gs_ref[...].astype(F32)).astype(BF)
    g2_ref[...] = g2
    width = g2.shape[1]
    before = dot_nt(g2, second_ref[:width])
    even = dot_nt(g2, second_ref[width : 2 * width])
    odd = dot_nt(g2, second_ref[2 * width :])
    ede_ref[...] = (even * ge_ref[...].astype(F32)).astype(BF)
    row = lax.broadcasted_iota(jnp.int32, before.shape, 0)
    later = jnp.where(
        row == before.shape[0] - 1, carry_ref[0:1, :], pltpu.roll(before, before.shape[0] - 1, 0)
    )
    carry_ref[0:1, :] = before[0:1]
    edo_ref[...] = ((odd + later) * go_ref[...].astype(F32)).astype(BF)
    front = lax.broadcasted_iota(jnp.int32, edh_ref.shape, 0)
    edh_ref[...] = jnp.where(front == 0, before[0:1] * gh_ref[...], 0.0).astype(BF)


SCAL_CORE, SCAL_SECTION, SCAL_X, SCAL_Z, SCAL_Z_LOW, SCAL_Z_HIGH, SCAL_LENGTHS = range(7)
TILE = 512


def gradient_tiles(left, right_ref, own_ref, oth_ref, at):
    turned, half = left.T, right_ref.shape[1] // 2
    for part, out_ref in enumerate((own_ref, oth_ref)):
        for first in range(0, half, TILE):
            width = min(TILE, half - first)
            piece = dot_nn(turned, right_ref[:, part * half + first : part * half + first + width])
            out_ref[:, at + first : at + first + width] = piece.astype(BF)
    return at + half


def gradients_kernel(*refs):
    *pairs, own_ref, oth_ref = refs
    at = 0
    for left_ref, right_ref in zip(pairs[::2], pairs[1::2]):
        at = gradient_tiles(left_ref[...], right_ref, own_ref, oth_ref, at)


def gradients(pairs, held=()):
    columns = sum(right.shape[1] // 2 for _, right in pairs)
    width = pairs[0][0].shape[1]
    return flat_call(
        gradients_kernel,
        [Far(v) if any(v is h for h in held) else v for pair in pairs for v in pair],
        [shape_of(width, columns)] * 2,
        flops=sum(2 * left.size * right.shape[1] for left, right in pairs), megabytes=9,
    )


def late_kernel(
    scal_ref, normed_ref, packed_ref, g2_ref, before_ref, even_ref, odd_ref, ede_ref, edo_ref, edh_ref,
    windows_ref, mh_ref, va_ref, vb_ref, vc_ref, ve_ref, vf_ref, own_ref, oth_ref, own_stem_ref, oth_stem_ref, stem_ref, *,
    channels,
):
    gradient_tiles(normed_ref[...], packed_ref, own_ref, oth_ref, 0)
    turned, width = g2_ref[...].T, g2_ref.shape[1]
    for n, ref in enumerate((before_ref, even_ref, odd_ref)):
        stem_ref[:, n * width : (n + 1) * width] = dot_nn(turned, ref[...]).astype(BF)
    windows = windows_ref[...].T
    first = dot_nn(windows[: 3 * LANES], ede_ref[...]) + dot_nn(windows[LANES:], edo_ref[...])
    first = first + dot_nn(mh_ref[...].T, edh_ref[...])
    vectors = [
        vf_ref[0:1], ve_ref[2:3], ve_ref[0:1], vf_ref[1:2], ve_ref[3:4], ve_ref[1:2],
        va_ref[0:1], vb_ref[0:1], vc_ref[0:1], va_ref[1:2], vb_ref[1:2], vc_ref[1:2],
        jnp.zeros((4, width), F32),
    ]
    taps = [first[n * LANES : n * LANES + channels] for n in range(first.shape[0] // LANES)]
    first = jnp.concatenate([*taps, jnp.concatenate(vectors, axis=0)], axis=0)
    stem_ref[:, 3 * width :] = first.T.astype(BF)
    core, half = scal_ref[SCAL_CORE], stem_ref.shape[1] // 2
    block = 16
    groups = width // (4 * block)
    for part, out_ref in enumerate((own_stem_ref, oth_stem_ref)):
        bit = core if part == 0 else 1 - core
        for group in range(groups):
            for section in range(2):
                source = pl.multiple_of(group * 4 * block + bit * 2 * block + section * block, block)
                rows = stem_ref[pl.ds(source, block), :]
                to = (section * groups + group) * 2 * block
                out_ref[to : to + block, :] = rows[:, :half]
                out_ref[to + block : to + 2 * block, :] = rows[:, half:]


def halves(scal_ref, bit, groups, size, total, keep_ref, send_ref, columns=slice(None)):
    for group in range(groups):
        for place, out_ref in ((scal_ref[bit], keep_ref), (1 - scal_ref[bit], send_ref)):
            source = pl.ds(pl.multiple_of((group * 2 + place) * size, size), size)
            out_ref[group * size : (group + 1) * size, columns] = total(source)


def first_kernel(scal_ref, *refs, cut, block):
    *parts, am_ref, as_ref, bm_ref, bg_ref = refs
    if len(parts) == 2:
        parts = [ref.at[:, span] for ref in parts for span in (slice(0, cut), slice(cut, None))]
        parts = [parts[0], parts[2], parts[1], parts[3]]
    low_own, low_got, high_own, high_got = parts
    low = lambda rows: low_own[rows, :] + low_got[rows, :]
    high = lambda rows: high_own[rows, :] + high_got[rows, :]
    rows = low_own.shape[0]
    halves(scal_ref, SCAL_X, rows // (2 * block), block, low, am_ref, as_ref)
    halves(scal_ref, SCAL_SECTION, 1, rows // 2, high, bm_ref, bg_ref)


def second_kernel(
    scal_ref, am_ref, ag_ref, bm_ref, bg_ref, akeep_ref, asend_ref, bkeep_ref, bsend_ref, *, block
):
    low = lambda rows: am_ref[rows, :] + ag_ref[rows, :]
    high = lambda rows: bm_ref[rows, :] + bg_ref[rows, :]
    rows = am_ref.shape[0]
    halves(scal_ref, SCAL_SECTION, 1, rows // 2, low, akeep_ref, asend_ref)
    halves(scal_ref, SCAL_X, rows // (2 * block), block, high, bkeep_ref, bsend_ref)


def third_kernel(scal_ref, am_ref, ag_ref, bm_ref, bg_ref, *out_refs, cut, block):
    for flip, out_ref in enumerate(out_refs):
        rows = pl.ds(pl.multiple_of((scal_ref[SCAL_Z] ^ flip) * block, block), block)
        out_ref[:, :cut] = am_ref[rows, :] + ag_ref[rows, :]
        out_ref[:, cut:] = bm_ref[rows, :] + bg_ref[rows, :]


def third_half_kernel(scal_ref, am_ref, ag_ref, bm_ref, bg_ref, keep_ref, send_ref, *, cut, block):
    low = lambda rows: am_ref[rows, :] + ag_ref[rows, :]
    high = lambda rows: bm_ref[rows, :] + bg_ref[rows, :]
    groups = am_ref.shape[0] // (2 * block)
    halves(scal_ref, SCAL_Z_LOW, groups, block, low, keep_ref, send_ref, slice(0, cut))
    halves(scal_ref, SCAL_Z_LOW, groups, block, high, keep_ref, send_ref, slice(cut, None))


def fourth_half_kernel(scal_ref, mine_ref, got_ref, keep_ref, send_ref, *, block):
    both = lambda rows: mine_ref[rows, :] + got_ref[rows, :]
    halves(scal_ref, SCAL_Z_HIGH, 1, block, both, keep_ref, send_ref)


def last_kernel(*refs, widths):
    count = len(refs) - len(widths)
    at = 0
    for out_ref, width in zip(refs[count:], widths):
        total = sum(ref[:, at : at + width].astype(F32) for ref in refs[:count])
        out_ref[...] = total
        at += width


def stem_last_kernel(scal_ref, mine_ref, got_ref, second_ref, first_ref, *vec_refs):
    mine, got = mine_ref[...], got_ref[...]
    lower = scal_ref[SCAL_SECTION] == 0
    block = mine.shape[0] // 2
    parts = []
    for half in (jnp.where(lower, mine, got), jnp.where(lower, got, mine)):
        parts.append(jnp.concatenate([half[:block], half[block:]], axis=1))
    full = jnp.concatenate(parts, axis=0)
    count, _, width = second_ref.shape
    channels = first_ref.shape[2]
    for n in range(count):
        second_ref[n] = full[:, n * width : (n + 1) * width]
        first_ref[n] = full[:, count * width + n * channels : count * width + (n + 1) * channels]
    turned = full[:, full.shape[1] - 2 * HEAD_DIM :].T
    at = turned.shape[0] - 16
    for n, ref in enumerate(vec_refs):
        ref[...] = turned[at + 3 * n : at + 3 * n + 3]


def sum_over_chips(own, oth, scal, cut, widths, direct=False):
    after = lambda value, other: value if other is None else tie(value, other)
    if not isinstance(own, tuple):
        own, oth = (own,), (oth,)
    parts = [v for mine, other in zip(own, oth) for v in (mine, swap(other, "tensor"))]
    rows, columns = own[0].shape[0], sum(v.shape[1] for v in own)
    block = rows // (2 * lax.axis_size("dp"))
    some = lambda n, w: shape_of(n, w)
    left, right = cut, columns - cut
    am, asend, bm, bsend = flat_call(
        functools.partial(first_kernel, cut=cut, block=block), parts,
        [some(rows // 2, left)] * 2 + [some(rows // 2, right)] * 2, scal, megabytes=6,
    )
    am = after(am, (yield am))
    ag, bg = flip_bit(asend, "dp", 1), swap(bsend, "section")
    am, asend, bm, bsend = flat_call(
        functools.partial(second_kernel, block=block), [am, ag, bm, bg],
        [some(rows // 4, left)] * 2 + [some(rows // 4, right)] * 2, scal, megabytes=6,
    )
    am = after(am, (yield am))
    ag, bg = swap(asend, "section"), flip_bit(bsend, "dp", 1)
    if direct:
        mine, *send = flat_call(
            functools.partial(third_kernel, cut=cut, block=block), [am, ag, bm, bg],
            [some(block, columns)] * (rows // (4 * block)), scal, megabytes=6,
        )
        mine = after(mine, (yield mine))
        got = [flip_bit(v, "dp", 2 * (n + 1)) for n, v in enumerate(send)]
    else:
        mine, send = flat_call(
            functools.partial(third_half_kernel, cut=cut, block=block), [am, ag, bm, bg],
            [some(2 * block, columns)] * 2, scal, megabytes=6,
        )
        mine = after(mine, (yield mine))
        mine, send = flat_call(
            functools.partial(fourth_half_kernel, block=block), [mine, flip_bit(send, "dp", 2)],
            [some(block, columns)] * 2, scal, megabytes=6,
        )
        mine = after(mine, (yield mine))
        got = [flip_bit(send, "dp", 4)]
    yield flat_call(
        functools.partial(last_kernel, widths=widths), [mine, *got],
        [shape_of(block, width, F32) for width in widths], megabytes=6,
    )


def tie(value, *others):
    return lax.optimization_barrier((value, *others))[0]


def swap(value, axis):
    return lax.ppermute(value, axis, [(0, 1), (1, 0)])


def flip_bit(value, axis, bit):
    count = lax.axis_size(axis)
    return lax.ppermute(value, axis, [(i, i ^ bit) for i in range(count)])


def add_low(left, right):
    return (left.astype(F32) + right.astype(F32)).astype(BF)


def halve(value, dim, place, send):
    mine = lax.dynamic_index_in_dim(value, place, dim, keepdims=False)
    other = lax.dynamic_index_in_dim(value, 1 - place, dim, keepdims=False)
    return mine, send(other)


def reduce_blocks(value, names):
    section, clip_group = lax.axis_index("section"), lax.axis_index("dp")
    dims = list(names)
    order = [name for name, _ in sorted(names.items(), key=lambda item: item[1])]
    held = value
    for step, name in enumerate(order):
        dim = [n for n in dims if n in order[step:]].index(name)
        if name == "section":
            mine, got = halve(held, dim, section, functools.partial(swap, axis="section"))
        else:
            place = (clip_group // name) % 2
            mine, got = halve(held, dim, place, functools.partial(flip_bit, axis="dp", bit=name))
        held = mine.astype(F32) + got.astype(F32)
        if step < len(order) - 1:
            held = held.astype(BF)
    return held


def dp_bits():
    count, bits = lax.axis_size("dp"), []
    while count > 1:
        count //= 2
        bits.append(count)
    return bits


def sum_projections(value):
    rows, columns = value.shape
    bits = dp_bits()
    lead = (2,) * (1 + len(bits))
    half = columns // 256 * 128
    out = []
    for which, part in enumerate((value[:, :half], value[:, half:])):
        shaped = part.reshape(*lead, rows // 2 ** len(lead), part.shape[1])
        early = {"section": 1, bits[-1]: 0} if which == 0 else {"section": 0, bits[-1]: 1}
        names = {"section": early["section"]}
        for at, bit in enumerate(bits):
            names[bit] = early.get(bit, 2 + at)
        out.append(reduce_blocks(shaped, names))
    return jnp.concatenate(out, axis=1)


def sum_stem(value):
    rows, columns = value.shape
    bits = dp_bits()
    place = lax.axis_index("tensor")
    groups = 2 ** len(bits)
    block = rows // (groups * 2)
    shaped = value.reshape(groups, 2, block, columns)
    mine, got = halve(shaped, 1, place, functools.partial(swap, axis="tensor"))
    held = add_low(mine, got)
    half = columns // 256 * 128
    out = []
    for which, part in enumerate((held[:, :, :half], held[:, :, half:])):
        shaped = part.reshape(*((2,) * len(bits)), 2, block // 2, part.shape[2])
        names = {bit: 2 + at for at, bit in enumerate(bits)}
        names[bits[-1]] = which
        names["section"] = 1 - which
        out.append(reduce_blocks(shaped, names))
    mine = jnp.concatenate(out, axis=1)
    got = swap(mine, "section")
    first = lax.axis_index("section") == 0
    return jnp.concatenate(
        [jnp.where(first, mine, got), jnp.where(first, got, mine)], axis=0
    )


def core_sum(pairs):
    full = [dot_tn(left, right).astype(BF) for left, right in pairs]
    mine = jnp.concatenate([v[:, : v.shape[1] // 2] for v in full], axis=1)
    sent = jnp.concatenate([v[:, v.shape[1] // 2 :] for v in full], axis=1)
    return add_low(mine, swap(sent, "tensor"))


def sinusoid_table(count, width_all):
    step_size = math.log(10000.0) / (width_all // 2 - 1)
    rates = np.exp(-step_size * np.arange(width_all // 2))
    angles = np.arange(count)[:, None] * rates[None, :]
    return np.concatenate([np.sin(angles), np.cos(angles)], axis=1).astype(np.float32)


def pad_rows(value, rows):
    return jnp.pad(value, ((0, rows - value.shape[0]), (0, 0)))


def round_up(count):
    return -(-count // CHUNK) * CHUNK


def body(
    mel,
    conv_first,
    conv_second,
    enc_gain,
    enc_shift,
    enc_qkv,
    enc_proj,
    enc_up,
    enc_down,
    cross_kv,
    text,
    lengths,
    dec_gain,
    dec_shift,
    dec_qkv,
    dec_proj,
    cross_query,
    cross_proj,
    dec_up,
    dec_down,
    cotangent,
):
    section = lax.axis_index("section")
    place = lax.axis_index("tensor")
    cores = lax.axis_size("tensor")
    width = text.shape[2]
    frames = mel.shape[1] // 2
    valid = frames // cores
    rows = round_up(valid)
    slots = text.shape[1]
    text_rows = round_up(slots)
    channels = mel.shape[2]

    group = lax.axis_index("dp")
    bits = [place, section, group % 2, group // 2, group // 2 % 2, group // 4 % 2]
    scal = jnp.concatenate([jnp.stack([bit.astype(jnp.int32) for bit in bits]), lengths])
    pair = lambda w: (w, swap(w, "tensor"))
    w_dqkv, w_eqkv, w_eproj, w_dproj, w_cq = map(pair, (dec_qkv, enc_qkv, enc_proj, dec_proj, cross_query))
    w_eup, w_edown, w_ckv = map(pair, (enc_up, enc_down, cross_kv))
    w_cproj, w_dup, w_ddown = map(pair, (cross_proj, dec_up, dec_down))
    early = [w[1] for w in (w_eproj, w_dproj, w_cq, w_cproj)]
    late = [w[1] for w in (w_eup, w_edown, w_ckv, w_dup, w_ddown)]
    eg, es = [enc_gain[i : i + 1] for i in range(3)], [enc_shift[i : i + 1] for i in range(3)]
    dg, ds = [dec_gain[i : i + 1] for i in range(3)], [dec_shift[i : i + 1] for i in range(3)]

    taps = conv_first.shape[0] * channels
    depth = -(-(taps + 12) // LANES) * LANES
    second = conv_second.reshape(-1, width)
    table = np.pad(sinusoid_table(frames, width), ((0, rows - valid), (0, 0)))
    table = jnp.asarray(np.stack([table[valid * core : valid * core + rows] for core in range(cores)]))

    dn_a, dq_self, dkv_self = rows_call(
        qkv_kernel, text_rows, [Clip(text)], [dg[0], ds[0], *w_dqkv],
        [(width, BF, Far), (width, BF), (2 * width, BF)], flops=2 * text_rows * width * 3 * width, scal=scal,
    )
    dkv_self_r = swap(dkv_self, "tensor")

    mel_rows = 2 * frames + 8 + 2 * (rows - valid) + 16
    even, odd, before, ge, go, gs, x0, gh, windows, halo = rows_call(
        functools.partial(stem_fwd_kernel, valid=valid), rows, [Far(table, 1, True)],
        [Far(jnp.swapaxes(mel, 1, 2)), Far(conv_first), Far(second)],
        [(width, BF, Far)] * 6 + [(width, F32)],
        sums=[((16, width), F32), ((rows, 4 * LANES), BF, Far), ((16, 3 * LANES), BF)],
        scratch=[pltpu.VMEM((8, width), F32), pltpu.VMEM((mel_rows, LANES), F32)],
        flops=2 * rows * width * 2000, scal=scal, told=True, megabytes=14,
    )
    en_a, eq, ekv = rows_call(
        qkv_kernel, rows, [tie(x0, dq_self, *early)], [eg[0], es[0], *w_eqkv],
        [(width, BF, Far), (width, BF), (2 * width, BF)], flops=2 * rows * width * 3 * width,
    )
    ekv_r = swap(ekv, "tensor")

    datt, drest, dstat = attention_fwd(dq_self, dkv_self, dkv_self_r, slots, scal)
    eq = tie(eq, datt)
    eatt, erest, estat = attention_fwd(eq, ekv, ekv_r, valid)
    units = 2 * enc_up.shape[1]
    x1, x2, en_b, ehid, eslope, memory, ckv = rows_call(
        enc_mid_kernel, rows, [x0, tie(eatt, *late)],
        [eg[1], es[1], eg[2], es[2], *w_eproj, *w_eup, *w_edown, *w_ckv],
        [
            (width, F32, Far), (width, F32, Far), (width, BF, Far), (units, BF, Far), (units, BF, Far),
            (width, BF, Far), (2 * width, BF),
        ],
        flops=2 * rows * width * (3 * width + 2 * units), megabytes=20,
    )
    ckv_r = swap(ckv, "tensor")
    y1, dn_b, cq = rows_call(
        dec_mid_kernel, text_rows, [Clip(text), tie(datt, ckv)], [dg[1], ds[1], *w_dproj, *w_cq],
        [(width, F32), (width, BF, Far), (width, BF)], flops=2 * text_rows * width * 2 * width, scal=scal,
    )

    crossed, crest, cstat = attention_fwd(cq, ckv, ckv_r, valid)
    dec_units = 2 * dec_up.shape[1]
    top_outs = [
        (width, BF), (dec_units, BF), (dec_units, BF), (width, BF), (width, BF), (width, BF), (width, F32),
    ]
    owned = lambda kind: shape_of(slots, width // 2, kind)
    decoded, decoded_sent, dn_c, dhid, dpre, dgb3, dgb2, dcrossed, u2, sums_c = flat_call(
        functools.partial(dec_top_kernel, valid=slots),
        [y1, crossed, Clip(cotangent), dg[2], ds[2], *w_cproj, *w_dup, *w_ddown],
        [owned(BF), owned(BF)] + [shape_of(text_rows, w, k) for w, k in top_outs] + [shape_of(8, width, F32)],
        scal=scal, scratch=[pltpu.VMEM((text_rows, dec_units), BF)],
        flops=2 * text_rows * width * (2 * width + 4 * dec_units), megabytes=12,
    )
    decoded_got = swap(decoded_sent, "section")
    fast = lax.axis_size("dp") == 8 and width % (4 * 8 * 16) == 0
    top_pairs = [(dn_c, dpre), (dgb3, dhid), (dgb2, crossed)]
    top_widths = [dec_up.shape[1], dec_down.shape[0], cross_proj.shape[0]]
    if fast:
        own, oth = gradients(top_pairs)
        top_steps = sum_over_chips(own, oth, scal, sum(top_widths) // 2, top_widths)
        dcrossed = tie(dcrossed, own)
    dcq, dckv, dckv_r = attention_bwd(cq, ckv, ckv_r, crossed, crest, cstat, dcrossed, valid)
    if fast:
        dcq = tie(dcq, next(top_steps))
    dckv_got = swap(dckv_r, "tensor")
    u1, dgb1, ddatt, sums_b = rows_call(
        dec_back_kernel, text_rows, [dcq, y1, u2], [dg[1], *w_cq, *w_dproj],
        [(width, F32), (width, BF, Far), (width, BF)], sums=[((8, width), F32)],
        flops=2 * text_rows * width * 2 * width,
    )
    dqs, dkvs, dkvs_r = attention_bwd(
        dq_self, dkv_self, dkv_self_r, datt, drest, dstat, ddatt, slots, scal
    )
    dkvs_got = swap(dkvs_r, "tensor")

    gkv, egb2, edpre, egb1, deatt, eu1, sums_e = rows_call(
        enc_back_kernel, rows, [tie(dckv, dqs), dckv_got, x2, x1, eslope],
        [eg[2], eg[1], *w_ckv, *w_eup, *w_edown, *w_eproj],
        [(2 * width, BF), (width, BF), (units, BF, Far), (width, BF), (width, BF), (width, F32, Far)],
        sums=[((8, width), F32)], flops=2 * rows * width * (3 * width + 2 * units), megabytes=13,
    )
    d_packed, sums_a, text_mine, text_sent = rows_call(
        dec_last_kernel, text_rows, [dqs, dkvs, dkvs_got, Clip(text), tie(u1, deatt)], [dg[0], *w_dqkv],
        [(2 * dec_qkv.shape[1], BF)],
        sums=[((8, width), F32), ((slots, width // 2), F32), ((slots, width // 2), BF)],
        flops=2 * text_rows * width * 3 * width, scal=scal, told=True,
    )
    text_got = swap(text_sent, "section")
    mid_pairs = [
        (dn_a, d_packed), (dn_b, dcq), (dgb1, datt), (egb1, eatt), (memory, gkv), (en_b, edpre), (egb2, ehid),
    ]
    mid_widths = [dec_qkv.shape[1], cross_query.shape[1], dec_proj.shape[0], enc_proj.shape[0]]
    mid_widths += [cross_kv.shape[1], enc_up.shape[1], enc_down.shape[0]]
    if fast:
        mid_pairs[0] = (dn_a, tie(d_packed, top_steps.send(d_packed)))
        own, oth = gradients(mid_pairs, [memory, en_b, edpre, ehid])
        mid_steps = sum_over_chips(own, oth, scal, sum(mid_widths) // 2, mid_widths)
        waits = [
            lambda: (own,), lambda: (top_steps.send(base_a),), lambda: (next(mid_steps),)
        ]
    else:
        waits = [lambda: ()] * 3

    pairs = width // (2 * HEAD_DIM)
    half = pairs // 2
    deatt = tie(deatt, *waits[0]())
    side = (eatt, erest, estat)
    base_a, dekv_a = attention_bwd_side(
        eq, ekv_r, *side, deatt, valid, pairs=(half + 1, pairs - 1)
    )
    deatt = tie(deatt, base_a, *waits[1]())
    base_b, dekv_r = attention_bwd_side(
        eq, ekv_r, *side, deatt, valid, pairs=(half, 1), earlier=(dekv_a,)
    )
    dekv_got = swap(dekv_r, "tensor")
    deatt = tie(deatt, base_b, *waits[2]())
    deq, dekv = attention_bwd_side(eq, ekv, *side, deatt, valid, (base_a, base_b), turn=half + 1)
    e_packed, g2, ede, edo, sums_f, edh = rows_call(
        stem_back_kernel, rows, [deq, dekv, dekv_got, x0, eu1, ge, go, gs],
        [eg[0], *w_eqkv, second, gh],
        [(2 * enc_qkv.shape[1], BF), (width, BF), (width, BF), (width, BF)],
        sums=[((8, width), F32), ((16, width), BF)], scratch=[pltpu.VMEM((8, width), F32)],
        reverse=True, flops=2 * rows * width * 6 * width,
    )
    sums, end = [sums_a, sums_b, sums_c, sums_e, sums_f], ()
    if fast:
        stem_width = 3 * width + depth
        late_columns = (enc_qkv.shape[1], enc_qkv.shape[1], stem_width // 2, stem_width // 2)
        own, oth, own_stem, oth_stem = flat_call(
            functools.partial(late_kernel, channels=channels),
            [
                en_a, tie(e_packed, top_steps.send(e_packed)), g2, before, even, odd, ede, edo, edh, windows, halo,
                *sums,
            ],
            [shape_of(width, columns) for columns in late_columns], scal=scal, scratch=[pltpu.VMEM((width, stem_width), BF)],
            flops=2 * rows * width * (3 * width + 3 * width + 2 * depth), megabytes=10,
        )
        own = tie(own, mid_steps.send(own))
        late_steps = sum_over_chips(
            (own, own_stem), (oth, oth_stem), scal, enc_qkv.shape[1], [enc_qkv.shape[1], stem_width // 2], True
        )
        top_sums = top_steps.send(next(late_steps))
        later = mid_steps.send(top_sums[0])
        later = mid_steps.send(late_steps.send(later))
        later = late_steps.send(later)
        end = (later,)
        mid_sums = mid_steps.send(later)
        late_qkv, stem = late_steps.send(mid_sums[0])
        block = 2 * width // (2 * lax.axis_size("dp") * cores)
        conv_second_grad, conv_first_grad, *vec = flat_call(
            stem_last_kernel, [stem, swap(stem, "section")],
            [
                jax.ShapeDtypeStruct((conv_second.shape[0], block, width), F32),
                jax.ShapeDtypeStruct((conv_first.shape[0], block, channels), F32),
            ] + [shape_of(3, block, F32)] * 4,
            scal=scal, megabytes=6,
        )
        conv_second_grad = conv_second_grad.transpose(0, 2, 1)
        conv_first_grad = conv_first_grad.transpose(0, 2, 1)
    else:
        cuts = lambda value, widths: jnp.split(value, list(np.cumsum(widths)[:-1]), axis=1)
        top_sums = cuts(sum_projections(core_sum(top_pairs)), top_widths)
        mid_sums = cuts(sum_projections(core_sum(mid_pairs)), mid_widths)
        late_qkv = sum_projections(core_sum([(en_a, e_packed)]))
        first_t = dot_tn(ede, windows[:, : 3 * LANES]) + dot_tn(edo, windows[:, LANES:]) + dot_tn(edh, halo)
        first_t = first_t.reshape(width, -1, LANES)[:, :, :channels].reshape(width, taps)
        vectors = jnp.concatenate(
            [
                sums_f[0:1], sums_e[2:3], sums_e[0:1], sums_f[1:2], sums_e[3:4], sums_e[1:2],
                sums_a[0:1], sums_b[0:1], sums_c[0:1], sums_a[1:2], sums_b[1:2], sums_c[1:2],
            ],
            axis=0,
        )
        stem = [dot_tn(g2, act) for act in (before, even, odd)] + [first_t, vectors.T]
        stem.append(jnp.zeros((width, depth - taps - vectors.shape[0]), F32))
        stem = sum_stem(jnp.concatenate([v.astype(BF) for v in stem], axis=1)).T
        conv_second_grad, conv_first_grad = stem[: 3 * width], stem[3 * width : 3 * width + taps]
        vec = [stem[3 * width + taps + 3 * n : 3 * width + taps + 3 * n + 3] for n in range(4)]

    owned = [jax.ShapeDtypeStruct((2, *text_mine.shape), kind) for kind in (BF, F32)]
    decoded, text_grad = flat_call(
        owners_kernel, [decoded, tie(text_mine, *end), decoded_got, text_got], owned, scal=scal, megabytes=4
    )

    d_up, d_down_t, d_cproj_t = top_sums
    d_qkv, d_cq, d_proj_t, e_proj_t, e_kv, e_up, e_down_t = mid_sums
    return (
        decoded,
        text_grad,
        conv_first_grad.reshape(*conv_first.shape[:2], -1),
        conv_second_grad.reshape(*conv_second.shape[:2], -1),
        vec[0],
        vec[1],
        late_qkv,
        e_proj_t.T,
        e_up,
        e_down_t.T,
        e_kv,
        vec[2],
        vec[3],
        d_qkv,
        d_proj_t.T,
        d_cq,
        d_cproj_t.T,
        d_up,
        d_down_t.T,
    )


def solution(mesh):
    in_specs = (
        P("dp", None, None),
        P(),
        P(),
        P(),
        P(),
        P(None, "tensor"),
        P("tensor", None),
        P(None, "tensor"),
        P("tensor", None),
        P(None, "tensor"),
        P("dp", "tensor", None),
        P("dp"),
        P(),
        P(),
        P(None, "tensor"),
        P("tensor", None),
        P(None, "tensor"),
        P("tensor", None),
        P(None, "tensor"),
        P("tensor", None),
        P("dp", "tensor", None),
    )
    out_specs = (
        P("dp", "tensor", "section"),
        P("dp", "tensor", "section"),
        P(None, None, ("dp", "tensor")),
        P(None, None, ("dp", "tensor")),
        P(None, ("dp", "tensor")),
        P(None, ("dp", "tensor")),
        P(("section", "dp"), "tensor"),
        P("tensor", ("section", "dp")),
        P(("section", "dp"), "tensor"),
        P("tensor", ("section", "dp")),
        P(("section", "dp"), "tensor"),
        P(None, ("dp", "tensor")),
        P(None, ("dp", "tensor")),
        P(("section", "dp"), "tensor"),
        P("tensor", ("section", "dp")),
        P(("section", "dp"), "tensor"),
        P("tensor", ("section", "dp")),
        P(("section", "dp"), "tensor"),
        P("tensor", ("section", "dp")),
    )
    return jax.shard_map(body, mesh=mesh, in_specs=in_specs, out_specs=out_specs, check_vma=False)
```

```python
import functools
import math

import jax
import jax.numpy as jnp
import numpy as np
from jax import lax
from jax.experimental import pallas as pl
from jax.experimental.pallas import tpu as pltpu
from jax.sharding import PartitionSpec as P

HEAD_DIM = 64
NEG = -1000000000.0
EPS = 1e-05
TINY = 1e-28
CHUNK = 256
LANES = 128
BF, F32 = jnp.bfloat16, jnp.float32
INV_SQRT2 = 0.7071067811865476
INV_SQRT2PI = 0.3989422804014327


def dot_nn(left, right):
    return lax.dot_general(left, right, (((1,), (0,)), ((), ())), preferred_element_type=F32)


def dot_nt(left, right):
    return lax.dot_general(left, right, (((1,), (1,)), ((), ())), preferred_element_type=F32)


def dot_tn(left, right):
    return lax.dot_general(left, right, (((0,), (0,)), ((), ())), preferred_element_type=F32)


def norm_stats(rows):
    centre = rows - jnp.mean(rows, axis=-1, keepdims=True)
    spread = jnp.mean(centre * centre, axis=-1, keepdims=True)
    inverse = lax.rsqrt(spread + EPS)
    return centre * inverse, inverse


def norm_back(unit, inverse, gain_row, upstream):
    scaled = upstream * gain_row
    first = jnp.mean(scaled, axis=-1, keepdims=True)
    second = jnp.mean(scaled * unit, axis=-1, keepdims=True)
    grad_rows = inverse * (scaled - first - unit * second)
    grad_gain = jnp.sum(upstream * unit, axis=0, keepdims=True)
    grad_bias = jnp.sum(upstream, axis=0, keepdims=True)
    return grad_rows, grad_gain, grad_bias


def gelu_pair(v):
    phi = 0.5 * (1.0 + lax.erf(v * INV_SQRT2))
    return v * phi, phi + (v * INV_SQRT2PI) * jnp.exp(-0.5 * (v * v))


def lanes(rows):
    return lax.broadcasted_iota(jnp.int32, (rows, 2 * HEAD_DIM), 1)

def key_aug(kv, valid, ones):
    lane = lanes(kv.shape[0])
    row = lax.broadcasted_iota(jnp.int32, kv.shape, 0)
    pad = jnp.where((lane > HEAD_DIM) & (lane <= HEAD_DIM + ones), 1.0, 0.0)
    pad = jnp.where((lane == HEAD_DIM) & (row >= valid), NEG, pad).astype(BF)
    return jnp.where(lane < HEAD_DIM, kv, pad)

def causal_bias(scal_ref, key_rows, query_rows, valid):
    place, length = scal_ref[SCAL_CORE], scal_ref[SCAL_LENGTHS + scal_ref[SCAL_SECTION]]
    key_id = lax.broadcasted_iota(jnp.int32, (2 * key_rows, query_rows), 0)
    query_id = lax.broadcasted_iota(jnp.int32, (2 * key_rows, query_rows), 1)
    query_pos = query_id + place * valid
    key_pos = jnp.where(key_id < key_rows, key_id + place * valid, key_id - key_rows + (1 - place) * valid)
    return jnp.where((key_pos <= query_pos) & (key_pos < length), 0.0, NEG)

def fwd_setup(q_ref, kl_ref, kr_ref, valid):
    lane_q = lanes(q_ref.shape[0])
    q_all = q_ref[...].astype(F32) * HEAD_DIM**-0.5
    wide = 2 * HEAD_DIM

    def operands(h):
        q = jnp.where(lane_q < HEAD_DIM, q_all if h == 0 else pltpu.roll(q_all, HEAD_DIM, 1), 0.0)
        kv = [ref[:, h * wide : (h + 1) * wide] for ref in (kl_ref, kr_ref)]
        turned = [v.T for v in kv]
        sub = lax.broadcasted_iota(jnp.int32, turned[0].shape, 0)
        ones = [jnp.where(sub == 0, jnp.ones_like(v), v) for v in turned]
        return q, [key_aug(v, valid, 1) for v in kv], turned, ones

    return lane_q, operands


def fwd_finish(parts, logs, shift, out_ref, rest_ref, stat_ref):
    queries = out_ref.shape[0]
    mixed = jnp.concatenate([v[HEAD_DIM:] / v[0:1] for v in parts], axis=0).T
    logs = [jnp.broadcast_to(v, (HEAD_DIM, queries)) for v in logs]
    stat = jnp.concatenate(logs[::-1], axis=0).T
    if shift is not None:
        stat = stat + shift
    rounded = mixed.astype(BF)
    out_ref[...] = rounded
    rest_ref[...] = (mixed - rounded.astype(F32)).astype(BF)
    stat_ref[...] = stat


def fwd_fast(q_ref, kl_ref, kr_ref, out_ref, rest_ref, stat_ref, bias, valid, kc, depth):
    rows, queries = kl_ref.shape[0], q_ref.shape[0]
    lane_q, operands = fwd_setup(q_ref, kl_ref, kr_ref, valid)
    tops, heads = [], []
    for h in range(2):
        q, keys, turned, ones = operands(h)
        size = 0.0
        for v in turned:
            k = v[:HEAD_DIM].astype(F32)
            size = jnp.maximum(size, jnp.max(jnp.sum(k * k, axis=0, keepdims=True), axis=1, keepdims=True))
        bound = jnp.sqrt(jnp.sum(q * q, axis=1, keepdims=True) * size)
        bound = bound.astype(BF).astype(F32)
        q = jnp.where(lane_q == HEAD_DIM, 1.0, jnp.where(lane_q == HEAD_DIM + 1, -bound, q)).astype(BF)
        heads.append((q, keys, ones)); tops.append(bound)
    def score(item):
        h, side, at = item
        s = dot_nt(heads[h][1][side][at : at + kc], heads[h][0])
        if bias is not None:
            s = s + bias[side * rows + at : side * rows + at + kc]
        return s
    items = [(h, side, at) for h in range(2) for side in range(2) for at in range(0, rows, kc)]
    parts = [0.0, 0.0]
    ahead = [score(i) for i in items[:depth]]
    for n, (h, side, at) in enumerate(items):
        if n + depth < len(items):
            ahead.append(score(items[n + depth]))
        p = jnp.exp(ahead.pop(0)).astype(BF)
        parts[h] = parts[h] + dot_nn(heads[h][2][side][:, at : at + kc], p)
    fwd_finish(parts, [jnp.log(v[0:1]) for v in parts], jnp.where(lane_q < HEAD_DIM, tops[1], tops[0]), out_ref, rest_ref, stat_ref)
    return jnp.minimum(parts[0][0:1], parts[1][0:1])


def fwd_safe(q_ref, kl_ref, kr_ref, out_ref, rest_ref, stat_ref, bias, valid):
    rows = kl_ref.shape[0]
    lane_q, operands = fwd_setup(q_ref, kl_ref, kr_ref, valid)
    parts, logs = [], []
    for h in range(2):
        q, keys, _, ones = operands(h)
        q = jnp.where(lane_q == HEAD_DIM, 1.0, q).astype(BF)
        scores = []
        for side in range(2):
            s = dot_nt(keys[side], q)
            if bias is not None:
                s = s + bias[side * rows : (side + 1) * rows]
            scores.append(s)
        top = jnp.maximum(jnp.max(scores[0], axis=0, keepdims=True), jnp.max(scores[1], axis=0, keepdims=True))
        parts.append(sum(dot_nn(ones[i], jnp.exp(scores[i] - top).astype(BF)) for i in range(2)))
        logs.append(top + jnp.log(parts[h][0:1]))
    fwd_finish(parts, logs, None, out_ref, rest_ref, stat_ref)


def views(refs, i, pairs):
    narrow, near, far = refs
    wide = 2 * HEAD_DIM
    j = (i + pairs // 2) % pairs if isinstance(i, int) else lax.rem(i + pairs // 2, pairs)
    at = (lambda n, w: pl.ds(n * w, w)) if isinstance(i, int) else (lambda n, w: pl.ds(pl.multiple_of(n * w, w), w))
    return [r.at[:, at(i, wide)] for r in narrow], [r.at[:, at(i, 2 * wide)] for r in near], [r.at[:, at(j, 2 * wide)] for r in far]


def fwd_kernel(*refs, valid, masked, kc, depth):
    scal_ref = refs[0] if masked else None
    q_ref, kl_ref, kr_ref, out_ref, rest_ref, stat_ref = refs[1:] if masked else refs
    pairs = q_ref.shape[1] // (2 * HEAD_DIM)
    bias = causal_bias(scal_ref, kl_ref.shape[0], q_ref.shape[0], valid) if masked else None
    least = None
    for i in range(pairs):
        (q, out, rest, stat), (kl,), (kr,) = views(((q_ref, out_ref, rest_ref, stat_ref), (kl_ref,), (kr_ref,)), i, pairs)
        low = fwd_fast(q, kl, kr, out, rest, stat, bias, valid, kc, depth)
        least = low if least is None else jnp.minimum(least, low)
        for ref in (rest_ref, stat_ref):
            push(ref, (slice(None), pl.ds(i * 2 * HEAD_DIM, 2 * HEAD_DIM)))
    for ref in (rest_ref, stat_ref):
        if isinstance(ref, Outgoing):
            ref.finish()

    @pl.when(jnp.min(least) < TINY)
    def _():
        @pl.loop(0, pairs)
        def _(i):
            (q, out, rest, stat), (kl,), (kr,) = views(((q_ref, out_ref, rest_ref, stat_ref), (kl_ref,), (kr_ref,)), i, pairs)
            again = causal_bias(scal_ref, kl_ref.shape[0], q_ref.shape[0], valid) if masked else None
            fwd_safe(q, kl, kr, out, rest, stat, again, valid)

        for ref in (rest_ref, stat_ref):
            if isinstance(ref, Outgoing):
                ref.again()


def split3(value):
    first = value.astype(BF); rest = value - first.astype(F32)
    second = rest.astype(BF); third = (rest - second.astype(F32)).astype(BF)
    return first.astype(F32), second.astype(F32), third.astype(F32)


def bwd_views(refs, i, pairs):
    q_ref, kl_ref, kr_ref, out_ref, rest_ref, stat_ref, up_ref, dq_ref, dkl_ref, dkr_ref = refs
    narrow = (q_ref, out_ref, rest_ref, stat_ref, up_ref, dq_ref)
    (q, out, rest, stat, up, dq), (kl, dkl), (kr, dkr) = views(
        (narrow, (kl_ref, dkl_ref), (kr_ref, dkr_ref)), i, pairs
    )
    return q, kl, kr, out, rest, stat, up, dq, dkl, dkr


def bwd_kernel(*refs, valid, masked):
    scal_ref = refs[0] if masked else None
    refs = refs[1:] if masked else refs
    q_ref, kl_ref = refs[:2]
    pairs = q_ref.shape[1] // (2 * HEAD_DIM)
    bias = causal_bias(scal_ref, kl_ref.shape[0], q_ref.shape[0], valid) if masked else None
    for i in range(pairs):
        q, kl, kr, out, rest, stat, up, dq, dkl, dkr = bwd_views(refs, i, pairs)
        fn = bwd_pair if masked else bwd_pair_s
        fn(q, out, rest, stat, up, dq, [(kl, dkl), (kr, dkr)], bias, valid)


def bwd_side_kernel(*refs, valid, far, first, count, joined, turn):
    q_ref, kv_ref, out_ref, rest_ref, stat_ref, up_ref, *more, dq_ref, dkv_ref = refs
    pairs = q_ref.shape[1] // (2 * HEAD_DIM)
    wide = 2 * HEAD_DIM
    base_refs = () if far else more
    if joined:
        earlier, at = more[0], dkv_ref.shape[1] - more[0].shape[1]
        dkv_ref[:, at:] = earlier[...]

    def one(i):
        (q, out, rest, stat, up), near, other = views(
            ((q_ref, out_ref, rest_ref, stat_ref, up_ref), () if far else (kv_ref,), (kv_ref,) if far else ()),
            (first + i) % pairs, pairs,
        )
        dq = dq_ref.at[:, i * wide : (i + 1) * wide]
        dkv = dkv_ref.at[:, i * 2 * wide : (i + 1) * 2 * wide]
        base = None
        if base_refs:
            each, at = base_refs[0].shape[1] // wide, (first + i - turn) % pairs
            base = base_refs[at // each].at[:, at % each * wide : (at % each + 1) * wide]
        bwd_pair(q, out, rest, stat, up, dq, [(*near, *other, dkv)], None, valid, base)

    for i in range(count):
        one(i)


def bwd_pair_s(q_ref, out_ref, rest_ref, stat_ref, up_ref, dq_ref, key_sides, bias, valid, base_ref=None):
    rows, queries, depth = key_sides[0][0].shape[0], q_ref.shape[0], 1
    kc = rows
    wide = 2 * HEAD_DIM
    lane_q, lane_k = lanes(queries), lanes(rows)
    low_q = lane_q < HEAD_DIM
    q_all = q_ref[...].astype(F32) * HEAD_DIM**-0.5
    up_all = up_ref[...].astype(F32)
    stat = stat_ref[...]
    prods = up_all * (out_ref[...].astype(F32) + rest_ref[...].astype(F32))
    q_turned = (q_all.astype(BF)).T
    up_turned = up_ref[...].T
    heads, both = [], []
    for h in range(2):
        q = q_all if h == 0 else pltpu.roll(q_all, HEAD_DIM, 1)
        lse = stat if h == 0 else pltpu.roll(stat, HEAD_DIM, 1)
        up = up_all if h == 1 else pltpu.roll(up_all, HEAD_DIM, 1)
        a0, a1, a2 = split3(-lse)
        pad = jnp.where(lane_q == HEAD_DIM, 1.0, jnp.where(lane_q == HEAD_DIM + 1, a0, jnp.where(lane_q == HEAD_DIM + 2, a1, jnp.where(lane_q == HEAD_DIM + 3, a2, 0.0))))
        q_aug = jnp.where(low_q, q, pad).astype(BF)
        centre = jnp.sum(jnp.where(low_q if h == 0 else ~low_q, prods, 0.0), axis=1, keepdims=True)
        d0, d1, d2 = split3(-centre)
        pad = jnp.where(lane_q == 0, d0, jnp.where(lane_q == 1, d1, jnp.where(lane_q == 2, d2, 0.0)))
        up_aug = jnp.where(low_q, pad, up).astype(BF)
        heads.append((q_aug, up_aug, q_turned[h * HEAD_DIM : (h + 1) * HEAD_DIM], up_turned[h * HEAD_DIM : (h + 1) * HEAD_DIM]))
        sides = []
        for ref, out in key_sides:
            kv = ref[:, h * wide : (h + 1) * wide]
            keys = key_aug(kv, valid, 3)
            values = jnp.where(lane_k < HEAD_DIM, jnp.where(lane_k < 3, 1.0, 0.0).astype(BF), kv)
            sides.append((keys, values, kv, out))
        both.append(sides)
    items = [(h, side, at) for h in range(2) for side in range(len(key_sides)) for at in range(0, rows, kc)]
    def score(item):
        h, side, at = item
        keys, values, _, _ = both[h][side]
        return dot_nt(heads[h][0], keys[at : at + kc]), dot_nt(heads[h][1], values[at : at + kc])
    ahead = [score(i) for i in items[:depth]]
    totals = [0.0, 0.0]
    for n, (h, side, at) in enumerate(items):
        if n + depth < len(items):
            ahead.append(score(items[n + depth]))
        s, dp = ahead.pop(0)
        p = jnp.exp(s)
        ds = (p * dp).astype(BF)
        p = p.astype(BF)
        _, _, kv, out = both[h][side]
        pair = jnp.concatenate([dot_nn(heads[h][2], ds), dot_nn(heads[h][3], p)], axis=0)
        out[at : at + kc, h * wide : (h + 1) * wide] = pair.T.astype(BF)
        totals[h] = totals[h] + dot_nn(ds, kv[at : at + kc])
    dq = jnp.where(low_q, totals[0], pltpu.roll(totals[1], HEAD_DIM, 1)) * HEAD_DIM**-0.5
    dq_ref[...] = dq.astype(BF)


def bwd_pair(q_ref, out_ref, rest_ref, stat_ref, up_ref, dq_ref, key_sides, bias, valid, base_ref=None):
    masked, depth = bias is not None, 1
    rows, queries = key_sides[0][0].shape[0], q_ref.shape[0]
    kc = rows
    wide = 2 * HEAD_DIM
    lane_q, lane_k = lanes(queries), lanes(rows)
    low_q = lane_q < HEAD_DIM
    q_all = q_ref[...].astype(F32) * HEAD_DIM**-0.5
    up_all = up_ref[...].astype(F32)
    stat = stat_ref[...]
    prods = up_all * (out_ref[...].astype(F32) + rest_ref[...].astype(F32))
    heads, both = [], []
    for h in range(2):
        q = q_all if h == 0 else pltpu.roll(q_all, HEAD_DIM, 1)
        lse = stat if h == 0 else pltpu.roll(stat, HEAD_DIM, 1)
        up = up_all if h == 1 else pltpu.roll(up_all, HEAD_DIM, 1)
        a0, a1, a2 = split3(-lse)
        pad = jnp.where(lane_q == HEAD_DIM, 1.0, jnp.where(lane_q == HEAD_DIM + 1, a0, jnp.where(lane_q == HEAD_DIM + 2, a1, jnp.where(lane_q == HEAD_DIM + 3, a2, 0.0))))
        q_aug = jnp.where(low_q, q, pad).astype(BF)
        q_rhs = jnp.where(low_q, q, 0.0).astype(BF)
        centre = jnp.sum(jnp.where(low_q if h == 0 else ~low_q, prods, 0.0), axis=1, keepdims=True)
        d0, d1, d2 = split3(-centre)
        pad = jnp.where(lane_q == 0, d0, jnp.where(lane_q == 1, d1, jnp.where(lane_q == 2, d2, 0.0)))
        up_aug = jnp.where(low_q, pad, up).astype(BF)
        up_rhs = jnp.where(low_q, 0.0, up).astype(BF)
        heads.append((q_aug, q_rhs, up_aug, up_rhs))
        sides = []
        for ref, out in key_sides:
            kv = ref[:, h * wide : (h + 1) * wide]
            keys = key_aug(kv, valid, 3)
            values = jnp.where(lane_k < HEAD_DIM, jnp.where(lane_k < 3, 1.0, 0.0).astype(BF), kv)
            sides.append((keys, values, kv.T, out))
        both.append(sides)
    items = [(h, side, at) for h in range(2) for side in range(len(key_sides)) for at in range(0, rows, kc)]
    def score(item):
        h, side, at = item
        keys, values, _, _ = both[h][side]
        s = dot_nt(keys[at : at + kc], heads[h][0])
        if masked:
            first = at + side * rows
            s = s + bias[first : first + kc]
        return s, dot_nt(values[at : at + kc], heads[h][2])
    ahead = [score(i) for i in items[:depth]]
    totals = [0.0, 0.0]
    for n, (h, side, at) in enumerate(items):
        if n + depth < len(items):
            ahead.append(score(items[n + depth]))
        s, dp = ahead.pop(0)
        p = jnp.exp(s)
        ds = (p * dp).astype(BF)
        p = p.astype(BF)
        _, _, turned, out = both[h][side]
        out[at : at + kc, h * wide : (h + 1) * wide] = (dot_nn(ds, heads[h][1]) + dot_nn(p, heads[h][3])).astype(BF)
        totals[h] = totals[h] + dot_nn(turned[:, at : at + kc], ds)
    turned_dq = [v[:HEAD_DIM] for v in totals]
    dq = jnp.concatenate(turned_dq, axis=0).T * HEAD_DIM**-0.5
    if base_ref is not None:
        dq = dq + base_ref[...]
    dq_ref[...] = dq.astype(dq_ref.dtype)


def shape_of(rows, width, kind=BF):
    return jax.ShapeDtypeStruct((rows, width), kind)


def params(megabytes, *semantics):
    return pltpu.CompilerParams(vmem_limit_bytes=megabytes * 2**20)


def attention_cost(q, kl, products):
    flops = 2 * products * q.shape[0] * 2 * kl.shape[0] * q.shape[1] * 3
    return pl.CostEstimate(
        flops=flops, bytes_accessed=8 * q.size + 6 * kl.size, transcendentals=0
    )


class Far:
    def __init__(self, value, pieces=1, by_core=False):
        self.value, self.pieces, self.by_core = value, pieces, by_core
        self.shape, self.dtype = value.shape[1:] if by_core else value.shape, value.dtype
        self.size = math.prod(self.shape)


class Clip:
    def __init__(self, value):
        self.value, self.shape, self.dtype, self.size = value, value.shape, value.dtype, value.size


class Incoming:
    def __init__(self, source, held, arrived, pieces):
        self.held, self.shape, self.dtype = held, held.shape, held.dtype
        rows = held.shape[0] // pieces
        self.spans = [pl.ds(n * rows, rows) for n in range(pieces)]
        self.copies = [
            pltpu.make_async_copy(source.at[span], held.at[span], arrived.at[n])
            for n, span in enumerate(self.spans)
        ]

    def start(self, n):
        if n < len(self.copies):
            self.copies[n].start()

    def wait(self, n):
        if self.copies[n] is not None:
            self.copies[n].wait()
            self.copies[n] = None

    def piece(self, n):
        return Piece(self, n)

    def settle(self):
        for n in range(len(self.copies)):
            self.wait(n)
        return self.held

    @property
    def at(self):
        return self.settle().at

    def __getitem__(self, index):
        return self.settle()[index]


class Piece:
    def __init__(self, whole, n):
        self.whole, self.n = whole, n
        rows = whole.held.shape[0] // len(whole.spans)
        self.shape, self.dtype = (rows, *whole.held.shape[1:]), whole.held.dtype

    def __getitem__(self, index):
        self.whole.wait(self.n)
        return self.whole.held.at[self.whole.spans[self.n]][index]


class Padded:
    def __init__(self, ref, section, rows):
        self.ref, self.section, self.rows = ref, section, rows
        self.shape, self.dtype = (rows, ref.shape[2]), ref.dtype

    def __getitem__(self, index):
        value = self.ref[self.section]
        behind = jnp.zeros((self.rows - value.shape[0], value.shape[1]), value.dtype)
        return jnp.concatenate([value, behind], axis=0)[index]


class Outgoing:
    def __init__(self, target, held, left):
        self.target, self.held, self.left, self.copies = target, held, left, []
        self.at, self.shape, self.dtype = held.at, held.shape, held.dtype

    def __setitem__(self, index, value):
        self.held[index] = value

    def push(self, index=(slice(None), slice(None))):
        copy = pltpu.make_async_copy(
            self.held.at[index], self.target.at[index], self.left.at[len(self.copies)]
        )
        copy.start()
        self.copies.append(copy)

    def finish(self):
        for copy in self.copies or ():
            copy.wait()
        self.copies = None

    def again(self):
        copy = pltpu.make_async_copy(self.held, self.target, self.left.at[0])
        copy.start()
        copy.wait()


def push(ref, *index):
    if isinstance(ref, Outgoing):
        ref.push(*index)


def in_vmem():
    return pl.BlockSpec(memory_space=pltpu.VMEM)


def in_hbm():
    return pl.BlockSpec(memory_space=pltpu.HBM)


def flat_call(kernel, operands, out_shape, scal=None, scratch=(), flops=0, megabytes=40):
    touched = sum(v.size * v.dtype.itemsize for v in operands)
    touched += sum(math.prod(v.shape) * v.dtype.itemsize for v in out_shape)
    far_in = [v for v in operands if isinstance(v, Far)]
    far_out = [v for v in out_shape if isinstance(v, Far)]
    extra = []
    for v in (*far_in, *far_out):
        extra += [pltpu.VMEM(v.shape, v.dtype), pltpu.SemaphoreType.DMA((v.pieces,))]
        megabytes += -(-v.size * v.dtype.itemsize // 2**20)

    def run(*refs):
        refs = list(refs)
        take = lambda count: [refs.pop(0) for _ in range(count)]
        head = take(0 if scal is None else 1)
        ins, outs, own = take(len(operands)), take(len(out_shape)), take(len(scratch))
        moving = []
        for n, v in enumerate(operands):
            if isinstance(v, Far):
                source = ins[n].at[head[0][SCAL_CORE]] if v.by_core else ins[n]
                ins[n] = Incoming(source, *take(2), v.pieces)
                moving.append(ins[n])
            elif isinstance(v, Clip):
                ins[n] = Padded(ins[n], head[0][SCAL_SECTION], round_up(v.shape[1]))
        for n, v in enumerate(out_shape):
            if isinstance(v, Far):
                outs[n] = Outgoing(outs[n], *take(2))
        for n in range(max((len(v.copies) for v in moving), default=0)):
            for v in moving:
                v.start(n)
        kernel(*head, *ins, *outs, *own)
        for v in moving:
            v.settle()
        for v in outs:
            if isinstance(v, Outgoing):
                if v.copies == []:
                    v.push()
                v.finish()

    bare = lambda v: v.value if isinstance(v, (Far, Clip)) else v
    pin = lambda v: pltpu.with_memory_space_constraint(v.value, pltpu.HBM) if isinstance(v, Far) else bare(v)
    pin_shape = lambda v: pltpu.HBM(v.shape, v.dtype) if isinstance(v, Far) else v
    place = lambda v: in_hbm() if isinstance(v, Far) else in_vmem()
    return pl.pallas_call(
        run,
        in_specs=([] if scal is None else [pl.BlockSpec(memory_space=pltpu.SMEM)])
        + [place(v) for v in operands],
        out_specs=[place(v) for v in out_shape],
        out_shape=[pin_shape(v) for v in out_shape],
        scratch_shapes=list(scratch) + extra,
        compiler_params=params(megabytes),
        cost_estimate=pl.CostEstimate(flops=flops, bytes_accessed=touched, transcendentals=0),
    )(*([] if scal is None else [scal]), *[pin(v) for v in operands])


def attention_flops(q, kl, products, share=1):
    return 2 * products * q.shape[0] * 2 * kl.shape[0] * q.shape[1] * 4 // share


def attention_fwd(q, kl, kr, valid, scal=None):
    return flat_call(
        functools.partial(fwd_kernel, valid=valid, masked=scal is not None, kc=kl.shape[0], depth=1),
        [q, kl, kr],
        [shape_of(*q.shape), Far(shape_of(*q.shape), 8), Far(shape_of(*q.shape, F32), 8)],
        scal=scal, flops=attention_flops(q, kl, 2), megabytes=24 if q.shape[0] > CHUNK else 12,
    )


def attention_bwd(q, kl, kr, out, rest, stat, up, valid, scal=None):
    return flat_call(
        functools.partial(bwd_kernel, valid=valid, masked=scal is not None),
        [q, kl, kr, out, rest, stat, up],
        [shape_of(*q.shape), shape_of(*kl.shape), shape_of(*kl.shape)],
        scal=scal, flops=attention_flops(q, kl, 5), megabytes=12,
    )


def attention_bwd_side(q, kv, out, rest, stat, up, valid, base=(), pairs=None, earlier=(), turn=0):
    far = not base
    total = q.shape[1] // (2 * HEAD_DIM)
    first, count = pairs or (0, total)
    width = kv.shape[1] // total * count + sum(v.shape[1] for v in earlier)
    return flat_call(
        functools.partial(
            bwd_side_kernel, valid=valid, far=far, first=first, count=count, joined=bool(earlier), turn=turn
        ),
        [q, kv, out, rest, stat, up, *base, *earlier],
        [shape_of(q.shape[0], q.shape[1] // total * count, F32 if far else BF), shape_of(kv.shape[0], width)],
        flops=attention_flops(q, kv, 5, 2), megabytes=21 if count > 2 else 14,
    )


def rows_call(
    kernel, rows, blocked, whole, outs, sums=(), scratch=(), reverse=False, flops=0, megabytes=10, scal=None,
    told=False,
):
    chunk_rows = next(n for n in (384, CHUNK) if rows % n == 0)
    steps = rows // chunk_rows
    order = list(range(steps))
    if reverse:
        order = order[::-1]

    def chunk_of(ref, chunk):
        if isinstance(ref, Incoming):
            return ref.piece(chunk)
        return ref if isinstance(ref, Padded) else ref.at[pl.ds(chunk * chunk_rows, chunk_rows)]

    def run(*refs):
        refs = list(refs)
        take = lambda count: [refs.pop(0) for _ in range(count)]
        head = take(0 if scal is None else 1)
        kept, by_chunk = take(len(whole)), take(len(blocked))
        out, total = take(len(outs)), take(len(sums))
        for n, chunk in enumerate(order):
            kernel(
                n, *(head if told else ()), *[chunk_of(r, chunk) for r in by_chunk], *kept,
                *[chunk_of(r, chunk) for r in out], *total, *refs,
            )
            for r in out:
                push(r, (pl.ds(chunk * chunk_rows, chunk_rows), slice(None)))

    out_shape = []
    for width, kind, *far in outs:
        shape = shape_of(rows, width, kind)
        out_shape.append(Far(shape, steps) if far else shape)
    for shape, kind, *far in sums:
        shape = jax.ShapeDtypeStruct(shape, kind)
        out_shape.append(Far(shape) if far else shape)
    blocked = [Far(v.value, steps, v.by_core) if isinstance(v, Far) else v for v in blocked]
    return flat_call(run, [*whole, *blocked], out_shape, scal, scratch, flops, megabytes)


def tap_weights(first_ref):
    pieces = []
    for tap in range(first_ref.shape[0]):
        rows = first_ref[tap]
        pieces += [rows, jnp.zeros((LANES - rows.shape[0], rows.shape[1]), rows.dtype)]
    return jnp.concatenate(pieces, axis=0)


def mel_windows(scal_ref, mel_ref, mel_rows_ref, windows_ref, halo_ref, valid):
    rows = windows_ref.shape[0]
    channels, frames = mel_ref.shape[1:]
    front = 8
    mel_rows_ref[...] = jnp.zeros_like(mel_rows_ref)
    mel_rows_ref[front : front + frames, :channels] = mel_ref[scal_ref[SCAL_SECTION]].astype(F32).T
    lanes_all = slice(None)
    for core in range(frames // (2 * valid)):

        @pl.when(scal_ref[SCAL_CORE] == core)
        def _():
            base = front + 2 * valid * core
            for n in range(4):
                taken = mel_rows_ref[pl.ds(base + n - 1, rows, stride=2), lanes_all]
                windows_ref[:, n * LANES : (n + 1) * LANES] = taken.astype(BF)
            halo_ref[...] = jnp.zeros_like(halo_ref)
            if core > 0:
                for n in range(3):
                    part = mel_rows_ref[pl.ds(base - 2 + n, 16), lanes_all]
                    first = lax.broadcasted_iota(jnp.int32, part.shape, 0) == 0
                    halo_ref[:, n * LANES : (n + 1) * LANES] = jnp.where(first, part, 0.0).astype(BF)


def stem_fwd_kernel(
    chunk, scal_ref, pos_ref, mel_ref, first_ref, second_ref,
    even_ref, odd_ref, before_ref, ge_ref, go_ref, gs_ref, x_ref, gh_ref, windows_ref, halo_ref,
    carry_ref, mel_rows_ref, *, valid,
):
    first = tap_weights(first_ref)
    if chunk == 0:
        mel_windows(scal_ref, mel_ref, mel_rows_ref, windows_ref, halo_ref, valid)
        push(windows_ref)
        act, slope = gelu_pair(dot_nn(halo_ref[...], first))
        carry_ref[...] = act[:8]
        gh_ref[...] = slope
    span = pl.ds(chunk * even_ref.shape[0], even_ref.shape[0])
    me_ref = windows_ref.at[span, : 3 * LANES]
    mo_ref = windows_ref.at[span, LANES:]

    width = even_ref.shape[1]
    even, slope = gelu_pair(dot_nn(me_ref[...], first))
    even = even.astype(BF)
    even_ref[...] = even
    ge_ref[...] = slope.astype(BF)
    odd, slope = gelu_pair(dot_nn(mo_ref[...], first))
    go_ref[...] = slope.astype(BF)
    row = lax.broadcasted_iota(jnp.int32, odd.shape, 0)
    before = jnp.where(row == 0, carry_ref[0:1, :], pltpu.roll(odd, 1, 0)).astype(BF)
    carry_ref[0:1, :] = odd[odd.shape[0] - 1 :]
    odd = odd.astype(BF)
    odd_ref[...] = odd
    before_ref[...] = before
    pre = dot_nn(before, second_ref[:width])
    pre += dot_nn(even, second_ref[width : 2 * width])
    pre += dot_nn(odd, second_ref[2 * width :])
    act, slope = gelu_pair(pre)
    gs_ref[...] = slope.astype(BF)
    x_ref[...] = act + pos_ref[...]


def qkv_kernel(step, x_ref, gain_ref, bias_ref, own_ref, oth_ref, normed_ref, q_ref, kv_ref):
    unit, _ = norm_stats(x_ref[...].astype(F32))
    normed = (unit * gain_ref[...] + bias_ref[...]).astype(BF)
    normed_ref[...] = normed
    heads = own_ref.shape[1] // (3 * HEAD_DIM)
    for part, w_ref in enumerate((own_ref, oth_ref)):
        packed = dot_nn(normed, w_ref[...]).astype(BF)
        for h in range(heads):
            at, to = h * 3 * HEAD_DIM, part * heads + h
            q_ref[:, to * HEAD_DIM : (to + 1) * HEAD_DIM] = packed[:, at : at + HEAD_DIM]
            kv_ref[:, to * 2 * HEAD_DIM : (to + 1) * 2 * HEAD_DIM] = packed[
                :, at + HEAD_DIM : at + 3 * HEAD_DIM
            ]


def two_parts(rows, own_ref, oth_ref):
    depth = own_ref.shape[0]
    return dot_nn(rows[:, :depth], own_ref[...]) + dot_nn(rows[:, depth:], oth_ref[...])


def two_parts_t(rows, own_ref, oth_ref):
    depth = own_ref.shape[1]
    return dot_nt(rows[:, :depth], own_ref[...]) + dot_nt(rows[:, depth:], oth_ref[...])


def enc_mid_kernel(
    step, x_ref, att_ref, gb_ref, bb_ref, gc_ref, bc_ref, po_ref, pt_ref, uo_ref, ut_ref, do_ref, dt_ref,
    ko_ref, kt_ref,
    x1_ref, x2_ref, normed_ref, hidden_ref, slope_ref, memory_ref, kv_ref,
):
    x1 = x_ref[...] + two_parts(att_ref[...], po_ref, pt_ref)
    x1_ref[...] = x1
    unit, _ = norm_stats(x1)
    normed = (unit * gb_ref[...] + bb_ref[...]).astype(BF)
    normed_ref[...] = normed
    half = uo_ref.shape[1]
    x2 = x1
    for part, (up_ref, down_ref) in enumerate(((uo_ref, do_ref), (ut_ref, dt_ref))):
        act, slope = gelu_pair(dot_nn(normed, up_ref[...]))
        act = act.astype(BF)
        hidden_ref[:, part * half : (part + 1) * half] = act
        slope_ref[:, part * half : (part + 1) * half] = slope.astype(BF)
        x2 = x2 + dot_nn(act, down_ref[...])
    x2_ref[...] = x2
    unit, _ = norm_stats(x2)
    memory = (unit * gc_ref[...] + bc_ref[...]).astype(BF)
    memory_ref[...] = memory
    half = ko_ref.shape[1]
    kv_ref[:, :half] = dot_nn(memory, ko_ref[...]).astype(BF)
    kv_ref[:, half:] = dot_nn(memory, kt_ref[...]).astype(BF)


def dec_mid_kernel(
    step, x_ref, att_ref, gain_ref, bias_ref, po_ref, pt_ref, qo_ref, qt_ref, y_ref, normed_ref, q_ref
):
    y = x_ref[...].astype(F32) + two_parts(att_ref[...], po_ref, pt_ref)
    y_ref[...] = y
    unit, _ = norm_stats(y)
    normed = (unit * gain_ref[...] + bias_ref[...]).astype(BF)
    normed_ref[...] = normed
    half = qo_ref.shape[1]
    q_ref[:, :half] = dot_nn(normed, qo_ref[...]).astype(BF)
    q_ref[:, half:] = dot_nn(normed, qt_ref[...]).astype(BF)


def mlp_back(gb, slope_ref, dpre_ref, uo_ref, ut_ref, do_ref, dt_ref):
    half = uo_ref.shape[1]
    total = 0.0
    for part, (up_ref, down_ref) in enumerate(((uo_ref, do_ref), (ut_ref, dt_ref))):
        span = slice(part * half, (part + 1) * half)
        dpre = (dot_nt(gb, down_ref[...]) * slope_ref[:, span].astype(F32)).astype(BF)
        dpre_ref[:, span] = dpre
        total = total + dot_nt(dpre, up_ref[...])
    return total


def section_halves(scal_ref, value, mine_ref, sent_ref):
    rows, half = mine_ref.shape
    left, right = value[:rows, :half], value[:rows, half:]
    lower = scal_ref[SCAL_SECTION] == 0
    mine_ref[...] = jnp.where(lower, left, right).astype(mine_ref.dtype)
    sent_ref[...] = jnp.where(lower, right, left).astype(sent_ref.dtype)


def owners_kernel(scal_ref, *refs):
    count = len(refs) // 2
    section, got_ref = scal_ref[SCAL_SECTION], refs[count]
    for n, (mine_ref, out_ref) in enumerate(zip(refs[:count], refs[count + 1 :])):
        rows = mine_ref.shape[0]
        out_ref[section] = mine_ref[...]
        out_ref[1 - section] = got_ref[n * rows : (n + 1) * rows, :].astype(out_ref.dtype)


def dec_top_kernel(
    scal_ref, y1_ref, crossed_ref, cot_ref, gain_ref, bias_ref, po_ref, pt_ref, uo_ref, ut_ref,
    do_ref, dt_ref,
    decoded_ref, sent_ref, normed_ref, hidden_ref, dpre_ref, gb3_ref, gb2_ref, dcrossed_ref, u2_ref,
    sums_ref, slope_ref, *, valid,
):
    rows = y1_ref.shape[0]
    y2 = y1_ref[...] + two_parts(crossed_ref[...], po_ref, pt_ref)
    unit, inverse = norm_stats(y2)
    normed = (unit * gain_ref[...] + bias_ref[...]).astype(BF)
    normed_ref[...] = normed
    push(normed_ref)
    half = uo_ref.shape[1]
    y3 = y2
    for part, (up_ref, down_ref) in enumerate(((uo_ref, do_ref), (ut_ref, dt_ref))):
        act, slope = gelu_pair(dot_nn(normed, up_ref[...]))
        act = act.astype(BF)
        hidden_ref[:, part * half : (part + 1) * half] = act
        slope_ref[:, part * half : (part + 1) * half] = slope.astype(BF)
        y3 = y3 + dot_nn(act, down_ref[...])
    push(hidden_ref)
    row = lax.broadcasted_iota(jnp.int32, y2.shape, 0)
    length = scal_ref[SCAL_LENGTHS + scal_ref[SCAL_SECTION]]
    live = ((row < valid) & (row + scal_ref[SCAL_CORE] * valid < length)).astype(F32)
    section_halves(scal_ref, y3 * live, decoded_ref, sent_ref)
    u3 = cot_ref[...].astype(F32) * live
    gb3 = u3.astype(BF)
    gb3_ref[...] = gb3
    push(gb3_ref)
    dnormed = mlp_back(gb3, slope_ref, dpre_ref, uo_ref, ut_ref, do_ref, dt_ref)
    push(dpre_ref)
    dy, dgain, dbias = norm_back(unit, inverse, gain_ref[...], dnormed)
    u2 = u3 + dy
    u2_ref[...] = u2
    gb2 = u2.astype(BF)
    gb2_ref[...] = gb2
    push(gb2_ref)
    half = po_ref.shape[0]
    dcrossed_ref[:, :half] = dot_nt(gb2, po_ref[...]).astype(BF)
    dcrossed_ref[:, half:] = dot_nt(gb2, pt_ref[...]).astype(BF)
    sums_ref[...] = jnp.zeros_like(sums_ref)
    sums_ref[0:1, :] = dgain
    sums_ref[1:2, :] = dbias


def dec_back_kernel(
    step, dq_ref, y1_ref, u2_ref, gain_ref, qo_ref, qt_ref, po_ref, pt_ref,
    u1_ref, gb1_ref, datt_ref, sums_ref,
):
    dnormed = two_parts_t(dq_ref[...], qo_ref, qt_ref)
    unit, inverse = norm_stats(y1_ref[...])
    dy, dgain, dbias = norm_back(unit, inverse, gain_ref[...], dnormed)
    u1 = u2_ref[...] + dy
    u1_ref[...] = u1
    gb1 = u1.astype(BF)
    gb1_ref[...] = gb1
    half = po_ref.shape[0]
    datt_ref[:, :half] = dot_nt(gb1, po_ref[...]).astype(BF)
    datt_ref[:, half:] = dot_nt(gb1, pt_ref[...]).astype(BF)
    sums_ref[...] = jnp.zeros_like(sums_ref)
    sums_ref[0:1, :] = dgain
    sums_ref[1:2, :] = dbias


def packed_back(dq_ref, dkl_ref, dkr_ref, own_ref, oth_ref, out_ref):
    dkv = (dkl_ref[...].astype(F32) + dkr_ref[...].astype(F32)).astype(BF)
    dq = dq_ref[...]
    heads = own_ref.shape[1] // (3 * HEAD_DIM)
    total = 0.0
    for part, w_ref in enumerate((own_ref, oth_ref)):
        pieces = []
        for h in range(part * heads, (part + 1) * heads):
            pieces.append(dq[:, h * HEAD_DIM : (h + 1) * HEAD_DIM])
            pieces.append(dkv[:, h * 2 * HEAD_DIM : (h + 1) * 2 * HEAD_DIM])
        packed = jnp.concatenate(pieces, axis=1)
        out_ref[:, part * w_ref.shape[1] : (part + 1) * w_ref.shape[1]] = packed
        total = total + dot_nt(packed, w_ref[...])
    return total


def dec_last_kernel(
    step, scal_ref, dq_ref, dkl_ref, dkr_ref, x_ref, u1_ref, gain_ref, own_ref, oth_ref,
    packed_ref, sums_ref, mine_ref, sent_ref,
):
    dnormed = packed_back(dq_ref, dkl_ref, dkr_ref, own_ref, oth_ref, packed_ref)
    unit, inverse = norm_stats(x_ref[...].astype(F32))
    dx, dgain, dbias = norm_back(unit, inverse, gain_ref[...], dnormed)
    section_halves(scal_ref, u1_ref[...] + dx, mine_ref, sent_ref)
    sums_ref[...] = jnp.zeros_like(sums_ref)
    sums_ref[0:1, :] = dgain
    sums_ref[1:2, :] = dbias


def enc_back_kernel(
    step, gl_ref, gr_ref, x2_ref, x1_ref, slope_ref, gc_ref, gb_ref, ko_ref, kt_ref, uo_ref, ut_ref,
    do_ref, dt_ref, po_ref, pt_ref,
    gkv_ref, gb2_ref, dpre_ref, gb1_ref, datt_ref, u1_ref, sums_ref,
):
    if step == 0:
        sums_ref[...] = jnp.zeros_like(sums_ref)

    gkv = (gl_ref[...].astype(F32) + gr_ref[...].astype(F32)).astype(BF)
    gkv_ref[...] = gkv
    dmemory = two_parts_t(gkv, ko_ref, kt_ref)
    unit, inverse = norm_stats(x2_ref[...])
    u2, dgain, dbias = norm_back(unit, inverse, gc_ref[...], dmemory)
    sums_ref[0:1, :] += dgain
    sums_ref[1:2, :] += dbias
    gb2 = u2.astype(BF)
    gb2_ref[...] = gb2
    dnormed = mlp_back(gb2, slope_ref, dpre_ref, uo_ref, ut_ref, do_ref, dt_ref)
    unit, inverse = norm_stats(x1_ref[...])
    dx, dgain, dbias = norm_back(unit, inverse, gb_ref[...], dnormed)
    sums_ref[2:3, :] += dgain
    sums_ref[3:4, :] += dbias
    u1 = u2 + dx
    u1_ref[...] = u1
    gb1 = u1.astype(BF)
    gb1_ref[...] = gb1
    half = po_ref.shape[0]
    datt_ref[:, :half] = dot_nt(gb1, po_ref[...]).astype(BF)
    datt_ref[:, half:] = dot_nt(gb1, pt_ref[...]).astype(BF)


def stem_back_kernel(
    step, dq_ref, dkl_ref, dkr_ref, x0_ref, u1_ref, ge_ref, go_ref, gs_ref, gain_ref, own_ref, oth_ref,
    second_ref, gh_ref,
    packed_ref, g2_ref, ede_ref, edo_ref, sums_ref, edh_ref, carry_ref,
):
    if step == 0:
        sums_ref[...] = jnp.zeros_like(sums_ref)
        carry_ref[...] = jnp.zeros_like(carry_ref)

    dnormed = packed_back(dq_ref, dkl_ref, dkr_ref, own_ref, oth_ref, packed_ref)
    unit, inverse = norm_stats(x0_ref[...])
    dx, dgain, dbias = norm_back(unit, inverse, gain_ref[...], dnormed)
    sums_ref[0:1, :] += dgain
    sums_ref[1:2, :] += dbias
    g2 = ((u1_ref[...] + dx) * gs_ref[...].astype(F32)).astype(BF)
    g2_ref[...] = g2
    width = g2.shape[1]
    before = dot_nt(g2, second_ref[:width])
    even = dot_nt(g2, second_ref[width : 2 * width])
    odd = dot_nt(g2, second_ref[2 * width :])
    ede_ref[...] = (even * ge_ref[...].astype(F32)).astype(BF)
    row = lax.broadcasted_iota(jnp.int32, before.shape, 0)
    later = jnp.where(
        row == before.shape[0] - 1, carry_ref[0:1, :], pltpu.roll(before, before.shape[0] - 1, 0)
    )
    carry_ref[0:1, :] = before[0:1]
    edo_ref[...] = ((odd + later) * go_ref[...].astype(F32)).astype(BF)
    front = lax.broadcasted_iota(jnp.int32, edh_ref.shape, 0)
    edh_ref[...] = jnp.where(front == 0, before[0:1] * gh_ref[...], 0.0).astype(BF)


SCAL_CORE, SCAL_SECTION, SCAL_X, SCAL_Z, SCAL_Z_LOW, SCAL_Z_HIGH, SCAL_LENGTHS = range(7)
TILE = 512


def gradient_tiles(left, right_ref, own_ref, oth_ref, at):
    turned, half = left.T, right_ref.shape[1] // 2
    for part, out_ref in enumerate((own_ref, oth_ref)):
        for first in range(0, half, TILE):
            width = min(TILE, half - first)
            piece = dot_nn(turned, right_ref[:, part * half + first : part * half + first + width])
            out_ref[:, at + first : at + first + width] = piece.astype(BF)
    return at + half


def gradients_kernel(*refs):
    *pairs, own_ref, oth_ref = refs
    at = 0
    for left_ref, right_ref in zip(pairs[::2], pairs[1::2]):
        at = gradient_tiles(left_ref[...], right_ref, own_ref, oth_ref, at)


def gradients(pairs, held=()):
    columns = sum(right.shape[1] // 2 for _, right in pairs)
    width = pairs[0][0].shape[1]
    return flat_call(
        gradients_kernel,
        [Far(v) if any(v is h for h in held) else v for pair in pairs for v in pair],
        [shape_of(width, columns)] * 2,
        flops=sum(2 * left.size * right.shape[1] for left, right in pairs), megabytes=9,
    )


def late_kernel(
    scal_ref, normed_ref, packed_ref, g2_ref, before_ref, even_ref, odd_ref, ede_ref, edo_ref, edh_ref,
    windows_ref, mh_ref, va_ref, vb_ref, vc_ref, ve_ref, vf_ref, own_ref, oth_ref, own_stem_ref, oth_stem_ref, stem_ref, *,
    channels,
):
    gradient_tiles(normed_ref[...], packed_ref, own_ref, oth_ref, 0)
    turned, width = g2_ref[...].T, g2_ref.shape[1]
    for n, ref in enumerate((before_ref, even_ref, odd_ref)):
        stem_ref[:, n * width : (n + 1) * width] = dot_nn(turned, ref[...]).astype(BF)
    windows = windows_ref[...].T
    first = dot_nn(windows[: 3 * LANES], ede_ref[...]) + dot_nn(windows[LANES:], edo_ref[...])
    first = first + dot_nn(mh_ref[...].T, edh_ref[...])
    vectors = [
        vf_ref[0:1], ve_ref[2:3], ve_ref[0:1], vf_ref[1:2], ve_ref[3:4], ve_ref[1:2],
        va_ref[0:1], vb_ref[0:1], vc_ref[0:1], va_ref[1:2], vb_ref[1:2], vc_ref[1:2],
        jnp.zeros((4, width), F32),
    ]
    taps = [first[n * LANES : n * LANES + channels] for n in range(first.shape[0] // LANES)]
    first = jnp.concatenate([*taps, jnp.concatenate(vectors, axis=0)], axis=0)
    stem_ref[:, 3 * width :] = first.T.astype(BF)
    core, half = scal_ref[SCAL_CORE], stem_ref.shape[1] // 2
    block = 16
    groups = width // (4 * block)
    for part, out_ref in enumerate((own_stem_ref, oth_stem_ref)):
        bit = core if part == 0 else 1 - core
        for group in range(groups):
            for section in range(2):
                source = pl.multiple_of(group * 4 * block + bit * 2 * block + section * block, block)
                rows = stem_ref[pl.ds(source, block), :]
                to = (section * groups + group) * 2 * block
                out_ref[to : to + block, :] = rows[:, :half]
                out_ref[to + block : to + 2 * block, :] = rows[:, half:]


def halves(scal_ref, bit, groups, size, total, keep_ref, send_ref, columns=slice(None)):
    for group in range(groups):
        for place, out_ref in ((scal_ref[bit], keep_ref), (1 - scal_ref[bit], send_ref)):
            source = pl.ds(pl.multiple_of((group * 2 + place) * size, size), size)
            out_ref[group * size : (group + 1) * size, columns] = total(source)


def first_kernel(scal_ref, *refs, cut, block):
    *parts, am_ref, as_ref, bm_ref, bg_ref = refs
    if len(parts) == 2:
        parts = [ref.at[:, span] for ref in parts for span in (slice(0, cut), slice(cut, None))]
        parts = [parts[0], parts[2], parts[1], parts[3]]
    low_own, low_got, high_own, high_got = parts
    low = lambda rows: low_own[rows, :] + low_got[rows, :]
    high = lambda rows: high_own[rows, :] + high_got[rows, :]
    rows = low_own.shape[0]
    halves(scal_ref, SCAL_X, rows // (2 * block), block, low, am_ref, as_ref)
    halves(scal_ref, SCAL_SECTION, 1, rows // 2, high, bm_ref, bg_ref)


def second_kernel(
    scal_ref, am_ref, ag_ref, bm_ref, bg_ref, akeep_ref, asend_ref, bkeep_ref, bsend_ref, *, block
):
    low = lambda rows: am_ref[rows, :] + ag_ref[rows, :]
    high = lambda rows: bm_ref[rows, :] + bg_ref[rows, :]
    rows = am_ref.shape[0]
    halves(scal_ref, SCAL_SECTION, 1, rows // 2, low, akeep_ref, asend_ref)
    halves(scal_ref, SCAL_X, rows // (2 * block), block, high, bkeep_ref, bsend_ref)


def third_kernel(scal_ref, am_ref, ag_ref, bm_ref, bg_ref, *out_refs, cut, block):
    for flip, out_ref in enumerate(out_refs):
        rows = pl.ds(pl.multiple_of((scal_ref[SCAL_Z] ^ flip) * block, block), block)
        out_ref[:, :cut] = am_ref[rows, :] + ag_ref[rows, :]
        out_ref[:, cut:] = bm_ref[rows, :] + bg_ref[rows, :]


def third_half_kernel(scal_ref, am_ref, ag_ref, bm_ref, bg_ref, keep_ref, send_ref, *, cut, block):
    low = lambda rows: am_ref[rows, :] + ag_ref[rows, :]
    high = lambda rows: bm_ref[rows, :] + bg_ref[rows, :]
    groups = am_ref.shape[0] // (2 * block)
    halves(scal_ref, SCAL_Z_LOW, groups, block, low, keep_ref, send_ref, slice(0, cut))
    halves(scal_ref, SCAL_Z_LOW, groups, block, high, keep_ref, send_ref, slice(cut, None))


def fourth_half_kernel(scal_ref, mine_ref, got_ref, keep_ref, send_ref, *, block):
    both = lambda rows: mine_ref[rows, :] + got_ref[rows, :]
    halves(scal_ref, SCAL_Z_HIGH, 1, block, both, keep_ref, send_ref)


def last_kernel(*refs, widths):
    count = len(refs) - len(widths)
    at = 0
    for out_ref, width in zip(refs[count:], widths):
        total = sum(ref[:, at : at + width].astype(F32) for ref in refs[:count])
        out_ref[...] = total
        at += width


def stem_last_kernel(scal_ref, mine_ref, got_ref, second_ref, first_ref, *vec_refs):
    mine, got = mine_ref[...], got_ref[...]
    lower = scal_ref[SCAL_SECTION] == 0
    block = mine.shape[0] // 2
    parts = []
    for half in (jnp.where(lower, mine, got), jnp.where(lower, got, mine)):
        parts.append(jnp.concatenate([half[:block], half[block:]], axis=1))
    full = jnp.concatenate(parts, axis=0)
    count, _, width = second_ref.shape
    channels = first_ref.shape[2]
    for n in range(count):
        second_ref[n] = full[:, n * width : (n + 1) * width]
        first_ref[n] = full[:, count * width + n * channels : count * width + (n + 1) * channels]
    turned = full[:, full.shape[1] - 2 * HEAD_DIM :].T
    at = turned.shape[0] - 16
    for n, ref in enumerate(vec_refs):
        ref[...] = turned[at + 3 * n : at + 3 * n + 3]


def sum_over_chips(own, oth, scal, cut, widths, direct=False):
    after = lambda value, other: value if other is None else tie(value, other)
    if not isinstance(own, tuple):
        own, oth = (own,), (oth,)
    parts = [v for mine, other in zip(own, oth) for v in (mine, swap(other, "tensor"))]
    rows, columns = own[0].shape[0], sum(v.shape[1] for v in own)
    block = rows // (2 * lax.axis_size("dp"))
    some = lambda n, w: shape_of(n, w)
    left, right = cut, columns - cut
    am, asend, bm, bsend = flat_call(
        functools.partial(first_kernel, cut=cut, block=block), parts,
        [some(rows // 2, left)] * 2 + [some(rows // 2, right)] * 2, scal, megabytes=6,
    )
    am = after(am, (yield am))
    ag, bg = flip_bit(asend, "dp", 1), swap(bsend, "section")
    am, asend, bm, bsend = flat_call(
        functools.partial(second_kernel, block=block), [am, ag, bm, bg],
        [some(rows // 4, left)] * 2 + [some(rows // 4, right)] * 2, scal, megabytes=6,
    )
    am = after(am, (yield am))
    ag, bg = swap(asend, "section"), flip_bit(bsend, "dp", 1)
    if direct:
        mine, *send = flat_call(
            functools.partial(third_kernel, cut=cut, block=block), [am, ag, bm, bg],
            [some(block, columns)] * (rows // (4 * block)), scal, megabytes=6,
        )
        mine = after(mine, (yield mine))
        got = [flip_bit(v, "dp", 2 * (n + 1)) for n, v in enumerate(send)]
    else:
        mine, send = flat_call(
            functools.partial(third_half_kernel, cut=cut, block=block), [am, ag, bm, bg],
            [some(2 * block, columns)] * 2, scal, megabytes=6,
        )
        mine = after(mine, (yield mine))
        mine, send = flat_call(
            functools.partial(fourth_half_kernel, block=block), [mine, flip_bit(send, "dp", 2)],
            [some(block, columns)] * 2, scal, megabytes=6,
        )
        mine = after(mine, (yield mine))
        got = [flip_bit(send, "dp", 4)]
    yield flat_call(
        functools.partial(last_kernel, widths=widths), [mine, *got],
        [shape_of(block, width, F32) for width in widths], megabytes=6,
    )


def tie(value, *others):
    return lax.optimization_barrier((value, *others))[0]


def swap(value, axis):
    return lax.ppermute(value, axis, [(0, 1), (1, 0)])


def flip_bit(value, axis, bit):
    count = lax.axis_size(axis)
    return lax.ppermute(value, axis, [(i, i ^ bit) for i in range(count)])


def add_low(left, right):
    return (left.astype(F32) + right.astype(F32)).astype(BF)


def halve(value, dim, place, send):
    mine = lax.dynamic_index_in_dim(value, place, dim, keepdims=False)
    other = lax.dynamic_index_in_dim(value, 1 - place, dim, keepdims=False)
    return mine, send(other)


def reduce_blocks(value, names):
    section, clip_group = lax.axis_index("section"), lax.axis_index("dp")
    dims = list(names)
    order = [name for name, _ in sorted(names.items(), key=lambda item: item[1])]
    held = value
    for step, name in enumerate(order):
        dim = [n for n in dims if n in order[step:]].index(name)
        if name == "section":
            mine, got = halve(held, dim, section, functools.partial(swap, axis="section"))
        else:
            place = (clip_group // name) % 2
            mine, got = halve(held, dim, place, functools.partial(flip_bit, axis="dp", bit=name))
        held = mine.astype(F32) + got.astype(F32)
        if step < len(order) - 1:
            held = held.astype(BF)
    return held


def dp_bits():
    count, bits = lax.axis_size("dp"), []
    while count > 1:
        count //= 2
        bits.append(count)
    return bits


def sum_projections(value):
    rows, columns = value.shape
    bits = dp_bits()
    lead = (2,) * (1 + len(bits))
    half = columns // 256 * 128
    out = []
    for which, part in enumerate((value[:, :half], value[:, half:])):
        shaped = part.reshape(*lead, rows // 2 ** len(lead), part.shape[1])
        early = {"section": 1, bits[-1]: 0} if which == 0 else {"section": 0, bits[-1]: 1}
        names = {"section": early["section"]}
        for at, bit in enumerate(bits):
            names[bit] = early.get(bit, 2 + at)
        out.append(reduce_blocks(shaped, names))
    return jnp.concatenate(out, axis=1)


def sum_stem(value):
    rows, columns = value.shape
    bits = dp_bits()
    place = lax.axis_index("tensor")
    groups = 2 ** len(bits)
    block = rows // (groups * 2)
    shaped = value.reshape(groups, 2, block, columns)
    mine, got = halve(shaped, 1, place, functools.partial(swap, axis="tensor"))
    held = add_low(mine, got)
    half = columns // 256 * 128
    out = []
    for which, part in enumerate((held[:, :, :half], held[:, :, half:])):
        shaped = part.reshape(*((2,) * len(bits)), 2, block // 2, part.shape[2])
        names = {bit: 2 + at for at, bit in enumerate(bits)}
        names[bits[-1]] = which
        names["section"] = 1 - which
        out.append(reduce_blocks(shaped, names))
    mine = jnp.concatenate(out, axis=1)
    got = swap(mine, "section")
    first = lax.axis_index("section") == 0
    return jnp.concatenate(
        [jnp.where(first, mine, got), jnp.where(first, got, mine)], axis=0
    )


def core_sum(pairs):
    full = [dot_tn(left, right).astype(BF) for left, right in pairs]
    mine = jnp.concatenate([v[:, : v.shape[1] // 2] for v in full], axis=1)
    sent = jnp.concatenate([v[:, v.shape[1] // 2 :] for v in full], axis=1)
    return add_low(mine, swap(sent, "tensor"))


def sinusoid_table(count, width_all):
    step_size = math.log(10000.0) / (width_all // 2 - 1)
    rates = np.exp(-step_size * np.arange(width_all // 2))
    angles = np.arange(count)[:, None] * rates[None, :]
    return np.concatenate([np.sin(angles), np.cos(angles)], axis=1).astype(np.float32)


def pad_rows(value, rows):
    return jnp.pad(value, ((0, rows - value.shape[0]), (0, 0)))


def round_up(count):
    return -(-count // CHUNK) * CHUNK


def body(
    mel,
    conv_first,
    conv_second,
    enc_gain,
    enc_shift,
    enc_qkv,
    enc_proj,
    enc_up,
    enc_down,
    cross_kv,
    text,
    lengths,
    dec_gain,
    dec_shift,
    dec_qkv,
    dec_proj,
    cross_query,
    cross_proj,
    dec_up,
    dec_down,
    cotangent,
):
    section = lax.axis_index("section")
    place = lax.axis_index("tensor")
    cores = lax.axis_size("tensor")
    width = text.shape[2]
    frames = mel.shape[1] // 2
    valid = frames // cores
    rows = round_up(valid)
    slots = text.shape[1]
    text_rows = round_up(slots)
    channels = mel.shape[2]

    group = lax.axis_index("dp")
    bits = [place, section, group % 2, group // 2, group // 2 % 2, group // 4 % 2]
    scal = jnp.concatenate([jnp.stack([bit.astype(jnp.int32) for bit in bits]), lengths])
    pair = lambda w: (w, swap(w, "tensor"))
    w_dqkv, w_eqkv, w_eproj, w_dproj, w_cq = map(pair, (dec_qkv, enc_qkv, enc_proj, dec_proj, cross_query))
    w_eup, w_edown, w_ckv = map(pair, (enc_up, enc_down, cross_kv))
    w_cproj, w_dup, w_ddown = map(pair, (cross_proj, dec_up, dec_down))
    early = [w[1] for w in (w_eproj, w_dproj, w_cq, w_cproj)]
    late = [w[1] for w in (w_eup, w_edown, w_ckv, w_dup, w_ddown)]
    eg, es = [enc_gain[i : i + 1] for i in range(3)], [enc_shift[i : i + 1] for i in range(3)]
    dg, ds = [dec_gain[i : i + 1] for i in range(3)], [dec_shift[i : i + 1] for i in range(3)]

    taps = conv_first.shape[0] * channels
    depth = -(-(taps + 12) // LANES) * LANES
    second = conv_second.reshape(-1, width)
    table = np.pad(sinusoid_table(frames, width), ((0, rows - valid), (0, 0)))
    table = jnp.asarray(np.stack([table[valid * core : valid * core + rows] for core in range(cores)]))

    dn_a, dq_self, dkv_self = rows_call(
        qkv_kernel, text_rows, [Clip(text)], [dg[0], ds[0], *w_dqkv],
        [(width, BF, Far), (width, BF), (2 * width, BF)], flops=2 * text_rows * width * 3 * width, scal=scal,
    )
    dkv_self_r = swap(dkv_self, "tensor")

    mel_rows = 2 * frames + 8 + 2 * (rows - valid) + 16
    even, odd, before, ge, go, gs, x0, gh, windows, halo = rows_call(
        functools.partial(stem_fwd_kernel, valid=valid), rows, [Far(table, 1, True)],
        [Far(jnp.swapaxes(mel, 1, 2)), Far(conv_first), Far(second)],
        [(width, BF, Far)] * 6 + [(width, F32)],
        sums=[((16, width), F32), ((rows, 4 * LANES), BF, Far), ((16, 3 * LANES), BF)],
        scratch=[pltpu.VMEM((8, width), F32), pltpu.VMEM((mel_rows, LANES), F32)],
        flops=2 * rows * width * 2000, scal=scal, told=True, megabytes=14,
    )
    en_a, eq, ekv = rows_call(
        qkv_kernel, rows, [tie(x0, dq_self, *early)], [eg[0], es[0], *w_eqkv],
        [(width, BF, Far), (width, BF), (2 * width, BF)], flops=2 * rows * width * 3 * width,
    )
    ekv_r = swap(ekv, "tensor")

    datt, drest, dstat = attention_fwd(dq_self, dkv_self, dkv_self_r, slots, scal)
    eq = tie(eq, datt)
    eatt, erest, estat = attention_fwd(eq, ekv, ekv_r, valid)
    units = 2 * enc_up.shape[1]
    x1, x2, en_b, ehid, eslope, memory, ckv = rows_call(
        enc_mid_kernel, rows, [x0, tie(eatt, *late)],
        [eg[1], es[1], eg[2], es[2], *w_eproj, *w_eup, *w_edown, *w_ckv],
        [
            (width, F32, Far), (width, F32, Far), (width, BF, Far), (units, BF, Far), (units, BF, Far),
            (width, BF, Far), (2 * width, BF),
        ],
        flops=2 * rows * width * (3 * width + 2 * units), megabytes=20,
    )
    ckv_r = swap(ckv, "tensor")
    y1, dn_b, cq = rows_call(
        dec_mid_kernel, text_rows, [Clip(text), tie(datt, ckv)], [dg[1], ds[1], *w_dproj, *w_cq],
        [(width, F32), (width, BF, Far), (width, BF)], flops=2 * text_rows * width * 2 * width, scal=scal,
    )

    crossed, crest, cstat = attention_fwd(cq, ckv, ckv_r, valid)
    dec_units = 2 * dec_up.shape[1]
    top_outs = [
        (width, BF), (dec_units, BF), (dec_units, BF), (width, BF), (width, BF), (width, BF), (width, F32),
    ]
    owned = lambda kind: shape_of(slots, width // 2, kind)
    decoded, decoded_sent, dn_c, dhid, dpre, dgb3, dgb2, dcrossed, u2, sums_c = flat_call(
        functools.partial(dec_top_kernel, valid=slots),
        [y1, crossed, Clip(cotangent), dg[2], ds[2], *w_cproj, *w_dup, *w_ddown],
        [owned(BF), owned(BF)] + [shape_of(text_rows, w, k) for w, k in top_outs] + [shape_of(8, width, F32)],
        scal=scal, scratch=[pltpu.VMEM((text_rows, dec_units), BF)],
        flops=2 * text_rows * width * (2 * width + 4 * dec_units), megabytes=12,
    )
    fast = lax.axis_size("dp") == 8 and width % (4 * 8 * 16) == 0
    top_pairs = [(dn_c, dpre), (dgb3, dhid), (dgb2, crossed)]
    top_widths = [dec_up.shape[1], dec_down.shape[0], cross_proj.shape[0]]
    if fast:
        own, oth = gradients(top_pairs)
        top_steps = sum_over_chips(own, oth, scal, sum(top_widths) // 2, top_widths)
        dcrossed = tie(dcrossed, own)
    dcq, dckv, dckv_r = attention_bwd(cq, ckv, ckv_r, crossed, crest, cstat, dcrossed, valid)
    if fast:
        dcq = tie(dcq, next(top_steps))
    dckv_got = swap(dckv_r, "tensor")
    u1, dgb1, ddatt, sums_b = rows_call(
        dec_back_kernel, text_rows, [dcq, y1, u2], [dg[1], *w_cq, *w_dproj],
        [(width, F32), (width, BF, Far), (width, BF)], sums=[((8, width), F32)],
        flops=2 * text_rows * width * 2 * width,
    )
    dqs, dkvs, dkvs_r = attention_bwd(
        dq_self, dkv_self, dkv_self_r, datt, drest, dstat, ddatt, slots, scal
    )
    dkvs_got = swap(dkvs_r, "tensor")

    gkv, egb2, edpre, egb1, deatt, eu1, sums_e = rows_call(
        enc_back_kernel, rows, [tie(dckv, dqs), dckv_got, x2, x1, eslope],
        [eg[2], eg[1], *w_ckv, *w_eup, *w_edown, *w_eproj],
        [(2 * width, BF), (width, BF), (units, BF, Far), (width, BF), (width, BF), (width, F32, Far)],
        sums=[((8, width), F32)], flops=2 * rows * width * (3 * width + 2 * units), megabytes=13,
    )
    d_packed, sums_a, text_mine, text_sent = rows_call(
        dec_last_kernel, text_rows, [dqs, dkvs, dkvs_got, Clip(text), tie(u1, deatt)], [dg[0], *w_dqkv],
        [(2 * dec_qkv.shape[1], BF)],
        sums=[((8, width), F32), ((slots, width // 2), F32), ((slots, width // 2), BF)],
        flops=2 * text_rows * width * 3 * width, scal=scal, told=True,
    )
    owners_got = swap(jnp.concatenate([decoded_sent, text_sent], axis=0), "section")
    mid_pairs = [
        (dn_a, d_packed), (dn_b, dcq), (dgb1, datt), (egb1, eatt), (memory, gkv), (en_b, edpre), (egb2, ehid),
    ]
    mid_widths = [dec_qkv.shape[1], cross_query.shape[1], dec_proj.shape[0], enc_proj.shape[0]]
    mid_widths += [cross_kv.shape[1], enc_up.shape[1], enc_down.shape[0]]
    if fast:
        mid_pairs[0] = (dn_a, tie(d_packed, top_steps.send(d_packed)))
        own, oth = gradients(mid_pairs, [memory, en_b, edpre, ehid])
        mid_steps = sum_over_chips(own, oth, scal, sum(mid_widths) // 2, mid_widths)
        waits = [
            lambda: (own,), lambda: (top_steps.send(base_a),), lambda: (next(mid_steps),)
        ]
    else:
        waits = [lambda: ()] * 3

    pairs = width // (2 * HEAD_DIM)
    half = pairs // 2
    deatt = tie(deatt, *waits[0]())
    side = (eatt, erest, estat)
    base_a, dekv_a = attention_bwd_side(
        eq, ekv_r, *side, deatt, valid, pairs=(half + 1, pairs - 1)
    )
    deatt = tie(deatt, base_a, *waits[1]())
    base_b, dekv_r = attention_bwd_side(
        eq, ekv_r, *side, deatt, valid, pairs=(half, 1), earlier=(dekv_a,)
    )
    dekv_got = swap(dekv_r, "tensor")
    deatt = tie(deatt, base_b, *waits[2]())
    deq, dekv = attention_bwd_side(eq, ekv, *side, deatt, valid, (base_a, base_b), turn=half + 1)
    e_packed, g2, ede, edo, sums_f, edh = rows_call(
        stem_back_kernel, rows, [deq, dekv, dekv_got, x0, eu1, ge, go, gs],
        [eg[0], *w_eqkv, second, gh],
        [(2 * enc_qkv.shape[1], BF), (width, BF), (width, BF), (width, BF)],
        sums=[((8, width), F32), ((16, width), BF)], scratch=[pltpu.VMEM((8, width), F32)],
        reverse=True, flops=2 * rows * width * 6 * width,
    )
    sums, end = [sums_a, sums_b, sums_c, sums_e, sums_f], ()
    if fast:
        stem_width = 3 * width + depth
        late_columns = (enc_qkv.shape[1], enc_qkv.shape[1], stem_width // 2, stem_width // 2)
        own, oth, own_stem, oth_stem = flat_call(
            functools.partial(late_kernel, channels=channels),
            [
                en_a, tie(e_packed, top_steps.send(e_packed)), g2, before, even, odd, ede, edo, edh, windows, halo,
                *sums,
            ],
            [shape_of(width, columns) for columns in late_columns], scal=scal, scratch=[pltpu.VMEM((width, stem_width), BF)],
            flops=2 * rows * width * (3 * width + 3 * width + 2 * depth), megabytes=10,
        )
        own = tie(own, mid_steps.send(own))
        late_steps = sum_over_chips(
            (own, own_stem), (oth, oth_stem), scal, enc_qkv.shape[1], [enc_qkv.shape[1], stem_width // 2], True
        )
        top_sums = top_steps.send(next(late_steps))
        later = mid_steps.send(top_sums[0])
        later = mid_steps.send(late_steps.send(later))
        later = late_steps.send(later)
        end = (later,)
        mid_sums = mid_steps.send(later)
        late_qkv, stem = late_steps.send(mid_sums[0])
        block = 2 * width // (2 * lax.axis_size("dp") * cores)
        conv_second_grad, conv_first_grad, *vec = flat_call(
            stem_last_kernel, [stem, swap(stem, "section")],
            [
                jax.ShapeDtypeStruct((conv_second.shape[0], block, width), F32),
                jax.ShapeDtypeStruct((conv_first.shape[0], block, channels), F32),
            ] + [shape_of(3, block, F32)] * 4,
            scal=scal, megabytes=6,
        )
        conv_second_grad = conv_second_grad.transpose(0, 2, 1)
        conv_first_grad = conv_first_grad.transpose(0, 2, 1)
    else:
        cuts = lambda value, widths: jnp.split(value, list(np.cumsum(widths)[:-1]), axis=1)
        top_sums = cuts(sum_projections(core_sum(top_pairs)), top_widths)
        mid_sums = cuts(sum_projections(core_sum(mid_pairs)), mid_widths)
        late_qkv = sum_projections(core_sum([(en_a, e_packed)]))
        first_t = dot_tn(ede, windows[:, : 3 * LANES]) + dot_tn(edo, windows[:, LANES:]) + dot_tn(edh, halo)
        first_t = first_t.reshape(width, -1, LANES)[:, :, :channels].reshape(width, taps)
        vectors = jnp.concatenate(
            [
                sums_f[0:1], sums_e[2:3], sums_e[0:1], sums_f[1:2], sums_e[3:4], sums_e[1:2],
                sums_a[0:1], sums_b[0:1], sums_c[0:1], sums_a[1:2], sums_b[1:2], sums_c[1:2],
            ],
            axis=0,
        )
        stem = [dot_tn(g2, act) for act in (before, even, odd)] + [first_t, vectors.T]
        stem.append(jnp.zeros((width, depth - taps - vectors.shape[0]), F32))
        stem = sum_stem(jnp.concatenate([v.astype(BF) for v in stem], axis=1)).T
        conv_second_grad, conv_first_grad = stem[: 3 * width], stem[3 * width : 3 * width + taps]
        vec = [stem[3 * width + taps + 3 * n : 3 * width + taps + 3 * n + 3] for n in range(4)]

    owned = [jax.ShapeDtypeStruct((2, *text_mine.shape), kind) for kind in (BF, F32)]
    decoded, text_grad = flat_call(
        owners_kernel, [decoded, tie(text_mine, *end), owners_got], owned, scal=scal, megabytes=4
    )

    d_up, d_down_t, d_cproj_t = top_sums
    d_qkv, d_cq, d_proj_t, e_proj_t, e_kv, e_up, e_down_t = mid_sums
    return (
        decoded,
        text_grad,
        conv_first_grad.reshape(*conv_first.shape[:2], -1),
        conv_second_grad.reshape(*conv_second.shape[:2], -1),
        vec[0],
        vec[1],
        late_qkv,
        e_proj_t.T,
        e_up,
        e_down_t.T,
        e_kv,
        vec[2],
        vec[3],
        d_qkv,
        d_proj_t.T,
        d_cq,
        d_cproj_t.T,
        d_up,
        d_down_t.T,
    )


def solution(mesh):
    in_specs = (
        P("dp", None, None),
        P(),
        P(),
        P(),
        P(),
        P(None, "tensor"),
        P("tensor", None),
        P(None, "tensor"),
        P("tensor", None),
        P(None, "tensor"),
        P("dp", "tensor", None),
        P("dp"),
        P(),
        P(),
        P(None, "tensor"),
        P("tensor", None),
        P(None, "tensor"),
        P("tensor", None),
        P(None, "tensor"),
        P("tensor", None),
        P("dp", "tensor", None),
    )
    out_specs = (
        P("dp", "tensor", "section"),
        P("dp", "tensor", "section"),
        P(None, None, ("dp", "tensor")),
        P(None, None, ("dp", "tensor")),
        P(None, ("dp", "tensor")),
        P(None, ("dp", "tensor")),
        P(("section", "dp"), "tensor"),
        P("tensor", ("section", "dp")),
        P(("section", "dp"), "tensor"),
        P("tensor", ("section", "dp")),
        P(("section", "dp"), "tensor"),
        P(None, ("dp", "tensor")),
        P(None, ("dp", "tensor")),
        P(("section", "dp"), "tensor"),
        P("tensor", ("section", "dp")),
        P(("section", "dp"), "tensor"),
        P("tensor", ("section", "dp")),
        P(("section", "dp"), "tensor"),
        P("tensor", ("section", "dp")),
    )
    return jax.shard_map(body, mesh=mesh, in_specs=in_specs, out_specs=out_specs, check_vma=False)
```
